128 devices in a mesh: grp: 4 (over x_hi, core), dp: 32 (over z, y, x_lo).
Axes of the slice: x: 4 (x_hi: 2, x_lo: 2; x = x_hi * 2 + x_lo), y: 4, z: 4, core: 2. Of those that a mesh axis runs over, the one named last changes fastest.
Arguments:
- tokens: bfloat16 [16384, 2048], P(('grp', 'dp')), may hold values from -6 to 6
- cotangent: bfloat16 [16384, 2048], P(('grp', 'dp')), may hold values from -6 to 6
- segment_ids: int32 [16384], P(('grp', 'dp')), may hold values from 0 to 15, as said below
- positions: int32 [16384], P(('grp', 'dp')), may hold values from 0 to 127, as said below
- padding: int32 [16384], P(('grp', 'dp')), may hold values from 0 to 1, as said below
- attn_gain: float32 [2048], replicated, may hold values from 0.5 to 1.5
- query_weight: float32 [2048, 2048], P('dp'), may hold values from -0.125 to 0.125
- key_weight: float32 [2048, 256], P('dp'), may hold values from -0.125 to 0.125
- value_weight: float32 [2048, 256], P('dp'), may hold values from -0.125 to 0.125
- output_weight: float32 [2048, 2048], P('dp'), may hold values from -0.5 to 0.5
- mlp_gain: float32 [2048], replicated, may hold values from 0.5 to 1.5
- gate_weight: float32 [2048, 5632], P('dp'), may hold values from -0.125 to 0.125
- up_weight: float32 [2048, 5632], P('dp'), may hold values from -0.125 to 0.125
- down_weight: float32 [5632, 2048], P('dp'), may hold values from -0.078125 to 0.078125
- attn_moment: float32 [2048], replicated, may hold values from -96 to 96
- query_moment: float32 [2048, 2048], P('dp', 'grp'), may hold values from -96 to 96
- key_moment: float32 [2048, 256], P('dp', 'grp'), may hold values from -96 to 96
- value_moment: float32 [2048, 256], P('dp', 'grp'), may hold values from -1536 to 1536
- output_moment: float32 [2048, 2048], P('dp', 'grp'), may hold values from -96 to 96
- mlp_moment: float32 [2048], replicated, may hold values from -96 to 96
- gate_moment: float32 [2048, 5632], P('dp', 'grp'), may hold values from -96 to 96
- up_moment: float32 [2048, 5632], P('dp', 'grp'), may hold values from -96 to 96
- down_moment: float32 [5632, 2048], P('dp', 'grp'), may hold values from -96 to 96
Outputs:
- block_output: bfloat16 [16384, 2048], P(('grp', 'dp'))
- input_grad: float32 [16384, 2048], P(('grp', 'dp'))
- attn_momentum: float32 [2048], replicated
- query_momentum: float32 [2048, 2048], P('dp', 'grp')
- key_momentum: float32 [2048, 256], P('dp', 'grp')
- value_momentum: float32 [2048, 256], P('dp', 'grp')
- output_momentum: float32 [2048, 2048], P('dp', 'grp')
- mlp_momentum: float32 [2048], replicated
- gate_momentum: float32 [2048, 5632], P('dp', 'grp')
- up_momentum: float32 [2048, 5632], P('dp', 'grp')
- down_momentum: float32 [5632, 2048], P('dp', 'grp')
- attn_updated: float32 [2048], replicated
- query_updated: float32 [2048, 2048], P('dp')
- key_updated: float32 [2048, 256], P('dp')
- value_updated: float32 [2048, 256], P('dp')
- output_updated: float32 [2048, 2048], P('dp')
- mlp_updated: float32 [2048], replicated
- gate_updated: float32 [2048, 5632], P('dp')
- up_updated: float32 [2048, 5632], P('dp')
- down_updated: float32 [5632, 2048], P('dp')
The draws below stay inside these ranges and needn't reach their ends.
Inputs may be any that keep to these rules, and one draw needn't show every extreme that they name: `segment_ids`: within each sequence of 128 tokens the segment numbers start at 0, never fall, and rise by one only at tokens whose place in the sequence is a multiple of 8. `positions`: A token's place in its document, 0 at each document's first token. `padding`: padding stands at the end of a sequence, at most 17 tokens of it.
All inputs are finite; a program needn't handle non-finite values.
Results may differ from the reference program's by a relative error of at most 0.028.
Values may be sent and summed in bfloat16 or wider, within the bound.
No kernel may reach another device: no remote copies, remote signals or barrier semaphores. Data moves between devices by JAX's collectives and lax.ppermute only.
A program may use at most 384 MiB of HBM per device.

```python
import math
import jax
import jax.numpy as jnp
from jax import lax

D = 2048
HEADS = 32
KV_HEADS = 4
HEAD_DIM = 64
FF = 5632
TOK_DEV = 128
QD = 2048
KVD = 256
TOKENS = 16384


def document_layout(key):
    seq_count = TOKENS // TOK_DEV
    block_count = TOK_DEV // 8
    column_index = jnp.arange(TOK_DEV, dtype=jnp.int32)
    row_ids = jnp.arange(seq_count, dtype=jnp.int32)[:, None]
    chosen = jax.random.randint(jax.random.fold_in(key, 41), (), 0, seq_count)
    crowded = (chosen + 1) % seq_count
    block_starts = jax.random.randint(jax.random.fold_in(key, 42), (seq_count, block_count), 0, max(2, TOK_DEV // 32)) == 0
    block_starts = jnp.logical_or(block_starts, row_ids == crowded)
    block_starts = jnp.logical_and(block_starts, row_ids != chosen)
    starts = jnp.logical_and(jnp.repeat(block_starts, 8, axis=1), (column_index % 8 == 0)[None, :])
    starts = jnp.logical_or(starts, column_index[None, :] == 0)
    segments = jnp.cumsum(starts.astype(jnp.int32), axis=1) - 1
    first_place = lax.cummax(jnp.where(starts, column_index[None, :], 0), axis=1)
    places = column_index[None, :] - first_place
    pad_tail = jax.random.randint(jax.random.fold_in(key, 43), (seq_count, 1), 1, TOK_DEV // 8 + 2)
    pad_tail = jnp.where(row_ids == chosen, 0, pad_tail)
    real_tokens = (column_index[None, :] < TOK_DEV - pad_tail).astype(jnp.int32)
    return (segments.reshape(-1), places.reshape(-1), real_tokens.reshape(-1))


def draw_segment_ids(key, part):
    layout = document_layout(key)
    return layout[0]


def draw_positions(key, part):
    layout = document_layout(key)
    return layout[1]


def draw_padding(key, part):
    layout = document_layout(key)
    return layout[2]


def shard_levels(key, shape, cuts, smallest, top_value):
    level = 1.0
    for position, shards_of in cuts:
        draws = jax.random.uniform(jax.random.fold_in(jax.random.fold_in(key, 6), position), (shards_of,), jnp.float32, smallest / len(cuts), top_value / len(cuts))
        level = level * jnp.repeat(jnp.exp(draws), shape[position] // shards_of).reshape((-1,) + (1,) * (len(shape) - 1 - position))
    return level


def noise(own_key, shape, scale, bound, shards=(), kind=jnp.bfloat16):
    level = shard_levels(own_key, shape, shards, -0.22, 0.18) if shards else 1.0
    values = jax.random.normal(own_key, shape, jnp.float32) * scale * level
    return jnp.minimum(jnp.maximum(values, -bound), bound).astype(kind)


def setup_inputs(seed: int = 0) -> dict:
    key_of = jax.random.split(jax.random.key(seed), 24)
    tokens = noise(key_of[0], (TOKENS, D), 1.0, 6.0, ((0, 128),))
    cotangent = noise(key_of[1], (TOKENS, D), 1.0, 6.0, ((0, 128),))
    segment_ids = draw_segment_ids(jax.random.fold_in(key_of[23], 71), 0)
    positions = draw_positions(jax.random.fold_in(key_of[23], 71), 0)
    padding = draw_padding(jax.random.fold_in(key_of[23], 71), 0)
    attn_gain = jnp.clip(1.0 + 0.1 * jax.random.normal(key_of[5], (D,), jnp.float32), 0.5, 1.5)
    query_weight = noise(key_of[6], (D, QD), D ** -0.5, 0.125, ((0, 32),), jnp.float32)
    key_weight = noise(key_of[7], (D, KVD), D ** -0.5, 0.125, ((0, 32),), jnp.float32)
    value_weight = noise(key_of[8], (D, KVD), D ** -0.5, 0.125, ((0, 32),), jnp.float32)
    output_weight = noise(key_of[9], (QD, D), (QD // 16) ** -0.5, 0.5, ((0, 32),), jnp.float32)
    mlp_gain = jnp.clip(1.0 + 0.1 * jax.random.normal(key_of[10], (D,), jnp.float32), 0.5, 1.5)
    gate_weight = noise(key_of[11], (D, FF), D ** -0.5, 0.125, ((0, 32),), jnp.float32)
    up_weight = noise(key_of[12], (D, FF), D ** -0.5, 0.125, ((0, 32),), jnp.float32)
    down_weight = noise(key_of[13], (FF, D), FF ** -0.5, 0.078125, ((0, 32),), jnp.float32)
    attn_moment = noise(key_of[14], (D,), 16.0, 96.0, (), jnp.float32)
    query_moment = noise(key_of[15], (D, QD), 16.0, 96.0, ((0, 32), (1, 4)), jnp.float32)
    key_moment = noise(key_of[16], (D, KVD), 16.0, 96.0, ((0, 32), (1, 4)), jnp.float32)
    value_moment = noise(key_of[17], (D, KVD), 256.0, 1536.0, ((0, 32), (1, 4)), jnp.float32)
    output_moment = noise(key_of[18], (QD, D), 16.0, 96.0, ((0, 32), (1, 4)), jnp.float32)
    mlp_moment = noise(key_of[19], (D,), 16.0, 96.0, (), jnp.float32)
    gate_moment = noise(key_of[20], (D, FF), 16.0, 96.0, ((0, 32), (1, 4)), jnp.float32)
    up_moment = noise(key_of[21], (D, FF), 16.0, 96.0, ((0, 32), (1, 4)), jnp.float32)
    down_moment = noise(key_of[22], (FF, D), 16.0, 96.0, ((0, 32), (1, 4)), jnp.float32)
    return dict(tokens=tokens, cotangent=cotangent, segment_ids=segment_ids, positions=positions, padding=padding, attn_gain=attn_gain, query_weight=query_weight, key_weight=key_weight, value_weight=value_weight, output_weight=output_weight, mlp_gain=mlp_gain, gate_weight=gate_weight, up_weight=up_weight, down_weight=down_weight, attn_moment=attn_moment, query_moment=query_moment, key_moment=key_moment, value_moment=value_moment, output_moment=output_moment, mlp_moment=mlp_moment, gate_moment=gate_moment, up_moment=up_moment, down_moment=down_moment)


epsilon = 1e-05
learn_rate = 0.005
score_scale = 0.125

@jax.custom_vjp
def low(v):
    return lax.optimization_barrier(v.astype(jnp.bfloat16)).astype(jnp.float32)

@jax.custom_vjp
def low_back(v):
    return v

def low_keep(v):
    return (low(v), None)

def low_pass(kept, grad):
    return (grad,)

def back_keep(v):
    return (v, None)

def back_low(kept, grad):
    return (low(grad),)
low.defvjp(low_keep, low_pass)
low_back.defvjp(back_keep, back_low)

def normalize(values, gain):
    return values * lax.rsqrt(lax.optimization_barrier(jnp.mean(values * values, axis=-1, keepdims=True)) + epsilon) * gain

def rotary_tables(places):
    half = HEAD_DIM // 2
    freq = 10000.0 ** (-(jnp.arange(half, dtype=jnp.float32) * 2.0 / HEAD_DIM))
    angles = places.astype(jnp.float32)[..., None] * freq
    cosine = jnp.concatenate([jnp.cos(angles), jnp.cos(angles)], axis=-1)
    sine = jnp.concatenate([jnp.sin(angles), jnp.sin(angles)], axis=-1)
    return (cosine, sine)

def rotate(values, cosine, sine):
    half = values.shape[-1] // 2
    turned = jnp.concatenate([-values[..., half:], values[..., :half]], axis=-1)
    return values * cosine + turned * sine

def product(left, matrix):
    return jnp.einsum('btd,de->bte', left, matrix, precision=lax.Precision.HIGHEST)

def attention_mask(segments, padding):
    column_index = jnp.arange(TOK_DEV, dtype=jnp.int32)
    causal = column_index[None, :] <= column_index[:, None]
    diagonal = column_index[None, :] == column_index[:, None]
    same_doc = segments[:, :, None] == segments[:, None, :]
    keyed = jnp.logical_or(padding[:, None, :] == 1, diagonal[None])
    return jnp.logical_and(jnp.logical_and(same_doc, causal[None]), keyed)

def block_layer(inputs, weights, segments, places, padding):
    gain_one, query_mat, key_mat, value_mat, out_mat, gain_two, gate_mat, up_mat, down_mat = weights
    batch = inputs.shape[0]
    groups = HEADS // KV_HEADS
    first_low = low(normalize(inputs, gain_one))
    query_lin = low_back(product(first_low, query_mat)).reshape(batch, TOK_DEV, KV_HEADS, groups, HEAD_DIM)
    key_lin = low_back(product(first_low, key_mat)).reshape(batch, TOK_DEV, KV_HEADS, HEAD_DIM)
    value_low = low(low_back(product(first_low, value_mat))).reshape(batch, TOK_DEV, KV_HEADS, HEAD_DIM)
    cosine, sine = rotary_tables(places)
    query_rot = low(rotate(query_lin, cosine[:, :, None, None, :], sine[:, :, None, None, :]))
    key_rot = low(rotate(key_lin, cosine[:, :, None, :], sine[:, :, None, :]))
    raw_scores = jnp.einsum('bqkgd,bskd->bkgqs', query_rot, key_rot, precision=lax.Precision.HIGHEST)
    scores = low_back(raw_scores * score_scale)
    allowed = attention_mask(segments, padding)[:, None, None]
    masked = jnp.where(allowed, scores, -1e+30)
    row_max = lax.optimization_barrier(jnp.max(masked, axis=-1, keepdims=True))
    log_total = row_max + jnp.log(lax.optimization_barrier(jnp.sum(jnp.exp(masked - row_max), axis=-1, keepdims=True)))
    probs = low(jnp.exp(masked - log_total))
    attended = jnp.einsum('bkgqs,bskd->bqkgd', probs, value_low, precision=lax.Precision.HIGHEST)
    attended = low(low_back(attended)).reshape(batch, TOK_DEV, QD)
    middle = inputs + low_back(product(attended, out_mat))
    second_low = low(normalize(middle, gain_two))
    gate = low_back(product(second_low, gate_mat))
    upper = low_back(product(second_low, up_mat))
    activated = low(jax.nn.silu(gate) * upper)
    return middle + low_back(product(activated, down_mat))

def reference(tokens, cotangent, segment_ids, positions, padding, attn_gain, query_weight, key_weight, value_weight, output_weight, mlp_gain, gate_weight, up_weight, down_weight, attn_moment, query_moment, key_moment, value_moment, output_moment, mlp_moment, gate_moment, up_moment, down_moment):
    masters = (attn_gain, query_weight, key_weight, value_weight, output_weight, mlp_gain, gate_weight, up_weight, down_weight)
    moments = (attn_moment, query_moment, key_moment, value_moment, output_moment, mlp_moment, gate_moment, up_moment, down_moment)
    lowered = tuple((low(weight) for weight in masters))
    seq_count = TOKENS // TOK_DEV
    per_step = math.gcd(seq_count, max(1, 4096 // TOK_DEV))
    step_count = seq_count // per_step

    def blocked(values):
        return values.reshape((step_count, per_step, TOK_DEV) + values.shape[1:])
    starting = tuple((jnp.zeros(weight.shape, jnp.float32) for weight in masters))

    def advance(totals, block):
        rows_in, grads_in, segments, places, pads = block

        def forward(inputs, weights):
            return block_layer(inputs, weights, segments, places, pads)
        result, pull = jax.vjp(forward, rows_in, lowered)
        grad_rows, grad_weights = pull(grads_in)
        return (tuple((total + grad for total, grad in zip(totals, grad_weights))), (result.astype(jnp.bfloat16), grad_rows))
    totals, (results, grad_rows) = lax.scan(advance, starting, (blocked(tokens.astype(jnp.float32)), blocked(cotangent.astype(jnp.float32)), blocked(segment_ids), blocked(positions), blocked(padding)))
    moved = tuple((0.5 * moment + 0.5 * total for moment, total in zip(moments, totals)))
    updated = tuple((master - learn_rate * step for master, step in zip(masters, moved)))
    return (results.reshape(TOKENS, D), grad_rows.reshape(TOKENS, D), moved[0], moved[1], moved[2], moved[3], moved[4], moved[5], moved[6], moved[7], moved[8], updated[0], updated[1], updated[2], updated[3], updated[4], updated[5], updated[6], updated[7], updated[8])
```

```python
import jax
import jax.numpy as jnp
from jax import lax
from jax.sharding import PartitionSpec as P

D = 2048
HEAD_DIM = 64
GROUPS = 8
ROWS = 128
MEMBERS = 4
SLOTS = ROWS * MEMBERS
QW = 512
KW = 64
QKVW = QW + 2 * KW
FW = 1408
GUW = 2 * FW
PANEL = 512
DOWN_ROWS = 176
OUT_ROWS = 64
W_ROWS = 64

epsilon = 1e-05
learn_rate = 0.005
score_scale = 0.125

BF = jnp.bfloat16
F32 = jnp.float32


def dp_index(z, y, x):
    return z * 8 + y * 2 + x


PLANES = [[dp_index(z, y, x) for z in range(4) for y in range(4)] for x in range(2)]
SWAP_X = [(i, i ^ 1) for i in range(32)]
SWAP_CORE = [(m, m ^ 1) for m in range(4)]
SWAP_FAR = [(m, m ^ 2) for m in range(4)]
TURN = [
    (m * 32 + z * 8 + q, z * 32 + m * 8 + q) for m in range(4) for z in range(4) for q in range(8)
]


def ring(place, k):
    return [(i, i + ((i // place + k) % 4 - i // place % 4) * place) for i in range(32)]


RING_Z = [ring(8, k) for k in (1, 2, 3)]
RING_Y = [ring(2, k) for k in (1, 2, 3)]


def swap_x(v):
    return lax.ppermute(v, "dp", SWAP_X)


def swap_core(v):
    return lax.ppermute(v, "grp", SWAP_CORE)


def swap_far(v):
    return lax.ppermute(v, "grp", SWAP_FAR)


def turn(v):
    return lax.ppermute(v, ("grp", "dp"), TURN)


def plane_gather(v):
    return lax.all_gather(v, "dp", axis=0, tiled=True, axis_index_groups=PLANES)


def plane_scatter(v):
    return lax.psum_scatter(
        v, "dp", scatter_dimension=0, tiled=True, axis_index_groups=PLANES
    )


def group_gather(v):
    pair = jnp.concatenate([v, swap_far(v)], axis=0)
    return jnp.concatenate([pair, swap_core(pair)], axis=0)


def group_scatter(partial):
    half = 2 * ROWS
    near = partial[:half] + swap_core(partial[half:].astype(BF)).astype(F32)
    return near[:ROWS] + swap_far(near[ROWS:].astype(BF)).astype(F32)


def pair_x(v, low):
    other = swap_x(v)
    return jnp.concatenate([jnp.where(low, v, other), jnp.where(low, other, v)], axis=0)


def sum_x(v, low):
    rows = v.shape[0] // 2
    mine = jnp.where(low, v[:rows], v[rows:])
    theirs = jnp.where(low, v[rows:], v[:rows])
    return mine.astype(F32) + swap_x(theirs).astype(F32)


def dot(left, right):
    return jnp.dot(left, right, preferred_element_type=F32)


def left_product(left, right):
    return lax.dot_general(left, right, (((0,), (0,)), ((), ())), preferred_element_type=F32)


def right_product(left, right):
    return lax.dot_general(left, right, (((1,), (1,)), ((), ())), preferred_element_type=F32)


def rounded_gain(gain):
    return lax.optimization_barrier(gain.astype(BF)).astype(F32)


def inverse_rms(v):
    return lax.rsqrt(jnp.mean(v * v, axis=-1, keepdims=True) + epsilon)


def norm_back(v, gain, grad):
    r = inverse_rms(v)
    n = v * r
    scaled = grad * gain
    return r * (scaled - n * jnp.mean(scaled * n, axis=-1, keepdims=True)), n


def turned(v):
    half = HEAD_DIM // 2
    lane = lax.broadcasted_iota(jnp.int32, v.shape, v.ndim - 1) % HEAD_DIM
    return jnp.where(lane < half, -jnp.roll(v, -half, axis=-1), jnp.roll(v, half, axis=-1))


def on_device(
    tokens,
    cotangent,
    segment_ids,
    positions,
    padding,
    attn_gain,
    query_weight,
    key_weight,
    value_weight,
    output_weight,
    mlp_gain,
    gate_weight,
    up_weight,
    down_weight,
    attn_moment,
    query_moment,
    key_moment,
    value_moment,
    output_moment,
    mlp_moment,
    gate_moment,
    up_moment,
    down_moment,
):
    member = lax.axis_index("grp")
    low = (lax.axis_index("dp") % 2) == 0

    def mine(weight, width):
        return lax.dynamic_slice_in_dim(weight, member * width, width, 1).astype(BF)

    out_block = turn(mine(output_weight, QW))
    attn_shard = jnp.concatenate(
        [mine(query_weight, QW), mine(key_weight, KW), mine(value_weight, KW), out_block], axis=1
    )
    attn_full = plane_gather(pair_x(attn_shard, low))
    qkv_full = attn_full[:, :QKVW]
    out_full = attn_full[:, QKVW:].reshape(4, QW, PANEL)

    gu_shard = pair_x(
        jnp.concatenate([mine(gate_weight, FW), mine(up_weight, FW)], axis=1), low
    )
    down_shard = pair_x(turn(mine(down_weight, PANEL)), low)
    pieces = [gu_shard[:, j * PANEL : (j + 1) * PANEL] for j in range(5)]
    tail = gu_shard[:, 5 * PANEL :]
    pieces.append(jnp.concatenate([tail[:W_ROWS], tail[W_ROWS:]], axis=1))
    pieces.append(down_shard)
    mlp_full = plane_gather(jnp.concatenate(pieces, axis=0)).reshape(16, 1056, PANEL)
    gu_panels = [mlp_full[:, j * 128 : (j + 1) * 128].reshape(D, PANEL) for j in range(5)]
    last = mlp_full[:, 640:704]
    gu_panels.append(
        jnp.stack([last[:, :, :256], last[:, :, 256:]], axis=1).reshape(D, 256)
    )
    down_full = mlp_full[:, 704:].reshape(4, FW, PANEL)

    places = jnp.stack([segment_ids, positions, padding])
    places = group_gather(places[None])
    segments, spots, pads = places[:, 0], places[:, 1], places[:, 2]
    rows_in = group_gather(tokens)
    grads_in = group_gather(cotangent)

    first_gain = rounded_gain(attn_gain)
    second_gain = rounded_gain(mlp_gain)
    inputs = rows_in.astype(F32)
    n_first = inputs * inverse_rms(inputs)
    first_low = (n_first * first_gain).astype(BF)

    qkv = dot(first_low, qkv_full)
    half = HEAD_DIM // 2
    freq = 10000.0 ** (-(jnp.arange(half, dtype=F32) * 2.0 / HEAD_DIM))
    angles = spots.reshape(SLOTS, 1).astype(F32) * jnp.tile(freq, 2)[None]
    cosine, sine = jnp.cos(angles), jnp.sin(angles)
    cosine_q, sine_q = jnp.tile(cosine, (1, GROUPS)), jnp.tile(sine, (1, GROUPS))

    q_lin, k_lin = qkv[:, :QW], qkv[:, QW : QW + KW]
    query_rot = (q_lin * cosine_q + turned(q_lin) * sine_q).astype(BF)
    key_rot = (k_lin * cosine + turned(k_lin) * sine).astype(BF)
    value_low = qkv[:, QW + KW :].astype(BF)
    query_rot = query_rot.reshape(MEMBERS, ROWS, GROUPS, HEAD_DIM)
    key_rot = key_rot.reshape(MEMBERS, ROWS, HEAD_DIM)
    value_low = value_low.reshape(MEMBERS, ROWS, HEAD_DIM)

    column = jnp.arange(ROWS, dtype=jnp.int32)
    allowed = jnp.logical_and(
        jnp.logical_and(
            segments[:, :, None] == segments[:, None, :],
            (column[None, :] <= column[:, None])[None],
        ),
        jnp.logical_or(pads[:, None, :] == 1, (column[None, :] == column[:, None])[None]),
    )
    scores = jnp.einsum("bqgd,bsd->bgqs", query_rot, key_rot, preferred_element_type=F32)
    masked = jnp.where(allowed[:, None], scores * score_scale, -1e30)
    row_max = jnp.max(masked, axis=-1, keepdims=True)
    log_total = row_max + jnp.log(jnp.sum(jnp.exp(masked - row_max), axis=-1, keepdims=True))
    probs = jnp.exp(masked - log_total)
    probs_low = probs.astype(BF)
    attended = jnp.einsum("bgqs,bsd->bqgd", probs_low, value_low, preferred_element_type=F32)
    attended_low = attended.reshape(SLOTS, QW).astype(BF)

    out_part = jnp.concatenate([dot(attended_low, out_full[c]) for c in range(4)], axis=1)
    middle = tokens.astype(F32) + group_scatter(out_part)
    second_low = (middle * inverse_rms(middle) * second_gain).astype(BF)
    second_all = group_gather(second_low)

    gu = jnp.concatenate([dot(second_all, panel) for panel in gu_panels], axis=1)
    gate, up = gu[:, :FW], gu[:, FW:]
    sig = 1.0 / (1.0 + jnp.exp(-gate))
    silu = gate * sig
    active = (silu * up).astype(BF)
    down_part = jnp.concatenate([dot(active, down_full[c]) for c in range(4)], axis=1)
    block_output = (middle + group_scatter(down_part)).astype(BF)

    grad_product = sum(
        right_product(grads_in[:, c * PANEL : (c + 1) * PANEL], down_full[c]) for c in range(4)
    )
    grad_gate = (grad_product * up * sig * (1.0 + gate * (1.0 - sig))).astype(BF)
    grad_up = (grad_product * silu).astype(BF)
    grad_gu = jnp.concatenate([grad_gate, grad_up], axis=1)

    cuts = [grad_gu[:, j * PANEL : (j + 1) * PANEL] for j in range(5)] + [grad_gu[:, 5 * PANEL :]]
    sends = [left_product(second_all, cut).astype(BF) for cut in cuts]
    send = [block.reshape(16, 128, PANEL) for block in sends[:5]]
    tail = sends[5].reshape(16, 2, W_ROWS, 256)
    send.append(jnp.concatenate([tail[:, 0], tail[:, 1]], axis=2))
    grad_down = jnp.concatenate(
        [left_product(active, grads_in[:, c * PANEL : (c + 1) * PANEL]) for c in range(4)], axis=0
    ).astype(BF)
    send.append(grad_down.reshape(16, 2 * DOWN_ROWS, PANEL))
    mlp_sum = plane_scatter(jnp.concatenate(send, axis=1).reshape(16 * 1056, PANEL))

    grad_second = sum(right_product(cut, panel) for cut, panel in zip(cuts, gu_panels))
    grad_second = group_scatter(grad_second)
    back, n_second = norm_back(middle, second_gain, grad_second)
    mlp_gain_part = jnp.sum(grad_second * n_second, axis=0)
    grad_middle = cotangent.astype(F32) + back
    middle_all = group_gather(grad_middle.astype(BF))

    grad_out = jnp.concatenate(
        [
            left_product(attended_low, middle_all[:, c * PANEL : (c + 1) * PANEL])
            for c in range(4)
        ],
        axis=0,
    )
    grad_attended = sum(
        right_product(middle_all[:, c * PANEL : (c + 1) * PANEL], out_full[c]) for c in range(4)
    ).astype(BF)
    grad_attended = grad_attended.reshape(MEMBERS, ROWS, GROUPS, HEAD_DIM)

    grad_value = jnp.einsum(
        "bgqs,bqgd->bsd", probs_low, grad_attended, preferred_element_type=F32
    )
    grad_probs = jnp.einsum(
        "bqgd,bsd->bgqs", grad_attended, value_low, preferred_element_type=F32
    )
    grad_scores = (
        probs * (grad_probs - jnp.sum(grad_probs * probs, axis=-1, keepdims=True))
    ).astype(BF)
    grad_query = (
        jnp.einsum("bgqs,bsd->bqgd", grad_scores, key_rot, preferred_element_type=F32) * score_scale
    ).reshape(SLOTS, QW)
    grad_key = (
        jnp.einsum("bgqs,bqgd->bsd", grad_scores, query_rot, preferred_element_type=F32)
        * score_scale
    ).reshape(SLOTS, KW)
    grad_query = grad_query * cosine_q - turned(grad_query) * sine_q
    grad_key = grad_key * cosine - turned(grad_key) * sine
    grad_qkv = jnp.concatenate(
        [grad_query.astype(BF), grad_key.astype(BF), grad_value.reshape(SLOTS, KW).astype(BF)],
        axis=1,
    )

    qkv_send = left_product(first_low, grad_qkv)
    attn_sum = plane_scatter(
        jnp.concatenate([qkv_send.astype(BF), grad_out.astype(BF)], axis=1)
    )

    grad_first = right_product(grad_qkv, qkv_full)
    attn_gain_part = jnp.sum(grad_first * n_first, axis=0)
    grad_first = group_scatter(grad_first)
    back, _ = norm_back(tokens.astype(F32), first_gain, grad_first)
    input_grad = grad_middle + back

    gains = jnp.stack([attn_gain_part, mlp_gain_part])
    for ring in (RING_Z, RING_Y):
        gains = gains + sum(lax.ppermute(gains, "dp", pairs) for pairs in ring)
    gains = gains + swap_x(gains)
    gains = gains + swap_far(gains)
    gains = gains + swap_core(gains)

    gu_rows = sum_x(
        jnp.concatenate(
            [mlp_sum[j * 128 : (j + 1) * 128] for j in range(5)]
            + [jnp.concatenate([mlp_sum[640:704, :256], mlp_sum[640:704, 256:]], axis=0)],
            axis=1,
        ),
        low,
    )
    down_rows = turn(sum_x(mlp_sum[704:], low).astype(BF)).astype(F32)
    attn_rows = sum_x(attn_sum, low)
    out_rows = turn(attn_rows[:, QKVW:].astype(BF)).astype(F32)

    def step(moment, total):
        return 0.5 * moment + 0.5 * total

    gate_momentum = step(gate_moment, gu_rows[:, :FW])
    up_momentum = step(up_moment, gu_rows[:, FW:])
    down_momentum = step(down_moment, down_rows)
    query_momentum = step(query_moment, attn_rows[:, :QW])
    key_momentum = step(key_moment, attn_rows[:, QW : QW + KW])
    value_momentum = step(value_moment, attn_rows[:, QW + KW : QKVW])
    output_momentum = step(output_moment, out_rows)

    mine_at = (member // 2) + 2 * (member % 2)

    def spread(momentum):
        rows, width = momentum.shape
        slots = group_gather(momentum.astype(BF)).reshape(MEMBERS, rows, width)
        return [
            lax.dynamic_index_in_dim(slots, mine_at ^ at, 0, keepdims=False) for at in (0, 2, 1, 3)
        ]

    def updated(weight, columns, start, width):
        moved = jnp.concatenate([block[:, start : start + width] for block in columns], axis=1)
        return weight - learn_rate * moved.astype(F32)

    attn_moved = spread(
        jnp.concatenate(
            [query_momentum, key_momentum, value_momentum, output_momentum], axis=1
        )
    )
    gu_moved = spread(jnp.concatenate([gate_momentum, up_momentum], axis=1))
    down_moved = spread(down_momentum)

    gains = 0.5 * jnp.stack([attn_moment, mlp_moment]) + 0.5 * gains
    return (
        block_output,
        input_grad,
        gains[0],
        query_momentum,
        key_momentum,
        value_momentum,
        output_momentum,
        gains[1],
        gate_momentum,
        up_momentum,
        down_momentum,
        attn_gain - learn_rate * gains[0],
        updated(query_weight, attn_moved, 0, QW),
        updated(key_weight, attn_moved, QW, KW),
        updated(value_weight, attn_moved, QW + KW, KW),
        updated(output_weight, attn_moved, QKVW, PANEL),
        mlp_gain - learn_rate * gains[1],
        updated(gate_weight, gu_moved, 0, FW),
        updated(up_weight, gu_moved, FW, FW),
        updated(down_weight, down_moved, 0, PANEL),
    )


def solution(mesh):
    rows = P(("grp", "dp"), None)
    flat = P(("grp", "dp"))
    weight = P("dp", None)
    moment = P("dp", "grp")
    whole = P()
    weights = (whole,) + (weight,) * 4 + (whole,) + (weight,) * 3
    moments = (whole,) + (moment,) * 4 + (whole,) + (moment,) * 3
    return jax.shard_map(
        on_device,
        mesh=mesh,
        in_specs=(rows, rows, flat, flat, flat) + weights + moments,
        out_specs=(rows, rows) + moments + weights,
        check_vma=False,
    )
```

```python
import jax
import jax.numpy as jnp
from jax import lax
from jax.experimental import pallas as pl
from jax.experimental.pallas import tpu as pltpu
from jax.sharding import PartitionSpec as P

D = 2048
HEAD_DIM = 64
GROUPS = 8
ROWS = 128
MEMBERS = 4
SLOTS = ROWS * MEMBERS
QW = 512
KW = 64
QKVW = QW + 2 * KW
FW = 1408
GUW = 2 * FW
PANEL = 512
DOWN_ROWS = 176
OUT_ROWS = 64
W_ROWS = 64

epsilon = 1e-05
learn_rate = 0.005
score_scale = 0.125

BF = jnp.bfloat16
F32 = jnp.float32


def dp_index(z, y, x):
    return z * 8 + y * 2 + x


PLANES = [[dp_index(z, y, x) for z in range(4) for y in range(4)] for x in range(2)]
SWAP_X = [(i, i ^ 1) for i in range(32)]
SWAP_CORE = [(m, m ^ 1) for m in range(4)]
SWAP_FAR = [(m, m ^ 2) for m in range(4)]
TURN = [
    (m * 32 + z * 8 + q, z * 32 + m * 8 + q) for m in range(4) for z in range(4) for q in range(8)
]
TURN_X = [(a, b ^ 1) for a, b in TURN]
SWAP_FAR_X = [(m * 32 + i, (m ^ 2) * 32 + (i ^ 1)) for m in range(4) for i in range(32)]


def ring(place, k):
    return [(i, i + ((i // place + k) % 4 - i // place % 4) * place) for i in range(32)]


RING_Z = [ring(8, k) for k in (1, 2, 3)]
RING_Y = [ring(2, k) for k in (1, 2, 3)]


def swap_x(v):
    return lax.ppermute(v, "dp", SWAP_X)


def swap_core(v):
    return lax.ppermute(v, "grp", SWAP_CORE)


def swap_far(v):
    return lax.ppermute(v, "grp", SWAP_FAR)


def turn(v):
    return lax.ppermute(v, ("grp", "dp"), TURN)


def turn_pair(v, low):
    own = turn(v)
    other = lax.ppermute(v, ("grp", "dp"), TURN_X)
    return jnp.concatenate([jnp.where(low, own, other), jnp.where(low, other, own)], axis=0)


def plane_gather(v):
    return lax.all_gather(v, "dp", axis=0, tiled=True, axis_index_groups=PLANES)


def plane_scatter(v):
    return lax.psum_scatter(
        v, "dp", scatter_dimension=0, tiled=True, axis_index_groups=PLANES
    )


def group_gather(v):
    pair = jnp.concatenate([v, swap_far(v)], axis=0)
    return jnp.concatenate([pair, swap_core(pair)], axis=0)


def group_scatter(partial):
    half = 2 * ROWS
    near = partial[:half] + swap_core(partial[half:].astype(BF)).astype(F32)
    return near[:ROWS] + swap_far(near[ROWS:].astype(BF)).astype(F32)


def pair_x(v, low):
    other = swap_x(v)
    return jnp.concatenate([jnp.where(low, v, other), jnp.where(low, other, v)], axis=0)


def sum_x(v, low):
    rows = v.shape[0] // 2
    mine = jnp.where(low, v[:rows], v[rows:])
    theirs = jnp.where(low, v[rows:], v[:rows])
    return mine.astype(F32) + swap_x(theirs).astype(F32)


def dot(left, right):
    return jnp.dot(left, right, preferred_element_type=F32)


def left_product(left, right):
    return lax.dot_general(left, right, (((0,), (0,)), ((), ())), preferred_element_type=F32)


def right_product(left, right):
    return lax.dot_general(left, right, (((1,), (1,)), ((), ())), preferred_element_type=F32)


def tail_in(full, tail, sems):
    return [pltpu.make_async_copy(full.at[:, pl.ds(640,64), pl.ds(256*h,256)], tail.at[:, pl.ds(64*h,64), :], sems.at[h]) for h in range(2)]

def mlp_kernel(s_ref, st_ref, c_ref, panel_ref, full, ggu_ref, act_ref, send,
               down, tail, gpan, gtail, gdown, in_sem, tail_sem, pan_sem, out_sem):
    j = pl.program_id(0)
    loads = [pltpu.make_async_copy(full.at[4*c+y, pl.ds(704,352), :], down.at[c, pl.ds(352*y,352), :], in_sem.at[4*c+y]) for c in range(4) for y in range(4)]
    tails = tail_in(full, tail, tail_sem)
    @pl.when(j == 0)
    def _():
        for l in loads: l.start()
        for t in tails: t.start()

    def panel_out(slot, at):
        return pltpu.make_async_copy(gpan.at[slot], send.at[:, pl.ds(128*at,128), :], pan_sem.at[slot])

    def block(weights, start, width):
        h = dot(s_ref[...], weights)
        gate, up = h[:, :width], h[:, width:]
        @pl.when(j == 0)
        def _():
            for l in loads: l.wait()
        prod = right_product(c_ref[:, :PANEL], down[0, pl.ds(start,width), :])
        for c in range(1,4):
            prod += right_product(c_ref[:, c*PANEL:(c+1)*PANEL], down[c, pl.ds(start,width), :])
        sig = 1.0/(1.0+jnp.exp(-gate))
        silu = gate*sig
        act = (silu*up).astype(BF)
        grad = jnp.concatenate([(prod*up*sig*(1.0+gate*(1.0-sig))).astype(BF),(prod*silu).astype(BF)],axis=1)
        ggu_ref[:, :2*width] = grad
        act_ref[:, :width] = act
        for c in range(4):
            gdown[c, pl.ds(start,width), :] = left_product(act, c_ref[:, c*PANEL:(c+1)*PANEL]).astype(BF)
        return dot(st_ref[...], grad).astype(BF)

    @pl.when(j < 5)
    def _():
        slot = lax.rem(j, 2)
        g = block(panel_ref[...].reshape(2048, PANEL), pl.multiple_of(256*j, 256), 256)
        @pl.when(j >= 2)
        def _():
            panel_out(slot, j-2).wait()
        gpan[slot] = g.reshape(16,128,PANEL)
        panel_out(slot, j).start()

    @pl.when(j == 5)
    def _():
        for t in tails: t.wait()
        g = block(tail[...].reshape(2048,256), 1280, 128)
        gtail[...] = g.reshape(16,128,256)
        outs = [pltpu.make_async_copy(gtail.at[:, pl.ds(64*h,64), :], send.at[:, pl.ds(640,64), pl.ds(256*h,256)], tail_sem.at[h]) for h in range(2)]
        outs += [pltpu.make_async_copy(gdown.at[c, pl.ds(352*y,352), :], send.at[4*c+y, pl.ds(704,352), :], out_sem.at[4*c+y]) for c in range(4) for y in range(4)]
        for o in outs: o.start()
        panel_out(1, 3).wait()
        panel_out(0, 4).wait()
        for o in outs: o.wait()

def whole(shape):
    return pl.BlockSpec(shape, lambda j: (0,)*len(shape), pipeline_mode=pl.Buffered(1))

def mlp_grads(s, st, cot, full):
    return pl.pallas_call(
        mlp_kernel, grid=(6,),
        in_specs=[whole((512,2048)), whole((2048,512)), whole((512,2048)),
                  pl.BlockSpec((16,128,PANEL), lambda j: (0, jnp.minimum(j,4), 0)),
                  pl.BlockSpec(memory_space=pl.ANY)],
        out_specs=[pl.BlockSpec((512,512), lambda j: (0,j)), pl.BlockSpec((512,256), lambda j:(0,j)), pl.BlockSpec(memory_space=pl.ANY)],
        out_shape=[jax.ShapeDtypeStruct((512,3072),BF), jax.ShapeDtypeStruct((512,1536),BF), jax.ShapeDtypeStruct((16,1056,PANEL),BF)],
        scratch_shapes=[pltpu.VMEM((4,FW,PANEL),BF), pltpu.VMEM((16,128,256),BF), pltpu.VMEM((2,16,128,PANEL),BF),
                        pltpu.VMEM((16,128,256),BF), pltpu.VMEM((4,FW,PANEL),BF),
                        pltpu.SemaphoreType.DMA((16,)), pltpu.SemaphoreType.DMA((2,)), pltpu.SemaphoreType.DMA((2,)), pltpu.SemaphoreType.DMA((16,))],
        compiler_params=pltpu.CompilerParams(vmem_limit_bytes=58*2**20, dimension_semantics=("arbitrary",)),
        cost_estimate=pl.CostEstimate(flops=18*10**9, bytes_accessed=45*10**6, transcendentals=10**6),
        name="mlp_grads",
    )(s, st, cot, full, full)

def second_kernel(g_ref, panel_ref, full, out_ref, tail, tail_sem):
    j = pl.program_id(0)
    tails = tail_in(full, tail, tail_sem)
    @pl.when(j == 0)
    def _():
        for t in tails: t.start()
        out_ref[...] = right_product(g_ref[...], panel_ref[...].reshape(2048,PANEL))
    @pl.when(jnp.logical_and(j > 0, j < 5))
    def _():
        out_ref[...] += right_product(g_ref[...], panel_ref[...].reshape(2048,PANEL))
    @pl.when(j == 5)
    def _():
        for t in tails: t.wait()
        out_ref[...] += right_product(g_ref[:, :256], tail[...].reshape(2048,256))

def second_grad(ggu, full):
    return pl.pallas_call(
        second_kernel, grid=(6,),
        in_specs=[pl.BlockSpec((512,512), lambda j:(0,j)), pl.BlockSpec((16,128,PANEL), lambda j: (0, jnp.minimum(j,4), 0)), pl.BlockSpec(memory_space=pl.ANY)],
        out_specs=pl.BlockSpec((512,2048), lambda j:(0,0)),
        out_shape=jax.ShapeDtypeStruct((512,2048),F32),
        scratch_shapes=[pltpu.VMEM((16,128,256),BF), pltpu.SemaphoreType.DMA((2,))],
        compiler_params=pltpu.CompilerParams(vmem_limit_bytes=40*2**20, dimension_semantics=("arbitrary",)),
        cost_estimate=pl.CostEstimate(flops=6*10**9, bytes_accessed=20*10**6, transcendentals=0),
        name="second_grad",
    )(ggu, full, full)


def rounded_gain(gain):
    return lax.optimization_barrier(gain.astype(BF)).astype(F32)


def inverse_rms(v):
    return lax.rsqrt(jnp.mean(v * v, axis=-1, keepdims=True) + epsilon)


def norm_back(v, gain, grad):
    r = inverse_rms(v)
    n = v * r
    scaled = grad * gain
    return r * (scaled - n * jnp.mean(scaled * n, axis=-1, keepdims=True)), n


def turned(v):
    half = HEAD_DIM // 2
    lane = lax.broadcasted_iota(jnp.int32, v.shape, v.ndim - 1) % HEAD_DIM
    return jnp.where(lane < half, -jnp.roll(v, -half, axis=-1), jnp.roll(v, half, axis=-1))


def panels(gate, up):
    blocks = []
    for at in range(0, FW, 256):
        blocks += [gate[:, at : at + 256], up[:, at : at + 256]]
    return jnp.concatenate(blocks, axis=1)


def unpanels(both):
    gate, up = [], []
    for at in range(0, FW, 256):
        width = min(256, FW - at)
        gate.append(both[:, 2 * at : 2 * at + width])
        up.append(both[:, 2 * at + width : 2 * at + 2 * width])
    return jnp.concatenate(gate, axis=1), jnp.concatenate(up, axis=1)


def on_device(
    tokens,
    cotangent,
    segment_ids,
    positions,
    padding,
    attn_gain,
    query_weight,
    key_weight,
    value_weight,
    output_weight,
    mlp_gain,
    gate_weight,
    up_weight,
    down_weight,
    attn_moment,
    query_moment,
    key_moment,
    value_moment,
    output_moment,
    mlp_moment,
    gate_moment,
    up_moment,
    down_moment,
):
    member = lax.axis_index("grp")
    low = (lax.axis_index("dp") % 2) == 0

    def mine(weight, width):
        return lax.dynamic_slice_in_dim(weight, member * width, width, 1).astype(BF)

    attn_shard = jnp.concatenate(
        [mine(query_weight, QW), mine(key_weight, KW), mine(value_weight, KW)], axis=1
    )
    attn_shard = jnp.concatenate(
        [pair_x(attn_shard, low), turn_pair(mine(output_weight, QW), low)], axis=1
    )
    attn_full = plane_gather(attn_shard)
    qkv_full = attn_full[:, :QKVW]
    out_full = attn_full[:, QKVW:].reshape(4, QW, PANEL)

    gu_shard = pair_x(panels(mine(gate_weight, FW), mine(up_weight, FW)), low)
    pieces = [gu_shard[:, j * PANEL : (j + 1) * PANEL] for j in range(5)]
    tail = gu_shard[:, 5 * PANEL :]
    pieces.append(jnp.concatenate([tail[:W_ROWS], tail[W_ROWS:]], axis=1))
    pieces.append(turn_pair(mine(down_weight, PANEL), low))
    mlp_full = plane_gather(jnp.concatenate(pieces, axis=0)).reshape(16, 1056, PANEL)

    places = jnp.stack([segment_ids, positions, padding])
    places = group_gather(places[None])
    segments, spots, pads = places[:, 0], places[:, 1], places[:, 2]
    rows_in = group_gather(tokens)
    grads_in = group_gather(cotangent)

    first_gain = rounded_gain(attn_gain)
    second_gain = rounded_gain(mlp_gain)
    inputs = rows_in.astype(F32)
    n_first = inputs * inverse_rms(inputs)
    first_low = (n_first * first_gain).astype(BF)

    qkv = dot(first_low, qkv_full)
    half = HEAD_DIM // 2
    freq = 10000.0 ** (-(jnp.arange(half, dtype=F32) * 2.0 / HEAD_DIM))
    angles = spots.reshape(SLOTS, 1).astype(F32) * jnp.tile(freq, 2)[None]
    cosine, sine = jnp.cos(angles), jnp.sin(angles)
    cosine_q, sine_q = jnp.tile(cosine, (1, GROUPS)), jnp.tile(sine, (1, GROUPS))

    q_lin, k_lin = qkv[:, :QW], qkv[:, QW : QW + KW]
    query_rot = (q_lin * cosine_q + turned(q_lin) * sine_q).astype(BF)
    key_rot = (k_lin * cosine + turned(k_lin) * sine).astype(BF)
    value_low = qkv[:, QW + KW :].astype(BF)
    query_rot = query_rot.reshape(MEMBERS, ROWS, GROUPS, HEAD_DIM)
    key_rot = key_rot.reshape(MEMBERS, ROWS, HEAD_DIM)
    value_low = value_low.reshape(MEMBERS, ROWS, HEAD_DIM)

    column = jnp.arange(ROWS, dtype=jnp.int32)
    allowed = jnp.logical_and(
        jnp.logical_and(
            segments[:, :, None] == segments[:, None, :],
            (column[None, :] <= column[:, None])[None],
        ),
        jnp.logical_or(pads[:, None, :] == 1, (column[None, :] == column[:, None])[None]),
    )
    scores = jnp.einsum("bqgd,bsd->bgqs", query_rot, key_rot, preferred_element_type=F32)
    masked = jnp.where(allowed[:, None], scores * score_scale, -1e30)
    row_max = jnp.max(masked, axis=-1, keepdims=True)
    log_total = row_max + jnp.log(jnp.sum(jnp.exp(masked - row_max), axis=-1, keepdims=True))
    probs = jnp.exp(masked - log_total)
    probs_low = probs.astype(BF)
    attended = jnp.einsum("bgqs,bsd->bqgd", probs_low, value_low, preferred_element_type=F32)
    attended_low = attended.reshape(SLOTS, QW).astype(BF)

    out_part = jnp.concatenate([dot(attended_low, out_full[c]) for c in range(4)], axis=1)
    middle = tokens.astype(F32) + group_scatter(out_part)
    second_low = (middle * inverse_rms(middle) * second_gain).astype(BF)
    second_all = group_gather(second_low)

    grad_gu, active, send = mlp_grads(second_all, second_all.T, grads_in, mlp_full)
    mlp_sum = plane_scatter(send.reshape(16 * 1056, PANEL))
    grad_second = second_grad(grad_gu, mlp_full)

    down_full = mlp_full[:, 704:].reshape(4, FW, PANEL)
    down_part = jnp.concatenate([dot(active[:, :FW], down_full[c]) for c in range(4)], axis=1)
    block_output = (middle + group_scatter(down_part)).astype(BF)

    grad_second = group_scatter(grad_second)
    back, n_second = norm_back(middle, second_gain, grad_second)
    mlp_gain_part = jnp.sum(grad_second * n_second, axis=0)
    grad_middle = cotangent.astype(F32) + back
    middle_all = group_gather(grad_middle.astype(BF))

    grad_out = jnp.concatenate(
        [
            left_product(attended_low, middle_all[:, c * PANEL : (c + 1) * PANEL])
            for c in range(4)
        ],
        axis=0,
    )
    grad_attended = sum(
        right_product(middle_all[:, c * PANEL : (c + 1) * PANEL], out_full[c]) for c in range(4)
    ).astype(BF)
    grad_attended = grad_attended.reshape(MEMBERS, ROWS, GROUPS, HEAD_DIM)

    grad_value = jnp.einsum(
        "bgqs,bqgd->bsd", probs_low, grad_attended, preferred_element_type=F32
    )
    grad_probs = jnp.einsum(
        "bqgd,bsd->bgqs", grad_attended, value_low, preferred_element_type=F32
    )
    grad_scores = (
        probs * (grad_probs - jnp.sum(grad_probs * probs, axis=-1, keepdims=True))
    ).astype(BF)
    grad_query = (
        jnp.einsum("bgqs,bsd->bqgd", grad_scores, key_rot, preferred_element_type=F32) * score_scale
    ).reshape(SLOTS, QW)
    grad_key = (
        jnp.einsum("bgqs,bqgd->bsd", grad_scores, query_rot, preferred_element_type=F32)
        * score_scale
    ).reshape(SLOTS, KW)
    grad_query = grad_query * cosine_q - turned(grad_query) * sine_q
    grad_key = grad_key * cosine - turned(grad_key) * sine
    grad_qkv = jnp.concatenate(
        [grad_query.astype(BF), grad_key.astype(BF), grad_value.reshape(SLOTS, KW).astype(BF)],
        axis=1,
    )

    qkv_send = left_product(first_low, grad_qkv)
    attn_sum = plane_scatter(
        jnp.concatenate([qkv_send.astype(BF), grad_out.astype(BF)], axis=1)
    )

    grad_first = right_product(grad_qkv, qkv_full)
    attn_gain_part = jnp.sum(grad_first * n_first, axis=0)
    grad_first = group_scatter(grad_first)
    back, _ = norm_back(tokens.astype(F32), first_gain, grad_first)
    input_grad = grad_middle + back

    gains = jnp.stack([attn_gain_part, mlp_gain_part])
    for ring in (RING_Z, RING_Y):
        gains = gains + sum(lax.ppermute(gains, "dp", pairs) for pairs in ring)
    gains = gains + swap_x(gains)
    gains = gains + swap_far(gains)
    gains = gains + swap_core(gains)

    qkv_part = attn_sum[:, :QKVW]
    out_part = turn(attn_sum[:, QKVW:])
    both = jnp.concatenate([qkv_part, out_part], axis=1)
    kept = jnp.where(low, both[:W_ROWS], both[W_ROWS:])
    given = jnp.where(low, both[W_ROWS:], both[:W_ROWS])
    own_total = kept.astype(F32) + swap_x(given).astype(F32)
    far_total = swap_far(kept).astype(F32) + lax.ppermute(
        given, ("grp", "dp"), SWAP_FAR_X
    ).astype(F32)
    totals = jnp.concatenate([own_total, far_total], axis=0).astype(BF)
    totals = jnp.concatenate([totals, swap_core(totals)], axis=0).astype(F32)
    own_moment = jnp.concatenate(
        [query_moment, key_moment, value_moment, output_moment], axis=1
    )
    moments = group_gather(own_moment.astype(BF)).astype(F32)
    own_moved = 0.5 * own_moment + 0.5 * own_total
    query_momentum = own_moved[:, :QW]
    key_momentum = own_moved[:, QW : QW + KW]
    value_momentum = own_moved[:, QW + KW : QKVW]
    output_momentum = own_moved[:, QKVW:]

    mine_at = (member // 2) + 2 * (member % 2)

    def in_order(slots):
        return [
            lax.dynamic_index_in_dim(slots, mine_at ^ at, 0, keepdims=False) for at in (0, 2, 1, 3)
        ]

    attn_moved = in_order((0.5 * moments + 0.5 * totals).reshape(MEMBERS, W_ROWS, QKVW + PANEL))

    gu_rows = sum_x(
        jnp.concatenate(
            [mlp_sum[j * 128 : (j + 1) * 128] for j in range(5)]
            + [jnp.concatenate([mlp_sum[640:704, :256], mlp_sum[640:704, 256:]], axis=0)],
            axis=1,
        ),
        low,
    )
    down_rows = turn(sum_x(mlp_sum[704:], low).astype(BF)).astype(F32)
    gate_rows, up_rows = unpanels(gu_rows)
    gate_momentum = 0.5 * gate_moment + 0.5 * gate_rows
    up_momentum = 0.5 * up_moment + 0.5 * up_rows
    down_momentum = 0.5 * down_moment + 0.5 * down_rows
    gu_moved = in_order(
        group_gather(jnp.concatenate([gate_momentum, up_momentum], axis=1).astype(BF)).reshape(
            MEMBERS, W_ROWS, GUW
        )
    )
    down_moved = in_order(
        group_gather(down_momentum.astype(BF)).reshape(MEMBERS, DOWN_ROWS, PANEL)
    )

    def updated(weight, columns, start, width):
        moved = jnp.concatenate([block[:, start : start + width] for block in columns], axis=1)
        return weight - learn_rate * moved.astype(F32)

    gains = 0.5 * jnp.stack([attn_moment, mlp_moment]) + 0.5 * gains
    return (
        block_output,
        input_grad,
        gains[0],
        query_momentum,
        key_momentum,
        value_momentum,
        output_momentum,
        gains[1],
        gate_momentum,
        up_momentum,
        down_momentum,
        attn_gain - learn_rate * gains[0],
        updated(query_weight, attn_moved, 0, QW),
        updated(key_weight, attn_moved, QW, KW),
        updated(value_weight, attn_moved, QW + KW, KW),
        updated(output_weight, attn_moved, QKVW, PANEL),
        mlp_gain - learn_rate * gains[1],
        updated(gate_weight, gu_moved, 0, FW),
        updated(up_weight, gu_moved, FW, FW),
        updated(down_weight, down_moved, 0, PANEL),
    )


def solution(mesh):
    rows = P(("grp", "dp"), None)
    flat = P(("grp", "dp"))
    weight = P("dp", None)
    moment = P("dp", "grp")
    whole = P()
    weights = (whole,) + (weight,) * 4 + (whole,) + (weight,) * 3
    moments = (whole,) + (moment,) * 4 + (whole,) + (moment,) * 3
    return jax.shard_map(
        on_device,
        mesh=mesh,
        in_specs=(rows, rows, flat, flat, flat) + weights + moments,
        out_specs=(rows, rows) + moments + weights,
        check_vma=False,
    )
```

```python
import jax
import jax.numpy as jnp
from jax import lax
from jax.experimental import pallas as pl
from jax.experimental.pallas import tpu as pltpu
from jax.sharding import PartitionSpec as P

D = 2048
HEAD_DIM = 64
GROUPS = 8
ROWS = 128
MEMBERS = 4
SLOTS = ROWS * MEMBERS
QW = 512
KW = 64
QKVW = QW + 2 * KW
FW = 1408
GUW = 2 * FW
PANEL = 512
DOWN_ROWS = 176
W_ROWS = 64

epsilon = 1e-05
learn_rate = 0.005
score_scale = 0.125

BF = jnp.bfloat16
F32 = jnp.float32

PLANES = [[z * 8 + y * 2 + x for z in range(4) for y in range(4)] for x in range(2)]
SWAP_X = [(i, i ^ 1) for i in range(32)]
SWAP_CORE = [(m, m ^ 1) for m in range(4)]
SWAP_FAR = [(m, m ^ 2) for m in range(4)]
SWAP_FAR_X = [(m * 32 + i, (m ^ 2) * 32 + (i ^ 1)) for m in range(4) for i in range(32)]
MZQ = [(m, z, q) for m in range(4) for z in range(4) for q in range(8)]


def spot(m, z, q):
    return m * 32 + z * 8 + q


TURN = [(spot(m, z, q), spot(z, m, q)) for m, z, q in MZQ]
TURN_X = [(spot(m, z, q), spot(z, m, q ^ 1)) for m, z, q in MZQ]
TURN_OUT = [[(spot(m, z, q), spot(z, (m + k) % 4, q)) for m, z, q in MZQ] for k in range(4)]
TURN_IN = [[(spot(m, z, q), spot((z + k) % 4, m, q)) for m, z, q in MZQ] for k in range(4)]


def ring(place, k):
    return [(i, i + ((i // place + k) % 4 - i // place % 4) * place) for i in range(32)]


RING_Z = [ring(8, k) for k in (1, 2, 3)]
RING_Y = [ring(2, k) for k in (1, 2, 3)]


def swap_x(v):
    return lax.ppermute(v, "dp", SWAP_X)


def swap_core(v):
    return lax.ppermute(v, "grp", SWAP_CORE)


def swap_far(v):
    return lax.ppermute(v, "grp", SWAP_FAR)


def everywhere(v, pairs):
    return lax.ppermute(v, ("grp", "dp"), pairs)


def plane_gather(v):
    return lax.all_gather(v, "dp", axis=0, tiled=True, axis_index_groups=PLANES)


def plane_scatter(v):
    return lax.psum_scatter(
        v, "dp", scatter_dimension=0, tiled=True, axis_index_groups=PLANES
    )


def ring_gather(v, pairs, at):
    rows = v.shape[0]
    out = jnp.zeros((4 * rows,) + v.shape[1:], v.dtype)
    for k, part in enumerate([v] + [lax.ppermute(v, "dp", p) for p in pairs]):
        out = lax.dynamic_update_slice_in_dim(out, part, lax.rem(at + 4 - k, 4) * rows, 0)
    return out


def ring_scatter(v, pairs, at, extra=None):
    rows = v.shape[0] // 4

    def chunk(k):
        part = lax.dynamic_slice_in_dim(v, lax.rem(at + k, 4) * rows, rows, 0)
        return part if extra is None else jnp.concatenate([part, extra], axis=1)

    total = chunk(0).astype(F32)
    for k, p in enumerate(pairs):
        total = total + lax.ppermute(chunk(k + 1), "dp", p).astype(F32)
    return total


def group_gather(v):
    pair = jnp.concatenate([v, swap_far(v)], axis=0)
    return jnp.concatenate([pair, swap_core(pair)], axis=0)


def group_scatter(partial):
    half = 2 * ROWS
    near = partial[:half] + swap_core(partial[half:].astype(BF)).astype(F32)
    return near[:ROWS] + swap_far(near[ROWS:].astype(BF)).astype(F32)


def in_order(own, other, low):
    return jnp.concatenate([jnp.where(low, own, other), jnp.where(low, other, own)], axis=0)


def pair_x(v, low):
    return in_order(v, swap_x(v), low)


def turn_pair(v, low):
    return in_order(everywhere(v, TURN), everywhere(v, TURN_X), low)


def halves(v, low):
    rows = v.shape[0] // 2
    return jnp.where(low, v[:rows], v[rows:]), jnp.where(low, v[rows:], v[:rows])


def two_parts(v):
    high = lax.reduce_precision(v, 8, 7)
    return jnp.concatenate([high.astype(BF), (v - high).astype(BF)], axis=0)


def one_part(v):
    rows = v.shape[0] // 2
    return v[:rows].astype(F32) + v[rows:].astype(F32)


def dot(left, right):
    return jnp.dot(left, right, preferred_element_type=F32)


def left_product(left, right):
    return lax.dot_general(left, right, (((0,), (0,)), ((), ())), preferred_element_type=F32)


def right_product(left, right):
    return lax.dot_general(left, right, (((1,), (1,)), ((), ())), preferred_element_type=F32)


def tail_in(full, tail, sems):
    return [pltpu.make_async_copy(full.at[:, pl.ds(640,64), pl.ds(256*h,256)], tail.at[:, pl.ds(64*h,64), :], sems.at[h]) for h in range(2)]

def mlp_kernel(s_ref, st_ref, c_ref, panel_ref, full, ggu_ref, act_ref, send,
               down, tail, gpan, gtail, gdown, in_sem, tail_sem, pan_sem, out_sem):
    j = pl.program_id(0)
    loads = [pltpu.make_async_copy(full.at[4*c+y, pl.ds(704,352), :], down.at[c, pl.ds(352*y,352), :], in_sem.at[4*c+y]) for c in range(4) for y in range(4)]
    tails = tail_in(full, tail, tail_sem)
    @pl.when(j == 0)
    def _():
        for l in loads: l.start()
        for t in tails: t.start()

    def panel_out(slot, at):
        return pltpu.make_async_copy(gpan.at[slot], send.at[:, pl.ds(128*at,128), :], pan_sem.at[slot])

    def block(weights, start, width):
        h = dot(s_ref[...], weights)
        gate, up = h[:, :width], h[:, width:]
        @pl.when(j == 0)
        def _():
            for l in loads: l.wait()
        prod = right_product(c_ref[:, :PANEL], down[0, pl.ds(start,width), :])
        for c in range(1,4):
            prod += right_product(c_ref[:, c*PANEL:(c+1)*PANEL], down[c, pl.ds(start,width), :])
        sig = 1.0/(1.0+jnp.exp(-gate))
        silu = gate*sig
        act = (silu*up).astype(BF)
        grad = jnp.concatenate([(prod*up*sig*(1.0+gate*(1.0-sig))).astype(BF),(prod*silu).astype(BF)],axis=1)
        ggu_ref[:, :2*width] = grad
        act_ref[:, :width] = act
        for c in range(4):
            gdown[c, pl.ds(start,width), :] = left_product(act, c_ref[:, c*PANEL:(c+1)*PANEL]).astype(BF)
        return dot(st_ref[...], grad).astype(BF)

    @pl.when(j < 5)
    def _():
        slot = lax.rem(j, 2)
        g = block(panel_ref[...].reshape(2048, PANEL), pl.multiple_of(256*j, 256), 256)
        @pl.when(j >= 2)
        def _():
            panel_out(slot, j-2).wait()
        gpan[slot] = g.reshape(16,128,PANEL)
        panel_out(slot, j).start()

    @pl.when(j == 5)
    def _():
        for t in tails: t.wait()
        g = block(tail[...].reshape(2048,256), 1280, 128)
        gtail[...] = g.reshape(16,128,256)
        outs = [pltpu.make_async_copy(gtail.at[:, pl.ds(64*h,64), :], send.at[:, pl.ds(640,64), pl.ds(256*h,256)], tail_sem.at[h]) for h in range(2)]
        outs += [pltpu.make_async_copy(gdown.at[c, pl.ds(352*y,352), :], send.at[4*c+y, pl.ds(704,352), :], out_sem.at[4*c+y]) for c in range(4) for y in range(4)]
        for o in outs: o.start()
        panel_out(1, 3).wait()
        panel_out(0, 4).wait()
        for o in outs: o.wait()

def whole(shape):
    return pl.BlockSpec(shape, lambda j: (0,)*len(shape), pipeline_mode=pl.Buffered(1))

def mlp_grads(s, st, cot, full):
    return pl.pallas_call(
        mlp_kernel, grid=(6,),
        in_specs=[whole((512,2048)), whole((2048,512)), whole((512,2048)),
                  pl.BlockSpec((16,128,PANEL), lambda j: (0, jnp.minimum(j,4), 0)),
                  pl.BlockSpec(memory_space=pl.ANY)],
        out_specs=[pl.BlockSpec((512,512), lambda j: (0,j)), pl.BlockSpec((512,256), lambda j:(0,j)), pl.BlockSpec(memory_space=pl.ANY)],
        out_shape=[jax.ShapeDtypeStruct((512,3072),BF), jax.ShapeDtypeStruct((512,1536),BF), jax.ShapeDtypeStruct((16,1056,PANEL),BF)],
        scratch_shapes=[pltpu.VMEM((4,FW,PANEL),BF), pltpu.VMEM((16,128,256),BF), pltpu.VMEM((2,16,128,PANEL),BF),
                        pltpu.VMEM((16,128,256),BF), pltpu.VMEM((4,FW,PANEL),BF),
                        pltpu.SemaphoreType.DMA((16,)), pltpu.SemaphoreType.DMA((2,)), pltpu.SemaphoreType.DMA((2,)), pltpu.SemaphoreType.DMA((16,))],
        compiler_params=pltpu.CompilerParams(vmem_limit_bytes=58*2**20, dimension_semantics=("arbitrary",)),
        cost_estimate=pl.CostEstimate(flops=18*10**9, bytes_accessed=45*10**6, transcendentals=10**6),
        name="mlp_grads",
    )(s, st, cot, full, full)

def second_kernel(g_ref, panel_ref, full, out_ref, tail, tail_sem):
    j = pl.program_id(0)
    tails = tail_in(full, tail, tail_sem)
    @pl.when(j == 0)
    def _():
        for t in tails: t.start()
        out_ref[...] = right_product(g_ref[...], panel_ref[...].reshape(2048,PANEL))
    @pl.when(jnp.logical_and(j > 0, j < 5))
    def _():
        out_ref[...] += right_product(g_ref[...], panel_ref[...].reshape(2048,PANEL))
    @pl.when(j == 5)
    def _():
        for t in tails: t.wait()
        out_ref[...] += right_product(g_ref[:, :256], tail[...].reshape(2048,256))

def second_grad(ggu, full):
    return pl.pallas_call(
        second_kernel, grid=(6,),
        in_specs=[pl.BlockSpec((512,512), lambda j:(0,j)), pl.BlockSpec((16,128,PANEL), lambda j: (0, jnp.minimum(j,4), 0)), pl.BlockSpec(memory_space=pl.ANY)],
        out_specs=pl.BlockSpec((512,2048), lambda j:(0,0)),
        out_shape=jax.ShapeDtypeStruct((512,2048),F32),
        scratch_shapes=[pltpu.VMEM((16,128,256),BF), pltpu.SemaphoreType.DMA((2,))],
        compiler_params=pltpu.CompilerParams(vmem_limit_bytes=40*2**20, dimension_semantics=("arbitrary",)),
        cost_estimate=pl.CostEstimate(flops=6*10**9, bytes_accessed=20*10**6, transcendentals=0),
        name="second_grad",
    )(ggu, full, full)


def down_kernel(act_ref, down_ref, out_ref):
    out_ref[...] = dot(act_ref[...], down_ref[...].reshape(FW, PANEL))


def down_product(active, full):
    return pl.pallas_call(
        down_kernel,
        grid=(4,),
        in_specs=[whole((SLOTS, FW)), pl.BlockSpec((4, 352, PANEL), lambda c: (c, 2, 0))],
        out_specs=pl.BlockSpec((SLOTS, PANEL), lambda c: (0, c)),
        out_shape=jax.ShapeDtypeStruct((SLOTS, D), F32),
        compiler_params=pltpu.CompilerParams(vmem_limit_bytes=32 * 2**20),
        cost_estimate=pl.CostEstimate(
            flops=3 * 10**9, bytes_accessed=12 * 10**6, transcendentals=0
        ),
        name="down_product",
    )(active, full)


LANES = 128


def lanes_of(v):
    return lax.broadcasted_iota(jnp.int32, v.shape, v.ndim - 1)


def quarter_turn(v):
    first = lanes_of(v) % HEAD_DIM < HEAD_DIM // 2
    return jnp.where(first, -pltpu.roll(v, 96, 1), pltpu.roll(v, 32, 1))


def doubled(v):
    left = lanes_of(v) < HEAD_DIM
    other = pltpu.roll(v, HEAD_DIM, 1)
    return jnp.where(left, v, other), jnp.where(left, other, v)


def head_rows(ref):
    blocks = []
    for g in range(GROUPS // 2):
        v = ref[:, g * LANES : (g + 1) * LANES].astype(F32)
        left = lanes_of(v) < HEAD_DIM
        blocks += [jnp.where(left, v, 0.0), jnp.where(left, 0.0, v)]
    return jnp.concatenate(blocks, axis=0).astype(BF)


def pair_columns(v, g):
    even = v[2 * g * ROWS : (2 * g + 1) * ROWS]
    odd = v[(2 * g + 1) * ROWS : (2 * g + 2) * ROWS]
    return jnp.where(lanes_of(even) < HEAD_DIM, even, odd)


def softmax_rows(heads, key2, mask):
    scores = right_product(heads, key2).reshape(GROUPS, ROWS, ROWS) * score_scale
    masked = jnp.where(mask[None] > 0.0, scores, -1e30)
    top = jnp.max(masked, axis=-1, keepdims=True)
    total = top + jnp.log(jnp.sum(jnp.exp(masked - top), axis=-1, keepdims=True))
    return jnp.exp(masked - total).reshape(GROUPS * ROWS, ROWS)


def attention_kernel(qkv_ref, cos_ref, sin_ref, mask_ref, query_ref, kv_ref, out_ref):
    cosine, sine = cos_ref[...], sin_ref[...]
    for g in range(GROUPS // 2):
        v = qkv_ref[:, g * LANES : (g + 1) * LANES]
        query_ref[:, g * LANES : (g + 1) * LANES] = (v * cosine + quarter_turn(v) * sine).astype(BF)
    v = qkv_ref[:, QW:]
    kv = jnp.where(lanes_of(v) < HEAD_DIM, v * cosine + quarter_turn(v) * sine, v)
    kv_ref[...] = kv.astype(BF)
    key2, value2 = doubled(kv)
    probs = softmax_rows(head_rows(query_ref), key2.astype(BF), mask_ref[0])
    heads = dot(probs.astype(BF), value2.astype(BF))
    for g in range(GROUPS // 2):
        out_ref[:, g * LANES : (g + 1) * LANES] = pair_columns(heads, g).astype(BF)


def attention_back_kernel(query_ref, kv_ref, grad_ref, cos_ref, sin_ref, mask_ref, out_ref):
    cosine, sine = cos_ref[...], sin_ref[...]
    key2, value2 = doubled(kv_ref[...].astype(F32))
    key2, value2 = key2.astype(BF), value2.astype(BF)
    heads, grads = head_rows(query_ref), head_rows(grad_ref)
    probs = softmax_rows(heads, key2, mask_ref[0])
    grad_value = left_product(probs.astype(BF), grads)
    grad_value = grad_value + pltpu.roll(grad_value, HEAD_DIM, 1)
    grad_probs = right_product(grads, value2)
    inner = jnp.sum(grad_probs * probs, axis=-1, keepdims=True)
    grad_scores = (probs * (grad_probs - inner)).astype(BF)
    grad_query = dot(grad_scores, key2)
    for g in range(GROUPS // 2):
        v = pair_columns(grad_query, g) * score_scale
        out_ref[:, g * LANES : (g + 1) * LANES] = (v * cosine - quarter_turn(v) * sine).astype(BF)
    grad_key = left_product(grad_scores, heads)
    v = (grad_key + pltpu.roll(grad_key, HEAD_DIM, 1)) * score_scale
    grad_key = v * cosine - quarter_turn(v) * sine
    out_ref[:, QW:] = jnp.where(lanes_of(v) < HEAD_DIM, grad_key, grad_value).astype(BF)


def row_block(width):
    return pl.BlockSpec((ROWS, width), lambda b: (b, 0))


MASK_BLOCK = pl.BlockSpec((1, ROWS, ROWS), lambda b: (b, 0, 0))


def attention(qkv, cosine, sine, mask):
    return pl.pallas_call(
        attention_kernel,
        grid=(MEMBERS,),
        in_specs=[row_block(QKVW), row_block(LANES), row_block(LANES), MASK_BLOCK],
        out_specs=[row_block(QW), row_block(LANES), row_block(QW)],
        out_shape=[
            jax.ShapeDtypeStruct((SLOTS, QW), BF),
            jax.ShapeDtypeStruct((SLOTS, LANES), BF),
            jax.ShapeDtypeStruct((SLOTS, QW), BF),
        ],
        compiler_params=pltpu.CompilerParams(vmem_limit_bytes=32 * 2**20),
        cost_estimate=pl.CostEstimate(
            flops=3 * 10**8, bytes_accessed=4 * 10**6, transcendentals=10**6
        ),
        name="attention",
    )(qkv, cosine, sine, mask)


def attention_back(query, kv, grad, cosine, sine, mask):
    return pl.pallas_call(
        attention_back_kernel,
        grid=(MEMBERS,),
        in_specs=[
            row_block(QW),
            row_block(LANES),
            row_block(QW),
            row_block(LANES),
            row_block(LANES),
            MASK_BLOCK,
        ],
        out_specs=row_block(QKVW),
        out_shape=jax.ShapeDtypeStruct((SLOTS, QKVW), BF),
        compiler_params=pltpu.CompilerParams(vmem_limit_bytes=32 * 2**20),
        cost_estimate=pl.CostEstimate(
            flops=8 * 10**8, bytes_accessed=4 * 10**6, transcendentals=10**6
        ),
        name="attention_back",
    )(query, kv, grad, cosine, sine, mask)


def rounded_gain(gain):
    return lax.optimization_barrier(gain.astype(BF)).astype(F32)


def inverse_rms(v):
    return lax.rsqrt(jnp.mean(v * v, axis=-1, keepdims=True) + epsilon)


def norm_back(v, gain, grad):
    r = inverse_rms(v)
    n = v * r
    scaled = grad * gain
    return r * (scaled - n * jnp.mean(scaled * n, axis=-1, keepdims=True)), n


def panels(gate, up):
    blocks = []
    for at in range(0, FW, 256):
        blocks += [gate[:, at : at + 256], up[:, at : at + 256]]
    return jnp.concatenate(blocks, axis=1)


def unpanels(both):
    gate, up = [], []
    for at in range(0, FW, 256):
        width = min(256, FW - at)
        gate.append(both[:, 2 * at : 2 * at + width])
        up.append(both[:, 2 * at + width : 2 * at + 2 * width])
    return jnp.concatenate(gate, axis=1), jnp.concatenate(up, axis=1)


def on_device(
    tokens,
    cotangent,
    segment_ids,
    positions,
    padding,
    attn_gain,
    query_weight,
    key_weight,
    value_weight,
    output_weight,
    mlp_gain,
    gate_weight,
    up_weight,
    down_weight,
    attn_moment,
    query_moment,
    key_moment,
    value_moment,
    output_moment,
    mlp_moment,
    gate_moment,
    up_moment,
    down_moment,
):
    member = lax.axis_index("grp")
    place = lax.axis_index("dp")
    z, y, low = place // 8, (place // 2) % 4, (place % 2) == 0

    def mine(weight, width):
        return lax.dynamic_slice_in_dim(weight, member * width, width, 1).astype(BF)

    gu_shard = pair_x(panels(mine(gate_weight, FW), mine(up_weight, FW)), low)
    pieces = [gu_shard[:, j * PANEL : (j + 1) * PANEL] for j in range(5)]
    tail = gu_shard[:, 5 * PANEL :]
    pieces.append(jnp.concatenate([tail[:W_ROWS], tail[W_ROWS:]], axis=1))
    pieces.append(turn_pair(mine(down_weight, PANEL), low))
    mlp_full = plane_gather(jnp.concatenate(pieces, axis=0)).reshape(16, 1056, PANEL)

    qkv_shard = jnp.concatenate(
        [mine(query_weight, QW), mine(key_weight, KW), mine(value_weight, KW)], axis=1
    )
    qkv_full = ring_gather(ring_gather(pair_x(qkv_shard, low), RING_Y, y), RING_Z, z)
    out_shard = mine(output_weight, QW)
    out_rows = jnp.zeros((W_ROWS, D), BF)
    for k in range(4):
        out_rows = lax.dynamic_update_slice_in_dim(
            out_rows, everywhere(out_shard, TURN_OUT[k]), lax.rem(z + 4 - k, 4) * PANEL, 1
        )
    out_full = ring_gather(pair_x(out_rows, low), RING_Y, y)

    places = jnp.stack([segment_ids, positions, padding])
    places = group_gather(places[None])
    segments, spots, pads = places[:, 0], places[:, 1], places[:, 2]
    rows_in = group_gather(tokens)
    grads_in = group_gather(cotangent)

    first_gain = rounded_gain(attn_gain)
    second_gain = rounded_gain(mlp_gain)
    inputs = rows_in.astype(F32)
    n_first = inputs * inverse_rms(inputs)
    first_low = (n_first * first_gain).astype(BF)

    half = HEAD_DIM // 2
    freq = 10000.0 ** (-(jnp.arange(half, dtype=F32) * 2.0 / HEAD_DIM))
    angles = spots.reshape(SLOTS, 1).astype(F32) * jnp.tile(freq, LANES // half)[None]
    cosine, sine = jnp.cos(angles), jnp.sin(angles)
    column = jnp.arange(ROWS, dtype=jnp.int32)
    allowed = jnp.logical_and(
        jnp.logical_and(
            segments[:, :, None] == segments[:, None, :],
            (column[None, :] <= column[:, None])[None],
        ),
        jnp.logical_or(pads[:, None, :] == 1, (column[None, :] == column[:, None])[None]),
    ).astype(F32)

    query_rot, kv, attended = attention(dot(first_low, qkv_full), cosine, sine, allowed)
    middle = tokens.astype(F32) + group_scatter(dot(attended, out_full))
    second_low = (middle * inverse_rms(middle) * second_gain).astype(BF)
    second_all = group_gather(second_low)

    grad_gu, active, send = mlp_grads(second_all, second_all.T, grads_in, mlp_full)
    mlp_sum = plane_scatter(send.reshape(16 * 1056, PANEL))
    grad_second = group_scatter(second_grad(grad_gu, mlp_full))
    back, n_second = norm_back(middle, second_gain, grad_second)
    mlp_gain_part = jnp.sum(grad_second * n_second, axis=0)
    grad_middle = cotangent.astype(F32) + back
    middle_all = group_gather(grad_middle.astype(BF))

    grad_attended = right_product(middle_all, out_full).astype(BF)
    grad_qkv = attention_back(query_rot, kv, grad_attended, cosine, sine, allowed)
    grad_qkv, active = lax.optimization_barrier((grad_qkv, active))

    qkv_part = ring_scatter(left_product(first_low, grad_qkv).astype(BF), RING_Z, z)
    out_part = ring_scatter(left_product(attended, middle_all).astype(BF), RING_Y, y).astype(BF)
    out_part = sum(
        everywhere(
            lax.dynamic_slice_in_dim(out_part, lax.rem(z + k, 4) * PANEL, PANEL, 1), TURN_IN[k]
        ).astype(F32)
        for k in range(4)
    )
    grad_first = right_product(grad_qkv, qkv_full)
    attn_gain_part = jnp.sum(grad_first * n_first, axis=0)
    gains = jnp.stack([attn_gain_part, mlp_gain_part]).reshape(32, LANES)
    gains = gains + sum(lax.ppermute(gains, "dp", p) for p in RING_Z)
    rider = jnp.concatenate([two_parts(gains), jnp.zeros((W_ROWS, LANES), BF)], axis=0)
    qkv_part = ring_scatter(qkv_part.astype(BF), RING_Y, y, rider)
    gains = two_parts(one_part(qkv_part[:W_ROWS, QKVW:]))

    both = jnp.concatenate([qkv_part[:, :QKVW], out_part], axis=1).astype(BF)
    kept, given = halves(both, low)
    width = QKVW + PANEL
    near = swap_x(jnp.concatenate([given, gains], axis=1))
    far = swap_far(jnp.concatenate([kept, gains], axis=1))
    far_x = everywhere(jnp.concatenate([given, gains], axis=1), SWAP_FAR_X)
    own_total = kept.astype(F32) + near[:, :width].astype(F32)
    far_total = far[:, :width].astype(F32) + far_x[:, :width].astype(F32)
    gains = sum(one_part(part) for part in (gains, near[:, width:], far[:, width:], far_x[:, width:]))
    totals = jnp.concatenate([own_total, far_total], axis=0).astype(BF)
    rider = jnp.concatenate([two_parts(gains), jnp.zeros((W_ROWS, LANES), BF)], axis=0)
    other = swap_core(jnp.concatenate([totals, rider], axis=1))
    gains = gains + one_part(other[:W_ROWS, width:])
    totals = jnp.concatenate([totals, other[:, :width]], axis=0).astype(F32)

    own_moment = jnp.concatenate(
        [query_moment, key_moment, value_moment, output_moment], axis=1
    )
    moments = group_gather(own_moment.astype(BF)).astype(F32)
    own_moved = 0.5 * own_moment + 0.5 * own_total
    query_momentum = own_moved[:, :QW]
    key_momentum = own_moved[:, QW : QW + KW]
    value_momentum = own_moved[:, QW + KW : QKVW]
    output_momentum = own_moved[:, QKVW:]

    mine_at = (member // 2) + 2 * (member % 2)

    def by_member(slots):
        return [
            lax.dynamic_index_in_dim(slots, mine_at ^ at, 0, keepdims=False) for at in (0, 2, 1, 3)
        ]

    attn_moved = by_member((0.5 * moments + 0.5 * totals).reshape(MEMBERS, W_ROWS, width))

    gu_part = jnp.concatenate(
        [mlp_sum[j * 128 : (j + 1) * 128] for j in range(5)]
        + [jnp.concatenate([mlp_sum[640:704, :256], mlp_sum[640:704, 256:]], axis=0)],
        axis=1,
    )
    kept, given = halves(gu_part, low)
    gate_rows, up_rows = unpanels(kept.astype(F32) + swap_x(given).astype(F32))
    kept, given = halves(mlp_sum[704:], low)
    down_rows = (kept.astype(F32) + swap_x(given).astype(F32)).astype(BF)
    down_rows = everywhere(down_rows, TURN).astype(F32)
    gate_momentum = 0.5 * gate_moment + 0.5 * gate_rows
    up_momentum = 0.5 * up_moment + 0.5 * up_rows
    down_momentum = 0.5 * down_moment + 0.5 * down_rows
    gu_moved = by_member(
        group_gather(jnp.concatenate([gate_momentum, up_momentum], axis=1).astype(BF)).reshape(
            MEMBERS, W_ROWS, GUW
        )
    )
    down_moved = by_member(
        group_gather(down_momentum.astype(BF)).reshape(MEMBERS, DOWN_ROWS, PANEL)
    )

    def updated(weight, columns, start, size):
        moved = jnp.concatenate([block[:, start : start + size] for block in columns], axis=1)
        return weight - learn_rate * moved.astype(F32)

    block_output = (middle + group_scatter(down_product(active, mlp_full))).astype(BF)
    back, _ = norm_back(tokens.astype(F32), first_gain, group_scatter(grad_first))
    input_grad = grad_middle + back

    gains = 0.5 * jnp.stack([attn_moment, mlp_moment]) + 0.5 * gains.reshape(2, D)
    return (
        block_output,
        input_grad,
        gains[0],
        query_momentum,
        key_momentum,
        value_momentum,
        output_momentum,
        gains[1],
        gate_momentum,
        up_momentum,
        down_momentum,
        attn_gain - learn_rate * gains[0],
        updated(query_weight, attn_moved, 0, QW),
        updated(key_weight, attn_moved, QW, KW),
        updated(value_weight, attn_moved, QW + KW, KW),
        updated(output_weight, attn_moved, QKVW, PANEL),
        mlp_gain - learn_rate * gains[1],
        updated(gate_weight, gu_moved, 0, FW),
        updated(up_weight, gu_moved, FW, FW),
        updated(down_weight, down_moved, 0, PANEL),
    )


def solution(mesh):
    rows = P(("grp", "dp"), None)
    flat = P(("grp", "dp"))
    weight = P("dp", None)
    moment = P("dp", "grp")
    everyone = P()
    weights = (everyone,) + (weight,) * 4 + (everyone,) + (weight,) * 3
    moments = (everyone,) + (moment,) * 4 + (everyone,) + (moment,) * 3
    return jax.shard_map(
        on_device,
        mesh=mesh,
        in_specs=(rows, rows, flat, flat, flat) + weights + moments,
        out_specs=(rows, rows) + moments + weights,
        check_vma=False,
    )
```

```python
import jax
import jax.numpy as jnp
from jax import lax
from jax.experimental import pallas as pl
from jax.experimental.pallas import tpu as pltpu
from jax.sharding import PartitionSpec as P

D = 2048
HEAD_DIM = 64
GROUPS = 8
ROWS = 128
MEMBERS = 4
SLOTS = ROWS * MEMBERS
QW = 512
KW = 64
QKVW = QW + 2 * KW
SPLIT = 384
FW = 1408
GUW = 2 * FW
PANEL = 512
DOWN_ROWS = 176
W_ROWS = 64

epsilon = 1e-05
learn_rate = 0.005
score_scale = 0.125

BF = jnp.bfloat16
F32 = jnp.float32

PLANES = [[z * 8 + y * 2 + x for z in range(4) for y in range(4)] for x in range(2)]
SWAP_X = [(i, i ^ 1) for i in range(32)]
SWAP_CORE = [(m, m ^ 1) for m in range(4)]
SWAP_FAR = [(m, m ^ 2) for m in range(4)]
SWAP_FAR_X = [(m * 32 + i, (m ^ 2) * 32 + (i ^ 1)) for m in range(4) for i in range(32)]
MZQ = [(m, z, q) for m in range(4) for z in range(4) for q in range(8)]


def spot(m, z, q):
    return m * 32 + z * 8 + q


TURN = [(spot(m, z, q), spot(z, m, q)) for m, z, q in MZQ]
TURN_X = [(spot(m, z, q), spot(z, m, q ^ 1)) for m, z, q in MZQ]
TURN_OUT = [[(spot(m, z, q), spot(z, (m + k) % 4, q)) for m, z, q in MZQ] for k in range(4)]
TURN_IN = [[(spot(m, z, q), spot((z + k) % 4, m, q)) for m, z, q in MZQ] for k in range(4)]


def ring(place, k):
    return [(i, i + ((i // place + k) % 4 - i // place % 4) * place) for i in range(32)]


RING_Z = [ring(8, k) for k in (1, 2, 3)]
RING_Y = [ring(2, k) for k in (1, 2, 3)]


def swap_x(v):
    return lax.ppermute(v, "dp", SWAP_X)


def swap_core(v):
    return lax.ppermute(v, "grp", SWAP_CORE)


def swap_far(v):
    return lax.ppermute(v, "grp", SWAP_FAR)


def everywhere(v, pairs):
    return lax.ppermute(v, ("grp", "dp"), pairs)


def plane_gather(v):
    return lax.all_gather(v, "dp", axis=0, tiled=True, axis_index_groups=PLANES)


def plane_scatter(v):
    return lax.psum_scatter(
        v, "dp", scatter_dimension=0, tiled=True, axis_index_groups=PLANES
    )


def ring_gather(v, pairs, at, axis=0):
    rows = v.shape[axis]
    out = jnp.zeros(v.shape[:axis] + (4 * rows,) + v.shape[axis + 1 :], v.dtype)
    for k, part in enumerate([v] + [lax.ppermute(v, "dp", p) for p in pairs]):
        out = lax.dynamic_update_slice_in_dim(out, part, lax.rem(at + 4 - k, 4) * rows, axis)
    return out


def ring_scatter(v, pairs, at, extra=None):
    rows = v.shape[0] // 4

    def chunk(k):
        part = lax.dynamic_slice_in_dim(v, lax.rem(at + k, 4) * rows, rows, 0)
        return part if extra is None else jnp.concatenate([part, extra], axis=1)

    total = chunk(0).astype(F32)
    for k, p in enumerate(pairs):
        total = total + lax.ppermute(chunk(k + 1), "dp", p).astype(F32)
    return total


def group_gather(v):
    pair = jnp.concatenate([v, swap_far(v)], axis=0)
    return jnp.concatenate([pair, swap_core(pair)], axis=0)


def group_scatter(partial):
    half = 2 * ROWS
    near = partial[:half] + swap_core(partial[half:].astype(BF)).astype(F32)
    return near[:ROWS] + swap_far(near[ROWS:].astype(BF)).astype(F32)


def in_order(own, other, low):
    return jnp.concatenate([jnp.where(low, own, other), jnp.where(low, other, own)], axis=0)


def pair_x(v, low):
    return in_order(v, swap_x(v), low)


def turn_pair(v, low):
    return in_order(everywhere(v, TURN), everywhere(v, TURN_X), low)


def halves(v, low):
    rows = v.shape[0] // 2
    return jnp.where(low, v[:rows], v[rows:]), jnp.where(low, v[rows:], v[:rows])


def two_parts(v):
    high = lax.reduce_precision(v, 8, 7)
    return jnp.concatenate([high.astype(BF), (v - high).astype(BF)], axis=0)


def one_part(v):
    rows = v.shape[0] // 2
    return v[:rows].astype(F32) + v[rows:].astype(F32)


def dot(left, right):
    return jnp.dot(left, right, preferred_element_type=F32)


def left_product(left, right):
    return lax.dot_general(left, right, (((0,), (0,)), ((), ())), preferred_element_type=F32)


def right_product(left, right):
    return lax.dot_general(left, right, (((1,), (1,)), ((), ())), preferred_element_type=F32)


def tail_in(full, tail, sems):
    return [pltpu.make_async_copy(full.at[:, pl.ds(640,64), pl.ds(256*h,256)], tail.at[:, pl.ds(64*h,64), :], sems.at[h]) for h in range(2)]

def mlp_kernel(s_ref, st_ref, c_ref, panel_ref, full, ggu_ref, act_ref, send,
               down, tail, gpan, gtail, gdown, in_sem, tail_sem, pan_sem, out_sem):
    j = pl.program_id(0)
    loads = [pltpu.make_async_copy(full.at[4*c+y, pl.ds(704,352), :], down.at[c, pl.ds(352*y,352), :], in_sem.at[4*c+y]) for c in range(4) for y in range(4)]
    tails = tail_in(full, tail, tail_sem)
    @pl.when(j == 0)
    def _():
        for l in loads: l.start()
        for t in tails: t.start()

    def panel_out(slot, at):
        return pltpu.make_async_copy(gpan.at[slot], send.at[:, pl.ds(128*at,128), :], pan_sem.at[slot])

    def block(weights, start, width):
        h = dot(s_ref[...], weights)
        gate, up = h[:, :width], h[:, width:]
        @pl.when(j == 0)
        def _():
            for l in loads: l.wait()
        prod = right_product(c_ref[:, :PANEL], down[0, pl.ds(start,width), :])
        for c in range(1,4):
            prod += right_product(c_ref[:, c*PANEL:(c+1)*PANEL], down[c, pl.ds(start,width), :])
        sig = 1.0/(1.0+jnp.exp(-gate))
        silu = gate*sig
        act = (silu*up).astype(BF)
        grad = jnp.concatenate([(prod*up*sig*(1.0+gate*(1.0-sig))).astype(BF),(prod*silu).astype(BF)],axis=1)
        ggu_ref[:, :2*width] = grad
        act_ref[:, :width] = act
        for c in range(4):
            gdown[c, pl.ds(start,width), :] = left_product(act, c_ref[:, c*PANEL:(c+1)*PANEL]).astype(BF)
        return dot(st_ref[...], grad).astype(BF)

    @pl.when(j < 5)
    def _():
        slot = lax.rem(j, 2)
        g = block(panel_ref[...].reshape(2048, PANEL), pl.multiple_of(256*j, 256), 256)
        @pl.when(j >= 2)
        def _():
            panel_out(slot, j-2).wait()
        gpan[slot] = g.reshape(16,128,PANEL)
        panel_out(slot, j).start()

    @pl.when(j == 5)
    def _():
        for t in tails: t.wait()
        g = block(tail[...].reshape(2048,256), 1280, 128)
        gtail[...] = g.reshape(16,128,256)
        outs = [pltpu.make_async_copy(gtail.at[:, pl.ds(64*h,64), :], send.at[:, pl.ds(640,64), pl.ds(256*h,256)], tail_sem.at[h]) for h in range(2)]
        outs += [pltpu.make_async_copy(gdown.at[c, pl.ds(352*y,352), :], send.at[4*c+y, pl.ds(704,352), :], out_sem.at[4*c+y]) for c in range(4) for y in range(4)]
        for o in outs: o.start()
        panel_out(1, 3).wait()
        panel_out(0, 4).wait()
        for o in outs: o.wait()

def whole(shape):
    return pl.BlockSpec(shape, lambda j: (0,)*len(shape), pipeline_mode=pl.Buffered(1))

def mlp_grads(s, st, cot, full):
    return pl.pallas_call(
        mlp_kernel, grid=(6,),
        in_specs=[whole((512,2048)), whole((2048,512)), whole((512,2048)),
                  pl.BlockSpec((16,128,PANEL), lambda j: (0, jnp.minimum(j,4), 0)),
                  pl.BlockSpec(memory_space=pl.ANY)],
        out_specs=[pl.BlockSpec((512,512), lambda j: (0,j)), pl.BlockSpec((512,256), lambda j:(0,j)), pl.BlockSpec(memory_space=pl.ANY)],
        out_shape=[jax.ShapeDtypeStruct((512,3072),BF), jax.ShapeDtypeStruct((512,1536),BF), jax.ShapeDtypeStruct((16,1056,PANEL),BF)],
        scratch_shapes=[pltpu.VMEM((4,FW,PANEL),BF), pltpu.VMEM((16,128,256),BF), pltpu.VMEM((2,16,128,PANEL),BF),
                        pltpu.VMEM((16,128,256),BF), pltpu.VMEM((4,FW,PANEL),BF),
                        pltpu.SemaphoreType.DMA((16,)), pltpu.SemaphoreType.DMA((2,)), pltpu.SemaphoreType.DMA((2,)), pltpu.SemaphoreType.DMA((16,))],
        compiler_params=pltpu.CompilerParams(vmem_limit_bytes=58*2**20, dimension_semantics=("arbitrary",)),
        cost_estimate=pl.CostEstimate(flops=18*10**9, bytes_accessed=45*10**6, transcendentals=10**6),
        name="mlp_grads",
    )(s, st, cot, full, full)

def second_kernel(g_ref, panel_ref, full, out_ref, tail, tail_sem):
    j = pl.program_id(0)
    tails = tail_in(full, tail, tail_sem)
    @pl.when(j == 0)
    def _():
        for t in tails: t.start()
        out_ref[...] = right_product(g_ref[...], panel_ref[...].reshape(2048,PANEL))
    @pl.when(jnp.logical_and(j > 0, j < 5))
    def _():
        out_ref[...] += right_product(g_ref[...], panel_ref[...].reshape(2048,PANEL))
    @pl.when(j == 5)
    def _():
        for t in tails: t.wait()
        out_ref[...] += right_product(g_ref[:, :256], tail[...].reshape(2048,256))

def second_grad(ggu, full):
    return pl.pallas_call(
        second_kernel, grid=(6,),
        in_specs=[pl.BlockSpec((512,512), lambda j:(0,j)), pl.BlockSpec((16,128,PANEL), lambda j: (0, jnp.minimum(j,4), 0)), pl.BlockSpec(memory_space=pl.ANY)],
        out_specs=pl.BlockSpec((512,2048), lambda j:(0,0)),
        out_shape=jax.ShapeDtypeStruct((512,2048),F32),
        scratch_shapes=[pltpu.VMEM((16,128,256),BF), pltpu.SemaphoreType.DMA((2,))],
        compiler_params=pltpu.CompilerParams(vmem_limit_bytes=40*2**20, dimension_semantics=("arbitrary",)),
        cost_estimate=pl.CostEstimate(flops=6*10**9, bytes_accessed=20*10**6, transcendentals=0),
        name="second_grad",
    )(ggu, full, full)


def down_kernel(act_ref, down_ref, out_ref):
    out_ref[...] = dot(act_ref[...], down_ref[...].reshape(FW, PANEL))


def down_product(active, full):
    return pl.pallas_call(
        down_kernel,
        grid=(4,),
        in_specs=[whole((SLOTS, FW)), pl.BlockSpec((4, 352, PANEL), lambda c: (c, 2, 0))],
        out_specs=pl.BlockSpec((SLOTS, PANEL), lambda c: (0, c)),
        out_shape=jax.ShapeDtypeStruct((SLOTS, D), F32),
        compiler_params=pltpu.CompilerParams(vmem_limit_bytes=32 * 2**20),
        cost_estimate=pl.CostEstimate(
            flops=3 * 10**9, bytes_accessed=12 * 10**6, transcendentals=0
        ),
        name="down_product",
    )(active, full)


LANES = 128


def lanes_of(v):
    return lax.broadcasted_iota(jnp.int32, v.shape, v.ndim - 1)


def quarter_turn(v):
    first = lanes_of(v) % HEAD_DIM < HEAD_DIM // 2
    return jnp.where(first, -pltpu.roll(v, 96, 1), pltpu.roll(v, 32, 1))


def doubled(v):
    left = lanes_of(v) < HEAD_DIM
    other = pltpu.roll(v, HEAD_DIM, 1)
    return jnp.where(left, v, other), jnp.where(left, other, v)


def head_rows(ref):
    blocks = []
    for g in range(GROUPS // 2):
        v = ref[:, g * LANES : (g + 1) * LANES].astype(F32)
        left = lanes_of(v) < HEAD_DIM
        blocks += [jnp.where(left, v, 0.0), jnp.where(left, 0.0, v)]
    return jnp.concatenate(blocks, axis=0).astype(BF)


def pair_columns(v, g):
    even = v[2 * g * ROWS : (2 * g + 1) * ROWS]
    odd = v[(2 * g + 1) * ROWS : (2 * g + 2) * ROWS]
    return jnp.where(lanes_of(even) < HEAD_DIM, even, odd)


def softmax_rows(heads, key2, mask):
    scores = right_product(heads, key2).reshape(GROUPS, ROWS, ROWS) * score_scale
    masked = jnp.where(mask[None] > 0.0, scores, -1e30)
    top = jnp.max(masked, axis=-1, keepdims=True)
    total = top + jnp.log(jnp.sum(jnp.exp(masked - top), axis=-1, keepdims=True))
    return jnp.exp(masked - total).reshape(GROUPS * ROWS, ROWS)


def attention_kernel(qkv_a, qkv_b, cos_ref, sin_ref, mask_ref, query_ref, kv_ref, out_ref):
    cosine, sine = cos_ref[...], sin_ref[...]
    for g in range(GROUPS // 2):
        v = qkv_a[:, g * LANES : (g + 1) * LANES] if g < 3 else qkv_b[:, :LANES]
        query_ref[:, g * LANES : (g + 1) * LANES] = (v * cosine + quarter_turn(v) * sine).astype(BF)
    v = qkv_b[:, QW - SPLIT :]
    kv = jnp.where(lanes_of(v) < HEAD_DIM, v * cosine + quarter_turn(v) * sine, v)
    kv_ref[...] = kv.astype(BF)
    key2, value2 = doubled(kv)
    probs = softmax_rows(head_rows(query_ref), key2.astype(BF), mask_ref[0])
    heads = dot(probs.astype(BF), value2.astype(BF))
    for g in range(GROUPS // 2):
        out_ref[:, g * LANES : (g + 1) * LANES] = pair_columns(heads, g).astype(BF)


def attention_back_kernel(query_ref, kv_ref, grad_ref, cos_ref, sin_ref, mask_ref, out_ref):
    cosine, sine = cos_ref[...], sin_ref[...]
    key2, value2 = doubled(kv_ref[...].astype(F32))
    key2, value2 = key2.astype(BF), value2.astype(BF)
    heads, grads = head_rows(query_ref), head_rows(grad_ref)
    probs = softmax_rows(heads, key2, mask_ref[0])
    grad_value = left_product(probs.astype(BF), grads)
    grad_value = grad_value + pltpu.roll(grad_value, HEAD_DIM, 1)
    grad_probs = right_product(grads, value2)
    inner = jnp.sum(grad_probs * probs, axis=-1, keepdims=True)
    grad_scores = (probs * (grad_probs - inner)).astype(BF)
    grad_query = dot(grad_scores, key2)
    for g in range(GROUPS // 2):
        v = pair_columns(grad_query, g) * score_scale
        out_ref[:, g * LANES : (g + 1) * LANES] = (v * cosine - quarter_turn(v) * sine).astype(BF)
    grad_key = left_product(grad_scores, heads)
    v = (grad_key + pltpu.roll(grad_key, HEAD_DIM, 1)) * score_scale
    grad_key = v * cosine - quarter_turn(v) * sine
    out_ref[:, QW:] = jnp.where(lanes_of(v) < HEAD_DIM, grad_key, grad_value).astype(BF)


def row_block(width):
    return pl.BlockSpec((ROWS, width), lambda b: (b, 0))


MASK_BLOCK = pl.BlockSpec((1, ROWS, ROWS), lambda b: (b, 0, 0))


def attention(qkv_a, qkv_b, cosine, sine, mask):
    return pl.pallas_call(
        attention_kernel,
        grid=(MEMBERS,),
        in_specs=[
            row_block(SPLIT),
            row_block(QKVW - SPLIT),
            row_block(LANES),
            row_block(LANES),
            MASK_BLOCK,
        ],
        out_specs=[row_block(QW), row_block(LANES), row_block(QW)],
        out_shape=[
            jax.ShapeDtypeStruct((SLOTS, QW), BF),
            jax.ShapeDtypeStruct((SLOTS, LANES), BF),
            jax.ShapeDtypeStruct((SLOTS, QW), BF),
        ],
        compiler_params=pltpu.CompilerParams(vmem_limit_bytes=32 * 2**20),
        cost_estimate=pl.CostEstimate(
            flops=3 * 10**8, bytes_accessed=4 * 10**6, transcendentals=10**6
        ),
        name="attention",
    )(qkv_a, qkv_b, cosine, sine, mask)


def attention_back(query, kv, grad, cosine, sine, mask):
    return pl.pallas_call(
        attention_back_kernel,
        grid=(MEMBERS,),
        in_specs=[
            row_block(QW),
            row_block(LANES),
            row_block(QW),
            row_block(LANES),
            row_block(LANES),
            MASK_BLOCK,
        ],
        out_specs=row_block(QKVW),
        out_shape=jax.ShapeDtypeStruct((SLOTS, QKVW), BF),
        compiler_params=pltpu.CompilerParams(vmem_limit_bytes=32 * 2**20),
        cost_estimate=pl.CostEstimate(
            flops=8 * 10**8, bytes_accessed=4 * 10**6, transcendentals=10**6
        ),
        name="attention_back",
    )(query, kv, grad, cosine, sine, mask)


def rounded_gain(gain):
    return lax.optimization_barrier(gain.astype(BF)).astype(F32)


def inverse_rms(v):
    return lax.rsqrt(jnp.mean(v * v, axis=-1, keepdims=True) + epsilon)


def norm_back(v, gain, grad):
    r = inverse_rms(v)
    n = v * r
    scaled = grad * gain
    return r * (scaled - n * jnp.mean(scaled * n, axis=-1, keepdims=True)), n


def panels(gate, up):
    blocks = []
    for at in range(0, FW, 256):
        blocks += [gate[:, at : at + 256], up[:, at : at + 256]]
    return jnp.concatenate(blocks, axis=1)


def on_device(
    tokens,
    cotangent,
    segment_ids,
    positions,
    padding,
    attn_gain,
    query_weight,
    key_weight,
    value_weight,
    output_weight,
    mlp_gain,
    gate_weight,
    up_weight,
    down_weight,
    attn_moment,
    query_moment,
    key_moment,
    value_moment,
    output_moment,
    mlp_moment,
    gate_moment,
    up_moment,
    down_moment,
):
    member = lax.axis_index("grp")
    place = lax.axis_index("dp")
    z, y, low = place // 8, (place // 2) % 4, (place % 2) == 0

    def mine(weight, width):
        return lax.dynamic_slice_in_dim(weight, member * width, width, 1).astype(BF)

    gu_shard = pair_x(panels(mine(gate_weight, FW), mine(up_weight, FW)), low)
    pieces = [gu_shard[:, j * PANEL : (j + 1) * PANEL] for j in range(5)]
    tail = gu_shard[:, 5 * PANEL :]
    pieces.append(jnp.concatenate([tail[:W_ROWS], tail[W_ROWS:]], axis=1))
    pieces.append(turn_pair(mine(down_weight, PANEL), low))
    mlp_full = plane_gather(jnp.concatenate(pieces, axis=0)).reshape(16, 1056, PANEL)

    qkv_shard = jnp.concatenate(
        [mine(query_weight, QW), mine(key_weight, KW), mine(value_weight, KW)], axis=1
    )
    qkv_shard = pair_x(qkv_shard, low)
    qkv_a = ring_gather(qkv_shard[:, :SPLIT], RING_Y, y)
    qkv_b = ring_gather(qkv_shard[:, SPLIT:], RING_Z, z).reshape(4, 128, QKVW - SPLIT)
    qkv_a, qkv_b, out_shard = lax.optimization_barrier((qkv_a, qkv_b, mine(output_weight, QW)))
    qkv_a = ring_gather(qkv_a, RING_Z, z)
    qkv_b = ring_gather(qkv_b, RING_Y, y, 1).reshape(D, QKVW - SPLIT)
    out_rows = jnp.zeros((W_ROWS, D), BF)
    for k in range(4):
        out_rows = lax.dynamic_update_slice_in_dim(
            out_rows, everywhere(out_shard, TURN_OUT[k]), lax.rem(z + 4 - k, 4) * PANEL, 1
        )
    out_rows = pair_x(out_rows, low)
    qkv_a, qkv_b, out_rows = lax.optimization_barrier((qkv_a, qkv_b, out_rows))
    out_full = ring_gather(out_rows, RING_Y, y)

    places = jnp.stack([segment_ids, positions, padding])
    places = group_gather(places[None])
    segments, spots, pads = places[:, 0], places[:, 1], places[:, 2]
    rows_in = group_gather(tokens)
    grads_in = group_gather(cotangent)
    own_moment = jnp.concatenate(
        [query_moment, key_moment, value_moment, output_moment], axis=1
    )
    grads_in, moments = lax.optimization_barrier((grads_in, group_gather(own_moment.astype(BF))))
    moments = moments.astype(F32)

    first_gain = rounded_gain(attn_gain)
    second_gain = rounded_gain(mlp_gain)
    inputs = rows_in.astype(F32)
    n_first = inputs * inverse_rms(inputs)
    first_low = (n_first * first_gain).astype(BF)

    half = HEAD_DIM // 2
    freq = 10000.0 ** (-(jnp.arange(half, dtype=F32) * 2.0 / HEAD_DIM))
    angles = spots.reshape(SLOTS, 1).astype(F32) * jnp.tile(freq, LANES // half)[None]
    cosine, sine = jnp.cos(angles), jnp.sin(angles)
    column = jnp.arange(ROWS, dtype=jnp.int32)
    allowed = jnp.logical_and(
        jnp.logical_and(
            segments[:, :, None] == segments[:, None, :],
            (column[None, :] <= column[:, None])[None],
        ),
        jnp.logical_or(pads[:, None, :] == 1, (column[None, :] == column[:, None])[None]),
    ).astype(F32)

    query_rot, kv, attended = attention(
        dot(first_low, qkv_a), dot(first_low, qkv_b), cosine, sine, allowed
    )
    middle = tokens.astype(F32) + group_scatter(dot(attended, out_full))
    second_low = (middle * inverse_rms(middle) * second_gain).astype(BF)
    second_all = group_gather(second_low)

    grad_gu, active, send = mlp_grads(second_all, second_all.T, grads_in, mlp_full)
    mlp_sum = plane_scatter(send.reshape(16 * 1056, PANEL))
    grad_second = group_scatter(second_grad(grad_gu, mlp_full))
    back, n_second = norm_back(middle, second_gain, grad_second)
    mlp_gain_part = jnp.sum(grad_second * n_second, axis=0)
    grad_middle = cotangent.astype(F32) + back
    middle_all = group_gather(grad_middle.astype(BF))

    down_part, middle_all = lax.optimization_barrier(
        (down_product(active, mlp_full), middle_all)
    )
    grad_attended = right_product(middle_all, out_full).astype(BF)
    grad_out = left_product(attended, middle_all).astype(BF)
    grad_attended, grad_out = lax.optimization_barrier((grad_attended, grad_out))
    block_output = (middle + group_scatter(down_part)).astype(BF)
    out_part = ring_scatter(grad_out, RING_Y, y).astype(BF)
    out_part = sum(
        everywhere(
            lax.dynamic_slice_in_dim(out_part, lax.rem(z + k, 4) * PANEL, PANEL, 1), TURN_IN[k]
        ).astype(F32)
        for k in range(4)
    )
    grad_qkv = attention_back(query_rot, kv, grad_attended, cosine, sine, allowed)
    qkv_part = left_product(first_low, grad_qkv).astype(BF)
    qkv_part, grad_qkv = lax.optimization_barrier((qkv_part, grad_qkv))
    qkv_part = ring_scatter(qkv_part, RING_Z, z)
    grad_first = right_product(grad_qkv[:, :SPLIT], qkv_a) + right_product(
        grad_qkv[:, SPLIT:], qkv_b
    )
    attn_gain_part = jnp.sum(grad_first * n_first, axis=0)
    back, _ = norm_back(tokens.astype(F32), first_gain, group_scatter(grad_first))
    input_grad = grad_middle + back

    gains = jnp.stack([attn_gain_part, mlp_gain_part]).reshape(32, LANES)
    gains = gains + sum(lax.ppermute(gains, "dp", p) for p in RING_Z)
    rider = jnp.concatenate([two_parts(gains), jnp.zeros((W_ROWS, LANES), BF)], axis=0)
    qkv_part = ring_scatter(qkv_part.astype(BF), RING_Y, y, rider)
    gains = two_parts(one_part(qkv_part[:W_ROWS, QKVW:]))

    both = jnp.concatenate([qkv_part[:, :QKVW], out_part], axis=1).astype(BF)
    both, mlp_sum = lax.optimization_barrier((both, mlp_sum))
    kept, given = halves(both, low)
    width = QKVW + PANEL
    near = swap_x(jnp.concatenate([given, gains], axis=1))
    far = swap_far(jnp.concatenate([kept, gains], axis=1))
    far_x = everywhere(jnp.concatenate([given, gains], axis=1), SWAP_FAR_X)
    own_total = kept.astype(F32) + near[:, :width].astype(F32)
    far_total = far[:, :width].astype(F32) + far_x[:, :width].astype(F32)
    gains = sum(one_part(part) for part in (gains, near[:, width:], far[:, width:], far_x[:, width:]))
    totals = jnp.concatenate([own_total, far_total], axis=0).astype(BF)
    rider = jnp.concatenate([two_parts(gains), jnp.zeros((W_ROWS, LANES), BF)], axis=0)
    other = swap_core(jnp.concatenate([totals, rider], axis=1))
    gains = gains + one_part(other[:W_ROWS, width:])
    totals = jnp.concatenate([totals, other[:, :width]], axis=0).astype(F32)

    own_moved = 0.5 * own_moment + 0.5 * own_total
    query_momentum = own_moved[:, :QW]
    key_momentum = own_moved[:, QW : QW + KW]
    value_momentum = own_moved[:, QW + KW : QKVW]
    output_momentum = own_moved[:, QKVW:]

    mine_at = (member // 2) + 2 * (member % 2)

    def by_member(slots):
        return [
            lax.dynamic_index_in_dim(slots, mine_at ^ at, 0, keepdims=False) for at in (0, 2, 1, 3)
        ]

    attn_moved = by_member((0.5 * moments + 0.5 * totals).reshape(MEMBERS, W_ROWS, width))

    body = mlp_sum[:640].reshape(5, 2, W_ROWS, PANEL)
    tail = jnp.pad(mlp_sum[640:704].reshape(W_ROWS, 2, 256), ((0, 0), (0, 0), (0, 256)))
    first = jnp.concatenate([body[:, 0], tail[None, :, 0]], axis=0)
    second = jnp.concatenate([body[:, 1], tail[None, :, 1]], axis=0)
    kept, given = jnp.where(low, first, second), jnp.where(low, second, first)
    gu_total = kept.astype(F32) + swap_x(given).astype(F32)
    gate_rows = jnp.concatenate(
        [gu_total[j, :, :256] for j in range(5)] + [gu_total[5, :, :128]], axis=1
    )
    up_rows = jnp.concatenate(
        [gu_total[j, :, 256:] for j in range(5)] + [gu_total[5, :, 128:256]], axis=1
    )
    kept, given = halves(mlp_sum[704:], low)
    down_rows = everywhere(kept, TURN).astype(F32) + everywhere(given, TURN_X).astype(F32)
    gate_momentum = 0.5 * gate_moment + 0.5 * gate_rows
    up_momentum = 0.5 * up_moment + 0.5 * up_rows
    down_momentum = 0.5 * down_moment + 0.5 * down_rows
    gu_moved = by_member(
        group_gather(jnp.concatenate([gate_momentum, up_momentum], axis=1).astype(BF)).reshape(
            MEMBERS, W_ROWS, GUW
        )
    )
    down_moved = by_member(
        group_gather(down_momentum.astype(BF)).reshape(MEMBERS, DOWN_ROWS, PANEL)
    )

    def updated(weight, columns, start, size):
        moved = jnp.concatenate([block[:, start : start + size] for block in columns], axis=1)
        return weight - learn_rate * moved.astype(F32)

    gains = 0.5 * jnp.stack([attn_moment, mlp_moment]) + 0.5 * gains.reshape(2, D)
    return (
        block_output,
        input_grad,
        gains[0],
        query_momentum,
        key_momentum,
        value_momentum,
        output_momentum,
        gains[1],
        gate_momentum,
        up_momentum,
        down_momentum,
        attn_gain - learn_rate * gains[0],
        updated(query_weight, attn_moved, 0, QW),
        updated(key_weight, attn_moved, QW, KW),
        updated(value_weight, attn_moved, QW + KW, KW),
        updated(output_weight, attn_moved, QKVW, PANEL),
        mlp_gain - learn_rate * gains[1],
        updated(gate_weight, gu_moved, 0, FW),
        updated(up_weight, gu_moved, FW, FW),
        updated(down_weight, down_moved, 0, PANEL),
    )


def solution(mesh):
    rows = P(("grp", "dp"), None)
    flat = P(("grp", "dp"))
    weight = P("dp", None)
    moment = P("dp", "grp")
    everyone = P()
    weights = (everyone,) + (weight,) * 4 + (everyone,) + (weight,) * 3
    moments = (everyone,) + (moment,) * 4 + (everyone,) + (moment,) * 3
    return jax.shard_map(
        on_device,
        mesh=mesh,
        in_specs=(rows, rows, flat, flat, flat) + weights + moments,
        out_specs=(rows, rows) + moments + weights,
        check_vma=False,
    )
```

```python
import jax
import jax.numpy as jnp
from jax import lax
from jax.experimental import pallas as pl
from jax.experimental.pallas import tpu as pltpu
from jax.sharding import PartitionSpec as P

D = 2048
HEAD_DIM = 64
GROUPS = 8
ROWS = 128
MEMBERS = 4
SLOTS = ROWS * MEMBERS
QW = 512
KW = 64
QKVW = QW + 2 * KW
FW = 1408
GUW = 2 * FW
PANEL = 512
DOWN_ROWS = 176
W_ROWS = 64

epsilon = 1e-05
learn_rate = 0.005
score_scale = 0.125

BF = jnp.bfloat16
F32 = jnp.float32

PLANES = [[z * 8 + y * 2 + x for z in range(4) for y in range(4)] for x in range(2)]
SWAP_X = [(i, i ^ 1) for i in range(32)]
SWAP_CORE = [(m, m ^ 1) for m in range(4)]
SWAP_FAR = [(m, m ^ 2) for m in range(4)]
SWAP_FAR_X = [(m * 32 + i, (m ^ 2) * 32 + (i ^ 1)) for m in range(4) for i in range(32)]
MZQ = [(m, z, q) for m in range(4) for z in range(4) for q in range(8)]


def spot(m, z, q):
    return m * 32 + z * 8 + q


TURN = [(spot(m, z, q), spot(z, m, q)) for m, z, q in MZQ]
TURN_X = [(spot(m, z, q), spot(z, m, q ^ 1)) for m, z, q in MZQ]
TURN_IN = [[(spot(m, z, q), spot((z + k) % 4, m, q)) for m, z, q in MZQ] for k in range(4)]
OWNED = [(spot(m, z, q), spot(z, m, (q & 3) * 2 + (q >> 2))) for m, z, q in MZQ]
RETURN = [(b, a) for a, b in OWNED]


def ring(place, k):
    return [(i, i + ((i // place + k) % 4 - i // place % 4) * place) for i in range(32)]


RING_Z = [ring(8, k) for k in (1, 2, 3)]
RING_Y = [ring(2, k) for k in (1, 2, 3)]


def swap_x(v):
    return lax.ppermute(v, "dp", SWAP_X)


def swap_core(v):
    return lax.ppermute(v, "grp", SWAP_CORE)


def swap_far(v):
    return lax.ppermute(v, "grp", SWAP_FAR)


def everywhere(v, pairs):
    return lax.ppermute(v, ("grp", "dp"), pairs)


def plane_gather(v):
    return lax.all_gather(v, "dp", axis=0, tiled=True, axis_index_groups=PLANES)


def plane_scatter(v):
    return lax.psum_scatter(
        v, "dp", scatter_dimension=0, tiled=True, axis_index_groups=PLANES
    )


def ring_scatter(v, pairs, at, extra=None):
    rows = v.shape[0] // 4

    def chunk(k):
        part = lax.dynamic_slice_in_dim(v, lax.rem(at + k, 4) * rows, rows, 0)
        return part if extra is None else jnp.concatenate([part, extra], axis=1)

    total = chunk(0).astype(F32)
    for k, p in enumerate(pairs):
        total = total + lax.ppermute(chunk(k + 1), "dp", p).astype(F32)
    return total


def group_gather(v):
    pair = jnp.concatenate([v, swap_far(v)], axis=0)
    return jnp.concatenate([pair, swap_core(pair)], axis=0)


def group_scatter_near(partial):
    half = 2 * ROWS
    return partial[:half] + swap_core(partial[half:].astype(BF)).astype(F32)


def group_scatter_far(near):
    return near[:ROWS] + swap_far(near[ROWS:].astype(BF)).astype(F32)


def group_scatter(partial):
    return group_scatter_far(group_scatter_near(partial))


def far_x(v):
    return everywhere(v, SWAP_FAR_X)


def row_gather(v):
    four = jnp.concatenate([v, swap_x(v), swap_far(v), far_x(v)], axis=0)
    return jnp.concatenate([four, swap_core(four)], axis=0)


def row_scatter(near):
    low_part, far_part, far_x_part = (
        near[k * ROWS : (k + 1) * ROWS].astype(BF) for k in (1, 2, 3)
    )
    return (
        near[:ROWS]
        + swap_x(low_part).astype(F32)
        + swap_far(far_part).astype(F32)
        + far_x(far_x_part).astype(F32)
    )


def in_order(own, other, low):
    return jnp.concatenate([jnp.where(low, own, other), jnp.where(low, other, own)], axis=0)


def pair_x(v, low):
    return in_order(v, swap_x(v), low)


def turn_pair(v, low):
    return in_order(everywhere(v, TURN), everywhere(v, TURN_X), low)


def halves(v, low):
    rows = v.shape[0] // 2
    return jnp.where(low, v[:rows], v[rows:]), jnp.where(low, v[rows:], v[:rows])


def two_parts(v):
    high = lax.reduce_precision(v, 8, 7)
    return jnp.concatenate([high.astype(BF), (v - high).astype(BF)], axis=0)


def one_part(v):
    rows = v.shape[0] // 2
    return v[:rows].astype(F32) + v[rows:].astype(F32)


def dot(left, right):
    return jnp.dot(left, right, preferred_element_type=F32)


def left_product(left, right):
    return lax.dot_general(left, right, (((0,), (0,)), ((), ())), preferred_element_type=F32)


def right_product(left, right):
    return lax.dot_general(left, right, (((1,), (1,)), ((), ())), preferred_element_type=F32)


ALL = 1024
UNITS = 704
LAST = 192
SHARD = 528


TAIL = [(256, 64, 256 * h, 64 * h, 0, 256) for h in range(2)]
TAIL += [(320, 32, 128 * h, 32 * h, 256, 128) for h in range(4)]


def tail_pieces(shard):
    for row, rows, column, at, start, width in TAIL:
        yield (
            shard.at[:, pl.ds(row, rows), pl.ds(column, width)],
            (slice(None), pl.ds(at, rows), pl.ds(start, width)),
        )


def tail_loads(full, tail, sems):
    return [
        pltpu.make_async_copy(src, tail.at[at], sems.at[i])
        for i, (src, at) in enumerate(tail_pieces(full))
    ]


def down_blocks(shard, down):
    return [
        (shard.at[4 * c + j, pl.ds(352, 176), :], down.at[c, pl.ds(176 * j, 176), :])
        for c in range(4)
        for j in range(4)
    ]


def mlp_kernel(s_ref, st_ref, c_ref, panel_ref, full, ggu_ref, act_ref, send,
               down, tail, gpan, gtail, gdown, in_sem, tail_sem, pan_sem, out_sem):
    step = pl.program_id(0)
    loads = [
        pltpu.make_async_copy(src, dst, in_sem.at[i])
        for i, (src, dst) in enumerate(down_blocks(full, down))
    ]
    tails = tail_loads(full, tail, tail_sem)

    @pl.when(step == 0)
    def _():
        for copy in loads + tails:
            copy.start()

    def panel_out(at):
        return pltpu.make_async_copy(
            gpan.at[at], send.at[:, pl.ds(128 * at, 128), :], pan_sem.at[at]
        )

    def block(weights, start, width, store):
        h = dot(s_ref[...], weights)
        gate, up = h[:, :width], h[:, width:]

        @pl.when(step == 0)
        def _():
            for copy in loads:
                copy.wait()

        prod = right_product(c_ref[:, :PANEL], down[0, pl.ds(start, width), :])
        for c in range(1, 4):
            prod += right_product(
                c_ref[:, c * PANEL : (c + 1) * PANEL], down[c, pl.ds(start, width), :]
            )
        sig = 1.0 / (1.0 + jnp.exp(-gate))
        silu = gate * sig
        act = (silu * up).astype(BF)
        ggu_ref[:, :width] = (prod * up * sig * (1.0 + gate * (1.0 - sig))).astype(BF)
        ggu_ref[:, width : 2 * width] = (prod * silu).astype(BF)
        act_ref[:, :width] = act
        for c in range(4):
            gdown[c, pl.ds(start, width), :] = left_product(
                act, c_ref[:, c * PANEL : (c + 1) * PANEL]
            ).astype(BF)
        store(dot(st_ref[...], ggu_ref[:, : 2 * width]).astype(BF))

    @pl.when(step < 2)
    def _():
        def store(grads):
            gpan[step] = grads.reshape(16, 128, PANEL)

        block(panel_ref[...].reshape(D, PANEL), pl.multiple_of(256 * step, 256), 256, store)
        panel_out(step).start()

    @pl.when(step == 2)
    def _():
        def store(grads):
            gtail[...] = grads.reshape(16, 128, 2 * LAST)

        for copy in tails:
            copy.wait()
        block(tail[...].reshape(D, 2 * LAST), 512, LAST, store)
        outs = [
            pltpu.make_async_copy(gtail.at[at], dst, tail_sem.at[i])
            for i, (dst, at) in enumerate(tail_pieces(send))
        ]
        outs += [
            pltpu.make_async_copy(src, dst, out_sem.at[i])
            for i, (dst, src) in enumerate(down_blocks(send, gdown))
        ]
        for copy in outs:
            copy.start()
        for copy in outs + [panel_out(0), panel_out(1)]:
            copy.wait()


def mlp_grads(s, st, cot, full):
    return pl.pallas_call(
        mlp_kernel,
        grid=(3,),
        in_specs=[pl.BlockSpec(memory_space=pltpu.VMEM)] * 3
        + [
            pl.BlockSpec((16, 128, PANEL), lambda i: (0, jnp.minimum(i, 1), 0)),
            pl.BlockSpec(memory_space=pl.ANY),
        ],
        out_specs=[
            pl.BlockSpec((ALL, 512), lambda i: (0, i)),
            pl.BlockSpec((ALL, 256), lambda i: (0, i)),
            pl.BlockSpec(memory_space=pl.ANY),
        ],
        out_shape=[
            jax.ShapeDtypeStruct((ALL, 1536), BF),
            jax.ShapeDtypeStruct((ALL, 768), BF),
            jax.ShapeDtypeStruct((16, SHARD, PANEL), BF),
        ],
        scratch_shapes=[
            pltpu.VMEM((4, UNITS, PANEL), BF),
            pltpu.VMEM((16, 128, 2 * LAST), BF),
            pltpu.VMEM((2, 16, 128, PANEL), BF),
            pltpu.VMEM((16, 128, 2 * LAST), BF),
            pltpu.VMEM((4, UNITS, PANEL), BF),
            pltpu.SemaphoreType.DMA((16,)),
            pltpu.SemaphoreType.DMA((6,)),
            pltpu.SemaphoreType.DMA((2,)),
            pltpu.SemaphoreType.DMA((16,)),
        ],
        compiler_params=pltpu.CompilerParams(vmem_limit_bytes=44 * 2**20),
        cost_estimate=pl.CostEstimate(
            flops=18 * 10**9, bytes_accessed=45 * 10**6, transcendentals=10**6
        ),
        name="mlp_grads",
    )(s, st, cot, full, full)


def second_kernel(g_ref, panel_ref, last_refs, near_ref, core_ref, tail):
    for row, rows, column, at, start, width in TAIL:
        tail[:, at : at + rows, start : start + width] = last_refs[row][
            :, :, column : column + width
        ]
    total = right_product(g_ref[:, :PANEL], panel_ref[:, :128].reshape(PANEL, PANEL))
    total += right_product(
        g_ref[:, PANEL : 2 * PANEL], panel_ref[:, 128:].reshape(PANEL, PANEL)
    )
    total += right_product(
        g_ref[:, 2 * PANEL : 2 * PANEL + 2 * LAST], tail[...].reshape(PANEL, 2 * LAST)
    )
    near_ref[...] = total[: ALL // 2]
    core_ref[...] = total[ALL // 2 :].astype(BF)


def second_grad(ggu, full):
    half = pl.BlockSpec((ALL // 2, PANEL), lambda i: (0, i))

    def kernel(g_ref, panel_ref, wide_ref, narrow_ref, near_ref, core_ref, tail):
        second_kernel(
            g_ref, panel_ref, {256: wide_ref, 320: narrow_ref}, near_ref, core_ref, tail
        )

    return pl.pallas_call(
        kernel,
        grid=(4,),
        in_specs=[
            pl.BlockSpec(memory_space=pltpu.VMEM),
            pl.BlockSpec((4, 256, PANEL), lambda i: (i, 0, 0)),
            pl.BlockSpec((4, 64, PANEL), lambda i: (i, 4, 0)),
            pl.BlockSpec((4, 32, PANEL), lambda i: (i, 10, 0)),
        ],
        out_specs=[half, half],
        out_shape=[
            jax.ShapeDtypeStruct((ALL // 2, D), F32),
            jax.ShapeDtypeStruct((ALL // 2, D), BF),
        ],
        scratch_shapes=[pltpu.VMEM((4, 128, 2 * LAST), BF)],
        compiler_params=pltpu.CompilerParams(vmem_limit_bytes=32 * 2**20),
        cost_estimate=pl.CostEstimate(
            flops=6 * 10**9, bytes_accessed=20 * 10**6, transcendentals=0
        ),
        name="second_grad",
    )(ggu, full, full, full)


def down_kernel(act_ref, down_ref, near_ref, core_ref):
    part = dot(act_ref[:, :UNITS], down_ref[...].reshape(UNITS, PANEL))
    near_ref[...] = part[: ALL // 2]
    core_ref[...] = part[ALL // 2 :].astype(BF)


def down_product(active, full):
    half = pl.BlockSpec((ALL // 2, PANEL), lambda c: (0, c))
    return pl.pallas_call(
        down_kernel,
        grid=(4,),
        in_specs=[
            pl.BlockSpec(memory_space=pltpu.VMEM),
            pl.BlockSpec((4, 176, PANEL), lambda c: (c, 2, 0)),
        ],
        out_specs=[half, half],
        out_shape=[
            jax.ShapeDtypeStruct((ALL // 2, D), F32),
            jax.ShapeDtypeStruct((ALL // 2, D), BF),
        ],
        compiler_params=pltpu.CompilerParams(vmem_limit_bytes=32 * 2**20),
        cost_estimate=pl.CostEstimate(
            flops=3 * 10**9, bytes_accessed=12 * 10**6, transcendentals=0
        ),
        name="down_product",
    )(active, full)


LANES = 128


def lanes_of(v):
    return lax.broadcasted_iota(jnp.int32, v.shape, v.ndim - 1)


def quarter_turn(v):
    first = lanes_of(v) % HEAD_DIM < HEAD_DIM // 2
    return jnp.where(first, -pltpu.roll(v, 96, 1), pltpu.roll(v, 32, 1))


def doubled(v):
    left = lanes_of(v) < HEAD_DIM
    other = pltpu.roll(v, HEAD_DIM, 1)
    return jnp.where(left, v, other), jnp.where(left, other, v)


def head_rows(ref):
    blocks = []
    for g in range(GROUPS // 2):
        v = ref[:, g * LANES : (g + 1) * LANES].astype(F32)
        left = lanes_of(v) < HEAD_DIM
        blocks += [jnp.where(left, v, 0.0), jnp.where(left, 0.0, v)]
    return jnp.concatenate(blocks, axis=0).astype(BF)


def pair_columns(v, g):
    even = v[2 * g * ROWS : (2 * g + 1) * ROWS]
    odd = v[(2 * g + 1) * ROWS : (2 * g + 2) * ROWS]
    return jnp.where(lanes_of(even) < HEAD_DIM, even, odd)


def softmax_rows(heads, key2, mask):
    scores = right_product(heads, key2).reshape(GROUPS, ROWS, ROWS) * score_scale
    masked = jnp.where(mask[None] > 0.0, scores, -1e30)
    top = jnp.max(masked, axis=-1, keepdims=True)
    total = top + jnp.log(jnp.sum(jnp.exp(masked - top), axis=-1, keepdims=True))
    return jnp.exp(masked - total).reshape(GROUPS * ROWS, ROWS)


def attention_kernel(qkv_ref, cos_ref, sin_ref, mask_ref, query_ref, kv_ref, out_ref):
    cosine, sine = cos_ref[...], sin_ref[...]
    for g in range(GROUPS // 2):
        v = qkv_ref[:, g * LANES : (g + 1) * LANES]
        query_ref[:, g * LANES : (g + 1) * LANES] = (v * cosine + quarter_turn(v) * sine).astype(BF)
    v = qkv_ref[:, QW:]
    kv = jnp.where(lanes_of(v) < HEAD_DIM, v * cosine + quarter_turn(v) * sine, v)
    kv_ref[...] = kv.astype(BF)
    key2, value2 = doubled(kv)
    probs = softmax_rows(head_rows(query_ref), key2.astype(BF), mask_ref[0])
    heads = dot(probs.astype(BF), value2.astype(BF))
    for g in range(GROUPS // 2):
        out_ref[:, g * LANES : (g + 1) * LANES] = pair_columns(heads, g).astype(BF)


def attention_back_kernel(query_ref, kv_ref, grad_ref, cos_ref, sin_ref, mask_ref, out_ref):
    cosine, sine = cos_ref[...], sin_ref[...]
    key2, value2 = doubled(kv_ref[...].astype(F32))
    key2, value2 = key2.astype(BF), value2.astype(BF)
    heads, grads = head_rows(query_ref), head_rows(grad_ref)
    probs = softmax_rows(heads, key2, mask_ref[0])
    grad_value = left_product(probs.astype(BF), grads)
    grad_value = grad_value + pltpu.roll(grad_value, HEAD_DIM, 1)
    grad_probs = right_product(grads, value2)
    inner = jnp.sum(grad_probs * probs, axis=-1, keepdims=True)
    grad_scores = (probs * (grad_probs - inner)).astype(BF)
    grad_query = dot(grad_scores, key2)
    for g in range(GROUPS // 2):
        v = pair_columns(grad_query, g) * score_scale
        out_ref[:, g * LANES : (g + 1) * LANES] = (v * cosine - quarter_turn(v) * sine).astype(BF)
    grad_key = left_product(grad_scores, heads)
    v = (grad_key + pltpu.roll(grad_key, HEAD_DIM, 1)) * score_scale
    grad_key = v * cosine - quarter_turn(v) * sine
    out_ref[:, QW:] = jnp.where(lanes_of(v) < HEAD_DIM, grad_key, grad_value).astype(BF)


def row_block(width):
    return pl.BlockSpec((ROWS, width), lambda b: (b, 0))


MASK_BLOCK = pl.BlockSpec((1, ROWS, ROWS), lambda b: (b, 0, 0))


def attention(qkv, cosine, sine, mask):
    return pl.pallas_call(
        attention_kernel,
        grid=(MEMBERS,),
        in_specs=[row_block(QKVW), row_block(LANES), row_block(LANES), MASK_BLOCK],
        out_specs=[row_block(QW), row_block(LANES), row_block(QW)],
        out_shape=[
            jax.ShapeDtypeStruct((SLOTS, QW), BF),
            jax.ShapeDtypeStruct((SLOTS, LANES), BF),
            jax.ShapeDtypeStruct((SLOTS, QW), BF),
        ],
        compiler_params=pltpu.CompilerParams(vmem_limit_bytes=32 * 2**20),
        cost_estimate=pl.CostEstimate(
            flops=3 * 10**8, bytes_accessed=4 * 10**6, transcendentals=10**6
        ),
        name="attention",
    )(qkv, cosine, sine, mask)


def attention_back(query, kv, grad, cosine, sine, mask):
    return pl.pallas_call(
        attention_back_kernel,
        grid=(MEMBERS,),
        in_specs=[
            row_block(QW),
            row_block(LANES),
            row_block(QW),
            row_block(LANES),
            row_block(LANES),
            MASK_BLOCK,
        ],
        out_specs=row_block(QKVW),
        out_shape=jax.ShapeDtypeStruct((SLOTS, QKVW), BF),
        compiler_params=pltpu.CompilerParams(vmem_limit_bytes=32 * 2**20),
        cost_estimate=pl.CostEstimate(
            flops=8 * 10**8, bytes_accessed=4 * 10**6, transcendentals=10**6
        ),
        name="attention_back",
    )(query, kv, grad, cosine, sine, mask)


def rounded_gain(gain):
    return lax.optimization_barrier(gain.astype(BF)).astype(F32)


def inverse_rms(v):
    return lax.rsqrt(jnp.mean(v * v, axis=-1, keepdims=True) + epsilon)


def norm_back(v, gain, grad):
    r = inverse_rms(v)
    n = v * r
    scaled = grad * gain
    return r * (scaled - n * jnp.mean(scaled * n, axis=-1, keepdims=True)), n


def panels(gate, up):
    blocks = []
    for at in range(0, UNITS, 256):
        blocks += [gate[:, at : at + 256], up[:, at : at + 256]]
    return jnp.concatenate(blocks, axis=1)


def unpanels(v):
    gate = [v[:, :256], v[:, 512:768], v[:, 1024 : 1024 + LAST]]
    up = [v[:, 256:512], v[:, 768:1024], v[:, 1024 + LAST :]]
    return jnp.concatenate(gate, axis=1), jnp.concatenate(up, axis=1)


def on_device(
    tokens,
    cotangent,
    segment_ids,
    positions,
    padding,
    attn_gain,
    query_weight,
    key_weight,
    value_weight,
    output_weight,
    mlp_gain,
    gate_weight,
    up_weight,
    down_weight,
    attn_moment,
    query_moment,
    key_moment,
    value_moment,
    output_moment,
    mlp_moment,
    gate_moment,
    up_moment,
    down_moment,
):
    member = lax.axis_index("grp")
    place = lax.axis_index("dp")
    z, y, low = place // 8, (place // 2) % 4, (place % 2) == 0

    def mine(weight, width):
        return lax.dynamic_slice_in_dim(weight, member * width, width, 1).astype(BF)

    attn_shard = jnp.concatenate(
        [mine(query_weight, QW), mine(key_weight, KW), mine(value_weight, KW)], axis=1
    )
    attn_shard = jnp.concatenate(
        [pair_x(attn_shard, low), turn_pair(mine(output_weight, QW), low)], axis=1
    )
    attn_full = plane_gather(attn_shard)
    qkv_full = attn_full[:, :QKVW]
    out_full = attn_full[:, QKVW:].reshape(4, QW, PANEL).transpose(1, 0, 2).reshape(QW, D)

    gate_mine, up_mine = mine(gate_weight, FW), mine(up_weight, FW)
    first = panels(gate_mine[:, :UNITS], up_mine[:, :UNITS])
    second = panels(gate_mine[:, UNITS:], up_mine[:, UNITS:])
    kept, given = jnp.where(low, first, second), jnp.where(low, second, first)
    gu_shard = in_order(kept, swap_x(given), low)
    tail = gu_shard[:, 2 * PANEL :]
    pieces = [
        gu_shard[:, :PANEL],
        gu_shard[:, PANEL : 2 * PANEL],
        jnp.concatenate([tail[:W_ROWS, :256], tail[W_ROWS:, :256]], axis=1),
        jnp.concatenate([tail[32 * h : 32 * h + 32, 256:] for h in range(4)], axis=1),
        everywhere(mine(down_weight, PANEL), OWNED),
    ]
    mlp_full = plane_gather(jnp.concatenate(pieces, axis=0)).reshape(16, SHARD, PANEL)

    places = jnp.stack([segment_ids, positions, padding])
    places = group_gather(places[None])
    segments, spots, pads = places[:, 0], places[:, 1], places[:, 2]
    rows_in = group_gather(tokens)
    own_moment = jnp.concatenate(
        [query_moment, key_moment, value_moment, output_moment], axis=1
    )
    grads_in, moments = lax.optimization_barrier(
        (row_gather(cotangent), group_gather(own_moment.astype(BF)))
    )
    moments = moments.astype(F32)

    first_gain = rounded_gain(attn_gain)
    second_gain = rounded_gain(mlp_gain)
    inputs = rows_in.astype(F32)
    n_first = inputs * inverse_rms(inputs)
    first_low = (n_first * first_gain).astype(BF)

    half = HEAD_DIM // 2
    freq = 10000.0 ** (-(jnp.arange(half, dtype=F32) * 2.0 / HEAD_DIM))
    angles = spots.reshape(SLOTS, 1).astype(F32) * jnp.tile(freq, LANES // half)[None]
    cosine, sine = jnp.cos(angles), jnp.sin(angles)
    column = jnp.arange(ROWS, dtype=jnp.int32)
    allowed = jnp.logical_and(
        jnp.logical_and(
            segments[:, :, None] == segments[:, None, :],
            (column[None, :] <= column[:, None])[None],
        ),
        jnp.logical_or(pads[:, None, :] == 1, (column[None, :] == column[:, None])[None]),
    ).astype(F32)

    query_rot, kv, attended = attention(dot(first_low, qkv_full), cosine, sine, allowed)
    middle = tokens.astype(F32) + group_scatter(dot(attended, out_full))
    second_low = (middle * inverse_rms(middle) * second_gain).astype(BF)
    second_all = row_gather(second_low)

    grad_gu, active, send = mlp_grads(second_all, second_all.T, grads_in, mlp_full)
    mlp_sum = plane_scatter(send.reshape(16 * SHARD, PANEL))
    second_near, second_core = second_grad(grad_gu, mlp_full)
    grad_second = row_scatter(second_near + swap_core(second_core).astype(F32))
    back, n_second = norm_back(middle, second_gain, grad_second)
    mlp_gain_part = jnp.sum(grad_second * n_second, axis=0)
    grad_middle = cotangent.astype(F32) + back
    middle_all = group_gather(grad_middle.astype(BF))
    down_near, down_core = down_product(active, mlp_full)
    down_near = down_near + swap_core(down_core).astype(F32)
    middle_all, down_near = lax.optimization_barrier((middle_all, down_near))

    grad_attended = right_product(middle_all, out_full).astype(BF)
    grad_out = left_product(attended, middle_all).astype(BF)
    grad_attended, grad_out = lax.optimization_barrier((grad_attended, grad_out))
    grad_qkv = attention_back(query_rot, kv, grad_attended, cosine, sine, allowed)

    qkv_part = left_product(first_low, grad_qkv).astype(BF)
    qkv_part, grad_qkv = lax.optimization_barrier((qkv_part, grad_qkv))
    qkv_part = ring_scatter(qkv_part, RING_Z, z)
    out_part = ring_scatter(grad_out, RING_Y, y).astype(BF)
    grad_first = right_product(grad_qkv, qkv_full)
    attn_gain_part = jnp.sum(grad_first * n_first, axis=0)
    gains = jnp.stack([attn_gain_part, mlp_gain_part]).reshape(32, LANES)
    gains, out_part = lax.optimization_barrier((gains, out_part))
    gains = gains + sum(lax.ppermute(gains, "dp", p) for p in RING_Z)
    out_part = sum(
        everywhere(
            lax.dynamic_slice_in_dim(out_part, lax.rem(z + k, 4) * PANEL, PANEL, 1), TURN_IN[k]
        ).astype(F32)
        for k in range(4)
    )
    first_near = group_scatter_near(grad_first)
    block_output = (middle + row_scatter(down_near)).astype(BF)
    qkv_part, first_near, block_output = lax.optimization_barrier(
        (qkv_part, first_near, block_output)
    )
    back, _ = norm_back(tokens.astype(F32), first_gain, group_scatter_far(first_near))
    input_grad = grad_middle + back
    rider = jnp.concatenate([two_parts(gains), jnp.zeros((W_ROWS, LANES), BF)], axis=0)
    qkv_part = ring_scatter(qkv_part.astype(BF), RING_Y, y, rider)
    gains = two_parts(one_part(qkv_part[:W_ROWS, QKVW:]))

    both = jnp.concatenate([qkv_part[:, :QKVW], out_part], axis=1).astype(BF)
    both, mlp_sum, input_grad = lax.optimization_barrier((both, mlp_sum, input_grad))
    kept, given = halves(both, low)
    width = QKVW + PANEL
    near = swap_x(jnp.concatenate([given, gains], axis=1))
    far = swap_far(jnp.concatenate([kept, gains], axis=1))
    both_far = far_x(jnp.concatenate([given, gains], axis=1))
    own_total = kept.astype(F32) + near[:, :width].astype(F32)
    far_total = far[:, :width].astype(F32) + both_far[:, :width].astype(F32)
    gains = sum(one_part(part) for part in (gains, near[:, width:], far[:, width:], both_far[:, width:]))
    totals = jnp.concatenate([own_total, far_total], axis=0).astype(BF)
    rider = jnp.concatenate([two_parts(gains), jnp.zeros((W_ROWS, LANES), BF)], axis=0)
    other = swap_core(jnp.concatenate([totals, rider], axis=1))
    gains = gains + one_part(other[:W_ROWS, width:])
    totals = jnp.concatenate([totals, other[:, :width]], axis=0).astype(F32)

    own_moved = 0.5 * own_moment + 0.5 * own_total
    query_momentum = own_moved[:, :QW]
    key_momentum = own_moved[:, QW : QW + KW]
    value_momentum = own_moved[:, QW + KW : QKVW]
    output_momentum = own_moved[:, QKVW:]

    mine_at = (member // 2) + 2 * (member % 2)

    def by_member(slots):
        return [
            lax.dynamic_index_in_dim(slots, mine_at ^ at, 0, keepdims=False) for at in (0, 2, 1, 3)
        ]

    attn_moved = by_member((0.5 * moments + 0.5 * totals).reshape(MEMBERS, W_ROWS, width))

    wide, narrow = mlp_sum[256:320], mlp_sum[320:352]
    gu_part = jnp.concatenate(
        [
            mlp_sum[:128],
            mlp_sum[128:256],
            jnp.concatenate([wide[:, :256], wide[:, 256:]], axis=0),
            jnp.concatenate([narrow[:, h * LANES : (h + 1) * LANES] for h in range(4)], axis=0),
        ],
        axis=1,
    )
    kept, given = halves(gu_part, low)
    other = swap_x(given)
    first = unpanels(jnp.where(low, kept, other))
    second = unpanels(jnp.where(low, other, kept))
    gate_rows = jnp.concatenate([first[0], second[0]], axis=1).astype(F32)
    up_rows = jnp.concatenate([first[1], second[1]], axis=1).astype(F32)
    down_rows = everywhere(mlp_sum[352:], RETURN).astype(F32)
    gate_momentum = 0.5 * gate_moment + 0.5 * gate_rows
    up_momentum = 0.5 * up_moment + 0.5 * up_rows
    down_momentum = 0.5 * down_moment + 0.5 * down_rows
    gu_moved = by_member(
        group_gather(jnp.concatenate([gate_momentum, up_momentum], axis=1).astype(BF)).reshape(
            MEMBERS, W_ROWS, GUW
        )
    )
    down_moved = by_member(
        group_gather(down_momentum.astype(BF)).reshape(MEMBERS, DOWN_ROWS, PANEL)
    )

    def updated(weight, columns, start, size):
        moved = jnp.concatenate([block[:, start : start + size] for block in columns], axis=1)
        return weight - learn_rate * moved.astype(F32)

    gains = 0.5 * jnp.stack([attn_moment, mlp_moment]) + 0.5 * gains.reshape(2, D)
    return (
        block_output,
        input_grad,
        gains[0],
        query_momentum,
        key_momentum,
        value_momentum,
        output_momentum,
        gains[1],
        gate_momentum,
        up_momentum,
        down_momentum,
        attn_gain - learn_rate * gains[0],
        updated(query_weight, attn_moved, 0, QW),
        updated(key_weight, attn_moved, QW, KW),
        updated(value_weight, attn_moved, QW + KW, KW),
        updated(output_weight, attn_moved, QKVW, PANEL),
        mlp_gain - learn_rate * gains[1],
        updated(gate_weight, gu_moved, 0, FW),
        updated(up_weight, gu_moved, FW, FW),
        updated(down_weight, down_moved, 0, PANEL),
    )


def solution(mesh):
    rows = P(("grp", "dp"), None)
    flat = P(("grp", "dp"))
    weight = P("dp", None)
    moment = P("dp", "grp")
    everyone = P()
    weights = (everyone,) + (weight,) * 4 + (everyone,) + (weight,) * 3
    moments = (everyone,) + (moment,) * 4 + (everyone,) + (moment,) * 3
    return jax.shard_map(
        on_device,
        mesh=mesh,
        in_specs=(rows, rows, flat, flat, flat) + weights + moments,
        out_specs=(rows, rows) + moments + weights,
        check_vma=False,
    )
```

```python
import jax
import jax.numpy as jnp
from jax import lax
from jax.experimental import pallas as pl
from jax.experimental.pallas import tpu as pltpu
from jax.sharding import PartitionSpec as P

D = 2048
HEAD_DIM = 64
GROUPS = 8
ROWS = 128
MEMBERS = 4
SLOTS = ROWS * MEMBERS
QW = 512
KW = 64
QKVW = QW + 2 * KW
FW = 1408
GUW = 2 * FW
PANEL = 512
DOWN_ROWS = 176
W_ROWS = 64

epsilon = 1e-05
learn_rate = 0.005
score_scale = 0.125

BF = jnp.bfloat16
F32 = jnp.float32

PLANES = [[z * 8 + y * 2 + x for z in range(4) for y in range(4)] for x in range(2)]
SWAP_X = [(i, i ^ 1) for i in range(32)]
SWAP_CORE = [(m, m ^ 1) for m in range(4)]
SWAP_FAR = [(m, m ^ 2) for m in range(4)]
SWAP_FAR_X = [(m * 32 + i, (m ^ 2) * 32 + (i ^ 1)) for m in range(4) for i in range(32)]
MZQ = [(m, z, q) for m in range(4) for z in range(4) for q in range(8)]


def spot(m, z, q):
    return m * 32 + z * 8 + q


TURN = [(spot(m, z, q), spot(z, m, q)) for m, z, q in MZQ]
TURN_X = [(spot(m, z, q), spot(z, m, q ^ 1)) for m, z, q in MZQ]
TURN_IN = [[(spot(m, z, q), spot((z + k) % 4, m, q)) for m, z, q in MZQ] for k in range(4)]
OWNED = [(spot(m, z, q), spot(z, m, (q & 3) * 2 + (q >> 2))) for m, z, q in MZQ]
RETURN = [(b, a) for a, b in OWNED]


def ring(place, k):
    return [(i, i + ((i // place + k) % 4 - i // place % 4) * place) for i in range(32)]


RING_Z = [ring(8, k) for k in (1, 2, 3)]
RING_Y = [ring(2, k) for k in (1, 2, 3)]


def swap_x(v):
    return lax.ppermute(v, "dp", SWAP_X)


def swap_core(v):
    return lax.ppermute(v, "grp", SWAP_CORE)


def swap_far(v):
    return lax.ppermute(v, "grp", SWAP_FAR)


def everywhere(v, pairs):
    return lax.ppermute(v, ("grp", "dp"), pairs)


def plane_gather(v):
    return lax.all_gather(v, "dp", axis=0, tiled=True, axis_index_groups=PLANES)


def plane_scatter(v):
    return lax.psum_scatter(
        v, "dp", scatter_dimension=0, tiled=True, axis_index_groups=PLANES
    )


def ring_scatter(v, pairs, at, extra=None):
    rows = v.shape[0] // 4

    def chunk(k):
        part = lax.dynamic_slice_in_dim(v, lax.rem(at + k, 4) * rows, rows, 0)
        return part if extra is None else jnp.concatenate([part, extra], axis=1)

    total = chunk(0).astype(F32)
    for k, p in enumerate(pairs):
        total = total + lax.ppermute(chunk(k + 1), "dp", p).astype(F32)
    return total


def group_gather(v):
    pair = jnp.concatenate([v, swap_far(v)], axis=0)
    return jnp.concatenate([pair, swap_core(pair)], axis=0)


def group_scatter_near(partial):
    half = 2 * ROWS
    return partial[:half] + swap_core(partial[half:].astype(BF)).astype(F32)


def group_scatter_far(near):
    return near[:ROWS] + swap_far(near[ROWS:].astype(BF)).astype(F32)


def group_scatter(partial):
    return group_scatter_far(group_scatter_near(partial))


def far_x(v):
    return everywhere(v, SWAP_FAR_X)


def row_gather(v):
    four = jnp.concatenate([v, swap_x(v), swap_far(v), far_x(v)], axis=0)
    return four, swap_core(four)


def row_scatter(near):
    low_part, far_part, far_x_part = (
        near[k * ROWS : (k + 1) * ROWS].astype(BF) for k in (1, 2, 3)
    )
    return (
        near[:ROWS]
        + swap_x(low_part).astype(F32)
        + swap_far(far_part).astype(F32)
        + far_x(far_x_part).astype(F32)
    )


def in_order(own, other, low):
    return jnp.concatenate([jnp.where(low, own, other), jnp.where(low, other, own)], axis=0)


def pair_x(v, low):
    return in_order(v, swap_x(v), low)


def turn_pair(v, low):
    return in_order(everywhere(v, TURN), everywhere(v, TURN_X), low)


def halves(v, low):
    rows = v.shape[0] // 2
    return jnp.where(low, v[:rows], v[rows:]), jnp.where(low, v[rows:], v[:rows])


def two_parts(v):
    high = lax.reduce_precision(v, 8, 7)
    return jnp.concatenate([high.astype(BF), (v - high).astype(BF)], axis=0)


def one_part(v):
    rows = v.shape[0] // 2
    return v[:rows].astype(F32) + v[rows:].astype(F32)


def dot(left, right):
    return jnp.dot(left, right, preferred_element_type=F32)


def left_product(left, right):
    return lax.dot_general(left, right, (((0,), (0,)), ((), ())), preferred_element_type=F32)


def right_product(left, right):
    return lax.dot_general(left, right, (((1,), (1,)), ((), ())), preferred_element_type=F32)


ALL = 1024
UNITS = 704
LAST = 192
SHARD = 528


TAIL = [(256, 64, 256 * h, 64 * h, 0, 256) for h in range(2)]
TAIL += [(320, 32, 128 * h, 32 * h, 256, 128) for h in range(4)]


def tail_pieces(shard):
    for row, rows, column, at, start, width in TAIL:
        yield (
            shard.at[:, pl.ds(row, rows), pl.ds(column, width)],
            (slice(None), pl.ds(at, rows), pl.ds(start, width)),
        )


def tail_loads(full, tail, sems):
    return [
        pltpu.make_async_copy(src, tail.at[at], sems.at[i])
        for i, (src, at) in enumerate(tail_pieces(full))
    ]


def down_blocks(shard, down):
    return [
        (shard.at[4 * c + j, pl.ds(352, 176), :], down.at[c, pl.ds(176 * j, 176), :])
        for c in range(4)
        for j in range(4)
    ]


def mlp_kernel(
    four_ref,
    core_ref,
    four_t_ref,
    core_t_ref,
    c_ref,
    panel_ref,
    full,
    ggu_ref,
    act_ref,
    send,
    down,
    tail,
    gpan,
    gtail,
    gdown,
    in_sem,
    tail_sem,
    pan_sem,
    out_sem,
):
    step = pl.program_id(0)
    loads = [
        pltpu.make_async_copy(src, dst, in_sem.at[i])
        for i, (src, dst) in enumerate(down_blocks(full, down))
    ]
    tails = tail_loads(full, tail, tail_sem)

    @pl.when(step == 0)
    def _():
        for copy in loads + tails:
            copy.start()

    def panel_out(at):
        return pltpu.make_async_copy(
            gpan.at[at], send.at[:, pl.ds(128 * at, 128), :], pan_sem.at[at]
        )

    def block(weights, start, width, store):
        halves_of = [dot(ref[...], weights) for ref in (four_ref, core_ref)]

        @pl.when(step == 0)
        def _():
            for copy in loads:
                copy.wait()

        for half, h in enumerate(halves_of):
            rows = pl.ds(half * (ALL // 2), ALL // 2)
            gate, up = h[:, :width], h[:, width:]
            prod = right_product(c_ref[rows, :PANEL], down[0, pl.ds(start, width), :])
            for c in range(1, 4):
                prod += right_product(
                    c_ref[rows, c * PANEL : (c + 1) * PANEL], down[c, pl.ds(start, width), :]
                )
            sig = 1.0 / (1.0 + jnp.exp(-gate))
            silu = gate * sig
            act_ref[rows, :width] = (silu * up).astype(BF)
            ggu_ref[rows, :width] = (prod * up * sig * (1.0 + gate * (1.0 - sig))).astype(BF)
            ggu_ref[rows, width : 2 * width] = (prod * silu).astype(BF)
        act = act_ref[:, :width]
        for c in range(4):
            gdown[c, pl.ds(start, width), :] = left_product(
                act, c_ref[:, c * PANEL : (c + 1) * PANEL]
            ).astype(BF)
        grads = dot(four_t_ref[...], ggu_ref[: ALL // 2, : 2 * width])
        grads += dot(core_t_ref[...], ggu_ref[ALL // 2 :, : 2 * width])
        store(grads.astype(BF))

    @pl.when(step < 2)
    def _():
        def store(grads):
            gpan[step] = grads.reshape(16, 128, PANEL)

        block(panel_ref[...].reshape(D, PANEL), pl.multiple_of(256 * step, 256), 256, store)
        panel_out(step).start()

    @pl.when(step == 2)
    def _():
        def store(grads):
            gtail[...] = grads.reshape(16, 128, 2 * LAST)

        for copy in tails:
            copy.wait()
        block(tail[...].reshape(D, 2 * LAST), 512, LAST, store)
        outs = [
            pltpu.make_async_copy(gtail.at[at], dst, tail_sem.at[i])
            for i, (dst, at) in enumerate(tail_pieces(send))
        ]
        outs += [
            pltpu.make_async_copy(src, dst, out_sem.at[i])
            for i, (dst, src) in enumerate(down_blocks(send, gdown))
        ]
        for copy in outs:
            copy.start()
        for copy in outs + [panel_out(0), panel_out(1)]:
            copy.wait()


def mlp_grads(four, core, four_t, core_t, cot, full):
    return pl.pallas_call(
        mlp_kernel,
        grid=(3,),
        in_specs=[pl.BlockSpec(memory_space=pltpu.VMEM)] * 5
        + [
            pl.BlockSpec((16, 128, PANEL), lambda i: (0, jnp.minimum(i, 1), 0)),
            pl.BlockSpec(memory_space=pl.ANY),
        ],
        out_specs=[
            pl.BlockSpec((ALL, 512), lambda i: (0, i)),
            pl.BlockSpec((ALL, 256), lambda i: (0, i)),
            pl.BlockSpec(memory_space=pl.ANY),
        ],
        out_shape=[
            jax.ShapeDtypeStruct((ALL, 1536), BF),
            jax.ShapeDtypeStruct((ALL, 768), BF),
            jax.ShapeDtypeStruct((16, SHARD, PANEL), BF),
        ],
        scratch_shapes=[
            pltpu.VMEM((4, UNITS, PANEL), BF),
            pltpu.VMEM((16, 128, 2 * LAST), BF),
            pltpu.VMEM((2, 16, 128, PANEL), BF),
            pltpu.VMEM((16, 128, 2 * LAST), BF),
            pltpu.VMEM((4, UNITS, PANEL), BF),
            pltpu.SemaphoreType.DMA((16,)),
            pltpu.SemaphoreType.DMA((6,)),
            pltpu.SemaphoreType.DMA((2,)),
            pltpu.SemaphoreType.DMA((16,)),
        ],
        compiler_params=pltpu.CompilerParams(vmem_limit_bytes=44 * 2**20),
        cost_estimate=pl.CostEstimate(
            flops=18 * 10**9, bytes_accessed=45 * 10**6, transcendentals=10**6
        ),
        name="mlp_grads",
    )(four, core, four_t, core_t, cot, full, full)


def second_kernel(g_ref, panel_ref, wide_ref, narrow_ref, out_ref, tail):
    for row, rows, column, at, start, width in TAIL:
        piece = wide_ref if row == 256 else narrow_ref
        tail[:, at : at + rows, start : start + width] = piece[:, :, column : column + width]
    total = right_product(g_ref[:, :PANEL], panel_ref[:, :128].reshape(PANEL, PANEL))
    total += right_product(
        g_ref[:, PANEL : 2 * PANEL], panel_ref[:, 128:].reshape(PANEL, PANEL)
    )
    total += right_product(
        g_ref[:, 2 * PANEL : 2 * PANEL + 2 * LAST], tail[...].reshape(PANEL, 2 * LAST)
    )
    out_ref[...] = total.astype(out_ref.dtype)


def second_grad(ggu, full, half, kind):
    return pl.pallas_call(
        second_kernel,
        grid=(4,),
        in_specs=[
            pl.BlockSpec((ALL // 2, 1536), lambda i: (half, 0)),
            pl.BlockSpec((4, 256, PANEL), lambda i: (i, 0, 0)),
            pl.BlockSpec((4, 64, PANEL), lambda i: (i, 4, 0)),
            pl.BlockSpec((4, 32, PANEL), lambda i: (i, 10, 0)),
        ],
        out_specs=pl.BlockSpec((ALL // 2, PANEL), lambda i: (0, i)),
        out_shape=jax.ShapeDtypeStruct((ALL // 2, D), kind),
        scratch_shapes=[pltpu.VMEM((4, 128, 2 * LAST), BF)],
        compiler_params=pltpu.CompilerParams(vmem_limit_bytes=32 * 2**20),
        cost_estimate=pl.CostEstimate(
            flops=3 * 10**9, bytes_accessed=10 * 10**6, transcendentals=0
        ),
        name="second_grad",
    )(ggu, full, full, full)


def down_kernel(act_ref, down_ref, near_ref, core_ref):
    part = dot(act_ref[:, :UNITS], down_ref[...].reshape(UNITS, PANEL))
    near_ref[...] = part[: ALL // 2]
    core_ref[...] = part[ALL // 2 :].astype(BF)


def down_product(active, full):
    half = pl.BlockSpec((ALL // 2, PANEL), lambda c: (0, c))
    return pl.pallas_call(
        down_kernel,
        grid=(4,),
        in_specs=[
            pl.BlockSpec(memory_space=pltpu.VMEM),
            pl.BlockSpec((4, 176, PANEL), lambda c: (c, 2, 0)),
        ],
        out_specs=[half, half],
        out_shape=[
            jax.ShapeDtypeStruct((ALL // 2, D), F32),
            jax.ShapeDtypeStruct((ALL // 2, D), BF),
        ],
        compiler_params=pltpu.CompilerParams(vmem_limit_bytes=32 * 2**20),
        cost_estimate=pl.CostEstimate(
            flops=3 * 10**9, bytes_accessed=12 * 10**6, transcendentals=0
        ),
        name="down_product",
    )(active, full)


def attention_grads_kernel(first_ref, grad_ref, attended_ref, middle_ref, out_ref):
    out_ref[:, :QKVW] = left_product(first_ref[...], grad_ref[...]).astype(BF)
    out_ref[:, QKVW:] = left_product(attended_ref[...], middle_ref[...]).astype(BF)


def attention_grads(first_low, grad_qkv, attended, middle_all):
    return pl.pallas_call(
        attention_grads_kernel,
        grid=(4,),
        in_specs=[
            pl.BlockSpec((SLOTS, PANEL), lambda i: (0, i)),
            pl.BlockSpec((SLOTS, QKVW), lambda i: (0, 0)),
            pl.BlockSpec((SLOTS, QW), lambda i: (0, 0)),
            pl.BlockSpec((SLOTS, PANEL), lambda i: (0, i)),
        ],
        out_specs=pl.BlockSpec((PANEL, QKVW + PANEL), lambda i: (i, 0)),
        out_shape=jax.ShapeDtypeStruct((D, QKVW + PANEL), BF),
        compiler_params=pltpu.CompilerParams(vmem_limit_bytes=32 * 2**20),
        cost_estimate=pl.CostEstimate(
            flops=25 * 10**8, bytes_accessed=10 * 10**6, transcendentals=0
        ),
        name="attention_grads",
    )(first_low, grad_qkv, attended, middle_all)


LANES = 128


def lanes_of(v):
    return lax.broadcasted_iota(jnp.int32, v.shape, v.ndim - 1)


def quarter_turn(v):
    first = lanes_of(v) % HEAD_DIM < HEAD_DIM // 2
    return jnp.where(first, -pltpu.roll(v, 96, 1), pltpu.roll(v, 32, 1))


def doubled(v):
    left = lanes_of(v) < HEAD_DIM
    other = pltpu.roll(v, HEAD_DIM, 1)
    return jnp.where(left, v, other), jnp.where(left, other, v)


def head_rows(ref):
    blocks = []
    for g in range(GROUPS // 2):
        v = ref[:, g * LANES : (g + 1) * LANES].astype(F32)
        left = lanes_of(v) < HEAD_DIM
        blocks += [jnp.where(left, v, 0.0), jnp.where(left, 0.0, v)]
    return jnp.concatenate(blocks, axis=0).astype(BF)


def pair_columns(v, g):
    even = v[2 * g * ROWS : (2 * g + 1) * ROWS]
    odd = v[(2 * g + 1) * ROWS : (2 * g + 2) * ROWS]
    return jnp.where(lanes_of(even) < HEAD_DIM, even, odd)


def softmax_rows(heads, key2, mask):
    scores = right_product(heads, key2).reshape(GROUPS, ROWS, ROWS) * score_scale
    masked = jnp.where(mask[None] > 0.0, scores, -1e30)
    top = jnp.max(masked, axis=-1, keepdims=True)
    total = top + jnp.log(jnp.sum(jnp.exp(masked - top), axis=-1, keepdims=True))
    return jnp.exp(masked - total).reshape(GROUPS * ROWS, ROWS)


def attention_kernel(qkv_ref, cos_ref, sin_ref, mask_ref, query_ref, kv_ref, out_ref):
    cosine, sine = cos_ref[...], sin_ref[...]
    for g in range(GROUPS // 2):
        v = qkv_ref[:, g * LANES : (g + 1) * LANES]
        query_ref[:, g * LANES : (g + 1) * LANES] = (v * cosine + quarter_turn(v) * sine).astype(BF)
    v = qkv_ref[:, QW:]
    kv = jnp.where(lanes_of(v) < HEAD_DIM, v * cosine + quarter_turn(v) * sine, v)
    kv_ref[...] = kv.astype(BF)
    key2, value2 = doubled(kv)
    probs = softmax_rows(head_rows(query_ref), key2.astype(BF), mask_ref[0])
    heads = dot(probs.astype(BF), value2.astype(BF))
    for g in range(GROUPS // 2):
        out_ref[:, g * LANES : (g + 1) * LANES] = pair_columns(heads, g).astype(BF)


def attention_back_kernel(query_ref, kv_ref, grad_ref, cos_ref, sin_ref, mask_ref, out_ref):
    cosine, sine = cos_ref[...], sin_ref[...]
    key2, value2 = doubled(kv_ref[...].astype(F32))
    key2, value2 = key2.astype(BF), value2.astype(BF)
    heads, grads = head_rows(query_ref), head_rows(grad_ref)
    probs = softmax_rows(heads, key2, mask_ref[0])
    grad_value = left_product(probs.astype(BF), grads)
    grad_value = grad_value + pltpu.roll(grad_value, HEAD_DIM, 1)
    grad_probs = right_product(grads, value2)
    inner = jnp.sum(grad_probs * probs, axis=-1, keepdims=True)
    grad_scores = (probs * (grad_probs - inner)).astype(BF)
    grad_query = dot(grad_scores, key2)
    for g in range(GROUPS // 2):
        v = pair_columns(grad_query, g) * score_scale
        out_ref[:, g * LANES : (g + 1) * LANES] = (v * cosine - quarter_turn(v) * sine).astype(BF)
    grad_key = left_product(grad_scores, heads)
    v = (grad_key + pltpu.roll(grad_key, HEAD_DIM, 1)) * score_scale
    grad_key = v * cosine - quarter_turn(v) * sine
    out_ref[:, QW:] = jnp.where(lanes_of(v) < HEAD_DIM, grad_key, grad_value).astype(BF)


def row_block(width):
    return pl.BlockSpec((ROWS, width), lambda b: (b, 0))


MASK_BLOCK = pl.BlockSpec((1, ROWS, ROWS), lambda b: (b, 0, 0))


def attention(qkv, cosine, sine, mask):
    return pl.pallas_call(
        attention_kernel,
        grid=(MEMBERS,),
        in_specs=[row_block(QKVW), row_block(LANES), row_block(LANES), MASK_BLOCK],
        out_specs=[row_block(QW), row_block(LANES), row_block(QW)],
        out_shape=[
            jax.ShapeDtypeStruct((SLOTS, QW), BF),
            jax.ShapeDtypeStruct((SLOTS, LANES), BF),
            jax.ShapeDtypeStruct((SLOTS, QW), BF),
        ],
        compiler_params=pltpu.CompilerParams(vmem_limit_bytes=32 * 2**20),
        cost_estimate=pl.CostEstimate(
            flops=3 * 10**8, bytes_accessed=4 * 10**6, transcendentals=10**6
        ),
        name="attention",
    )(qkv, cosine, sine, mask)


def attention_back(query, kv, grad, cosine, sine, mask):
    return pl.pallas_call(
        attention_back_kernel,
        grid=(MEMBERS,),
        in_specs=[
            row_block(QW),
            row_block(LANES),
            row_block(QW),
            row_block(LANES),
            row_block(LANES),
            MASK_BLOCK,
        ],
        out_specs=row_block(QKVW),
        out_shape=jax.ShapeDtypeStruct((SLOTS, QKVW), BF),
        compiler_params=pltpu.CompilerParams(vmem_limit_bytes=32 * 2**20),
        cost_estimate=pl.CostEstimate(
            flops=8 * 10**8, bytes_accessed=4 * 10**6, transcendentals=10**6
        ),
        name="attention_back",
    )(query, kv, grad, cosine, sine, mask)


def rounded_gain(gain):
    return lax.optimization_barrier(gain.astype(BF)).astype(F32)


def inverse_rms(v):
    return lax.rsqrt(jnp.mean(v * v, axis=-1, keepdims=True) + epsilon)


def norm_back(v, gain, grad):
    r = inverse_rms(v)
    n = v * r
    scaled = grad * gain
    return r * (scaled - n * jnp.mean(scaled * n, axis=-1, keepdims=True)), n


def panels(gate, up):
    blocks = []
    for at in range(0, UNITS, 256):
        blocks += [gate[:, at : at + 256], up[:, at : at + 256]]
    return jnp.concatenate(blocks, axis=1)


def unpanels(v):
    gate = [v[:, :256], v[:, 512:768], v[:, 1024 : 1024 + LAST]]
    up = [v[:, 256:512], v[:, 768:1024], v[:, 1024 + LAST :]]
    return jnp.concatenate(gate, axis=1), jnp.concatenate(up, axis=1)


def on_device(
    tokens,
    cotangent,
    segment_ids,
    positions,
    padding,
    attn_gain,
    query_weight,
    key_weight,
    value_weight,
    output_weight,
    mlp_gain,
    gate_weight,
    up_weight,
    down_weight,
    attn_moment,
    query_moment,
    key_moment,
    value_moment,
    output_moment,
    mlp_moment,
    gate_moment,
    up_moment,
    down_moment,
):
    member = lax.axis_index("grp")
    place = lax.axis_index("dp")
    z, y, low = place // 8, (place // 2) % 4, (place % 2) == 0

    def mine(weight, width):
        return lax.dynamic_slice_in_dim(weight, member * width, width, 1).astype(BF)

    attn_shard = jnp.concatenate(
        [mine(query_weight, QW), mine(key_weight, KW), mine(value_weight, KW)], axis=1
    )
    attn_shard = jnp.concatenate(
        [pair_x(attn_shard, low), turn_pair(mine(output_weight, QW), low)], axis=1
    )
    attn_full = plane_gather(attn_shard)

    gate_mine, up_mine = mine(gate_weight, FW), mine(up_weight, FW)
    first = panels(gate_mine[:, :UNITS], up_mine[:, :UNITS])
    second = panels(gate_mine[:, UNITS:], up_mine[:, UNITS:])
    kept, given = jnp.where(low, first, second), jnp.where(low, second, first)
    gu_shard = in_order(kept, swap_x(given), low)
    tail = gu_shard[:, 2 * PANEL :]
    pieces = [
        gu_shard[:, :PANEL],
        gu_shard[:, PANEL : 2 * PANEL],
        jnp.concatenate([tail[:W_ROWS, :256], tail[W_ROWS:, :256]], axis=1),
        jnp.concatenate([tail[32 * h : 32 * h + 32, 256:] for h in range(4)], axis=1),
        everywhere(mine(down_weight, PANEL), OWNED),
    ]
    mlp_full = plane_gather(jnp.concatenate(pieces, axis=0)).reshape(16, SHARD, PANEL)

    places = jnp.stack([segment_ids, positions, padding])
    places = group_gather(places[None])
    segments, spots, pads = places[:, 0], places[:, 1], places[:, 2]
    rows_in = group_gather(tokens)
    own_moment = jnp.concatenate(
        [query_moment, key_moment, value_moment, output_moment], axis=1
    )
    moments = group_gather(own_moment.astype(BF))
    grads_in = row_gather(cotangent)
    attn_full, moments, grads_in = lax.optimization_barrier((attn_full, moments, grads_in))
    grads_in = jnp.concatenate(grads_in, axis=0)
    moments = moments.astype(F32)
    qkv_full = attn_full[:, :QKVW]
    out_full = attn_full[:, QKVW:].reshape(4, QW, PANEL).transpose(1, 0, 2).reshape(QW, D)

    first_gain = rounded_gain(attn_gain)
    second_gain = rounded_gain(mlp_gain)
    inputs = rows_in.astype(F32)
    n_first = inputs * inverse_rms(inputs)
    first_low = (n_first * first_gain).astype(BF)

    half = HEAD_DIM // 2
    freq = 10000.0 ** (-(jnp.arange(half, dtype=F32) * 2.0 / HEAD_DIM))
    angles = spots.reshape(SLOTS, 1).astype(F32) * jnp.tile(freq, LANES // half)[None]
    cosine, sine = jnp.cos(angles), jnp.sin(angles)
    column = jnp.arange(ROWS, dtype=jnp.int32)
    allowed = jnp.logical_and(
        jnp.logical_and(
            segments[:, :, None] == segments[:, None, :],
            (column[None, :] <= column[:, None])[None],
        ),
        jnp.logical_or(pads[:, None, :] == 1, (column[None, :] == column[:, None])[None]),
    ).astype(F32)

    query_rot, kv, attended = attention(dot(first_low, qkv_full), cosine, sine, allowed)
    middle = tokens.astype(F32) + group_scatter(dot(attended, out_full))
    second_low = (middle * inverse_rms(middle) * second_gain).astype(BF)
    four, core_four = row_gather(second_low)
    grad_gu, active, send = mlp_grads(four, core_four, four.T, core_four.T, grads_in, mlp_full)
    mlp_sum = plane_scatter(send.reshape(16 * SHARD, PANEL))

    second_core = swap_core(second_grad(grad_gu, mlp_full, 1, BF))
    grad_second = row_scatter(
        second_grad(grad_gu, mlp_full, 0, F32) + second_core.astype(F32)
    )
    back, n_second = norm_back(middle, second_gain, grad_second)
    mlp_gain_part = jnp.sum(grad_second * n_second, axis=0)
    grad_middle = cotangent.astype(F32) + back
    middle_all = group_gather(grad_middle.astype(BF))
    grad_attended = right_product(middle_all, out_full).astype(BF)
    grad_qkv = attention_back(query_rot, kv, grad_attended, cosine, sine, allowed)
    attn_send = attention_grads(first_low, grad_qkv, attended, middle_all)
    attn_sum = plane_scatter(attn_send)

    attn_send, grad_qkv, active = lax.optimization_barrier((attn_send, grad_qkv, active))
    grad_first = right_product(grad_qkv, qkv_full)
    attn_gain_part = jnp.sum(grad_first * n_first, axis=0)
    gains = jnp.stack([attn_gain_part, mlp_gain_part]).reshape(32, LANES)
    for pairs in (RING_Z, RING_Y):
        gains = gains + sum(lax.ppermute(gains, "dp", p) for p in pairs)
    back, _ = norm_back(tokens.astype(F32), first_gain, group_scatter(grad_first))
    input_grad = grad_middle + back
    down_near, down_core = down_product(active, mlp_full)
    down_near = down_near + swap_core(down_core).astype(F32)
    block_output = (middle + row_scatter(down_near)).astype(BF)

    mine_at = (member // 2) + 2 * (member % 2)

    def by_member(slots):
        return [
            lax.dynamic_index_in_dim(slots, mine_at ^ at, 0, keepdims=False) for at in (0, 2, 1, 3)
        ]

    def updated(weight, columns, start, size):
        moved = jnp.concatenate([block[:, start : start + size] for block in columns], axis=1)
        return weight - learn_rate * moved.astype(F32)

    wide, narrow = mlp_sum[256:320], mlp_sum[320:352]
    gu_part = jnp.concatenate(
        [
            mlp_sum[:128],
            mlp_sum[128:256],
            jnp.concatenate([wide[:, :256], wide[:, 256:]], axis=0),
            jnp.concatenate([narrow[:, h * LANES : (h + 1) * LANES] for h in range(4)], axis=0),
        ],
        axis=1,
    )
    kept, given = halves(gu_part, low)
    other = swap_x(given)
    first = unpanels(jnp.where(low, kept, other))
    second = unpanels(jnp.where(low, other, kept))
    gate_rows = jnp.concatenate([first[0], second[0]], axis=1).astype(F32)
    up_rows = jnp.concatenate([first[1], second[1]], axis=1).astype(F32)
    down_rows = everywhere(mlp_sum[352:], RETURN).astype(F32)
    gate_momentum = 0.5 * gate_moment + 0.5 * gate_rows
    up_momentum = 0.5 * up_moment + 0.5 * up_rows
    down_momentum = 0.5 * down_moment + 0.5 * down_rows
    gu_moved = by_member(
        group_gather(jnp.concatenate([gate_momentum, up_momentum], axis=1).astype(BF)).reshape(
            MEMBERS, W_ROWS, GUW
        )
    )
    down_moved = by_member(
        group_gather(down_momentum.astype(BF)).reshape(MEMBERS, DOWN_ROWS, PANEL)
    )

    mlp_done = (
        gate_momentum,
        up_momentum,
        down_momentum,
        updated(gate_weight, gu_moved, 0, FW),
        updated(up_weight, gu_moved, FW, FW),
        updated(down_weight, down_moved, 0, PANEL),
    )
    attn_sum, gains, input_grad, block_output, mlp_done = lax.optimization_barrier(
        (attn_sum, gains, input_grad, block_output, mlp_done)
    )
    gate_momentum, up_momentum, down_momentum, gate_updated, up_updated, down_updated = mlp_done

    turned = everywhere(attn_sum[:, QKVW:], TURN)
    both = jnp.concatenate([attn_sum[:, :QKVW], turned], axis=1)
    gains = two_parts(gains)
    kept, given = halves(both, low)
    width = QKVW + PANEL
    near = swap_x(jnp.concatenate([given, gains], axis=1))
    far = swap_far(jnp.concatenate([kept, gains], axis=1))
    both_far = far_x(jnp.concatenate([given, gains], axis=1))
    own_total = kept.astype(F32) + near[:, :width].astype(F32)
    far_total = far[:, :width].astype(F32) + both_far[:, :width].astype(F32)
    gains = sum(one_part(part) for part in (gains, near[:, width:], far[:, width:], both_far[:, width:]))
    totals = jnp.concatenate([own_total, far_total], axis=0).astype(BF)
    rider = jnp.concatenate([two_parts(gains), jnp.zeros((W_ROWS, LANES), BF)], axis=0)
    other = swap_core(jnp.concatenate([totals, rider], axis=1))
    gains = gains + one_part(other[:W_ROWS, width:])
    totals = jnp.concatenate([totals, other[:, :width]], axis=0).astype(F32)

    own_moved = 0.5 * own_moment + 0.5 * own_total
    query_momentum = own_moved[:, :QW]
    key_momentum = own_moved[:, QW : QW + KW]
    value_momentum = own_moved[:, QW + KW : QKVW]
    output_momentum = own_moved[:, QKVW:]

    attn_moved = by_member((0.5 * moments + 0.5 * totals).reshape(MEMBERS, W_ROWS, width))

    gains = 0.5 * jnp.stack([attn_moment, mlp_moment]) + 0.5 * gains.reshape(2, D)
    return (
        block_output,
        input_grad,
        gains[0],
        query_momentum,
        key_momentum,
        value_momentum,
        output_momentum,
        gains[1],
        gate_momentum,
        up_momentum,
        down_momentum,
        attn_gain - learn_rate * gains[0],
        updated(query_weight, attn_moved, 0, QW),
        updated(key_weight, attn_moved, QW, KW),
        updated(value_weight, attn_moved, QW + KW, KW),
        updated(output_weight, attn_moved, QKVW, PANEL),
        mlp_gain - learn_rate * gains[1],
        gate_updated,
        up_updated,
        down_updated,
    )


def solution(mesh):
    rows = P(("grp", "dp"), None)
    flat = P(("grp", "dp"))
    weight = P("dp", None)
    moment = P("dp", "grp")
    everyone = P()
    weights = (everyone,) + (weight,) * 4 + (everyone,) + (weight,) * 3
    moments = (everyone,) + (moment,) * 4 + (everyone,) + (moment,) * 3
    return jax.shard_map(
        on_device,
        mesh=mesh,
        in_specs=(rows, rows, flat, flat, flat) + weights + moments,
        out_specs=(rows, rows) + moments + weights,
        check_vma=False,
    )
```

```python
import jax
import jax.numpy as jnp
from jax import lax
from jax.experimental import pallas as pl
from jax.experimental.pallas import tpu as pltpu
from jax.sharding import PartitionSpec as P

D = 2048
HEAD_DIM = 64
GROUPS = 8
ROWS = 128
MEMBERS = 4
SLOTS = ROWS * MEMBERS
QW = 512
KW = 64
QKVW = QW + 2 * KW
FW = 1408
GUW = 2 * FW
PANEL = 512
DOWN_ROWS = 176
W_ROWS = 64

epsilon = 1e-05
learn_rate = 0.005
score_scale = 0.125

BF = jnp.bfloat16
F32 = jnp.float32

PLANES = [[z * 8 + y * 2 + x for z in range(4) for y in range(4)] for x in range(2)]
SWAP_X = [(i, i ^ 1) for i in range(32)]
SWAP_CORE = [(m, m ^ 1) for m in range(4)]
SWAP_FAR = [(m, m ^ 2) for m in range(4)]
SWAP_FAR_X = [(m * 32 + i, (m ^ 2) * 32 + (i ^ 1)) for m in range(4) for i in range(32)]
MZQ = [(m, z, q) for m in range(4) for z in range(4) for q in range(8)]


def spot(m, z, q):
    return m * 32 + z * 8 + q


TURN = [(spot(m, z, q), spot(z, m, q)) for m, z, q in MZQ]
TURN_X = [(spot(m, z, q), spot(z, m, q ^ 1)) for m, z, q in MZQ]
TURN_IN = [[(spot(m, z, q), spot((z + k) % 4, m, q)) for m, z, q in MZQ] for k in range(4)]
OWNED = [(spot(m, z, q), spot(z, m, (q & 3) * 2 + (q >> 2))) for m, z, q in MZQ]
RETURN = [(b, a) for a, b in OWNED]


def ring(place, k):
    return [(i, i + ((i // place + k) % 4 - i // place % 4) * place) for i in range(32)]


RING_Z = [ring(8, k) for k in (1, 2, 3)]
RING_Y = [ring(2, k) for k in (1, 2, 3)]


def swap_x(v):
    return lax.ppermute(v, "dp", SWAP_X)


def swap_core(v):
    return lax.ppermute(v, "grp", SWAP_CORE)


def swap_far(v):
    return lax.ppermute(v, "grp", SWAP_FAR)


def everywhere(v, pairs):
    return lax.ppermute(v, ("grp", "dp"), pairs)


def plane_gather(v):
    return lax.all_gather(v, "dp", axis=0, tiled=True, axis_index_groups=PLANES)


def plane_scatter(v):
    return lax.psum_scatter(
        v, "dp", scatter_dimension=0, tiled=True, axis_index_groups=PLANES
    )


def ring_scatter(v, pairs, at, extra=None):
    rows = v.shape[0] // 4

    def chunk(k):
        part = lax.dynamic_slice_in_dim(v, lax.rem(at + k, 4) * rows, rows, 0)
        return part if extra is None else jnp.concatenate([part, extra], axis=1)

    total = chunk(0).astype(F32)
    for k, p in enumerate(pairs):
        total = total + lax.ppermute(chunk(k + 1), "dp", p).astype(F32)
    return total


def group_gather(v):
    pair = jnp.concatenate([v, swap_far(v)], axis=0)
    return jnp.concatenate([pair, swap_core(pair)], axis=0)


def group_scatter_near(partial):
    half = 2 * ROWS
    return partial[:half] + swap_core(partial[half:].astype(BF)).astype(F32)


def group_scatter_far(near):
    return near[:ROWS] + swap_far(near[ROWS:].astype(BF)).astype(F32)


def group_scatter(partial):
    return group_scatter_far(group_scatter_near(partial))


def far_x(v):
    return everywhere(v, SWAP_FAR_X)


def row_gather(v):
    four = jnp.concatenate([v, swap_x(v), swap_far(v), far_x(v)], axis=0)
    return four, swap_core(four)


def row_scatter(near):
    low_part, far_part, far_x_part = (
        near[k * ROWS : (k + 1) * ROWS].astype(BF) for k in (1, 2, 3)
    )
    return (
        near[:ROWS]
        + swap_x(low_part).astype(F32)
        + swap_far(far_part).astype(F32)
        + far_x(far_x_part).astype(F32)
    )


def in_order(own, other, low):
    return jnp.concatenate([jnp.where(low, own, other), jnp.where(low, other, own)], axis=0)


def pair_x(v, low):
    return in_order(v, swap_x(v), low)


def turn_pair(v, low):
    return in_order(everywhere(v, TURN), everywhere(v, TURN_X), low)


def halves(v, low):
    rows = v.shape[0] // 2
    return jnp.where(low, v[:rows], v[rows:]), jnp.where(low, v[rows:], v[:rows])


def two_parts(v):
    high = lax.reduce_precision(v, 8, 7)
    return jnp.concatenate([high.astype(BF), (v - high).astype(BF)], axis=0)


def one_part(v):
    rows = v.shape[0] // 2
    return v[:rows].astype(F32) + v[rows:].astype(F32)


def dot(left, right):
    return jnp.dot(left, right, preferred_element_type=F32)


def left_product(left, right):
    return lax.dot_general(left, right, (((0,), (0,)), ((), ())), preferred_element_type=F32)


def right_product(left, right):
    return lax.dot_general(left, right, (((1,), (1,)), ((), ())), preferred_element_type=F32)


ALL = 1024
UNITS = 704
LAST = 192
SHARD = 528


TAIL = [(256, 64, 256 * h, 64 * h, 0, 256) for h in range(2)]
TAIL += [(320, 32, 128 * h, 32 * h, 256, 128) for h in range(4)]


def tail_pieces(shard):
    for row, rows, column, at, start, width in TAIL:
        yield (
            shard.at[:, pl.ds(row, rows), pl.ds(column, width)],
            (slice(None), pl.ds(at, rows), pl.ds(start, width)),
        )


def tail_loads(full, tail, sems):
    return [
        pltpu.make_async_copy(src, tail.at[at], sems.at[i])
        for i, (src, at) in enumerate(tail_pieces(full))
    ]


def down_blocks(shard, down):
    return [
        (shard.at[4 * c + j, pl.ds(352, 176), :], down.at[c, pl.ds(176 * j, 176), :])
        for c in range(4)
        for j in range(4)
    ]


def mlp_kernel(
    four_ref,
    core_ref,
    four_t_ref,
    core_t_ref,
    cot_four_ref,
    cot_core_ref,
    panel_ref,
    full,
    ggu_ref,
    act_ref,
    send,
    down,
    tail,
    gpan,
    gtail,
    gdown,
    in_sem,
    tail_sem,
    pan_sem,
    out_sem,
):
    step = pl.program_id(0)
    loads = [
        pltpu.make_async_copy(src, dst, in_sem.at[i])
        for i, (src, dst) in enumerate(down_blocks(full, down))
    ]
    tails = tail_loads(full, tail, tail_sem)

    @pl.when(step == 0)
    def _():
        for copy in loads + tails:
            copy.start()

    def panel_out(at):
        return pltpu.make_async_copy(
            gpan.at[at], send.at[:, pl.ds(128 * at, 128), :], pan_sem.at[at]
        )

    def block(weights, start, width, store):
        halves_of = [dot(ref[...], weights) for ref in (four_ref, core_ref)]

        @pl.when(step == 0)
        def _():
            for copy in loads:
                copy.wait()

        for half, (h, c_ref) in enumerate(zip(halves_of, (cot_four_ref, cot_core_ref))):
            rows = pl.ds(half * (ALL // 2), ALL // 2)
            gate, up = h[:, :width], h[:, width:]
            prod = right_product(c_ref[:, :PANEL], down[0, pl.ds(start, width), :])
            for c in range(1, 4):
                prod += right_product(
                    c_ref[:, c * PANEL : (c + 1) * PANEL], down[c, pl.ds(start, width), :]
                )
            sig = 1.0 / (1.0 + jnp.exp(-gate))
            silu = gate * sig
            act_ref[rows, :width] = (silu * up).astype(BF)
            ggu_ref[rows, :width] = (prod * up * sig * (1.0 + gate * (1.0 - sig))).astype(BF)
            ggu_ref[rows, width : 2 * width] = (prod * silu).astype(BF)
        for c in range(4):
            columns = slice(c * PANEL, (c + 1) * PANEL)
            grads = left_product(act_ref[: ALL // 2, :width], cot_four_ref[:, columns])
            grads += left_product(act_ref[ALL // 2 :, :width], cot_core_ref[:, columns])
            gdown[c, pl.ds(start, width), :] = grads.astype(BF)
        grads = dot(four_t_ref[...], ggu_ref[: ALL // 2, : 2 * width])
        grads += dot(core_t_ref[...], ggu_ref[ALL // 2 :, : 2 * width])
        store(grads.astype(BF))

    @pl.when(step < 2)
    def _():
        def store(grads):
            gpan[step] = grads.reshape(16, 128, PANEL)

        block(panel_ref[...].reshape(D, PANEL), pl.multiple_of(256 * step, 256), 256, store)
        panel_out(step).start()

    @pl.when(step == 2)
    def _():
        def store(grads):
            gtail[...] = grads.reshape(16, 128, 2 * LAST)

        for copy in tails:
            copy.wait()
        block(tail[...].reshape(D, 2 * LAST), 512, LAST, store)
        outs = [
            pltpu.make_async_copy(gtail.at[at], dst, tail_sem.at[i])
            for i, (dst, at) in enumerate(tail_pieces(send))
        ]
        outs += [
            pltpu.make_async_copy(src, dst, out_sem.at[i])
            for i, (dst, src) in enumerate(down_blocks(send, gdown))
        ]
        for copy in outs:
            copy.start()
        for copy in outs + [panel_out(0), panel_out(1)]:
            copy.wait()


def mlp_grads(four, core, four_t, core_t, cot_four, cot_core, full):
    return pl.pallas_call(
        mlp_kernel,
        grid=(3,),
        in_specs=[pl.BlockSpec(memory_space=pltpu.VMEM)] * 6
        + [
            pl.BlockSpec((16, 128, PANEL), lambda i: (0, jnp.minimum(i, 1), 0)),
            pl.BlockSpec(memory_space=pl.ANY),
        ],
        out_specs=[
            pl.BlockSpec((ALL, 512), lambda i: (0, i)),
            pl.BlockSpec((ALL, 256), lambda i: (0, i)),
            pl.BlockSpec(memory_space=pl.ANY),
        ],
        out_shape=[
            jax.ShapeDtypeStruct((ALL, 1536), BF),
            jax.ShapeDtypeStruct((ALL, 768), BF),
            jax.ShapeDtypeStruct((16, SHARD, PANEL), BF),
        ],
        scratch_shapes=[
            pltpu.VMEM((4, UNITS, PANEL), BF),
            pltpu.VMEM((16, 128, 2 * LAST), BF),
            pltpu.VMEM((2, 16, 128, PANEL), BF),
            pltpu.VMEM((16, 128, 2 * LAST), BF),
            pltpu.VMEM((4, UNITS, PANEL), BF),
            pltpu.SemaphoreType.DMA((16,)),
            pltpu.SemaphoreType.DMA((6,)),
            pltpu.SemaphoreType.DMA((2,)),
            pltpu.SemaphoreType.DMA((16,)),
        ],
        compiler_params=pltpu.CompilerParams(vmem_limit_bytes=44 * 2**20),
        cost_estimate=pl.CostEstimate(
            flops=18 * 10**9, bytes_accessed=45 * 10**6, transcendentals=10**6
        ),
        name="mlp_grads",
    )(four, core, four_t, core_t, cot_four, cot_core, full, full)


def second_kernel(g_ref, panel_ref, wide_ref, narrow_ref, out_ref, tail):
    for row, rows, column, at, start, width in TAIL:
        piece = wide_ref if row == 256 else narrow_ref
        tail[:, at : at + rows, start : start + width] = piece[:, :, column : column + width]
    total = right_product(g_ref[:, :PANEL], panel_ref[:, :128].reshape(PANEL, PANEL))
    total += right_product(
        g_ref[:, PANEL : 2 * PANEL], panel_ref[:, 128:].reshape(PANEL, PANEL)
    )
    total += right_product(
        g_ref[:, 2 * PANEL : 2 * PANEL + 2 * LAST], tail[...].reshape(PANEL, 2 * LAST)
    )
    out_ref[...] = total.astype(out_ref.dtype)


def second_grad(ggu, full, half, kind):
    return pl.pallas_call(
        second_kernel,
        grid=(4,),
        in_specs=[
            pl.BlockSpec((ALL // 2, 1536), lambda i: (half, 0)),
            pl.BlockSpec((4, 256, PANEL), lambda i: (i, 0, 0)),
            pl.BlockSpec((4, 64, PANEL), lambda i: (i, 4, 0)),
            pl.BlockSpec((4, 32, PANEL), lambda i: (i, 10, 0)),
        ],
        out_specs=pl.BlockSpec((ALL // 2, PANEL), lambda i: (0, i)),
        out_shape=jax.ShapeDtypeStruct((ALL // 2, D), kind),
        scratch_shapes=[pltpu.VMEM((4, 128, 2 * LAST), BF)],
        compiler_params=pltpu.CompilerParams(vmem_limit_bytes=32 * 2**20),
        cost_estimate=pl.CostEstimate(
            flops=3 * 10**9, bytes_accessed=10 * 10**6, transcendentals=0
        ),
        name="second_grad",
    )(ggu, full, full, full)


def down_kernel(act_ref, down_ref, near_ref, core_ref):
    part = dot(act_ref[:, :UNITS], down_ref[...].reshape(UNITS, PANEL))
    near_ref[...] = part[: ALL // 2]
    core_ref[...] = part[ALL // 2 :].astype(BF)


def down_product(active, full):
    half = pl.BlockSpec((ALL // 2, PANEL), lambda c: (0, c))
    return pl.pallas_call(
        down_kernel,
        grid=(4,),
        in_specs=[
            pl.BlockSpec(memory_space=pltpu.VMEM),
            pl.BlockSpec((4, 176, PANEL), lambda c: (c, 2, 0)),
        ],
        out_specs=[half, half],
        out_shape=[
            jax.ShapeDtypeStruct((ALL // 2, D), F32),
            jax.ShapeDtypeStruct((ALL // 2, D), BF),
        ],
        compiler_params=pltpu.CompilerParams(vmem_limit_bytes=32 * 2**20),
        cost_estimate=pl.CostEstimate(
            flops=3 * 10**9, bytes_accessed=12 * 10**6, transcendentals=0
        ),
        name="down_product",
    )(active, full)


LANES = 128


def lanes_of(v):
    return lax.broadcasted_iota(jnp.int32, v.shape, v.ndim - 1)


def quarter_turn(v):
    first = lanes_of(v) % HEAD_DIM < HEAD_DIM // 2
    return jnp.where(first, -pltpu.roll(v, 96, 1), pltpu.roll(v, 32, 1))


def doubled(v):
    left = lanes_of(v) < HEAD_DIM
    other = pltpu.roll(v, HEAD_DIM, 1)
    return jnp.where(left, v, other), jnp.where(left, other, v)


def head_rows(ref):
    blocks = []
    for g in range(GROUPS // 2):
        v = ref[:, g * LANES : (g + 1) * LANES].astype(F32)
        left = lanes_of(v) < HEAD_DIM
        blocks += [jnp.where(left, v, 0.0), jnp.where(left, 0.0, v)]
    return jnp.concatenate(blocks, axis=0).astype(BF)


def pair_columns(v, g):
    even = v[2 * g * ROWS : (2 * g + 1) * ROWS]
    odd = v[(2 * g + 1) * ROWS : (2 * g + 2) * ROWS]
    return jnp.where(lanes_of(even) < HEAD_DIM, even, odd)


def softmax_rows(heads, key2, mask):
    scores = right_product(heads, key2).reshape(GROUPS, ROWS, ROWS) * score_scale
    masked = jnp.where(mask[None] > 0.0, scores, -1e30)
    top = jnp.max(masked, axis=-1, keepdims=True)
    total = top + jnp.log(jnp.sum(jnp.exp(masked - top), axis=-1, keepdims=True))
    return jnp.exp(masked - total).reshape(GROUPS * ROWS, ROWS)


def seq_rows(step):
    return pl.ds(pl.multiple_of(jnp.minimum(step, MEMBERS - 1) * ROWS, ROWS), ROWS)


def attention_kernel(
    first_ref,
    weight_ref,
    cos_ref,
    sin_ref,
    mask_ref,
    query_ref,
    kv_ref,
    att_ref,
    near_ref,
    core_ref,
    qkv,
    att,
):
    step = pl.program_id(0)

    @pl.when(step == 0)
    def _():
        qkv[...] = dot(first_ref[...], weight_ref[:, QW:])

    @pl.when(step < MEMBERS)
    def _():
        rows = seq_rows(step)
        cosine, sine = cos_ref[...], sin_ref[...]
        for g in range(GROUPS // 2):
            v = qkv[rows, g * LANES : (g + 1) * LANES]
            query_ref[:, g * LANES : (g + 1) * LANES] = (
                v * cosine + quarter_turn(v) * sine
            ).astype(BF)
        v = qkv[rows, QW:]
        kv = jnp.where(lanes_of(v) < HEAD_DIM, v * cosine + quarter_turn(v) * sine, v)
        kv_ref[...] = kv.astype(BF)
        key2, value2 = doubled(kv)
        probs = softmax_rows(head_rows(query_ref), key2.astype(BF), mask_ref[0])
        heads = dot(probs.astype(BF), value2.astype(BF))
        for g in range(GROUPS // 2):
            pair = pair_columns(heads, g).astype(BF)
            att_ref[:, g * LANES : (g + 1) * LANES] = pair
            att[rows, g * LANES : (g + 1) * LANES] = pair

    @pl.when(step >= MEMBERS)
    def _():
        block = pl.ds(pl.multiple_of((step - MEMBERS) * QW, QW), QW)
        part = dot(att[...], weight_ref[block, :QW])
        near_ref[...] = part[: SLOTS // 2]
        core_ref[...] = part[SLOTS // 2 :].astype(BF)


def attention_back_kernel(
    middle_ref,
    weight_ref,
    first_ref,
    att_ref,
    query_ref,
    kv_ref,
    cos_ref,
    sin_ref,
    mask_ref,
    grad_ref,
    send_ref,
    upstream,
    grads,
):
    step = pl.program_id(0)

    @pl.when(step == 0)
    def _():
        total = right_product(middle_ref[:, :PANEL], weight_ref[:QW, :QW])
        for c in range(1, 4):
            total += right_product(
                middle_ref[:, c * PANEL : (c + 1) * PANEL],
                weight_ref[c * QW : (c + 1) * QW, :QW],
            )
        upstream[...] = total.astype(BF)

    @pl.when(step < MEMBERS)
    def _():
        rows = seq_rows(step)
        cosine, sine = cos_ref[...], sin_ref[...]
        key2, value2 = doubled(kv_ref[...].astype(F32))
        key2, value2 = key2.astype(BF), value2.astype(BF)
        heads, lifted = head_rows(query_ref), head_rows(upstream.at[rows])
        probs = softmax_rows(heads, key2, mask_ref[0])
        grad_value = left_product(probs.astype(BF), lifted)
        grad_value = grad_value + pltpu.roll(grad_value, HEAD_DIM, 1)
        grad_probs = right_product(lifted, value2)
        inner = jnp.sum(grad_probs * probs, axis=-1, keepdims=True)
        grad_scores = (probs * (grad_probs - inner)).astype(BF)
        grad_query = dot(grad_scores, key2)
        for g in range(GROUPS // 2):
            v = pair_columns(grad_query, g) * score_scale
            v = (v * cosine - quarter_turn(v) * sine).astype(BF)
            grad_ref[:, g * LANES : (g + 1) * LANES] = v
            grads[rows, g * LANES : (g + 1) * LANES] = v
        grad_key = left_product(grad_scores, heads)
        v = (grad_key + pltpu.roll(grad_key, HEAD_DIM, 1)) * score_scale
        grad_key = v * cosine - quarter_turn(v) * sine
        v = jnp.where(lanes_of(v) < HEAD_DIM, grad_key, grad_value).astype(BF)
        grad_ref[:, QW:] = v
        grads[rows, QW:] = v

    @pl.when(step >= MEMBERS)
    def _():
        block = pl.ds(pl.multiple_of((step - MEMBERS) * PANEL, PANEL), PANEL)
        send_ref[:, :QW] = left_product(att_ref[...], middle_ref[:, block]).astype(BF)
        send_ref[:, QW:] = left_product(first_ref[:, block], grads[...]).astype(BF)


def all_of(shape):
    return pl.BlockSpec(shape, lambda s: (0,) * len(shape), pipeline_mode=pl.Buffered(1))


def by_seq(width):
    return pl.BlockSpec((ROWS, width), lambda s: (jnp.minimum(s, MEMBERS - 1), 0))


MASK_BLOCK = pl.BlockSpec((1, ROWS, ROWS), lambda s: (jnp.minimum(s, MEMBERS - 1), 0, 0))


def attention(first_low, weights, cosine, sine, mask):
    half = pl.BlockSpec((SLOTS // 2, PANEL), lambda s: (0, jnp.maximum(s - MEMBERS, 0)))
    return pl.pallas_call(
        attention_kernel,
        grid=(2 * MEMBERS,),
        in_specs=[
            all_of((SLOTS, D)),
            all_of((D, QW + QKVW)),
            by_seq(LANES),
            by_seq(LANES),
            MASK_BLOCK,
        ],
        out_specs=[by_seq(QW), by_seq(LANES), by_seq(QW), half, half],
        out_shape=[
            jax.ShapeDtypeStruct((SLOTS, QW), BF),
            jax.ShapeDtypeStruct((SLOTS, LANES), BF),
            jax.ShapeDtypeStruct((SLOTS, QW), BF),
            jax.ShapeDtypeStruct((SLOTS // 2, D), F32),
            jax.ShapeDtypeStruct((SLOTS // 2, D), BF),
        ],
        scratch_shapes=[pltpu.VMEM((SLOTS, QKVW), F32), pltpu.VMEM((SLOTS, QW), BF)],
        compiler_params=pltpu.CompilerParams(vmem_limit_bytes=40 * 2**20),
        cost_estimate=pl.CostEstimate(
            flops=3 * 10**9, bytes_accessed=12 * 10**6, transcendentals=10**6
        ),
        name="attention",
    )(first_low, weights, cosine, sine, mask)


def attention_back(middle_all, weights, first_low, attended, query, kv, cosine, sine, mask):
    return pl.pallas_call(
        attention_back_kernel,
        grid=(2 * MEMBERS,),
        in_specs=[
            all_of((SLOTS, D)),
            all_of((D, QW + QKVW)),
            all_of((SLOTS, D)),
            all_of((SLOTS, QW)),
            by_seq(QW),
            by_seq(LANES),
            by_seq(LANES),
            by_seq(LANES),
            MASK_BLOCK,
        ],
        out_specs=[
            by_seq(QKVW),
            pl.BlockSpec((PANEL, QW + QKVW), lambda s: (jnp.maximum(s - MEMBERS, 0), 0)),
        ],
        out_shape=[
            jax.ShapeDtypeStruct((SLOTS, QKVW), BF),
            jax.ShapeDtypeStruct((D, QW + QKVW), BF),
        ],
        scratch_shapes=[pltpu.VMEM((SLOTS, QW), BF), pltpu.VMEM((SLOTS, QKVW), BF)],
        compiler_params=pltpu.CompilerParams(vmem_limit_bytes=40 * 2**20),
        cost_estimate=pl.CostEstimate(
            flops=5 * 10**9, bytes_accessed=16 * 10**6, transcendentals=10**6
        ),
        name="attention_back",
    )(middle_all, weights, first_low, attended, query, kv, cosine, sine, mask)


def rounded_gain(gain):
    return lax.optimization_barrier(gain.astype(BF)).astype(F32)


def inverse_rms(v):
    return lax.rsqrt(jnp.mean(v * v, axis=-1, keepdims=True) + epsilon)


def norm_back(v, gain, grad):
    r = inverse_rms(v)
    n = v * r
    scaled = grad * gain
    return r * (scaled - n * jnp.mean(scaled * n, axis=-1, keepdims=True)), n


def panels(gate, up):
    blocks = []
    for at in range(0, UNITS, 256):
        blocks += [gate[:, at : at + 256], up[:, at : at + 256]]
    return jnp.concatenate(blocks, axis=1)


def unpanels(v):
    gate = [v[:, :256], v[:, 512:768], v[:, 1024 : 1024 + LAST]]
    up = [v[:, 256:512], v[:, 768:1024], v[:, 1024 + LAST :]]
    return jnp.concatenate(gate, axis=1), jnp.concatenate(up, axis=1)


def on_device(
    tokens,
    cotangent,
    segment_ids,
    positions,
    padding,
    attn_gain,
    query_weight,
    key_weight,
    value_weight,
    output_weight,
    mlp_gain,
    gate_weight,
    up_weight,
    down_weight,
    attn_moment,
    query_moment,
    key_moment,
    value_moment,
    output_moment,
    mlp_moment,
    gate_moment,
    up_moment,
    down_moment,
):
    member = lax.axis_index("grp")
    place = lax.axis_index("dp")
    z, y, low = place // 8, (place // 2) % 4, (place % 2) == 0

    def mine(weight, width):
        return lax.dynamic_slice_in_dim(weight, member * width, width, 1).astype(BF)

    attn_shard = jnp.concatenate(
        [mine(query_weight, QW), mine(key_weight, KW), mine(value_weight, KW)], axis=1
    )
    attn_shard = jnp.concatenate(
        [turn_pair(mine(output_weight, QW), low), pair_x(attn_shard, low)], axis=1
    )
    attn_full = plane_gather(attn_shard)

    gate_mine, up_mine = mine(gate_weight, FW), mine(up_weight, FW)
    first = panels(gate_mine[:, :UNITS], up_mine[:, :UNITS])
    second = panels(gate_mine[:, UNITS:], up_mine[:, UNITS:])
    kept, given = jnp.where(low, first, second), jnp.where(low, second, first)
    gu_shard = in_order(kept, swap_x(given), low)
    tail = gu_shard[:, 2 * PANEL :]
    pieces = [
        gu_shard[:, :PANEL],
        gu_shard[:, PANEL : 2 * PANEL],
        jnp.concatenate([tail[:W_ROWS, :256], tail[W_ROWS:, :256]], axis=1),
        jnp.concatenate([tail[32 * h : 32 * h + 32, 256:] for h in range(4)], axis=1),
        everywhere(mine(down_weight, PANEL), OWNED),
    ]
    mlp_full = plane_gather(jnp.concatenate(pieces, axis=0)).reshape(16, SHARD, PANEL)

    places = jnp.stack([segment_ids, positions, padding])
    places = group_gather(places[None])
    segments, spots, pads = places[:, 0], places[:, 1], places[:, 2]
    rows_in = group_gather(tokens)
    rows_in, upstream = lax.optimization_barrier((rows_in, cotangent))
    cot_four, cot_core = row_gather(upstream)
    own_moment = jnp.concatenate(
        [query_moment, key_moment, value_moment, output_moment], axis=1
    )
    moments = group_gather(own_moment.astype(BF))

    first_gain = rounded_gain(attn_gain)
    second_gain = rounded_gain(mlp_gain)
    inputs = rows_in.astype(F32)
    n_first = inputs * inverse_rms(inputs)
    first_low = (n_first * first_gain).astype(BF)

    half = HEAD_DIM // 2
    freq = 10000.0 ** (-(jnp.arange(half, dtype=F32) * 2.0 / HEAD_DIM))
    angles = spots.reshape(SLOTS, 1).astype(F32) * jnp.tile(freq, LANES // half)[None]
    cosine, sine = jnp.cos(angles), jnp.sin(angles)
    column = jnp.arange(ROWS, dtype=jnp.int32)
    allowed = jnp.logical_and(
        jnp.logical_and(
            segments[:, :, None] == segments[:, None, :],
            (column[None, :] <= column[:, None])[None],
        ),
        jnp.logical_or(pads[:, None, :] == 1, (column[None, :] == column[:, None])[None]),
    ).astype(F32)

    attn_full, first_low, cosine, sine, allowed, cot_four = lax.optimization_barrier(
        (attn_full, first_low, cosine, sine, allowed, cot_four)
    )
    query_rot, kv, attended, near, core = attention(first_low, attn_full, cosine, sine, allowed)
    middle = tokens.astype(F32) + group_scatter_far(near + swap_core(core).astype(F32))
    second_low = (middle * inverse_rms(middle) * second_gain).astype(BF)
    four, core_four = row_gather(second_low)
    core_four, cot_core, moments = lax.optimization_barrier((core_four, cot_core, moments))
    moments = moments.astype(F32)
    grad_gu, active, send = mlp_grads(
        four, core_four, four.T, core_four.T, cot_four, cot_core, mlp_full
    )
    mlp_sum = plane_scatter(send.reshape(16 * SHARD, PANEL))

    second_core = swap_core(second_grad(grad_gu, mlp_full, 1, BF))
    grad_second = row_scatter(
        second_grad(grad_gu, mlp_full, 0, F32) + second_core.astype(F32)
    )
    back, n_second = norm_back(middle, second_gain, grad_second)
    mlp_gain_part = jnp.sum(grad_second * n_second, axis=0)
    grad_middle = cotangent.astype(F32) + back
    middle_all = group_gather(grad_middle.astype(BF))
    grad_qkv, attn_send = attention_back(
        middle_all, attn_full, first_low, attended, query_rot, kv, cosine, sine, allowed
    )
    attn_sum = plane_scatter(attn_send)

    attn_send, grad_qkv, active, mlp_sum = lax.optimization_barrier(
        (attn_send, grad_qkv, active, mlp_sum)
    )
    grad_first = right_product(grad_qkv, attn_full[:, QW:])
    attn_gain_part = jnp.sum(grad_first * n_first, axis=0)
    gains = jnp.stack([attn_gain_part, mlp_gain_part]).reshape(32, LANES)
    for pairs in (RING_Z, RING_Y):
        gains = gains + sum(lax.ppermute(gains, "dp", p) for p in pairs)
    back, _ = norm_back(tokens.astype(F32), first_gain, group_scatter(grad_first))
    input_grad = grad_middle + back
    down_near, down_core = down_product(active, mlp_full)
    down_near = down_near + swap_core(down_core).astype(F32)
    block_output = (middle + row_scatter(down_near)).astype(BF)

    mine_at = (member // 2) + 2 * (member % 2)

    def by_member(slots):
        return [
            lax.dynamic_index_in_dim(slots, mine_at ^ at, 0, keepdims=False) for at in (0, 2, 1, 3)
        ]

    def updated(weight, columns, start, size):
        moved = jnp.concatenate([block[:, start : start + size] for block in columns], axis=1)
        return weight - learn_rate * moved.astype(F32)

    wide, narrow = mlp_sum[256:320], mlp_sum[320:352]
    gu_part = jnp.concatenate(
        [
            mlp_sum[:128],
            mlp_sum[128:256],
            jnp.concatenate([wide[:, :256], wide[:, 256:]], axis=0),
            jnp.concatenate([narrow[:, h * LANES : (h + 1) * LANES] for h in range(4)], axis=0),
        ],
        axis=1,
    )
    kept, given = halves(gu_part, low)
    other = swap_x(given)
    first = unpanels(jnp.where(low, kept, other))
    second = unpanels(jnp.where(low, other, kept))
    gate_rows = jnp.concatenate([first[0], second[0]], axis=1).astype(F32)
    up_rows = jnp.concatenate([first[1], second[1]], axis=1).astype(F32)
    down_rows = everywhere(mlp_sum[352:], RETURN).astype(F32)
    gate_momentum = 0.5 * gate_moment + 0.5 * gate_rows
    up_momentum = 0.5 * up_moment + 0.5 * up_rows
    down_momentum = 0.5 * down_moment + 0.5 * down_rows
    gu_moved = by_member(
        group_gather(jnp.concatenate([gate_momentum, up_momentum], axis=1).astype(BF)).reshape(
            MEMBERS, W_ROWS, GUW
        )
    )
    down_moved = by_member(
        group_gather(down_momentum.astype(BF)).reshape(MEMBERS, DOWN_ROWS, PANEL)
    )

    mlp_done = (
        gate_momentum,
        up_momentum,
        down_momentum,
        updated(gate_weight, gu_moved, 0, FW),
        updated(up_weight, gu_moved, FW, FW),
        updated(down_weight, down_moved, 0, PANEL),
    )
    attn_sum, gains, input_grad, block_output, mlp_done = lax.optimization_barrier(
        (attn_sum, gains, input_grad, block_output, mlp_done)
    )
    gate_momentum, up_momentum, down_momentum, gate_updated, up_updated, down_updated = mlp_done

    turned = everywhere(attn_sum[:, :QW], TURN)
    both = jnp.concatenate([attn_sum[:, QW:], turned], axis=1)
    gains = two_parts(gains)
    kept, given = halves(both, low)
    width = QKVW + PANEL
    near = swap_x(jnp.concatenate([given, gains], axis=1))
    far = swap_far(jnp.concatenate([kept, gains], axis=1))
    both_far = far_x(jnp.concatenate([given, gains], axis=1))
    own_total = kept.astype(F32) + near[:, :width].astype(F32)
    far_total = far[:, :width].astype(F32) + both_far[:, :width].astype(F32)
    gains = sum(one_part(part) for part in (gains, near[:, width:], far[:, width:], both_far[:, width:]))
    totals = jnp.concatenate([own_total, far_total], axis=0).astype(BF)
    rider = jnp.concatenate([two_parts(gains), jnp.zeros((W_ROWS, LANES), BF)], axis=0)
    other = swap_core(jnp.concatenate([totals, rider], axis=1))
    gains = gains + one_part(other[:W_ROWS, width:])
    totals = jnp.concatenate([totals, other[:, :width]], axis=0).astype(F32)

    own_moved = 0.5 * own_moment + 0.5 * own_total
    query_momentum = own_moved[:, :QW]
    key_momentum = own_moved[:, QW : QW + KW]
    value_momentum = own_moved[:, QW + KW : QKVW]
    output_momentum = own_moved[:, QKVW:]

    attn_moved = by_member((0.5 * moments + 0.5 * totals).reshape(MEMBERS, W_ROWS, width))

    gains = 0.5 * jnp.stack([attn_moment, mlp_moment]) + 0.5 * gains.reshape(2, D)
    return (
        block_output,
        input_grad,
        gains[0],
        query_momentum,
        key_momentum,
        value_momentum,
        output_momentum,
        gains[1],
        gate_momentum,
        up_momentum,
        down_momentum,
        attn_gain - learn_rate * gains[0],
        updated(query_weight, attn_moved, 0, QW),
        updated(key_weight, attn_moved, QW, KW),
        updated(value_weight, attn_moved, QW + KW, KW),
        updated(output_weight, attn_moved, QKVW, PANEL),
        mlp_gain - learn_rate * gains[1],
        gate_updated,
        up_updated,
        down_updated,
    )


def solution(mesh):
    rows = P(("grp", "dp"), None)
    flat = P(("grp", "dp"))
    weight = P("dp", None)
    moment = P("dp", "grp")
    everyone = P()
    weights = (everyone,) + (weight,) * 4 + (everyone,) + (weight,) * 3
    moments = (everyone,) + (moment,) * 4 + (everyone,) + (moment,) * 3
    return jax.shard_map(
        on_device,
        mesh=mesh,
        in_specs=(rows, rows, flat, flat, flat) + weights + moments,
        out_specs=(rows, rows) + moments + weights,
        check_vma=False,
    )
```

```python
import jax
import jax.numpy as jnp
from jax import lax
from jax.experimental import pallas as pl
from jax.experimental.pallas import tpu as pltpu
from jax.sharding import PartitionSpec as P

D = 2048
HEAD_DIM = 64
GROUPS = 8
ROWS = 128
MEMBERS = 4
SLOTS = ROWS * MEMBERS
QW = 512
KW = 64
QKVW = QW + 2 * KW
FW = 1408
GUW = 2 * FW
PANEL = 512
DOWN_ROWS = 176
W_ROWS = 64

epsilon = 1e-05
learn_rate = 0.005
score_scale = 0.125

BF = jnp.bfloat16
F32 = jnp.float32

PLANES = [[z * 8 + y * 2 + x for z in range(4) for y in range(4)] for x in range(2)]
SWAP_X = [(i, i ^ 1) for i in range(32)]
SWAP_CORE = [(m, m ^ 1) for m in range(4)]
SWAP_FAR = [(m, m ^ 2) for m in range(4)]
SWAP_FAR_X = [(m * 32 + i, (m ^ 2) * 32 + (i ^ 1)) for m in range(4) for i in range(32)]
MZQ = [(m, z, q) for m in range(4) for z in range(4) for q in range(8)]


def spot(m, z, q):
    return m * 32 + z * 8 + q


TURN = [(spot(m, z, q), spot(z, m, q)) for m, z, q in MZQ]
TURN_X = [(spot(m, z, q), spot(z, m, q ^ 1)) for m, z, q in MZQ]
TURN_IN = [[(spot(m, z, q), spot((z + k) % 4, m, q)) for m, z, q in MZQ] for k in range(4)]
OWNED = [(spot(m, z, q), spot(z, m, (q & 3) * 2 + (q >> 2))) for m, z, q in MZQ]
RETURN = [(b, a) for a, b in OWNED]


def ring(place, k):
    return [(i, i + ((i // place + k) % 4 - i // place % 4) * place) for i in range(32)]


RING_Z = [ring(8, k) for k in (1, 2, 3)]
RING_Y = [ring(2, k) for k in (1, 2, 3)]


def swap_x(v):
    return lax.ppermute(v, "dp", SWAP_X)


def swap_core(v):
    return lax.ppermute(v, "grp", SWAP_CORE)


def swap_far(v):
    return lax.ppermute(v, "grp", SWAP_FAR)


def everywhere(v, pairs):
    return lax.ppermute(v, ("grp", "dp"), pairs)


def plane_gather(v):
    return lax.all_gather(v, "dp", axis=0, tiled=True, axis_index_groups=PLANES)


def plane_scatter(v):
    return lax.psum_scatter(
        v, "dp", scatter_dimension=0, tiled=True, axis_index_groups=PLANES
    )


def ring_scatter(v, pairs, at, extra=None):
    rows = v.shape[0] // 4

    def chunk(k):
        part = lax.dynamic_slice_in_dim(v, lax.rem(at + k, 4) * rows, rows, 0)
        return part if extra is None else jnp.concatenate([part, extra], axis=1)

    total = chunk(0).astype(F32)
    for k, p in enumerate(pairs):
        total = total + lax.ppermute(chunk(k + 1), "dp", p).astype(F32)
    return total


def group_gather(v):
    pair = jnp.concatenate([v, swap_far(v)], axis=0)
    return jnp.concatenate([pair, swap_core(pair)], axis=0)


def group_scatter_near(partial):
    half = 2 * ROWS
    return partial[:half] + swap_core(partial[half:].astype(BF)).astype(F32)


def group_scatter_far(near):
    return near[:ROWS] + swap_far(near[ROWS:].astype(BF)).astype(F32)


def group_scatter(partial):
    return group_scatter_far(group_scatter_near(partial))


def far_x(v):
    return everywhere(v, SWAP_FAR_X)


def row_gather(v):
    four = jnp.concatenate([v, swap_x(v), swap_far(v), far_x(v)], axis=0)
    return four, swap_core(four)


def row_scatter(near):
    low_part, far_part, far_x_part = (
        near[k * ROWS : (k + 1) * ROWS].astype(BF) for k in (1, 2, 3)
    )
    return (
        near[:ROWS]
        + swap_x(low_part).astype(F32)
        + swap_far(far_part).astype(F32)
        + far_x(far_x_part).astype(F32)
    )


def in_order(own, other, low):
    return jnp.concatenate([jnp.where(low, own, other), jnp.where(low, other, own)], axis=0)


def pair_x(v, low):
    return in_order(v, swap_x(v), low)


def turn_pair(v, low):
    return in_order(everywhere(v, TURN), everywhere(v, TURN_X), low)


def halves(v, low):
    rows = v.shape[0] // 2
    return jnp.where(low, v[:rows], v[rows:]), jnp.where(low, v[rows:], v[:rows])


def two_parts(v):
    high = lax.reduce_precision(v, 8, 7)
    return jnp.concatenate([high.astype(BF), (v - high).astype(BF)], axis=0)


def one_part(v):
    rows = v.shape[0] // 2
    return v[:rows].astype(F32) + v[rows:].astype(F32)


def dot(left, right):
    return jnp.dot(left, right, preferred_element_type=F32)


def left_product(left, right):
    return lax.dot_general(left, right, (((0,), (0,)), ((), ())), preferred_element_type=F32)


def right_product(left, right):
    return lax.dot_general(left, right, (((1,), (1,)), ((), ())), preferred_element_type=F32)


ALL = 1024
UNITS = 704
LAST = 192
SHARD = 528


TAIL = [(256, 64, 256 * h, 64 * h, 0, 256) for h in range(2)]
TAIL += [(320, 32, 128 * h, 32 * h, 256, 128) for h in range(4)]


def tail_pieces(shard):
    for row, rows, column, at, start, width in TAIL:
        yield (
            shard.at[:, pl.ds(row, rows), pl.ds(column, width)],
            (slice(None), pl.ds(at, rows), pl.ds(start, width)),
        )


def tail_loads(full, tail, sems):
    return [
        pltpu.make_async_copy(src, tail.at[at], sems.at[i])
        for i, (src, at) in enumerate(tail_pieces(full))
    ]


def down_blocks(shard, down):
    return [
        (shard.at[4 * c + j, pl.ds(352, 176), :], down.at[c, pl.ds(176 * j, 176), :])
        for c in range(4)
        for j in range(4)
    ]


def mlp_kernel(
    four_ref,
    core_ref,
    four_t_ref,
    core_t_ref,
    cot_four,
    cot_core,
    panel_ref,
    full,
    ggu_ref,
    act_ref,
    send,
    down,
    tail,
    gpan,
    gtail,
    gdown,
    cot_four_ref,
    cot_core_ref,
    in_sem,
    tail_sem,
    pan_sem,
    out_sem,
):
    step = pl.program_id(0)
    loads = [
        pltpu.make_async_copy(src, dst, in_sem.at[i])
        for i, (src, dst) in enumerate(
            [(cot_four, cot_four_ref), (cot_core, cot_core_ref)] + down_blocks(full, down)
        )
    ]
    tails = tail_loads(full, tail, tail_sem)

    @pl.when(step == 0)
    def _():
        for copy in loads + tails:
            copy.start()

    def panel_out(at):
        return pltpu.make_async_copy(
            gpan.at[at], send.at[:, pl.ds(128 * at, 128), :], pan_sem.at[at]
        )

    def block(weights, start, width, store):
        halves_of = [dot(ref[...], weights) for ref in (four_ref, core_ref)]

        @pl.when(step == 0)
        def _():
            for copy in loads:
                copy.wait()

        for half, (h, c_ref) in enumerate(zip(halves_of, (cot_four_ref, cot_core_ref))):
            rows = pl.ds(half * (ALL // 2), ALL // 2)
            gate, up = h[:, :width], h[:, width:]
            prod = right_product(c_ref[:, :PANEL], down[0, pl.ds(start, width), :])
            for c in range(1, 4):
                prod += right_product(
                    c_ref[:, c * PANEL : (c + 1) * PANEL], down[c, pl.ds(start, width), :]
                )
            sig = 1.0 / (1.0 + jnp.exp(-gate))
            silu = gate * sig
            act_ref[rows, :width] = (silu * up).astype(BF)
            ggu_ref[rows, :width] = (prod * up * sig * (1.0 + gate * (1.0 - sig))).astype(BF)
            ggu_ref[rows, width : 2 * width] = (prod * silu).astype(BF)
        for c in range(4):
            columns = slice(c * PANEL, (c + 1) * PANEL)
            grads = left_product(act_ref[: ALL // 2, :width], cot_four_ref[:, columns])
            grads += left_product(act_ref[ALL // 2 :, :width], cot_core_ref[:, columns])
            gdown[c, pl.ds(start, width), :] = grads.astype(BF)
        grads = dot(four_t_ref[...], ggu_ref[: ALL // 2, : 2 * width])
        grads += dot(core_t_ref[...], ggu_ref[ALL // 2 :, : 2 * width])
        store(grads.astype(BF))

    @pl.when(step < 2)
    def _():
        def store(grads):
            gpan[step] = grads.reshape(16, 128, PANEL)

        block(panel_ref[...].reshape(D, PANEL), pl.multiple_of(256 * step, 256), 256, store)
        panel_out(step).start()

    @pl.when(step == 2)
    def _():
        def store(grads):
            gtail[...] = grads.reshape(16, 128, 2 * LAST)

        for copy in tails:
            copy.wait()
        block(tail[...].reshape(D, 2 * LAST), 512, LAST, store)
        outs = [
            pltpu.make_async_copy(gtail.at[at], dst, tail_sem.at[i])
            for i, (dst, at) in enumerate(tail_pieces(send))
        ]
        outs += [
            pltpu.make_async_copy(src, dst, out_sem.at[i])
            for i, (dst, src) in enumerate(down_blocks(send, gdown))
        ]
        for copy in outs:
            copy.start()
        for copy in outs + [panel_out(0), panel_out(1)]:
            copy.wait()


def mlp_grads(four, core, four_t, core_t, cot_four, cot_core, full):
    return pl.pallas_call(
        mlp_kernel,
        grid=(3,),
        in_specs=[pl.BlockSpec(memory_space=pltpu.VMEM)] * 4
        + [pl.BlockSpec(memory_space=pl.ANY)] * 2
        + [
            pl.BlockSpec((16, 128, PANEL), lambda i: (0, jnp.minimum(i, 1), 0)),
            pl.BlockSpec(memory_space=pl.ANY),
        ],
        out_specs=[
            pl.BlockSpec((ALL, 512), lambda i: (0, i)),
            pl.BlockSpec((ALL, 256), lambda i: (0, i)),
            pl.BlockSpec(memory_space=pl.ANY),
        ],
        out_shape=[
            jax.ShapeDtypeStruct((ALL, 1536), BF),
            jax.ShapeDtypeStruct((ALL, 768), BF),
            jax.ShapeDtypeStruct((16, SHARD, PANEL), BF),
        ],
        scratch_shapes=[
            pltpu.VMEM((4, UNITS, PANEL), BF),
            pltpu.VMEM((16, 128, 2 * LAST), BF),
            pltpu.VMEM((2, 16, 128, PANEL), BF),
            pltpu.VMEM((16, 128, 2 * LAST), BF),
            pltpu.VMEM((4, UNITS, PANEL), BF),
            pltpu.VMEM((ALL // 2, D), BF),
            pltpu.VMEM((ALL // 2, D), BF),
            pltpu.SemaphoreType.DMA((18,)),
            pltpu.SemaphoreType.DMA((6,)),
            pltpu.SemaphoreType.DMA((2,)),
            pltpu.SemaphoreType.DMA((16,)),
        ],
        compiler_params=pltpu.CompilerParams(vmem_limit_bytes=44 * 2**20),
        cost_estimate=pl.CostEstimate(
            flops=18 * 10**9, bytes_accessed=45 * 10**6, transcendentals=10**6
        ),
        name="mlp_grads",
    )(four, core, four_t, core_t, cot_four, cot_core, full, full)


def second_kernel(g_ref, panel_ref, wide_ref, narrow_ref, out_ref, tail):
    for row, rows, column, at, start, width in TAIL:
        piece = wide_ref if row == 256 else narrow_ref
        tail[:, at : at + rows, start : start + width] = piece[:, :, column : column + width]
    total = right_product(g_ref[:, :PANEL], panel_ref[:, :128].reshape(PANEL, PANEL))
    total += right_product(
        g_ref[:, PANEL : 2 * PANEL], panel_ref[:, 128:].reshape(PANEL, PANEL)
    )
    total += right_product(
        g_ref[:, 2 * PANEL : 2 * PANEL + 2 * LAST], tail[...].reshape(PANEL, 2 * LAST)
    )
    out_ref[...] = total.astype(out_ref.dtype)


def second_grad(ggu, full, half, kind):
    return pl.pallas_call(
        second_kernel,
        grid=(4,),
        in_specs=[
            pl.BlockSpec((ALL // 2, 1536), lambda i: (half, 0)),
            pl.BlockSpec((4, 256, PANEL), lambda i: (i, 0, 0)),
            pl.BlockSpec((4, 64, PANEL), lambda i: (i, 4, 0)),
            pl.BlockSpec((4, 32, PANEL), lambda i: (i, 10, 0)),
        ],
        out_specs=pl.BlockSpec((ALL // 2, PANEL), lambda i: (0, i)),
        out_shape=jax.ShapeDtypeStruct((ALL // 2, D), kind),
        scratch_shapes=[pltpu.VMEM((4, 128, 2 * LAST), BF)],
        compiler_params=pltpu.CompilerParams(vmem_limit_bytes=58 * 2**20),
        cost_estimate=pl.CostEstimate(
            flops=3 * 10**9, bytes_accessed=10 * 10**6, transcendentals=0
        ),
        name="second_grad",
    )(ggu, full, full, full)


def down_kernel(act_ref, down_ref, near_ref, core_ref):
    part = dot(act_ref[:, :UNITS], down_ref[...].reshape(UNITS, PANEL))
    near_ref[...] = part[: ALL // 2]
    core_ref[...] = part[ALL // 2 :].astype(BF)


def down_product(active, full):
    half = pl.BlockSpec((ALL // 2, PANEL), lambda c: (0, c))
    return pl.pallas_call(
        down_kernel,
        grid=(4,),
        in_specs=[
            pl.BlockSpec(memory_space=pltpu.VMEM),
            pl.BlockSpec((4, 176, PANEL), lambda c: (c, 2, 0)),
        ],
        out_specs=[half, half],
        out_shape=[
            jax.ShapeDtypeStruct((ALL // 2, D), F32),
            jax.ShapeDtypeStruct((ALL // 2, D), BF),
        ],
        compiler_params=pltpu.CompilerParams(vmem_limit_bytes=58 * 2**20),
        cost_estimate=pl.CostEstimate(
            flops=3 * 10**9, bytes_accessed=12 * 10**6, transcendentals=0
        ),
        name="down_product",
    )(active, full)


LANES = 128


def lanes_of(v):
    return lax.broadcasted_iota(jnp.int32, v.shape, v.ndim - 1)


def quarter_turn(v):
    first = lanes_of(v) % HEAD_DIM < HEAD_DIM // 2
    return jnp.where(first, -pltpu.roll(v, 96, 1), pltpu.roll(v, 32, 1))


def doubled(v):
    left = lanes_of(v) < HEAD_DIM
    other = pltpu.roll(v, HEAD_DIM, 1)
    return jnp.where(left, v, other), jnp.where(left, other, v)


def head_rows(ref):
    blocks = []
    for g in range(GROUPS // 2):
        v = ref[:, g * LANES : (g + 1) * LANES].astype(F32)
        left = lanes_of(v) < HEAD_DIM
        blocks += [jnp.where(left, v, 0.0), jnp.where(left, 0.0, v)]
    return jnp.concatenate(blocks, axis=0).astype(BF)


def pair_columns(v, g):
    even = v[2 * g * ROWS : (2 * g + 1) * ROWS]
    odd = v[(2 * g + 1) * ROWS : (2 * g + 2) * ROWS]
    return jnp.where(lanes_of(even) < HEAD_DIM, even, odd)


def softmax_rows(heads, key2, mask):
    scores = right_product(heads, key2).reshape(GROUPS, ROWS, ROWS) * score_scale
    masked = jnp.where(mask[None] > 0.0, scores, -1e30)
    top = jnp.max(masked, axis=-1, keepdims=True)
    total = top + jnp.log(jnp.sum(jnp.exp(masked - top), axis=-1, keepdims=True))
    return jnp.exp(masked - total).reshape(GROUPS * ROWS, ROWS)


def seq_rows(step):
    return pl.ds(pl.multiple_of(jnp.minimum(step, MEMBERS - 1) * ROWS, ROWS), ROWS)


def attention_kernel(
    first_ref,
    weight_ref,
    cos_ref,
    sin_ref,
    mask_ref,
    query_ref,
    kv_ref,
    att_ref,
    near_ref,
    core_ref,
    qkv,
    att,
):
    step = pl.program_id(0)

    @pl.when(step == 0)
    def _():
        qkv[...] = dot(first_ref[...], weight_ref[:, QW:])

    @pl.when(step < MEMBERS)
    def _():
        rows = seq_rows(step)
        cosine, sine = cos_ref[...], sin_ref[...]
        for g in range(GROUPS // 2):
            v = qkv[rows, g * LANES : (g + 1) * LANES]
            query_ref[:, g * LANES : (g + 1) * LANES] = (
                v * cosine + quarter_turn(v) * sine
            ).astype(BF)
        v = qkv[rows, QW:]
        kv = jnp.where(lanes_of(v) < HEAD_DIM, v * cosine + quarter_turn(v) * sine, v)
        kv_ref[...] = kv.astype(BF)
        key2, value2 = doubled(kv)
        probs = softmax_rows(head_rows(query_ref), key2.astype(BF), mask_ref[0])
        heads = dot(probs.astype(BF), value2.astype(BF))
        for g in range(GROUPS // 2):
            pair = pair_columns(heads, g).astype(BF)
            att_ref[:, g * LANES : (g + 1) * LANES] = pair
            att[rows, g * LANES : (g + 1) * LANES] = pair

    @pl.when(step >= MEMBERS)
    def _():
        block = pl.ds(pl.multiple_of((step - MEMBERS) * QW, QW), QW)
        part = dot(att[...], weight_ref[block, :QW])
        near_ref[...] = part[: SLOTS // 2]
        core_ref[...] = part[SLOTS // 2 :].astype(BF)


def attention_back_kernel(
    middle_ref,
    weight_ref,
    first_ref,
    att_ref,
    query_ref,
    kv_ref,
    cos_ref,
    sin_ref,
    mask_ref,
    grad_ref,
    send_ref,
    upstream,
    grads,
):
    step = pl.program_id(0)

    @pl.when(step == 0)
    def _():
        total = right_product(middle_ref[:, :PANEL], weight_ref[:QW, :QW])
        for c in range(1, 4):
            total += right_product(
                middle_ref[:, c * PANEL : (c + 1) * PANEL],
                weight_ref[c * QW : (c + 1) * QW, :QW],
            )
        upstream[...] = total.astype(BF)

    @pl.when(step < MEMBERS)
    def _():
        rows = seq_rows(step)
        cosine, sine = cos_ref[...], sin_ref[...]
        key2, value2 = doubled(kv_ref[...].astype(F32))
        key2, value2 = key2.astype(BF), value2.astype(BF)
        heads, lifted = head_rows(query_ref), head_rows(upstream.at[rows])
        probs = softmax_rows(heads, key2, mask_ref[0])
        grad_value = left_product(probs.astype(BF), lifted)
        grad_value = grad_value + pltpu.roll(grad_value, HEAD_DIM, 1)
        grad_probs = right_product(lifted, value2)
        inner = jnp.sum(grad_probs * probs, axis=-1, keepdims=True)
        grad_scores = (probs * (grad_probs - inner)).astype(BF)
        grad_query = dot(grad_scores, key2)
        for g in range(GROUPS // 2):
            v = pair_columns(grad_query, g) * score_scale
            v = (v * cosine - quarter_turn(v) * sine).astype(BF)
            grad_ref[:, g * LANES : (g + 1) * LANES] = v
            grads[rows, g * LANES : (g + 1) * LANES] = v
        grad_key = left_product(grad_scores, heads)
        v = (grad_key + pltpu.roll(grad_key, HEAD_DIM, 1)) * score_scale
        grad_key = v * cosine - quarter_turn(v) * sine
        v = jnp.where(lanes_of(v) < HEAD_DIM, grad_key, grad_value).astype(BF)
        grad_ref[:, QW:] = v
        grads[rows, QW:] = v

    @pl.when(step >= MEMBERS)
    def _():
        block = pl.ds(pl.multiple_of((step - MEMBERS) * PANEL, PANEL), PANEL)
        send_ref[:, :QW] = left_product(att_ref[...], middle_ref[:, block]).astype(BF)
        send_ref[:, QW:] = left_product(first_ref[:, block], grads[...]).astype(BF)


def all_of(shape):
    return pl.BlockSpec(shape, lambda s: (0,) * len(shape), pipeline_mode=pl.Buffered(1))


def by_seq(width):
    return pl.BlockSpec((ROWS, width), lambda s: (jnp.minimum(s, MEMBERS - 1), 0))


MASK_BLOCK = pl.BlockSpec((1, ROWS, ROWS), lambda s: (jnp.minimum(s, MEMBERS - 1), 0, 0))


def attention(first_low, weights, cosine, sine, mask):
    half = pl.BlockSpec((SLOTS // 2, PANEL), lambda s: (0, jnp.maximum(s - MEMBERS, 0)))
    return pl.pallas_call(
        attention_kernel,
        grid=(2 * MEMBERS,),
        in_specs=[
            all_of((SLOTS, D)),
            all_of((D, QW + QKVW)),
            by_seq(LANES),
            by_seq(LANES),
            MASK_BLOCK,
        ],
        out_specs=[by_seq(QW), by_seq(LANES), by_seq(QW), half, half],
        out_shape=[
            jax.ShapeDtypeStruct((SLOTS, QW), BF),
            jax.ShapeDtypeStruct((SLOTS, LANES), BF),
            jax.ShapeDtypeStruct((SLOTS, QW), BF),
            jax.ShapeDtypeStruct((SLOTS // 2, D), F32),
            jax.ShapeDtypeStruct((SLOTS // 2, D), BF),
        ],
        scratch_shapes=[pltpu.VMEM((SLOTS, QKVW), F32), pltpu.VMEM((SLOTS, QW), BF)],
        compiler_params=pltpu.CompilerParams(vmem_limit_bytes=40 * 2**20),
        cost_estimate=pl.CostEstimate(
            flops=3 * 10**9, bytes_accessed=12 * 10**6, transcendentals=10**6
        ),
        name="attention",
    )(first_low, weights, cosine, sine, mask)


def attention_back(middle_all, weights, first_low, attended, query, kv, cosine, sine, mask):
    return pl.pallas_call(
        attention_back_kernel,
        grid=(2 * MEMBERS,),
        in_specs=[
            all_of((SLOTS, D)),
            all_of((D, QW + QKVW)),
            all_of((SLOTS, D)),
            all_of((SLOTS, QW)),
            by_seq(QW),
            by_seq(LANES),
            by_seq(LANES),
            by_seq(LANES),
            MASK_BLOCK,
        ],
        out_specs=[
            by_seq(QKVW),
            pl.BlockSpec((PANEL, QW + QKVW), lambda s: (jnp.maximum(s - MEMBERS, 0), 0)),
        ],
        out_shape=[
            jax.ShapeDtypeStruct((SLOTS, QKVW), BF),
            jax.ShapeDtypeStruct((D, QW + QKVW), BF),
        ],
        scratch_shapes=[pltpu.VMEM((SLOTS, QW), BF), pltpu.VMEM((SLOTS, QKVW), BF)],
        compiler_params=pltpu.CompilerParams(vmem_limit_bytes=40 * 2**20),
        cost_estimate=pl.CostEstimate(
            flops=5 * 10**9, bytes_accessed=16 * 10**6, transcendentals=10**6
        ),
        name="attention_back",
    )(middle_all, weights, first_low, attended, query, kv, cosine, sine, mask)


def rounded_gain(gain):
    return lax.optimization_barrier(gain.astype(BF)).astype(F32)


def inverse_rms(v):
    return lax.rsqrt(jnp.mean(v * v, axis=-1, keepdims=True) + epsilon)


def norm_back(v, gain, grad):
    r = inverse_rms(v)
    n = v * r
    scaled = grad * gain
    return r * (scaled - n * jnp.mean(scaled * n, axis=-1, keepdims=True)), n


def panels(gate, up):
    blocks = []
    for at in range(0, UNITS, 256):
        blocks += [gate[:, at : at + 256], up[:, at : at + 256]]
    return jnp.concatenate(blocks, axis=1)


def unpanels(v):
    gate = [v[:, :256], v[:, 512:768], v[:, 1024 : 1024 + LAST]]
    up = [v[:, 256:512], v[:, 768:1024], v[:, 1024 + LAST :]]
    return jnp.concatenate(gate, axis=1), jnp.concatenate(up, axis=1)


def on_device(
    tokens,
    cotangent,
    segment_ids,
    positions,
    padding,
    attn_gain,
    query_weight,
    key_weight,
    value_weight,
    output_weight,
    mlp_gain,
    gate_weight,
    up_weight,
    down_weight,
    attn_moment,
    query_moment,
    key_moment,
    value_moment,
    output_moment,
    mlp_moment,
    gate_moment,
    up_moment,
    down_moment,
):
    member = lax.axis_index("grp")
    place = lax.axis_index("dp")
    z, y, low = place // 8, (place // 2) % 4, (place % 2) == 0

    def mine(weight, width):
        return lax.dynamic_slice_in_dim(weight, member * width, width, 1).astype(BF)

    attn_shard = jnp.concatenate(
        [mine(query_weight, QW), mine(key_weight, KW), mine(value_weight, KW)], axis=1
    )
    attn_shard = jnp.concatenate(
        [turn_pair(mine(output_weight, QW), low), pair_x(attn_shard, low)], axis=1
    )
    attn_full = plane_gather(attn_shard)

    gate_mine, up_mine = mine(gate_weight, FW), mine(up_weight, FW)
    first = panels(gate_mine[:, :UNITS], up_mine[:, :UNITS])
    second = panels(gate_mine[:, UNITS:], up_mine[:, UNITS:])
    kept, given = jnp.where(low, first, second), jnp.where(low, second, first)
    gu_shard = in_order(kept, swap_x(given), low)
    tail = gu_shard[:, 2 * PANEL :]
    pieces = [
        gu_shard[:, :PANEL],
        gu_shard[:, PANEL : 2 * PANEL],
        jnp.concatenate([tail[:W_ROWS, :256], tail[W_ROWS:, :256]], axis=1),
        jnp.concatenate([tail[32 * h : 32 * h + 32, 256:] for h in range(4)], axis=1),
        everywhere(mine(down_weight, PANEL), OWNED),
    ]
    mlp_full = plane_gather(jnp.concatenate(pieces, axis=0)).reshape(16, SHARD, PANEL)

    places = jnp.stack([segment_ids, positions, padding])[None]
    rows_in = group_gather(tokens)
    places, upstream = lax.optimization_barrier(
        (jnp.concatenate([places, swap_far(places)], axis=0), cotangent)
    )
    cot_four, cot_core = row_gather(upstream)
    places = jnp.concatenate([places, swap_core(places)], axis=0)
    segments, spots, pads = places[:, 0], places[:, 1], places[:, 2]
    own_moment = jnp.concatenate(
        [query_moment, key_moment, value_moment, output_moment], axis=1
    )
    moments = group_gather(own_moment.astype(BF))

    first_gain = rounded_gain(attn_gain)
    second_gain = rounded_gain(mlp_gain)
    inputs = rows_in.astype(F32)
    n_first = inputs * inverse_rms(inputs)
    first_low = (n_first * first_gain).astype(BF)

    half = HEAD_DIM // 2
    freq = 10000.0 ** (-(jnp.arange(half, dtype=F32) * 2.0 / HEAD_DIM))
    angles = spots.reshape(SLOTS, 1).astype(F32) * jnp.tile(freq, LANES // half)[None]
    cosine, sine = jnp.cos(angles), jnp.sin(angles)
    column = jnp.arange(ROWS, dtype=jnp.int32)
    allowed = jnp.logical_and(
        jnp.logical_and(
            segments[:, :, None] == segments[:, None, :],
            (column[None, :] <= column[:, None])[None],
        ),
        jnp.logical_or(pads[:, None, :] == 1, (column[None, :] == column[:, None])[None]),
    ).astype(F32)

    attn_full, first_low, cosine, sine, allowed, cot_four = lax.optimization_barrier(
        (attn_full, first_low, cosine, sine, allowed, cot_four)
    )
    query_rot, kv, attended, near, core = attention(first_low, attn_full, cosine, sine, allowed)
    near, moments = lax.optimization_barrier((near + swap_core(core).astype(F32), moments))
    moments = moments.astype(F32)
    middle = tokens.astype(F32) + group_scatter_far(near)
    second_low = (middle * inverse_rms(middle) * second_gain).astype(BF)
    four, core_four = row_gather(second_low)
    four_t = four.T
    core_four, four_t, cot_core = lax.optimization_barrier((core_four, four_t, cot_core))
    grad_gu, active, send = mlp_grads(
        four, core_four, four_t, core_four.T, cot_four, cot_core, mlp_full
    )
    mlp_sum = plane_scatter(send.reshape(16 * SHARD, PANEL))

    second_core = swap_core(second_grad(grad_gu, mlp_full, 1, BF))
    grad_second = row_scatter(
        second_grad(grad_gu, mlp_full, 0, F32) + second_core.astype(F32)
    )
    back, n_second = norm_back(middle, second_gain, grad_second)
    mlp_gain_part = jnp.sum(grad_second * n_second, axis=0)
    grad_middle = cotangent.astype(F32) + back
    middle_all = group_gather(grad_middle.astype(BF))
    down_near, down_core = down_product(active, mlp_full)
    middle_all, down_near = lax.optimization_barrier(
        (middle_all, down_near + swap_core(down_core).astype(F32))
    )
    block_output = (middle + row_scatter(down_near)).astype(BF)
    grad_qkv, attn_send = attention_back(
        middle_all, attn_full, first_low, attended, query_rot, kv, cosine, sine, allowed
    )
    attn_send, grad_qkv, block_output = lax.optimization_barrier(
        (attn_send, grad_qkv, block_output)
    )
    attn_sum = plane_scatter(attn_send)

    grad_qkv, mlp_sum = lax.optimization_barrier((grad_qkv, mlp_sum))
    grad_first = right_product(grad_qkv, attn_full[:, QW:])
    attn_gain_part = jnp.sum(grad_first * n_first, axis=0)
    gains = jnp.stack([attn_gain_part, mlp_gain_part]).reshape(32, LANES)
    for pairs in (RING_Z, RING_Y):
        gains = gains + sum(lax.ppermute(gains, "dp", p) for p in pairs)
    back, _ = norm_back(tokens.astype(F32), first_gain, group_scatter(grad_first))
    input_grad = grad_middle + back

    mine_at = (member // 2) + 2 * (member % 2)

    def by_member(slots):
        return [
            lax.dynamic_index_in_dim(slots, mine_at ^ at, 0, keepdims=False) for at in (0, 2, 1, 3)
        ]

    def updated(weight, columns, start, size):
        moved = jnp.concatenate([block[:, start : start + size] for block in columns], axis=1)
        return weight - learn_rate * moved.astype(F32)

    wide, narrow = mlp_sum[256:320], mlp_sum[320:352]
    gu_part = jnp.concatenate(
        [
            mlp_sum[:128],
            mlp_sum[128:256],
            jnp.concatenate([wide[:, :256], wide[:, 256:]], axis=0),
            jnp.concatenate([narrow[:, h * LANES : (h + 1) * LANES] for h in range(4)], axis=0),
        ],
        axis=1,
    )
    kept, given = halves(gu_part, low)
    other = swap_x(given)
    first = unpanels(jnp.where(low, kept, other))
    second = unpanels(jnp.where(low, other, kept))
    gate_rows = jnp.concatenate([first[0], second[0]], axis=1).astype(F32)
    up_rows = jnp.concatenate([first[1], second[1]], axis=1).astype(F32)
    down_rows = everywhere(mlp_sum[352:], RETURN).astype(F32)
    gate_momentum = 0.5 * gate_moment + 0.5 * gate_rows
    up_momentum = 0.5 * up_moment + 0.5 * up_rows
    down_momentum = 0.5 * down_moment + 0.5 * down_rows
    gu_moved = by_member(
        group_gather(jnp.concatenate([gate_momentum, up_momentum], axis=1).astype(BF)).reshape(
            MEMBERS, W_ROWS, GUW
        )
    )
    down_moved = by_member(
        group_gather(down_momentum.astype(BF)).reshape(MEMBERS, DOWN_ROWS, PANEL)
    )

    mlp_done = (
        gate_momentum,
        up_momentum,
        down_momentum,
        updated(gate_weight, gu_moved, 0, FW),
        updated(up_weight, gu_moved, FW, FW),
        updated(down_weight, down_moved, 0, PANEL),
    )
    attn_sum, gains, input_grad, block_output, mlp_done = lax.optimization_barrier(
        (attn_sum, gains, input_grad, block_output, mlp_done)
    )
    gate_momentum, up_momentum, down_momentum, gate_updated, up_updated, down_updated = mlp_done

    turned = everywhere(attn_sum[:, :QW], TURN)
    both = jnp.concatenate([attn_sum[:, QW:], turned], axis=1)
    gains = two_parts(gains)
    kept, given = halves(both, low)
    width = QKVW + PANEL
    near = swap_x(jnp.concatenate([given, gains], axis=1))
    far = swap_far(jnp.concatenate([kept, gains], axis=1))
    both_far = far_x(jnp.concatenate([given, gains], axis=1))
    own_total = kept.astype(F32) + near[:, :width].astype(F32)
    far_total = far[:, :width].astype(F32) + both_far[:, :width].astype(F32)
    gains = sum(one_part(part) for part in (gains, near[:, width:], far[:, width:], both_far[:, width:]))
    totals = jnp.concatenate([own_total, far_total], axis=0).astype(BF)
    rider = jnp.concatenate([two_parts(gains), jnp.zeros((W_ROWS, LANES), BF)], axis=0)
    other = swap_core(jnp.concatenate([totals, rider], axis=1))
    gains = gains + one_part(other[:W_ROWS, width:])
    totals = jnp.concatenate([totals, other[:, :width]], axis=0).astype(F32)

    own_moved = 0.5 * own_moment + 0.5 * own_total
    query_momentum = own_moved[:, :QW]
    key_momentum = own_moved[:, QW : QW + KW]
    value_momentum = own_moved[:, QW + KW : QKVW]
    output_momentum = own_moved[:, QKVW:]

    attn_moved = by_member((0.5 * moments + 0.5 * totals).reshape(MEMBERS, W_ROWS, width))

    gains = 0.5 * jnp.stack([attn_moment, mlp_moment]) + 0.5 * gains.reshape(2, D)
    return (
        block_output,
        input_grad,
        gains[0],
        query_momentum,
        key_momentum,
        value_momentum,
        output_momentum,
        gains[1],
        gate_momentum,
        up_momentum,
        down_momentum,
        attn_gain - learn_rate * gains[0],
        updated(query_weight, attn_moved, 0, QW),
        updated(key_weight, attn_moved, QW, KW),
        updated(value_weight, attn_moved, QW + KW, KW),
        updated(output_weight, attn_moved, QKVW, PANEL),
        mlp_gain - learn_rate * gains[1],
        gate_updated,
        up_updated,
        down_updated,
    )


def solution(mesh):
    rows = P(("grp", "dp"), None)
    flat = P(("grp", "dp"))
    weight = P("dp", None)
    moment = P("dp", "grp")
    everyone = P()
    weights = (everyone,) + (weight,) * 4 + (everyone,) + (weight,) * 3
    moments = (everyone,) + (moment,) * 4 + (everyone,) + (moment,) * 3
    return jax.shard_map(
        on_device,
        mesh=mesh,
        in_specs=(rows, rows, flat, flat, flat) + weights + moments,
        out_specs=(rows, rows) + moments + weights,
        check_vma=False,
    )
```

```python
import jax
import jax.numpy as jnp
from jax import lax
from jax.experimental import pallas as pl
from jax.experimental.pallas import tpu as pltpu
from jax.sharding import PartitionSpec as P

D = 2048
HEAD_DIM = 64
GROUPS = 8
ROWS = 128
MEMBERS = 4
SLOTS = ROWS * MEMBERS
QW = 512
KW = 64
QKVW = QW + 2 * KW
FW = 1408
GUW = 2 * FW
PANEL = 512
DOWN_ROWS = 176
W_ROWS = 64

epsilon = 1e-05
learn_rate = 0.005
score_scale = 0.125

BF = jnp.bfloat16
F32 = jnp.float32

PLANES = [[z * 8 + y * 2 + x for z in range(4) for y in range(4)] for x in range(2)]
SWAP_X = [(i, i ^ 1) for i in range(32)]
SWAP_CORE = [(m, m ^ 1) for m in range(4)]
SWAP_FAR = [(m, m ^ 2) for m in range(4)]
SWAP_FAR_X = [(m * 32 + i, (m ^ 2) * 32 + (i ^ 1)) for m in range(4) for i in range(32)]
MZQ = [(m, z, q) for m in range(4) for z in range(4) for q in range(8)]


def spot(m, z, q):
    return m * 32 + z * 8 + q


TURN = [(spot(m, z, q), spot(z, m, q)) for m, z, q in MZQ]
TURN_X = [(spot(m, z, q), spot(z, m, q ^ 1)) for m, z, q in MZQ]
TURN_IN = [[(spot(m, z, q), spot((z + k) % 4, m, q)) for m, z, q in MZQ] for k in range(4)]
OWNED = [(spot(m, z, q), spot(z, m, (q & 3) * 2 + (q >> 2))) for m, z, q in MZQ]
RETURN = [(b, a) for a, b in OWNED]


def ring(place, k):
    return [(i, i + ((i // place + k) % 4 - i // place % 4) * place) for i in range(32)]


RING_Z = [ring(8, k) for k in (1, 2, 3)]
RING_Y = [ring(2, k) for k in (1, 2, 3)]


def swap_x(v):
    return lax.ppermute(v, "dp", SWAP_X)


def swap_core(v):
    return lax.ppermute(v, "grp", SWAP_CORE)


def swap_far(v):
    return lax.ppermute(v, "grp", SWAP_FAR)


def everywhere(v, pairs):
    return lax.ppermute(v, ("grp", "dp"), pairs)


def plane_gather(v):
    return lax.all_gather(v, "dp", axis=0, tiled=True, axis_index_groups=PLANES)


def plane_scatter(v):
    return lax.psum_scatter(
        v, "dp", scatter_dimension=0, tiled=True, axis_index_groups=PLANES
    )


def ring_scatter(v, pairs, at, extra=None):
    rows = v.shape[0] // 4

    def chunk(k):
        part = lax.dynamic_slice_in_dim(v, lax.rem(at + k, 4) * rows, rows, 0)
        return part if extra is None else jnp.concatenate([part, extra], axis=1)

    total = chunk(0).astype(F32)
    for k, p in enumerate(pairs):
        total = total + lax.ppermute(chunk(k + 1), "dp", p).astype(F32)
    return total


def group_gather(v):
    pair = jnp.concatenate([v, swap_far(v)], axis=0)
    return jnp.concatenate([pair, swap_core(pair)], axis=0)


def group_scatter_near(partial):
    half = 2 * ROWS
    return partial[:half] + swap_core(partial[half:].astype(BF)).astype(F32)


def group_scatter_far(near):
    return near[:ROWS] + swap_far(near[ROWS:].astype(BF)).astype(F32)


def group_scatter(partial):
    return group_scatter_far(group_scatter_near(partial))


def far_x(v):
    return everywhere(v, SWAP_FAR_X)


def row_gather(v):
    four = jnp.concatenate([v, swap_x(v), swap_far(v), far_x(v)], axis=0)
    return four, swap_core(four)


def row_scatter(own, rest, core):
    own = own + core[:ROWS].astype(F32)
    rest = (rest.astype(F32) + core[ROWS:].astype(F32)).astype(BF)
    low_part, far_part, far_x_part = (rest[k * ROWS : (k + 1) * ROWS] for k in range(3))
    return (
        own
        + swap_x(low_part).astype(F32)
        + swap_far(far_part).astype(F32)
        + far_x(far_x_part).astype(F32)
    )


def in_order(own, other, low):
    return jnp.concatenate([jnp.where(low, own, other), jnp.where(low, other, own)], axis=0)


def pair_x(v, low):
    return in_order(v, swap_x(v), low)


def turn_pair(v, low):
    return in_order(everywhere(v, TURN), everywhere(v, TURN_X), low)


def halves(v, low):
    rows = v.shape[0] // 2
    return jnp.where(low, v[:rows], v[rows:]), jnp.where(low, v[rows:], v[:rows])


def two_parts(v):
    high = lax.reduce_precision(v, 8, 7)
    return jnp.concatenate([high.astype(BF), (v - high).astype(BF)], axis=0)


def one_part(v):
    rows = v.shape[0] // 2
    return v[:rows].astype(F32) + v[rows:].astype(F32)


def dot(left, right):
    return jnp.dot(left, right, preferred_element_type=F32)


def left_product(left, right):
    return lax.dot_general(left, right, (((0,), (0,)), ((), ())), preferred_element_type=F32)


def right_product(left, right):
    return lax.dot_general(left, right, (((1,), (1,)), ((), ())), preferred_element_type=F32)


ALL = 1024
UNITS = 704
LAST = 192
SHARD = 528


TAIL = [(256, 64, 256 * h, 64 * h, 0, 256) for h in range(2)]
TAIL += [(320, 32, 128 * h, 32 * h, 256, 128) for h in range(4)]


def tail_pieces(shard):
    for row, rows, column, at, start, width in TAIL:
        yield (
            shard.at[:, pl.ds(row, rows), pl.ds(column, width)],
            (slice(None), pl.ds(at, rows), pl.ds(start, width)),
        )


def tail_loads(full, tail, sems):
    return [
        pltpu.make_async_copy(src, tail.at[at], sems.at[i])
        for i, (src, at) in enumerate(tail_pieces(full))
    ]


def down_blocks(shard, down):
    return [
        (shard.at[4 * c + j, pl.ds(352, 176), :], down.at[c, pl.ds(176 * j, 176), :])
        for c in range(4)
        for j in range(4)
    ]


def mlp_kernel(
    four,
    core,
    cot_four,
    cot_core,
    panel_ref,
    full,
    ggu_ref,
    act_ref,
    send,
    down,
    tail,
    gpan,
    gtail,
    gdown,
    four_ref,
    core_ref,
    cot_four_ref,
    cot_core_ref,
    in_sem,
    row_sem,
    tail_sem,
    pan_sem,
    out_sem,
):
    step = pl.program_id(0)
    loads = [
        pltpu.make_async_copy(src, dst, in_sem.at[i])
        for i, (src, dst) in enumerate(
            [(cot_four, cot_four_ref), (cot_core, cot_core_ref)] + down_blocks(full, down)
        )
    ]
    rows_in = [
        pltpu.make_async_copy(src, dst, row_sem.at[i])
        for i, (src, dst) in enumerate([(four, four_ref), (core, core_ref)])
    ]
    tails = tail_loads(full, tail, tail_sem)

    @pl.when(step == 0)
    def _():
        for copy in rows_in + loads + tails:
            copy.start()

    def panel_out(at):
        return pltpu.make_async_copy(
            gpan.at[at], send.at[:, pl.ds(128 * at, 128), :], pan_sem.at[at]
        )

    def block(weights, start, width, store):
        halves_of = []
        for copy, ref in zip(rows_in, (four_ref, core_ref)):
            pl.when(step == 0)(copy.wait)
            halves_of.append(dot(ref[...], weights))

        @pl.when(step == 0)
        def _():
            for copy in loads:
                copy.wait()

        for half, (h, c_ref) in enumerate(zip(halves_of, (cot_four_ref, cot_core_ref))):
            rows = pl.ds(half * (ALL // 2), ALL // 2)
            gate, up = h[:, :width], h[:, width:]
            prod = right_product(c_ref[:, :PANEL], down[0, pl.ds(start, width), :])
            for c in range(1, 4):
                prod += right_product(
                    c_ref[:, c * PANEL : (c + 1) * PANEL], down[c, pl.ds(start, width), :]
                )
            sig = 1.0 / (1.0 + jnp.exp(-gate))
            silu = gate * sig
            act_ref[rows, :width] = (silu * up).astype(BF)
            ggu_ref[rows, :width] = (prod * up * sig * (1.0 + gate * (1.0 - sig))).astype(BF)
            ggu_ref[rows, width : 2 * width] = (prod * silu).astype(BF)
        for c in range(4):
            columns = slice(c * PANEL, (c + 1) * PANEL)
            grads = left_product(act_ref[: ALL // 2, :width], cot_four_ref[:, columns])
            grads += left_product(act_ref[ALL // 2 :, :width], cot_core_ref[:, columns])
            gdown[c, pl.ds(start, width), :] = grads.astype(BF)
        grads = left_product(four_ref[...], ggu_ref[: ALL // 2, : 2 * width])
        grads += left_product(core_ref[...], ggu_ref[ALL // 2 :, : 2 * width])
        store(grads.astype(BF))

    @pl.when(step < 2)
    def _():
        def store(grads):
            gpan[step] = grads.reshape(16, 128, PANEL)

        block(panel_ref[...].reshape(D, PANEL), pl.multiple_of(256 * step, 256), 256, store)
        panel_out(step).start()

    @pl.when(step == 2)
    def _():
        def store(grads):
            gtail[...] = grads.reshape(16, 128, 2 * LAST)

        for copy in tails:
            copy.wait()
        block(tail[...].reshape(D, 2 * LAST), 512, LAST, store)
        outs = [
            pltpu.make_async_copy(gtail.at[at], dst, tail_sem.at[i])
            for i, (dst, at) in enumerate(tail_pieces(send))
        ]
        outs += [
            pltpu.make_async_copy(src, dst, out_sem.at[i])
            for i, (dst, src) in enumerate(down_blocks(send, gdown))
        ]
        for copy in outs:
            copy.start()
        for copy in outs + [panel_out(0), panel_out(1)]:
            copy.wait()


def mlp_grads(four, core, cot_four, cot_core, full):
    return pl.pallas_call(
        mlp_kernel,
        grid=(3,),
        in_specs=[pl.BlockSpec(memory_space=pl.ANY)] * 4
        + [
            pl.BlockSpec((16, 128, PANEL), lambda i: (0, jnp.minimum(i, 1), 0)),
            pl.BlockSpec(memory_space=pl.ANY),
        ],
        out_specs=[
            pl.BlockSpec((ALL, 512), lambda i: (0, i)),
            pl.BlockSpec((ALL, 256), lambda i: (0, i)),
            pl.BlockSpec(memory_space=pl.ANY),
        ],
        out_shape=[
            jax.ShapeDtypeStruct((ALL, 1536), BF),
            jax.ShapeDtypeStruct((ALL, 768), BF),
            jax.ShapeDtypeStruct((16, SHARD, PANEL), BF),
        ],
        scratch_shapes=[
            pltpu.VMEM((4, UNITS, PANEL), BF),
            pltpu.VMEM((16, 128, 2 * LAST), BF),
            pltpu.VMEM((2, 16, 128, PANEL), BF),
            pltpu.VMEM((16, 128, 2 * LAST), BF),
            pltpu.VMEM((4, UNITS, PANEL), BF),
            pltpu.VMEM((ALL // 2, D), BF),
            pltpu.VMEM((ALL // 2, D), BF),
            pltpu.VMEM((ALL // 2, D), BF),
            pltpu.VMEM((ALL // 2, D), BF),
            pltpu.SemaphoreType.DMA((18,)),
            pltpu.SemaphoreType.DMA((2,)),
            pltpu.SemaphoreType.DMA((6,)),
            pltpu.SemaphoreType.DMA((2,)),
            pltpu.SemaphoreType.DMA((16,)),
        ],
        compiler_params=pltpu.CompilerParams(vmem_limit_bytes=56 * 2**20),
        cost_estimate=pl.CostEstimate(
            flops=18 * 10**9, bytes_accessed=45 * 10**6, transcendentals=10**6
        ),
        name="mlp_grads",
    )(four, core, cot_four, cot_core, full, full)


def split_rows(total, rest_ref, own_ref=None):
    if own_ref is None:
        rest_ref[...] = total.astype(BF)
    else:
        own_ref[...] = total[:ROWS]
        rest_ref[...] = total[ROWS : ALL // 2].astype(BF)


def second_kernel(g_ref, panel_ref, wide_ref, narrow_ref, *outs):
    *outs, tail = outs
    for row, rows, column, at, start, width in TAIL:
        piece = wide_ref if row == 256 else narrow_ref
        tail[:, at : at + rows, start : start + width] = piece[:, :, column : column + width]
    total = right_product(g_ref[:, :PANEL], panel_ref[:, :128].reshape(PANEL, PANEL))
    total += right_product(
        g_ref[:, PANEL : 2 * PANEL], panel_ref[:, 128:].reshape(PANEL, PANEL)
    )
    total += right_product(
        g_ref[:, 2 * PANEL : 2 * PANEL + 2 * LAST], tail[...].reshape(PANEL, 2 * LAST)
    )
    split_rows(total, *outs)


def second_grad(ggu, full, half):
    rows = [ALL // 2] if half else [ALL // 2 - ROWS, ROWS]
    return pl.pallas_call(
        second_kernel,
        grid=(4,),
        in_specs=[
            pl.BlockSpec((ALL // 2, 1536), lambda i: (half, 0)),
            pl.BlockSpec((4, 256, PANEL), lambda i: (i, 0, 0)),
            pl.BlockSpec((4, 64, PANEL), lambda i: (i, 4, 0)),
            pl.BlockSpec((4, 32, PANEL), lambda i: (i, 10, 0)),
        ],
        out_specs=[pl.BlockSpec((r, PANEL), lambda i: (0, i)) for r in rows],
        out_shape=[jax.ShapeDtypeStruct((r, D), kind) for r, kind in zip(rows, (BF, F32))],
        scratch_shapes=[pltpu.VMEM((4, 128, 2 * LAST), BF)],
        compiler_params=pltpu.CompilerParams(vmem_limit_bytes=58 * 2**20),
        cost_estimate=pl.CostEstimate(
            flops=3 * 10**9, bytes_accessed=10 * 10**6, transcendentals=0
        ),
        name="second_grad",
    )(ggu, full, full, full)


def down_kernel(act_ref, down_ref, core_ref, rest_ref, own_ref):
    part = dot(act_ref[:, :UNITS], down_ref[...].reshape(UNITS, PANEL))
    split_rows(part, rest_ref, own_ref)
    core_ref[...] = part[ALL // 2 :].astype(BF)


def down_product(active, full):
    rows = [ALL // 2, ALL // 2 - ROWS, ROWS]
    return pl.pallas_call(
        down_kernel,
        grid=(4,),
        in_specs=[
            pl.BlockSpec((ALL, 768), lambda c: (0, 0)),
            pl.BlockSpec((4, 176, PANEL), lambda c: (c, 2, 0)),
        ],
        out_specs=[pl.BlockSpec((r, PANEL), lambda c: (0, c)) for r in rows],
        out_shape=[jax.ShapeDtypeStruct((r, D), kind) for r, kind in zip(rows, (BF, BF, F32))],
        compiler_params=pltpu.CompilerParams(vmem_limit_bytes=58 * 2**20),
        cost_estimate=pl.CostEstimate(
            flops=3 * 10**9, bytes_accessed=12 * 10**6, transcendentals=0
        ),
        name="down_product",
    )(active, full)


LANES = 128


def lanes_of(v):
    return lax.broadcasted_iota(jnp.int32, v.shape, v.ndim - 1)


def quarter_turn(v):
    first = lanes_of(v) % HEAD_DIM < HEAD_DIM // 2
    return jnp.where(first, -pltpu.roll(v, 96, 1), pltpu.roll(v, 32, 1))


def doubled(v):
    left = lanes_of(v) < HEAD_DIM
    other = pltpu.roll(v, HEAD_DIM, 1)
    return jnp.where(left, v, other), jnp.where(left, other, v)


def head_rows(ref):
    blocks = []
    for g in range(GROUPS // 2):
        v = ref[:, g * LANES : (g + 1) * LANES].astype(F32)
        left = lanes_of(v) < HEAD_DIM
        blocks += [jnp.where(left, v, 0.0), jnp.where(left, 0.0, v)]
    return jnp.concatenate(blocks, axis=0).astype(BF)


def pair_columns(v, g):
    even = v[2 * g * ROWS : (2 * g + 1) * ROWS]
    odd = v[(2 * g + 1) * ROWS : (2 * g + 2) * ROWS]
    return jnp.where(lanes_of(even) < HEAD_DIM, even, odd)


def softmax_rows(heads, key2, mask):
    scores = right_product(heads, key2).reshape(GROUPS, ROWS, ROWS) * score_scale
    masked = jnp.where(mask[None] > 0.0, scores, -1e30)
    top = jnp.max(masked, axis=-1, keepdims=True)
    total = top + jnp.log(jnp.sum(jnp.exp(masked - top), axis=-1, keepdims=True))
    return jnp.exp(masked - total).reshape(GROUPS * ROWS, ROWS)


def seq_rows(step):
    return pl.ds(pl.multiple_of(jnp.minimum(step, MEMBERS - 1) * ROWS, ROWS), ROWS)


def attention_kernel(
    first_ref,
    weight_ref,
    cos_ref,
    sin_ref,
    mask_ref,
    query_ref,
    kv_ref,
    att_ref,
    near_ref,
    core_ref,
    qkv,
    att,
):
    step = pl.program_id(0)

    @pl.when(step == 0)
    def _():
        qkv[...] = dot(first_ref[...], weight_ref[:, QW:])

    @pl.when(step < MEMBERS)
    def _():
        rows = seq_rows(step)
        cosine, sine = cos_ref[...], sin_ref[...]
        for g in range(GROUPS // 2):
            v = qkv[rows, g * LANES : (g + 1) * LANES]
            query_ref[:, g * LANES : (g + 1) * LANES] = (
                v * cosine + quarter_turn(v) * sine
            ).astype(BF)
        v = qkv[rows, QW:]
        kv = jnp.where(lanes_of(v) < HEAD_DIM, v * cosine + quarter_turn(v) * sine, v)
        kv_ref[...] = kv.astype(BF)
        key2, value2 = doubled(kv)
        probs = softmax_rows(head_rows(query_ref), key2.astype(BF), mask_ref[0])
        heads = dot(probs.astype(BF), value2.astype(BF))
        for g in range(GROUPS // 2):
            pair = pair_columns(heads, g).astype(BF)
            att_ref[:, g * LANES : (g + 1) * LANES] = pair
            att[rows, g * LANES : (g + 1) * LANES] = pair

    @pl.when(step >= MEMBERS)
    def _():
        block = pl.ds(pl.multiple_of((step - MEMBERS) * QW, QW), QW)
        part = dot(att[...], weight_ref[block, :QW])
        near_ref[...] = part[: SLOTS // 2]
        core_ref[...] = part[SLOTS // 2 :].astype(BF)


def attention_back_kernel(
    middle_ref,
    weight_ref,
    first_ref,
    att_ref,
    query_ref,
    kv_ref,
    cos_ref,
    sin_ref,
    mask_ref,
    grad_ref,
    send_ref,
    upstream,
    grads,
):
    step = pl.program_id(0)

    @pl.when(step == 0)
    def _():
        total = right_product(middle_ref[:, :PANEL], weight_ref[:QW, :QW])
        for c in range(1, 4):
            total += right_product(
                middle_ref[:, c * PANEL : (c + 1) * PANEL],
                weight_ref[c * QW : (c + 1) * QW, :QW],
            )
        upstream[...] = total.astype(BF)

    @pl.when(step < MEMBERS)
    def _():
        rows = seq_rows(step)
        cosine, sine = cos_ref[...], sin_ref[...]
        key2, value2 = doubled(kv_ref[...].astype(F32))
        key2, value2 = key2.astype(BF), value2.astype(BF)
        heads, lifted = head_rows(query_ref), head_rows(upstream.at[rows])
        probs = softmax_rows(heads, key2, mask_ref[0])
        grad_value = left_product(probs.astype(BF), lifted)
        grad_value = grad_value + pltpu.roll(grad_value, HEAD_DIM, 1)
        grad_probs = right_product(lifted, value2)
        inner = jnp.sum(grad_probs * probs, axis=-1, keepdims=True)
        grad_scores = (probs * (grad_probs - inner)).astype(BF)
        grad_query = dot(grad_scores, key2)
        for g in range(GROUPS // 2):
            v = pair_columns(grad_query, g) * score_scale
            v = (v * cosine - quarter_turn(v) * sine).astype(BF)
            grad_ref[:, g * LANES : (g + 1) * LANES] = v
            grads[rows, g * LANES : (g + 1) * LANES] = v
        grad_key = left_product(grad_scores, heads)
        v = (grad_key + pltpu.roll(grad_key, HEAD_DIM, 1)) * score_scale
        grad_key = v * cosine - quarter_turn(v) * sine
        v = jnp.where(lanes_of(v) < HEAD_DIM, grad_key, grad_value).astype(BF)
        grad_ref[:, QW:] = v
        grads[rows, QW:] = v

    @pl.when(step >= MEMBERS)
    def _():
        block = pl.ds(pl.multiple_of((step - MEMBERS) * PANEL, PANEL), PANEL)
        send_ref[:, :QW] = left_product(att_ref[...], middle_ref[:, block]).astype(BF)
        send_ref[:, QW:] = left_product(first_ref[:, block], grads[...]).astype(BF)


def all_of(shape):
    return pl.BlockSpec(shape, lambda s: (0,) * len(shape), pipeline_mode=pl.Buffered(1))


def by_seq(width):
    return pl.BlockSpec((ROWS, width), lambda s: (jnp.minimum(s, MEMBERS - 1), 0))


MASK_BLOCK = pl.BlockSpec((1, ROWS, ROWS), lambda s: (jnp.minimum(s, MEMBERS - 1), 0, 0))


def attention(first_low, weights, cosine, sine, mask):
    half = pl.BlockSpec((SLOTS // 2, PANEL), lambda s: (0, jnp.maximum(s - MEMBERS, 0)))
    return pl.pallas_call(
        attention_kernel,
        grid=(2 * MEMBERS,),
        in_specs=[
            all_of((SLOTS, D)),
            all_of((D, QW + QKVW)),
            by_seq(LANES),
            by_seq(LANES),
            MASK_BLOCK,
        ],
        out_specs=[by_seq(QW), by_seq(LANES), by_seq(QW), half, half],
        out_shape=[
            jax.ShapeDtypeStruct((SLOTS, QW), BF),
            jax.ShapeDtypeStruct((SLOTS, LANES), BF),
            jax.ShapeDtypeStruct((SLOTS, QW), BF),
            jax.ShapeDtypeStruct((SLOTS // 2, D), F32),
            jax.ShapeDtypeStruct((SLOTS // 2, D), BF),
        ],
        scratch_shapes=[pltpu.VMEM((SLOTS, QKVW), F32), pltpu.VMEM((SLOTS, QW), BF)],
        compiler_params=pltpu.CompilerParams(vmem_limit_bytes=40 * 2**20),
        cost_estimate=pl.CostEstimate(
            flops=3 * 10**9, bytes_accessed=12 * 10**6, transcendentals=10**6
        ),
        name="attention",
    )(first_low, weights, cosine, sine, mask)


def attention_back(middle_all, weights, first_low, attended, query, kv, cosine, sine, mask):
    return pl.pallas_call(
        attention_back_kernel,
        grid=(2 * MEMBERS,),
        in_specs=[
            all_of((SLOTS, D)),
            all_of((D, QW + QKVW)),
            all_of((SLOTS, D)),
            all_of((SLOTS, QW)),
            by_seq(QW),
            by_seq(LANES),
            by_seq(LANES),
            by_seq(LANES),
            MASK_BLOCK,
        ],
        out_specs=[
            by_seq(QKVW),
            pl.BlockSpec((PANEL, QW + QKVW), lambda s: (jnp.maximum(s - MEMBERS, 0), 0)),
        ],
        out_shape=[
            jax.ShapeDtypeStruct((SLOTS, QKVW), BF),
            jax.ShapeDtypeStruct((D, QW + QKVW), BF),
        ],
        scratch_shapes=[pltpu.VMEM((SLOTS, QW), BF), pltpu.VMEM((SLOTS, QKVW), BF)],
        compiler_params=pltpu.CompilerParams(vmem_limit_bytes=40 * 2**20),
        cost_estimate=pl.CostEstimate(
            flops=5 * 10**9, bytes_accessed=16 * 10**6, transcendentals=10**6
        ),
        name="attention_back",
    )(middle_all, weights, first_low, attended, query, kv, cosine, sine, mask)


def rounded_gain(gain):
    return lax.optimization_barrier(gain.astype(BF)).astype(F32)


def inverse_rms(v):
    return lax.rsqrt(jnp.mean(v * v, axis=-1, keepdims=True) + epsilon)


def norm_back(v, gain, grad):
    r = inverse_rms(v)
    n = v * r
    scaled = grad * gain
    return r * (scaled - n * jnp.mean(scaled * n, axis=-1, keepdims=True)), n


def panels(gate, up):
    blocks = []
    for at in range(0, UNITS, 256):
        blocks += [gate[:, at : at + 256], up[:, at : at + 256]]
    return jnp.concatenate(blocks, axis=1)


def unpanels(v):
    gate = [v[:, :256], v[:, 512:768], v[:, 1024 : 1024 + LAST]]
    up = [v[:, 256:512], v[:, 768:1024], v[:, 1024 + LAST :]]
    return jnp.concatenate(gate, axis=1), jnp.concatenate(up, axis=1)


def on_device(
    tokens,
    cotangent,
    segment_ids,
    positions,
    padding,
    attn_gain,
    query_weight,
    key_weight,
    value_weight,
    output_weight,
    mlp_gain,
    gate_weight,
    up_weight,
    down_weight,
    attn_moment,
    query_moment,
    key_moment,
    value_moment,
    output_moment,
    mlp_moment,
    gate_moment,
    up_moment,
    down_moment,
):
    member = lax.axis_index("grp")
    place = lax.axis_index("dp")
    z, y, low = place // 8, (place // 2) % 4, (place % 2) == 0

    def mine(weight, width):
        return lax.dynamic_slice_in_dim(weight, member * width, width, 1).astype(BF)

    attn_shard = jnp.concatenate(
        [mine(query_weight, QW), mine(key_weight, KW), mine(value_weight, KW)], axis=1
    )
    attn_shard = jnp.concatenate(
        [turn_pair(mine(output_weight, QW), low), pair_x(attn_shard, low)], axis=1
    )
    attn_full = plane_gather(attn_shard)

    gate_mine, up_mine = mine(gate_weight, FW), mine(up_weight, FW)
    first = panels(gate_mine[:, :UNITS], up_mine[:, :UNITS])
    second = panels(gate_mine[:, UNITS:], up_mine[:, UNITS:])
    kept, given = jnp.where(low, first, second), jnp.where(low, second, first)
    gu_shard = in_order(kept, swap_x(given), low)
    tail = gu_shard[:, 2 * PANEL :]
    pieces = [
        gu_shard[:, :PANEL],
        gu_shard[:, PANEL : 2 * PANEL],
        jnp.concatenate([tail[:W_ROWS, :256], tail[W_ROWS:, :256]], axis=1),
        jnp.concatenate([tail[32 * h : 32 * h + 32, 256:] for h in range(4)], axis=1),
        everywhere(mine(down_weight, PANEL), OWNED),
    ]
    mlp_full = plane_gather(jnp.concatenate(pieces, axis=0)).reshape(16, SHARD, PANEL)

    places = jnp.stack([segment_ids, positions, padding])[None]
    rows_in = group_gather(tokens)
    places, upstream = lax.optimization_barrier(
        (jnp.concatenate([places, swap_far(places)], axis=0), cotangent)
    )
    cot_four, cot_core = row_gather(upstream)
    places = jnp.concatenate([places, swap_core(places)], axis=0)
    segments, spots, pads = places[:, 0], places[:, 1], places[:, 2]

    first_gain = rounded_gain(attn_gain)
    second_gain = rounded_gain(mlp_gain)
    inputs = rows_in.astype(F32)
    n_first = inputs * inverse_rms(inputs)
    first_low = (n_first * first_gain).astype(BF)

    half = HEAD_DIM // 2
    freq = 10000.0 ** (-(jnp.arange(half, dtype=F32) * 2.0 / HEAD_DIM))
    angles = spots.reshape(SLOTS, 1).astype(F32) * jnp.tile(freq, LANES // half)[None]
    cosine, sine = jnp.cos(angles), jnp.sin(angles)
    column = jnp.arange(ROWS, dtype=jnp.int32)
    allowed = jnp.logical_and(
        jnp.logical_and(
            segments[:, :, None] == segments[:, None, :],
            (column[None, :] <= column[:, None])[None],
        ),
        jnp.logical_or(pads[:, None, :] == 1, (column[None, :] == column[:, None])[None]),
    ).astype(F32)

    attn_full, first_low, cosine, sine, allowed, cot_four = lax.optimization_barrier(
        (attn_full, first_low, cosine, sine, allowed, cot_four)
    )
    query_rot, kv, attended, near, core = attention(first_low, attn_full, cosine, sine, allowed)
    middle = tokens.astype(F32) + group_scatter_far(near + swap_core(core).astype(F32))
    second_low = (middle * inverse_rms(middle) * second_gain).astype(BF)
    four, core_four = row_gather(second_low)
    core_four, cot_core = lax.optimization_barrier((core_four, cot_core))
    grad_gu, active, send = mlp_grads(four, core_four, cot_four, cot_core, mlp_full)
    mlp_sum = plane_scatter(send.reshape(16 * SHARD, PANEL))

    second_core = swap_core(second_grad(grad_gu, mlp_full, 1)[0])
    second_rest, second_own = second_grad(grad_gu, mlp_full, 0)
    grad_second = row_scatter(second_own, second_rest, second_core)
    back, n_second = norm_back(middle, second_gain, grad_second)
    mlp_gain_part = jnp.sum(grad_second * n_second, axis=0)
    grad_middle = cotangent.astype(F32) + back
    middle_all = group_gather(grad_middle.astype(BF))
    down_core, down_rest, down_own = down_product(active, mlp_full)
    middle_all, down_core = lax.optimization_barrier((middle_all, swap_core(down_core)))
    block_output = (middle + row_scatter(down_own, down_rest, down_core)).astype(BF)
    grad_qkv, attn_send = attention_back(
        middle_all, attn_full, first_low, attended, query_rot, kv, cosine, sine, allowed
    )
    attn_sum = plane_scatter(attn_send)

    own_moment = jnp.concatenate(
        [query_moment, key_moment, value_moment, output_moment], axis=1
    )
    grad_qkv, mlp_sum, block_output, own_moment = lax.optimization_barrier(
        (grad_qkv, mlp_sum, block_output, own_moment)
    )
    grad_first = right_product(grad_qkv, attn_full[:, QW:])
    attn_gain_part = jnp.sum(grad_first * n_first, axis=0)
    gains = jnp.stack([attn_gain_part, mlp_gain_part]).reshape(32, LANES)
    for pairs in (RING_Z, RING_Y):
        gains = gains + sum(lax.ppermute(gains, "dp", p) for p in pairs)
    back, _ = norm_back(tokens.astype(F32), first_gain, group_scatter(grad_first))
    input_grad = grad_middle + back

    mine_at = (member // 2) + 2 * (member % 2)

    def by_member(slots):
        return [
            lax.dynamic_index_in_dim(slots, mine_at ^ at, 0, keepdims=False) for at in (0, 2, 1, 3)
        ]

    def updated(weight, columns, start, size):
        moved = jnp.concatenate([block[:, start : start + size] for block in columns], axis=1)
        return weight - learn_rate * moved.astype(F32)

    wide, narrow = mlp_sum[256:320], mlp_sum[320:352]
    gu_part = jnp.concatenate(
        [
            mlp_sum[:128],
            mlp_sum[128:256],
            jnp.concatenate([wide[:, :256], wide[:, 256:]], axis=0),
            jnp.concatenate([narrow[:, h * LANES : (h + 1) * LANES] for h in range(4)], axis=0),
        ],
        axis=1,
    )
    kept, given = halves(gu_part, low)
    other = swap_x(given)
    first = unpanels(jnp.where(low, kept, other))
    second = unpanels(jnp.where(low, other, kept))
    gate_rows = jnp.concatenate([first[0], second[0]], axis=1).astype(F32)
    up_rows = jnp.concatenate([first[1], second[1]], axis=1).astype(F32)
    down_rows = everywhere(mlp_sum[352:], RETURN).astype(F32)
    gate_momentum = 0.5 * gate_moment + 0.5 * gate_rows
    up_momentum = 0.5 * up_moment + 0.5 * up_rows
    down_momentum = 0.5 * down_moment + 0.5 * down_rows
    gu_moved = by_member(
        group_gather(jnp.concatenate([gate_momentum, up_momentum], axis=1).astype(BF)).reshape(
            MEMBERS, W_ROWS, GUW
        )
    )
    down_moved = by_member(
        group_gather(down_momentum.astype(BF)).reshape(MEMBERS, DOWN_ROWS, PANEL)
    )

    mlp_done = (
        gate_momentum,
        up_momentum,
        down_momentum,
        updated(gate_weight, gu_moved, 0, FW),
        updated(up_weight, gu_moved, FW, FW),
        updated(down_weight, down_moved, 0, PANEL),
    )
    moments = group_gather(own_moment.astype(BF))
    attn_sum, gains, input_grad, moments, mlp_done = lax.optimization_barrier(
        (attn_sum, gains, input_grad, moments, mlp_done)
    )
    moments = moments.astype(F32)
    gate_momentum, up_momentum, down_momentum, gate_updated, up_updated, down_updated = mlp_done

    turned = everywhere(attn_sum[:, :QW], TURN)
    both = jnp.concatenate([attn_sum[:, QW:], turned], axis=1)
    gains = two_parts(gains)
    kept, given = halves(both, low)
    width = QKVW + PANEL
    near = swap_x(jnp.concatenate([given, gains], axis=1))
    far = swap_far(jnp.concatenate([kept, gains], axis=1))
    both_far = far_x(jnp.concatenate([given, gains], axis=1))
    own_total = kept.astype(F32) + near[:, :width].astype(F32)
    far_total = far[:, :width].astype(F32) + both_far[:, :width].astype(F32)
    gains = sum(one_part(part) for part in (gains, near[:, width:], far[:, width:], both_far[:, width:]))
    totals = jnp.concatenate([own_total, far_total], axis=0).astype(BF)
    rider = jnp.concatenate([two_parts(gains), jnp.zeros((W_ROWS, LANES), BF)], axis=0)
    other = swap_core(jnp.concatenate([totals, rider], axis=1))
    gains = gains + one_part(other[:W_ROWS, width:])
    totals = jnp.concatenate([totals, other[:, :width]], axis=0).astype(F32)

    own_moved = 0.5 * own_moment + 0.5 * own_total
    query_momentum = own_moved[:, :QW]
    key_momentum = own_moved[:, QW : QW + KW]
    value_momentum = own_moved[:, QW + KW : QKVW]
    output_momentum = own_moved[:, QKVW:]

    attn_moved = by_member((0.5 * moments + 0.5 * totals).reshape(MEMBERS, W_ROWS, width))

    gains = 0.5 * jnp.stack([attn_moment, mlp_moment]) + 0.5 * gains.reshape(2, D)
    return (
        block_output,
        input_grad,
        gains[0],
        query_momentum,
        key_momentum,
        value_momentum,
        output_momentum,
        gains[1],
        gate_momentum,
        up_momentum,
        down_momentum,
        attn_gain - learn_rate * gains[0],
        updated(query_weight, attn_moved, 0, QW),
        updated(key_weight, attn_moved, QW, KW),
        updated(value_weight, attn_moved, QW + KW, KW),
        updated(output_weight, attn_moved, QKVW, PANEL),
        mlp_gain - learn_rate * gains[1],
        gate_updated,
        up_updated,
        down_updated,
    )


def solution(mesh):
    rows = P(("grp", "dp"), None)
    flat = P(("grp", "dp"))
    weight = P("dp", None)
    moment = P("dp", "grp")
    everyone = P()
    weights = (everyone,) + (weight,) * 4 + (everyone,) + (weight,) * 3
    moments = (everyone,) + (moment,) * 4 + (everyone,) + (moment,) * 3
    return jax.shard_map(
        on_device,
        mesh=mesh,
        in_specs=(rows, rows, flat, flat, flat) + weights + moments,
        out_specs=(rows, rows) + moments + weights,
        check_vma=False,
    )
```

```python
import jax
import jax.numpy as jnp
from jax import lax
from jax.experimental import pallas as pl
from jax.experimental.pallas import tpu as pltpu
from jax.sharding import PartitionSpec as P

D = 2048
HEAD_DIM = 64
GROUPS = 8
ROWS = 128
MEMBERS = 4
SLOTS = ROWS * MEMBERS
QW = 512
KW = 64
QKVW = QW + 2 * KW
FW = 1408
GUW = 2 * FW
PANEL = 512
DOWN_ROWS = 176
W_ROWS = 64

epsilon = 1e-05
learn_rate = 0.005
score_scale = 0.125

BF = jnp.bfloat16
F32 = jnp.float32

PLANES = [[z * 8 + y * 2 + x for z in range(4) for y in range(4)] for x in range(2)]
SWAP_X = [(i, i ^ 1) for i in range(32)]
SWAP_CORE = [(m, m ^ 1) for m in range(4)]
SWAP_FAR = [(m, m ^ 2) for m in range(4)]
SWAP_FAR_X = [(m * 32 + i, (m ^ 2) * 32 + (i ^ 1)) for m in range(4) for i in range(32)]
MZQ = [(m, z, q) for m in range(4) for z in range(4) for q in range(8)]


def spot(m, z, q):
    return m * 32 + z * 8 + q


TURN = [(spot(m, z, q), spot(z, m, q)) for m, z, q in MZQ]
TURN_X = [(spot(m, z, q), spot(z, m, q ^ 1)) for m, z, q in MZQ]
TURN_IN = [[(spot(m, z, q), spot((z + k) % 4, m, q)) for m, z, q in MZQ] for k in range(4)]
OWNED = [(spot(m, z, q), spot(z, m, (q & 3) * 2 + (q >> 2))) for m, z, q in MZQ]
RETURN = [(b, a) for a, b in OWNED]


def ring(place, k):
    return [(i, i + ((i // place + k) % 4 - i // place % 4) * place) for i in range(32)]


RING_Z = [ring(8, k) for k in (1, 2, 3)]
RING_Y = [ring(2, k) for k in (1, 2, 3)]


def swap_x(v):
    return lax.ppermute(v, "dp", SWAP_X)


def swap_core(v):
    return lax.ppermute(v, "grp", SWAP_CORE)


def swap_far(v):
    return lax.ppermute(v, "grp", SWAP_FAR)


def everywhere(v, pairs):
    return lax.ppermute(v, ("grp", "dp"), pairs)


def plane_gather(v):
    return lax.all_gather(v, "dp", axis=0, tiled=True, axis_index_groups=PLANES)


def plane_scatter(v):
    return lax.psum_scatter(
        v, "dp", scatter_dimension=0, tiled=True, axis_index_groups=PLANES
    )


def ring_scatter(v, pairs, at, extra=None):
    rows = v.shape[0] // 4

    def chunk(k):
        part = lax.dynamic_slice_in_dim(v, lax.rem(at + k, 4) * rows, rows, 0)
        return part if extra is None else jnp.concatenate([part, extra], axis=1)

    total = chunk(0).astype(F32)
    for k, p in enumerate(pairs):
        total = total + lax.ppermute(chunk(k + 1), "dp", p).astype(F32)
    return total


def group_gather(v):
    pair = jnp.concatenate([v, swap_far(v)], axis=0)
    return jnp.concatenate([pair, swap_core(pair)], axis=0)


def group_scatter_far(near):
    return near[:ROWS] + swap_far(near[ROWS:].astype(BF)).astype(F32)


def far_x(v):
    return everywhere(v, SWAP_FAR_X)


def row_gather(v):
    four = jnp.concatenate([v, swap_x(v), swap_far(v), far_x(v)], axis=0)
    return four, swap_core(four)


def row_scatter(own, rest, core):
    own = own + core[:ROWS].astype(F32)
    rest = (rest.astype(F32) + core[ROWS:].astype(F32)).astype(BF)
    low_part, far_part, far_x_part = (rest[k * ROWS : (k + 1) * ROWS] for k in range(3))
    return (
        own
        + swap_x(low_part).astype(F32)
        + swap_far(far_part).astype(F32)
        + far_x(far_x_part).astype(F32)
    )


def in_order(own, other, low):
    return jnp.concatenate([jnp.where(low, own, other), jnp.where(low, other, own)], axis=0)


def pair_x(v, low):
    return in_order(v, swap_x(v), low)


def turn_pair(v, low):
    return in_order(everywhere(v, TURN), everywhere(v, TURN_X), low)


def halves(v, low):
    rows = v.shape[0] // 2
    return jnp.where(low, v[:rows], v[rows:]), jnp.where(low, v[rows:], v[:rows])


def two_parts(v):
    high = lax.reduce_precision(v, 8, 7)
    return jnp.concatenate([high.astype(BF), (v - high).astype(BF)], axis=0)


def one_part(v):
    rows = v.shape[0] // 2
    return v[:rows].astype(F32) + v[rows:].astype(F32)


def dot(left, right):
    return jnp.dot(left, right, preferred_element_type=F32)


def left_product(left, right):
    return lax.dot_general(left, right, (((0,), (0,)), ((), ())), preferred_element_type=F32)


def right_product(left, right):
    return lax.dot_general(left, right, (((1,), (1,)), ((), ())), preferred_element_type=F32)


ALL = 1024
UNITS = 704
LAST = 192
SHARD = 528


TAIL = [(256, 64, 256 * h, 64 * h, 0, 256) for h in range(2)]
TAIL += [(320, 32, 128 * h, 32 * h, 256, 128) for h in range(4)]


def tail_pieces(shard):
    for row, rows, column, at, start, width in TAIL:
        yield (
            shard.at[:, pl.ds(row, rows), pl.ds(column, width)],
            (slice(None), pl.ds(at, rows), pl.ds(start, width)),
        )


def tail_loads(full, tail, sems):
    return [
        pltpu.make_async_copy(src, tail.at[at], sems.at[i])
        for i, (src, at) in enumerate(tail_pieces(full))
    ]


def down_blocks(shard, down):
    return [
        (shard.at[4 * c + j, pl.ds(352, 176), :], down.at[c, pl.ds(176 * j, 176), :])
        for c in range(4)
        for j in range(4)
    ]


def mlp_kernel(
    four,
    core,
    cot_four,
    cot_core,
    panel_ref,
    full,
    ggu_ref,
    act_ref,
    send,
    down,
    tail,
    gpan,
    gtail,
    gdown,
    four_ref,
    core_ref,
    cot_four_ref,
    cot_core_ref,
    in_sem,
    row_sem,
    tail_sem,
    pan_sem,
    out_sem,
):
    step = pl.program_id(0)
    loads = [
        pltpu.make_async_copy(src, dst, in_sem.at[i])
        for i, (src, dst) in enumerate(
            [(cot_four, cot_four_ref), (cot_core, cot_core_ref)] + down_blocks(full, down)
        )
    ]
    rows_in = [
        pltpu.make_async_copy(src, dst, row_sem.at[i])
        for i, (src, dst) in enumerate([(four, four_ref), (core, core_ref)])
    ]
    tails = tail_loads(full, tail, tail_sem)

    @pl.when(step == 0)
    def _():
        for copy in rows_in + loads + tails:
            copy.start()

    def panel_out(at):
        return pltpu.make_async_copy(
            gpan.at[at], send.at[:, pl.ds(128 * at, 128), :], pan_sem.at[at]
        )

    def block(weights, start, width, store):
        halves_of = []
        for copy, ref in zip(rows_in, (four_ref, core_ref)):
            pl.when(step == 0)(copy.wait)
            halves_of.append(dot(ref[...], weights))

        @pl.when(step == 0)
        def _():
            for copy in loads:
                copy.wait()

        for half, (h, c_ref) in enumerate(zip(halves_of, (cot_four_ref, cot_core_ref))):
            rows = pl.ds(half * (ALL // 2), ALL // 2)
            gate, up = h[:, :width], h[:, width:]
            prod = right_product(c_ref[:, :PANEL], down[0, pl.ds(start, width), :])
            for c in range(1, 4):
                prod += right_product(
                    c_ref[:, c * PANEL : (c + 1) * PANEL], down[c, pl.ds(start, width), :]
                )
            sig = 1.0 / (1.0 + jnp.exp(-gate))
            silu = gate * sig
            act_ref[rows, :width] = (silu * up).astype(BF)
            ggu_ref[rows, :width] = (prod * up * sig * (1.0 + gate * (1.0 - sig))).astype(BF)
            ggu_ref[rows, width : 2 * width] = (prod * silu).astype(BF)
        for c in range(4):
            columns = slice(c * PANEL, (c + 1) * PANEL)
            grads = left_product(act_ref[: ALL // 2, :width], cot_four_ref[:, columns])
            grads += left_product(act_ref[ALL // 2 :, :width], cot_core_ref[:, columns])
            gdown[c, pl.ds(start, width), :] = grads.astype(BF)
        grads = left_product(four_ref[...], ggu_ref[: ALL // 2, : 2 * width])
        grads += left_product(core_ref[...], ggu_ref[ALL // 2 :, : 2 * width])
        store(grads.astype(BF))

    @pl.when(step < 2)
    def _():
        def store(grads):
            gpan[step] = grads.reshape(16, 128, PANEL)

        block(panel_ref[...].reshape(D, PANEL), pl.multiple_of(256 * step, 256), 256, store)
        panel_out(step).start()

    @pl.when(step == 2)
    def _():
        def store(grads):
            gtail[...] = grads.reshape(16, 128, 2 * LAST)

        for copy in tails:
            copy.wait()
        block(tail[...].reshape(D, 2 * LAST), 512, LAST, store)
        outs = [
            pltpu.make_async_copy(gtail.at[at], dst, tail_sem.at[i])
            for i, (dst, at) in enumerate(tail_pieces(send))
        ]
        outs += [
            pltpu.make_async_copy(src, dst, out_sem.at[i])
            for i, (dst, src) in enumerate(down_blocks(send, gdown))
        ]
        for copy in outs:
            copy.start()
        for copy in outs + [panel_out(0), panel_out(1)]:
            copy.wait()


def mlp_grads(four, core, cot_four, cot_core, full):
    return pl.pallas_call(
        mlp_kernel,
        grid=(3,),
        in_specs=[pl.BlockSpec(memory_space=pl.ANY)] * 4
        + [
            pl.BlockSpec((16, 128, PANEL), lambda i: (0, jnp.minimum(i, 1), 0)),
            pl.BlockSpec(memory_space=pl.ANY),
        ],
        out_specs=[
            pl.BlockSpec((ALL, 512), lambda i: (0, i)),
            pl.BlockSpec((ALL, 256), lambda i: (0, i)),
            pl.BlockSpec(memory_space=pl.ANY),
        ],
        out_shape=[
            jax.ShapeDtypeStruct((ALL, 1536), BF),
            jax.ShapeDtypeStruct((ALL, 768), BF),
            jax.ShapeDtypeStruct((16, SHARD, PANEL), BF),
        ],
        scratch_shapes=[
            pltpu.VMEM((4, UNITS, PANEL), BF),
            pltpu.VMEM((16, 128, 2 * LAST), BF),
            pltpu.VMEM((2, 16, 128, PANEL), BF),
            pltpu.VMEM((16, 128, 2 * LAST), BF),
            pltpu.VMEM((4, UNITS, PANEL), BF),
            pltpu.VMEM((ALL // 2, D), BF),
            pltpu.VMEM((ALL // 2, D), BF),
            pltpu.VMEM((ALL // 2, D), BF),
            pltpu.VMEM((ALL // 2, D), BF),
            pltpu.SemaphoreType.DMA((18,)),
            pltpu.SemaphoreType.DMA((2,)),
            pltpu.SemaphoreType.DMA((6,)),
            pltpu.SemaphoreType.DMA((2,)),
            pltpu.SemaphoreType.DMA((16,)),
        ],
        compiler_params=pltpu.CompilerParams(vmem_limit_bytes=56 * 2**20),
        cost_estimate=pl.CostEstimate(
            flops=18 * 10**9, bytes_accessed=45 * 10**6, transcendentals=10**6
        ),
        name="mlp_grads",
    )(four, core, cot_four, cot_core, full, full)


def split_rows(total, rest_ref, own_ref=None):
    if own_ref is None:
        rest_ref[...] = total.astype(BF)
    else:
        own_ref[...] = total[:ROWS]
        rest_ref[...] = total[ROWS : ALL // 2].astype(BF)


def second_kernel(g_ref, panel_ref, wide_ref, narrow_ref, *outs):
    *outs, tail = outs
    for row, rows, column, at, start, width in TAIL:
        piece = wide_ref if row == 256 else narrow_ref
        tail[:, at : at + rows, start : start + width] = piece[:, :, column : column + width]
    total = right_product(g_ref[:, :PANEL], panel_ref[:, :128].reshape(PANEL, PANEL))
    total += right_product(
        g_ref[:, PANEL : 2 * PANEL], panel_ref[:, 128:].reshape(PANEL, PANEL)
    )
    total += right_product(
        g_ref[:, 2 * PANEL : 2 * PANEL + 2 * LAST], tail[...].reshape(PANEL, 2 * LAST)
    )
    split_rows(total, *outs)


def second_grad(ggu, full, half):
    rows = [ALL // 2] if half else [ALL // 2 - ROWS, ROWS]
    return pl.pallas_call(
        second_kernel,
        grid=(4,),
        in_specs=[
            pl.BlockSpec((ALL // 2, 1536), lambda i: (half, 0)),
            pl.BlockSpec((4, 256, PANEL), lambda i: (i, 0, 0)),
            pl.BlockSpec((4, 64, PANEL), lambda i: (i, 4, 0)),
            pl.BlockSpec((4, 32, PANEL), lambda i: (i, 10, 0)),
        ],
        out_specs=[pl.BlockSpec((r, PANEL), lambda i: (0, i)) for r in rows],
        out_shape=[jax.ShapeDtypeStruct((r, D), kind) for r, kind in zip(rows, (BF, F32))],
        scratch_shapes=[pltpu.VMEM((4, 128, 2 * LAST), BF)],
        compiler_params=pltpu.CompilerParams(vmem_limit_bytes=58 * 2**20),
        cost_estimate=pl.CostEstimate(
            flops=3 * 10**9, bytes_accessed=10 * 10**6, transcendentals=0
        ),
        name="second_grad",
    )(ggu, full, full, full)


def down_kernel(act_ref, down_ref, core_ref, rest_ref, own_ref):
    part = dot(act_ref[:, :UNITS], down_ref[...].reshape(UNITS, PANEL))
    split_rows(part, rest_ref, own_ref)
    core_ref[...] = part[ALL // 2 :].astype(BF)


def down_product(active, full):
    rows = [ALL // 2, ALL // 2 - ROWS, ROWS]
    return pl.pallas_call(
        down_kernel,
        grid=(4,),
        in_specs=[
            pl.BlockSpec((ALL, 768), lambda c: (0, 0)),
            pl.BlockSpec((4, 176, PANEL), lambda c: (c, 2, 0)),
        ],
        out_specs=[pl.BlockSpec((r, PANEL), lambda c: (0, c)) for r in rows],
        out_shape=[jax.ShapeDtypeStruct((r, D), kind) for r, kind in zip(rows, (BF, BF, F32))],
        compiler_params=pltpu.CompilerParams(vmem_limit_bytes=58 * 2**20),
        cost_estimate=pl.CostEstimate(
            flops=3 * 10**9, bytes_accessed=12 * 10**6, transcendentals=0
        ),
        name="down_product",
    )(active, full)


LANES = 128


def lanes_of(v):
    return lax.broadcasted_iota(jnp.int32, v.shape, v.ndim - 1)


def quarter_turn(v):
    first = lanes_of(v) % HEAD_DIM < HEAD_DIM // 2
    return jnp.where(first, -pltpu.roll(v, 96, 1), pltpu.roll(v, 32, 1))


def doubled(v):
    left = lanes_of(v) < HEAD_DIM
    other = pltpu.roll(v, HEAD_DIM, 1)
    return jnp.where(left, v, other), jnp.where(left, other, v)


def head_rows(ref):
    blocks = []
    for g in range(GROUPS // 2):
        v = ref[:, g * LANES : (g + 1) * LANES].astype(F32)
        left = lanes_of(v) < HEAD_DIM
        blocks += [jnp.where(left, v, 0.0), jnp.where(left, 0.0, v)]
    return jnp.concatenate(blocks, axis=0).astype(BF)


def pair_columns(v, g):
    even = v[2 * g * ROWS : (2 * g + 1) * ROWS]
    odd = v[(2 * g + 1) * ROWS : (2 * g + 2) * ROWS]
    return jnp.where(lanes_of(even) < HEAD_DIM, even, odd)


def softmax_rows(heads, key2, mask):
    scores = right_product(heads, key2).reshape(GROUPS, ROWS, ROWS) * score_scale
    masked = jnp.where(mask[None] > 0.0, scores, -1e30)
    top = jnp.max(masked, axis=-1, keepdims=True)
    total = top + jnp.log(jnp.sum(jnp.exp(masked - top), axis=-1, keepdims=True))
    return jnp.exp(masked - total).reshape(GROUPS * ROWS, ROWS)


def seq_rows(step):
    return pl.ds(pl.multiple_of(jnp.minimum(step, MEMBERS - 1) * ROWS, ROWS), ROWS)


def attention_kernel(
    first_ref,
    weight_ref,
    cos_ref,
    sin_ref,
    mask_ref,
    query_ref,
    kv_ref,
    att_ref,
    near_ref,
    core_ref,
    qkv,
    att,
):
    step = pl.program_id(0)

    @pl.when(step == 0)
    def _():
        qkv[...] = dot(first_ref[...], weight_ref[:, QW:])

    @pl.when(step < MEMBERS)
    def _():
        rows = seq_rows(step)
        cosine, sine = cos_ref[...], sin_ref[...]
        for g in range(GROUPS // 2):
            v = qkv[rows, g * LANES : (g + 1) * LANES]
            query_ref[:, g * LANES : (g + 1) * LANES] = (
                v * cosine + quarter_turn(v) * sine
            ).astype(BF)
        v = qkv[rows, QW:]
        kv = jnp.where(lanes_of(v) < HEAD_DIM, v * cosine + quarter_turn(v) * sine, v)
        kv_ref[...] = kv.astype(BF)
        key2, value2 = doubled(kv)
        probs = softmax_rows(head_rows(query_ref), key2.astype(BF), mask_ref[0])
        heads = dot(probs.astype(BF), value2.astype(BF))
        for g in range(GROUPS // 2):
            pair = pair_columns(heads, g).astype(BF)
            att_ref[:, g * LANES : (g + 1) * LANES] = pair
            att[rows, g * LANES : (g + 1) * LANES] = pair

    @pl.when(step >= MEMBERS)
    def _():
        block = pl.ds(pl.multiple_of((step - MEMBERS) * QW, QW), QW)
        part = dot(att[...], weight_ref[block, :QW])
        near_ref[...] = part[: SLOTS // 2]
        core_ref[...] = part[SLOTS // 2 :].astype(BF)


def attention_back_kernel(
    middle_ref,
    weight_ref,
    first_ref,
    att_ref,
    query_ref,
    kv_ref,
    cos_ref,
    sin_ref,
    mask_ref,
    grad_ref,
    send_ref,
    upstream,
    grads,
):
    step = pl.program_id(0)

    @pl.when(step == 0)
    def _():
        total = right_product(middle_ref[:, :PANEL], weight_ref[:QW, :QW])
        for c in range(1, 4):
            total += right_product(
                middle_ref[:, c * PANEL : (c + 1) * PANEL],
                weight_ref[c * QW : (c + 1) * QW, :QW],
            )
        upstream[...] = total.astype(BF)

    @pl.when(step < MEMBERS)
    def _():
        rows = seq_rows(step)
        cosine, sine = cos_ref[...], sin_ref[...]
        key2, value2 = doubled(kv_ref[...].astype(F32))
        key2, value2 = key2.astype(BF), value2.astype(BF)
        heads, lifted = head_rows(query_ref), head_rows(upstream.at[rows])
        probs = softmax_rows(heads, key2, mask_ref[0])
        grad_value = left_product(probs.astype(BF), lifted)
        grad_value = grad_value + pltpu.roll(grad_value, HEAD_DIM, 1)
        grad_probs = right_product(lifted, value2)
        inner = jnp.sum(grad_probs * probs, axis=-1, keepdims=True)
        grad_scores = (probs * (grad_probs - inner)).astype(BF)
        grad_query = dot(grad_scores, key2)
        for g in range(GROUPS // 2):
            v = pair_columns(grad_query, g) * score_scale
            v = (v * cosine - quarter_turn(v) * sine).astype(BF)
            grad_ref[:, g * LANES : (g + 1) * LANES] = v
            grads[rows, g * LANES : (g + 1) * LANES] = v
        grad_key = left_product(grad_scores, heads)
        v = (grad_key + pltpu.roll(grad_key, HEAD_DIM, 1)) * score_scale
        grad_key = v * cosine - quarter_turn(v) * sine
        v = jnp.where(lanes_of(v) < HEAD_DIM, grad_key, grad_value).astype(BF)
        grad_ref[:, QW:] = v
        grads[rows, QW:] = v

    @pl.when(step >= MEMBERS)
    def _():
        block = pl.ds(pl.multiple_of((step - MEMBERS) * PANEL, PANEL), PANEL)
        send_ref[:, :QW] = left_product(att_ref[...], middle_ref[:, block]).astype(BF)
        send_ref[:, QW:] = left_product(first_ref[:, block], grads[...]).astype(BF)


def all_of(shape):
    return pl.BlockSpec(shape, lambda s: (0,) * len(shape), pipeline_mode=pl.Buffered(1))


def by_seq(width):
    return pl.BlockSpec((ROWS, width), lambda s: (jnp.minimum(s, MEMBERS - 1), 0))


MASK_BLOCK = pl.BlockSpec((1, ROWS, ROWS), lambda s: (jnp.minimum(s, MEMBERS - 1), 0, 0))


def attention(first_low, weights, cosine, sine, mask):
    half = pl.BlockSpec((SLOTS // 2, PANEL), lambda s: (0, jnp.maximum(s - MEMBERS, 0)))
    return pl.pallas_call(
        attention_kernel,
        grid=(2 * MEMBERS,),
        in_specs=[
            all_of((SLOTS, D)),
            all_of((D, QW + QKVW)),
            by_seq(LANES),
            by_seq(LANES),
            MASK_BLOCK,
        ],
        out_specs=[by_seq(QW), by_seq(LANES), by_seq(QW), half, half],
        out_shape=[
            jax.ShapeDtypeStruct((SLOTS, QW), BF),
            jax.ShapeDtypeStruct((SLOTS, LANES), BF),
            jax.ShapeDtypeStruct((SLOTS, QW), BF),
            jax.ShapeDtypeStruct((SLOTS // 2, D), F32),
            jax.ShapeDtypeStruct((SLOTS // 2, D), BF),
        ],
        scratch_shapes=[pltpu.VMEM((SLOTS, QKVW), F32), pltpu.VMEM((SLOTS, QW), BF)],
        compiler_params=pltpu.CompilerParams(vmem_limit_bytes=40 * 2**20),
        cost_estimate=pl.CostEstimate(
            flops=3 * 10**9, bytes_accessed=12 * 10**6, transcendentals=10**6
        ),
        name="attention",
    )(first_low, weights, cosine, sine, mask)


def attention_back(middle_all, weights, first_low, attended, query, kv, cosine, sine, mask):
    return pl.pallas_call(
        attention_back_kernel,
        grid=(2 * MEMBERS,),
        in_specs=[
            all_of((SLOTS, D)),
            all_of((D, QW + QKVW)),
            all_of((SLOTS, D)),
            all_of((SLOTS, QW)),
            by_seq(QW),
            by_seq(LANES),
            by_seq(LANES),
            by_seq(LANES),
            MASK_BLOCK,
        ],
        out_specs=[
            by_seq(QKVW),
            pl.BlockSpec((PANEL, QW + QKVW), lambda s: (jnp.maximum(s - MEMBERS, 0), 0)),
        ],
        out_shape=[
            jax.ShapeDtypeStruct((SLOTS, QKVW), BF),
            jax.ShapeDtypeStruct((D, QW + QKVW), BF),
        ],
        scratch_shapes=[pltpu.VMEM((SLOTS, QW), BF), pltpu.VMEM((SLOTS, QKVW), BF)],
        compiler_params=pltpu.CompilerParams(vmem_limit_bytes=40 * 2**20),
        cost_estimate=pl.CostEstimate(
            flops=5 * 10**9, bytes_accessed=16 * 10**6, transcendentals=10**6
        ),
        name="attention_back",
    )(middle_all, weights, first_low, attended, query, kv, cosine, sine, mask)


def first_kernel(grad_ref, weight_ref, rows_ref, rms_ref, near_ref, core_ref, gain_ref):
    grad = right_product(grad_ref[...], weight_ref[:, QW:])
    normed = rows_ref[...].astype(F32) * rms_ref[...]
    gain_ref[...] = jnp.sum(grad * normed, axis=0, keepdims=True)
    near_ref[...] = grad[: SLOTS // 2]
    core_ref[...] = grad[SLOTS // 2 :].astype(BF)


def first_grad(grad_qkv, weights, rows_in, rms):
    half = pl.BlockSpec((SLOTS // 2, PANEL), lambda i: (0, i))
    return pl.pallas_call(
        first_kernel,
        grid=(4,),
        in_specs=[
            all_of((SLOTS, QKVW)),
            pl.BlockSpec((PANEL, QW + QKVW), lambda i: (i, 0)),
            pl.BlockSpec((SLOTS, PANEL), lambda i: (0, i)),
            all_of((SLOTS, 1)),
        ],
        out_specs=[half, half, pl.BlockSpec((1, PANEL), lambda i: (0, i))],
        out_shape=[
            jax.ShapeDtypeStruct((SLOTS // 2, D), F32),
            jax.ShapeDtypeStruct((SLOTS // 2, D), BF),
            jax.ShapeDtypeStruct((1, D), F32),
        ],
        compiler_params=pltpu.CompilerParams(vmem_limit_bytes=32 * 2**20),
        cost_estimate=pl.CostEstimate(
            flops=14 * 10**8, bytes_accessed=12 * 10**6, transcendentals=0
        ),
        name="first_grad",
    )(grad_qkv, weights, rows_in, rms)


def update_kernel(
    at_ref,
    own_ref,
    near_ref,
    core_ref,
    moments_ref,
    moment_ref,
    query_ref,
    key_ref,
    value_ref,
    output_ref,
    query_moved,
    key_moved,
    value_moved,
    output_moved,
    query_new,
    key_new,
    value_new,
    output_new,
    moved,
):
    width = QKVW + PANEL
    own = 0.5 * moment_ref[...] + 0.5 * own_ref[...]
    query_moved[...] = own[:, :QW]
    key_moved[...] = own[:, QW : QW + KW]
    value_moved[...] = own[:, QW + KW : QKVW]
    output_moved[...] = own[:, QKVW:]
    rows = near_ref.shape[0]
    moved[:rows] = 0.5 * moments_ref[:rows].astype(F32) + 0.5 * near_ref[...].astype(F32)
    moved[rows:] = 0.5 * moments_ref[rows:].astype(F32) + 0.5 * core_ref[:, :width].astype(F32)
    pairs = []
    for a, order in enumerate((0, 2, 1, 3)):
        slot = pl.ds(pl.multiple_of((at_ref[0] ^ order) * W_ROWS, W_ROWS), W_ROWS)
        columns = slice(a * QW, (a + 1) * QW)
        query_new[:, columns] = query_ref[:, columns] - learn_rate * moved[slot, :QW]
        output_new[:, columns] = output_ref[:, columns] - learn_rate * moved[slot, QKVW:]
        pairs.append(moved[slot, QW:QKVW])
    for a in (0, 2):
        even, odd = pairs[a], pairs[a + 1]
        left = lanes_of(even) < HEAD_DIM
        key = jnp.where(left, even, pltpu.roll(odd, HEAD_DIM, 1))
        value = jnp.where(left, pltpu.roll(even, HEAD_DIM, 1), odd)
        columns = slice(a * KW, (a + 2) * KW)
        key_new[:, columns] = key_ref[:, columns] - learn_rate * key
        value_new[:, columns] = value_ref[:, columns] - learn_rate * value


def attention_update(at, own, near, core, moments, moment, weights):
    shapes = [(W_ROWS, w) for w in (QW, KW, KW, QW)] + [w.shape for w in weights]
    vmem = pl.BlockSpec(memory_space=pltpu.VMEM)
    return pl.pallas_call(
        update_kernel,
        in_specs=[pl.BlockSpec(memory_space=pltpu.SMEM)] + [vmem] * 9,
        out_specs=[vmem] * 8,
        out_shape=[jax.ShapeDtypeStruct(shape, F32) for shape in shapes],
        scratch_shapes=[pltpu.VMEM((MEMBERS * W_ROWS, QKVW + PANEL), F32)],
        compiler_params=pltpu.CompilerParams(vmem_limit_bytes=16 * 2**20),
        cost_estimate=pl.CostEstimate(
            flops=10**6, bytes_accessed=6 * 10**6, transcendentals=0
        ),
        name="attention_update",
    )(at, own, near, core, moments, moment, *weights)


def rounded_gain(gain):
    return lax.optimization_barrier(gain.astype(BF)).astype(F32)


def inverse_rms(v):
    return lax.rsqrt(jnp.mean(v * v, axis=-1, keepdims=True) + epsilon)


def norm_back(v, gain, grad):
    r = inverse_rms(v)
    n = v * r
    scaled = grad * gain
    return r * (scaled - n * jnp.mean(scaled * n, axis=-1, keepdims=True)), n


def panels(gate, up):
    blocks = []
    for at in range(0, UNITS, 256):
        blocks += [gate[:, at : at + 256], up[:, at : at + 256]]
    return jnp.concatenate(blocks, axis=1)


def unpanels(v):
    gate = [v[:, :256], v[:, 512:768], v[:, 1024 : 1024 + LAST]]
    up = [v[:, 256:512], v[:, 768:1024], v[:, 1024 + LAST :]]
    return jnp.concatenate(gate, axis=1), jnp.concatenate(up, axis=1)


def on_device(
    tokens,
    cotangent,
    segment_ids,
    positions,
    padding,
    attn_gain,
    query_weight,
    key_weight,
    value_weight,
    output_weight,
    mlp_gain,
    gate_weight,
    up_weight,
    down_weight,
    attn_moment,
    query_moment,
    key_moment,
    value_moment,
    output_moment,
    mlp_moment,
    gate_moment,
    up_moment,
    down_moment,
):
    member = lax.axis_index("grp")
    place = lax.axis_index("dp")
    z, y, low = place // 8, (place // 2) % 4, (place % 2) == 0

    def mine(weight, width):
        return lax.dynamic_slice_in_dim(weight, member * width, width, 1).astype(BF)

    attn_shard = jnp.concatenate(
        [mine(query_weight, QW), mine(key_weight, KW), mine(value_weight, KW)], axis=1
    )
    attn_shard = jnp.concatenate(
        [turn_pair(mine(output_weight, QW), low), pair_x(attn_shard, low)], axis=1
    )
    attn_full = plane_gather(attn_shard)

    gate_mine, up_mine = mine(gate_weight, FW), mine(up_weight, FW)
    first = panels(gate_mine[:, :UNITS], up_mine[:, :UNITS])
    second = panels(gate_mine[:, UNITS:], up_mine[:, UNITS:])
    kept, given = jnp.where(low, first, second), jnp.where(low, second, first)
    gu_shard = in_order(kept, swap_x(given), low)
    tail = gu_shard[:, 2 * PANEL :]
    pieces = [
        gu_shard[:, :PANEL],
        gu_shard[:, PANEL : 2 * PANEL],
        jnp.concatenate([tail[:W_ROWS, :256], tail[W_ROWS:, :256]], axis=1),
        jnp.concatenate([tail[32 * h : 32 * h + 32, 256:] for h in range(4)], axis=1),
        everywhere(mine(down_weight, PANEL), OWNED),
    ]
    mlp_full = plane_gather(jnp.concatenate(pieces, axis=0)).reshape(16, SHARD, PANEL)

    places = jnp.stack([segment_ids, positions, padding])[None]
    rows_in = group_gather(tokens)
    own_moment = jnp.concatenate(
        [query_moment, key_moment, value_moment, output_moment], axis=1
    )
    moments = own_moment.astype(BF)
    places, moments, upstream = lax.optimization_barrier(
        (
            jnp.concatenate([places, swap_far(places)], axis=0),
            jnp.concatenate([moments, swap_far(moments)], axis=0),
            cotangent,
        )
    )
    cot_four, cot_core = row_gather(upstream)
    places = jnp.concatenate([places, swap_core(places)], axis=0)
    moments = jnp.concatenate([moments, swap_core(moments)], axis=0)
    segments, spots, pads = places[:, 0], places[:, 1], places[:, 2]

    first_gain = rounded_gain(attn_gain)
    second_gain = rounded_gain(mlp_gain)
    inputs = rows_in.astype(F32)
    rms = inverse_rms(inputs)
    first_low = (inputs * rms * first_gain).astype(BF)

    half = HEAD_DIM // 2
    freq = 10000.0 ** (-(jnp.arange(half, dtype=F32) * 2.0 / HEAD_DIM))
    angles = spots.reshape(SLOTS, 1).astype(F32) * jnp.tile(freq, LANES // half)[None]
    cosine, sine = jnp.cos(angles), jnp.sin(angles)
    column = jnp.arange(ROWS, dtype=jnp.int32)
    allowed = jnp.logical_and(
        jnp.logical_and(
            segments[:, :, None] == segments[:, None, :],
            (column[None, :] <= column[:, None])[None],
        ),
        jnp.logical_or(pads[:, None, :] == 1, (column[None, :] == column[:, None])[None]),
    ).astype(F32)

    attn_full, first_low, cosine, sine, allowed, cot_four, moments = lax.optimization_barrier(
        (attn_full, first_low, cosine, sine, allowed, cot_four, moments)
    )
    query_rot, kv, attended, near, core = attention(first_low, attn_full, cosine, sine, allowed)
    middle = tokens.astype(F32) + group_scatter_far(near + swap_core(core).astype(F32))
    second_low = (middle * inverse_rms(middle) * second_gain).astype(BF)
    four, core_four = row_gather(second_low)
    core_four, cot_core = lax.optimization_barrier((core_four, cot_core))
    grad_gu, active, send = mlp_grads(four, core_four, cot_four, cot_core, mlp_full)
    mlp_sum = plane_scatter(send.reshape(16 * SHARD, PANEL))

    second_core = swap_core(second_grad(grad_gu, mlp_full, 1)[0])
    second_rest, second_own = second_grad(grad_gu, mlp_full, 0)
    grad_second = row_scatter(second_own, second_rest, second_core)
    back, n_second = norm_back(middle, second_gain, grad_second)
    mlp_gain_part = jnp.sum(grad_second * n_second, axis=0)
    grad_middle = cotangent.astype(F32) + back
    middle_all = group_gather(grad_middle.astype(BF))
    down_core, down_rest, down_own = down_product(active, mlp_full)
    middle_all, down_core = lax.optimization_barrier((middle_all, swap_core(down_core)))
    grad_qkv, attn_send = attention_back(
        middle_all, attn_full, first_low, attended, query_rot, kv, cosine, sine, allowed
    )
    attn_sum = plane_scatter(attn_send)

    grad_qkv, mlp_sum, down_core = lax.optimization_barrier((grad_qkv, mlp_sum, down_core))
    block_output = (middle + row_scatter(down_own, down_rest, down_core)).astype(BF)
    near, core, attn_gain_part = first_grad(grad_qkv, attn_full, rows_in, rms)
    gains = jnp.concatenate([attn_gain_part, mlp_gain_part[None]], axis=0).reshape(32, LANES)
    for pairs in (RING_Z, RING_Y):
        gains = gains + sum(lax.ppermute(gains, "dp", p) for p in pairs)
    near = near + swap_core(core).astype(F32)
    back, _ = norm_back(tokens.astype(F32), first_gain, group_scatter_far(near))
    input_grad = grad_middle + back

    mine_at = (member // 2) + 2 * (member % 2)

    def by_member(slots):
        return [
            lax.dynamic_index_in_dim(slots, mine_at ^ at, 0, keepdims=False) for at in (0, 2, 1, 3)
        ]

    def updated(weight, columns, start, size):
        moved = jnp.concatenate([block[:, start : start + size] for block in columns], axis=1)
        return weight - learn_rate * moved.astype(F32)

    wide, narrow = mlp_sum[256:320], mlp_sum[320:352]
    gu_part = jnp.concatenate(
        [
            mlp_sum[:128],
            mlp_sum[128:256],
            jnp.concatenate([wide[:, :256], wide[:, 256:]], axis=0),
            jnp.concatenate([narrow[:, h * LANES : (h + 1) * LANES] for h in range(4)], axis=0),
        ],
        axis=1,
    )
    kept, given = halves(gu_part, low)
    other = swap_x(given)
    first = unpanels(jnp.where(low, kept, other))
    second = unpanels(jnp.where(low, other, kept))
    gate_rows = jnp.concatenate([first[0], second[0]], axis=1).astype(F32)
    up_rows = jnp.concatenate([first[1], second[1]], axis=1).astype(F32)
    down_rows = everywhere(mlp_sum[352:], RETURN).astype(F32)
    gate_momentum = 0.5 * gate_moment + 0.5 * gate_rows
    up_momentum = 0.5 * up_moment + 0.5 * up_rows
    down_momentum = 0.5 * down_moment + 0.5 * down_rows
    gu_moved = by_member(
        group_gather(jnp.concatenate([gate_momentum, up_momentum], axis=1).astype(BF)).reshape(
            MEMBERS, W_ROWS, GUW
        )
    )
    down_moved = by_member(
        group_gather(down_momentum.astype(BF)).reshape(MEMBERS, DOWN_ROWS, PANEL)
    )

    mlp_done = (
        gate_momentum,
        up_momentum,
        down_momentum,
        updated(gate_weight, gu_moved, 0, FW),
        updated(up_weight, gu_moved, FW, FW),
        updated(down_weight, down_moved, 0, PANEL),
    )
    attn_sum, gains, input_grad, block_output, mlp_done = lax.optimization_barrier(
        (attn_sum, gains, input_grad, block_output, mlp_done)
    )
    gate_momentum, up_momentum, down_momentum, gate_updated, up_updated, down_updated = mlp_done

    turned = everywhere(attn_sum[:, :QW], TURN)
    both = jnp.concatenate([attn_sum[:, QW:], turned], axis=1)
    gains = two_parts(gains)
    kept, given = halves(both, low)
    width = QKVW + PANEL
    near = swap_x(jnp.concatenate([given, gains], axis=1))
    far = swap_far(jnp.concatenate([kept, gains], axis=1))
    both_far = far_x(jnp.concatenate([given, gains], axis=1))
    own_total = kept.astype(F32) + near[:, :width].astype(F32)
    far_total = far[:, :width].astype(F32) + both_far[:, :width].astype(F32)
    gains = sum(one_part(part) for part in (gains, near[:, width:], far[:, width:], both_far[:, width:]))
    totals = jnp.concatenate([own_total, far_total], axis=0).astype(BF)
    rider = jnp.concatenate([two_parts(gains), jnp.zeros((W_ROWS, LANES), BF)], axis=0)
    other = swap_core(jnp.concatenate([totals, rider], axis=1))
    gains = gains + one_part(other[:W_ROWS, width:])
    attn_done = attention_update(
        mine_at.astype(jnp.int32).reshape(1),
        own_total,
        totals,
        other,
        moments,
        own_moment,
        (query_weight, key_weight, value_weight, output_weight),
    )

    gains = 0.5 * jnp.stack([attn_moment, mlp_moment]) + 0.5 * gains.reshape(2, D)
    return (
        block_output,
        input_grad,
        gains[0],
        *attn_done[:4],
        gains[1],
        gate_momentum,
        up_momentum,
        down_momentum,
        attn_gain - learn_rate * gains[0],
        *attn_done[4:],
        mlp_gain - learn_rate * gains[1],
        gate_updated,
        up_updated,
        down_updated,
    )


def solution(mesh):
    rows = P(("grp", "dp"), None)
    flat = P(("grp", "dp"))
    weight = P("dp", None)
    moment = P("dp", "grp")
    everyone = P()
    weights = (everyone,) + (weight,) * 4 + (everyone,) + (weight,) * 3
    moments = (everyone,) + (moment,) * 4 + (everyone,) + (moment,) * 3
    return jax.shard_map(
        on_device,
        mesh=mesh,
        in_specs=(rows, rows, flat, flat, flat) + weights + moments,
        out_specs=(rows, rows) + moments + weights,
        check_vma=False,
    )
```

```python
import jax
import jax.numpy as jnp
from jax import lax
from jax.experimental import pallas as pl
from jax.experimental.pallas import tpu as pltpu
from jax.sharding import PartitionSpec as P

D = 2048
HEAD_DIM = 64
GROUPS = 8
ROWS = 128
MEMBERS = 4
SLOTS = ROWS * MEMBERS
QW = 512
KW = 64
QKVW = QW + 2 * KW
FW = 1408
GUW = 2 * FW
PANEL = 512
DOWN_ROWS = 176
W_ROWS = 64

epsilon = 1e-05
learn_rate = 0.005
score_scale = 0.125

BF = jnp.bfloat16
F32 = jnp.float32

PLANES = [[z * 8 + y * 2 + x for z in range(4) for y in range(4)] for x in range(2)]
SWAP_X = [(i, i ^ 1) for i in range(32)]
SWAP_CORE = [(m, m ^ 1) for m in range(4)]
SWAP_FAR = [(m, m ^ 2) for m in range(4)]
SWAP_FAR_X = [(m * 32 + i, (m ^ 2) * 32 + (i ^ 1)) for m in range(4) for i in range(32)]
MZQ = [(m, z, q) for m in range(4) for z in range(4) for q in range(8)]


def spot(m, z, q):
    return m * 32 + z * 8 + q


TURN = [(spot(m, z, q), spot(z, m, q)) for m, z, q in MZQ]
TURN_X = [(spot(m, z, q), spot(z, m, q ^ 1)) for m, z, q in MZQ]
TURN_IN = [[(spot(m, z, q), spot((z + k) % 4, m, q)) for m, z, q in MZQ] for k in range(4)]
OWNED = [(spot(m, z, q), spot(z, m, (q & 3) * 2 + (q >> 2))) for m, z, q in MZQ]
RETURN = [(b, a) for a, b in OWNED]


def ring(place, k):
    return [(i, i + ((i // place + k) % 4 - i // place % 4) * place) for i in range(32)]


RING_Z = [ring(8, k) for k in (1, 2, 3)]
RING_Y = [ring(2, k) for k in (1, 2, 3)]


def swap_x(v):
    return lax.ppermute(v, "dp", SWAP_X)


def swap_core(v):
    return lax.ppermute(v, "grp", SWAP_CORE)


def swap_far(v):
    return lax.ppermute(v, "grp", SWAP_FAR)


def everywhere(v, pairs):
    return lax.ppermute(v, ("grp", "dp"), pairs)


def plane_gather(v):
    return lax.all_gather(v, "dp", axis=0, tiled=True, axis_index_groups=PLANES)


def plane_scatter(v):
    return lax.psum_scatter(
        v, "dp", scatter_dimension=0, tiled=True, axis_index_groups=PLANES
    )


def ring_scatter(v, pairs, at, extra=None):
    rows = v.shape[0] // 4

    def chunk(k):
        part = lax.dynamic_slice_in_dim(v, lax.rem(at + k, 4) * rows, rows, 0)
        return part if extra is None else jnp.concatenate([part, extra], axis=1)

    total = chunk(0).astype(F32)
    for k, p in enumerate(pairs):
        total = total + lax.ppermute(chunk(k + 1), "dp", p).astype(F32)
    return total


def group_gather(v):
    pair = jnp.concatenate([v, swap_far(v)], axis=0)
    return jnp.concatenate([pair, swap_core(pair)], axis=0)


def group_scatter_far(near):
    return near[:ROWS] + swap_far(near[ROWS:].astype(BF)).astype(F32)


def far_x(v):
    return everywhere(v, SWAP_FAR_X)


def row_gather(v):
    four = jnp.concatenate([v, swap_x(v), swap_far(v), far_x(v)], axis=0)
    return four, swap_core(four)


def row_scatter(own, rest, core):
    own = own + core[:ROWS].astype(F32)
    rest = (rest.astype(F32) + core[ROWS:].astype(F32)).astype(BF)
    low_part, far_part, far_x_part = (rest[k * ROWS : (k + 1) * ROWS] for k in range(3))
    return (
        own
        + swap_x(low_part).astype(F32)
        + swap_far(far_part).astype(F32)
        + far_x(far_x_part).astype(F32)
    )


def in_order(own, other, low):
    return jnp.concatenate([jnp.where(low, own, other), jnp.where(low, other, own)], axis=0)


def pair_x(v, low):
    return in_order(v, swap_x(v), low)


def turn_pair(v, low):
    return in_order(everywhere(v, TURN), everywhere(v, TURN_X), low)


def halves(v, low):
    rows = v.shape[0] // 2
    return jnp.where(low, v[:rows], v[rows:]), jnp.where(low, v[rows:], v[:rows])


def two_parts(v):
    high = lax.reduce_precision(v, 8, 7)
    return jnp.concatenate([high.astype(BF), (v - high).astype(BF)], axis=0)


def one_part(v):
    rows = v.shape[0] // 2
    return v[:rows].astype(F32) + v[rows:].astype(F32)


def dot(left, right):
    return jnp.dot(left, right, preferred_element_type=F32)


def left_product(left, right):
    return lax.dot_general(left, right, (((0,), (0,)), ((), ())), preferred_element_type=F32)


def right_product(left, right):
    return lax.dot_general(left, right, (((1,), (1,)), ((), ())), preferred_element_type=F32)


ALL = 1024
UNITS = 704
LAST = 192
SHARD = 528


TAIL = [(256, 64, 256 * h, 64 * h, 0, 256) for h in range(2)]
TAIL += [(320, 32, 128 * h, 32 * h, 256, 128) for h in range(4)]


def tail_pieces(shard):
    for row, rows, column, at, start, width in TAIL:
        yield (
            shard.at[:, pl.ds(row, rows), pl.ds(column, width)],
            (slice(None), pl.ds(at, rows), pl.ds(start, width)),
        )


def tail_loads(full, tail, sems):
    return [
        pltpu.make_async_copy(src, tail.at[at], sems.at[i])
        for i, (src, at) in enumerate(tail_pieces(full))
    ]


def down_blocks(shard, down):
    return [
        (shard.at[4 * c + j, pl.ds(352, 176), :], down.at[c, pl.ds(176 * j, 176), :])
        for c in range(4)
        for j in range(4)
    ]


def mlp_kernel(
    four,
    core,
    cot_four,
    cot_core,
    panel_ref,
    full,
    ggu_ref,
    act_ref,
    send,
    down,
    tail,
    gpan,
    gtail,
    gdown,
    four_ref,
    core_ref,
    cot_four_ref,
    cot_core_ref,
    in_sem,
    row_sem,
    tail_sem,
    pan_sem,
    out_sem,
):
    step = pl.program_id(0)
    loads = [
        pltpu.make_async_copy(src, dst, in_sem.at[i])
        for i, (src, dst) in enumerate(
            [(cot_four, cot_four_ref), (cot_core, cot_core_ref)] + down_blocks(full, down)
        )
    ]
    rows_in = [
        pltpu.make_async_copy(src, dst, row_sem.at[i])
        for i, (src, dst) in enumerate([(four, four_ref), (core, core_ref)])
    ]
    tails = tail_loads(full, tail, tail_sem)

    @pl.when(step == 0)
    def _():
        for copy in rows_in + loads + tails:
            copy.start()
        for copy in rows_in + loads:
            copy.wait()

    def panel_out(at):
        return pltpu.make_async_copy(
            gpan.at[at], send.at[:, pl.ds(128 * at, 128), :], pan_sem.at[at]
        )

    def block(weights, start, width, store):
        halves_of = [dot(ref[...], weights) for ref in (four_ref, core_ref)]

        for half, (h, c_ref) in enumerate(zip(halves_of, (cot_four_ref, cot_core_ref))):
            rows = pl.ds(half * (ALL // 2), ALL // 2)
            gate, up = h[:, :width], h[:, width:]
            prod = right_product(c_ref[:, :PANEL], down[0, pl.ds(start, width), :])
            for c in range(1, 4):
                prod += right_product(
                    c_ref[:, c * PANEL : (c + 1) * PANEL], down[c, pl.ds(start, width), :]
                )
            sig = 1.0 / (1.0 + jnp.exp(-gate))
            silu = gate * sig
            act_ref[rows, :width] = (silu * up).astype(BF)
            ggu_ref[rows, :width] = (prod * up * sig * (1.0 + gate * (1.0 - sig))).astype(BF)
            ggu_ref[rows, width : 2 * width] = (prod * silu).astype(BF)
        for c in range(4):
            columns = slice(c * PANEL, (c + 1) * PANEL)
            grads = left_product(act_ref[: ALL // 2, :width], cot_four_ref[:, columns])
            grads += left_product(act_ref[ALL // 2 :, :width], cot_core_ref[:, columns])
            gdown[c, pl.ds(start, width), :] = grads.astype(BF)
        grads = left_product(four_ref[...], ggu_ref[: ALL // 2, : 2 * width])
        grads += left_product(core_ref[...], ggu_ref[ALL // 2 :, : 2 * width])
        store(grads.astype(BF))

    @pl.when(step < 2)
    def _():
        def store(grads):
            gpan[step] = grads.reshape(16, 128, PANEL)

        block(panel_ref[...].reshape(D, PANEL), pl.multiple_of(256 * step, 256), 256, store)
        panel_out(step).start()

    @pl.when(step == 2)
    def _():
        def store(grads):
            gtail[...] = grads.reshape(16, 128, 2 * LAST)

        for copy in tails:
            copy.wait()
        block(tail[...].reshape(D, 2 * LAST), 512, LAST, store)
        outs = [
            pltpu.make_async_copy(gtail.at[at], dst, tail_sem.at[i])
            for i, (dst, at) in enumerate(tail_pieces(send))
        ]
        outs += [
            pltpu.make_async_copy(src, dst, out_sem.at[i])
            for i, (dst, src) in enumerate(down_blocks(send, gdown))
        ]
        for copy in outs:
            copy.start()
        for copy in outs + [panel_out(0), panel_out(1)]:
            copy.wait()


def mlp_grads(four, core, cot_four, cot_core, full):
    return pl.pallas_call(
        mlp_kernel,
        grid=(3,),
        in_specs=[pl.BlockSpec(memory_space=pl.ANY)] * 4
        + [
            pl.BlockSpec((16, 128, PANEL), lambda i: (0, jnp.minimum(i, 1), 0)),
            pl.BlockSpec(memory_space=pl.ANY),
        ],
        out_specs=[
            pl.BlockSpec((ALL, 512), lambda i: (0, i)),
            pl.BlockSpec((ALL, 256), lambda i: (0, i)),
            pl.BlockSpec(memory_space=pl.ANY),
        ],
        out_shape=[
            jax.ShapeDtypeStruct((ALL, 1536), BF),
            jax.ShapeDtypeStruct((ALL, 768), BF),
            jax.ShapeDtypeStruct((16, SHARD, PANEL), BF),
        ],
        scratch_shapes=[
            pltpu.VMEM((4, UNITS, PANEL), BF),
            pltpu.VMEM((16, 128, 2 * LAST), BF),
            pltpu.VMEM((2, 16, 128, PANEL), BF),
            pltpu.VMEM((16, 128, 2 * LAST), BF),
            pltpu.VMEM((4, UNITS, PANEL), BF),
            pltpu.VMEM((ALL // 2, D), BF),
            pltpu.VMEM((ALL // 2, D), BF),
            pltpu.VMEM((ALL // 2, D), BF),
            pltpu.VMEM((ALL // 2, D), BF),
            pltpu.SemaphoreType.DMA((18,)),
            pltpu.SemaphoreType.DMA((2,)),
            pltpu.SemaphoreType.DMA((6,)),
            pltpu.SemaphoreType.DMA((2,)),
            pltpu.SemaphoreType.DMA((16,)),
        ],
        compiler_params=pltpu.CompilerParams(vmem_limit_bytes=56 * 2**20),
        cost_estimate=pl.CostEstimate(
            flops=18 * 10**9, bytes_accessed=45 * 10**6, transcendentals=10**6
        ),
        name="mlp_grads",
    )(four, core, cot_four, cot_core, full, full)


def split_rows(total, rest_ref, own_ref=None):
    if own_ref is None:
        rest_ref[...] = total.astype(BF)
    else:
        own_ref[...] = total[:ROWS]
        rest_ref[...] = total[ROWS : ALL // 2].astype(BF)


def second_kernel(g_ref, panel_ref, wide_ref, narrow_ref, *outs):
    *outs, tail = outs
    for row, rows, column, at, start, width in TAIL:
        piece = wide_ref if row == 256 else narrow_ref
        tail[:, at : at + rows, start : start + width] = piece[:, :, column : column + width]
    total = right_product(g_ref[:, :PANEL], panel_ref[:, :128].reshape(PANEL, PANEL))
    total += right_product(
        g_ref[:, PANEL : 2 * PANEL], panel_ref[:, 128:].reshape(PANEL, PANEL)
    )
    total += right_product(
        g_ref[:, 2 * PANEL : 2 * PANEL + 2 * LAST], tail[...].reshape(PANEL, 2 * LAST)
    )
    split_rows(total, *outs)


def second_grad(ggu, full, half):
    rows = [ALL // 2] if half else [ALL // 2 - ROWS, ROWS]
    return pl.pallas_call(
        second_kernel,
        grid=(4,),
        in_specs=[
            pl.BlockSpec((ALL // 2, 1536), lambda i: (half, 0)),
            pl.BlockSpec((4, 256, PANEL), lambda i: (i, 0, 0)),
            pl.BlockSpec((4, 64, PANEL), lambda i: (i, 4, 0)),
            pl.BlockSpec((4, 32, PANEL), lambda i: (i, 10, 0)),
        ],
        out_specs=[pl.BlockSpec((r, PANEL), lambda i: (0, i)) for r in rows],
        out_shape=[jax.ShapeDtypeStruct((r, D), kind) for r, kind in zip(rows, (BF, F32))],
        scratch_shapes=[pltpu.VMEM((4, 128, 2 * LAST), BF)],
        compiler_params=pltpu.CompilerParams(vmem_limit_bytes=58 * 2**20),
        cost_estimate=pl.CostEstimate(
            flops=3 * 10**9, bytes_accessed=10 * 10**6, transcendentals=0
        ),
        name="second_grad",
    )(ggu, full, full, full)


def down_kernel(act_ref, down_ref, core_ref, rest_ref, own_ref):
    part = dot(act_ref[:, :UNITS], down_ref[...].reshape(UNITS, PANEL))
    split_rows(part, rest_ref, own_ref)
    core_ref[...] = part[ALL // 2 :].astype(BF)


def down_product(active, full):
    rows = [ALL // 2, ALL // 2 - ROWS, ROWS]
    return pl.pallas_call(
        down_kernel,
        grid=(4,),
        in_specs=[
            pl.BlockSpec((ALL, 768), lambda c: (0, 0)),
            pl.BlockSpec((4, 176, PANEL), lambda c: (c, 2, 0)),
        ],
        out_specs=[pl.BlockSpec((r, PANEL), lambda c: (0, c)) for r in rows],
        out_shape=[jax.ShapeDtypeStruct((r, D), kind) for r, kind in zip(rows, (BF, BF, F32))],
        compiler_params=pltpu.CompilerParams(vmem_limit_bytes=58 * 2**20),
        cost_estimate=pl.CostEstimate(
            flops=3 * 10**9, bytes_accessed=12 * 10**6, transcendentals=0
        ),
        name="down_product",
    )(active, full)


LANES = 128


def lanes_of(v):
    return lax.broadcasted_iota(jnp.int32, v.shape, v.ndim - 1)


def quarter_turn(v):
    first = lanes_of(v) % HEAD_DIM < HEAD_DIM // 2
    return jnp.where(first, -pltpu.roll(v, 96, 1), pltpu.roll(v, 32, 1))


def doubled(v):
    left = lanes_of(v) < HEAD_DIM
    other = pltpu.roll(v, HEAD_DIM, 1)
    return jnp.where(left, v, other), jnp.where(left, other, v)


def head_rows(ref):
    blocks = []
    for g in range(GROUPS // 2):
        v = ref[:, g * LANES : (g + 1) * LANES].astype(F32)
        left = lanes_of(v) < HEAD_DIM
        blocks += [jnp.where(left, v, 0.0), jnp.where(left, 0.0, v)]
    return jnp.concatenate(blocks, axis=0).astype(BF)


def pair_columns(v, g):
    even = v[2 * g * ROWS : (2 * g + 1) * ROWS]
    odd = v[(2 * g + 1) * ROWS : (2 * g + 2) * ROWS]
    return jnp.where(lanes_of(even) < HEAD_DIM, even, odd)


def softmax_rows(heads, key2, mask):
    scores = right_product(heads, key2).reshape(GROUPS, ROWS, ROWS) * score_scale
    masked = jnp.where(mask[None] > 0.0, scores, -1e30)
    top = jnp.max(masked, axis=-1, keepdims=True)
    total = top + jnp.log(jnp.sum(jnp.exp(masked - top), axis=-1, keepdims=True))
    return jnp.exp(masked - total).reshape(GROUPS * ROWS, ROWS)


def seq_rows(step):
    return pl.ds(pl.multiple_of(jnp.minimum(step, MEMBERS - 1) * ROWS, ROWS), ROWS)


def attention_kernel(
    first_ref,
    weight_ref,
    cos_ref,
    sin_ref,
    mask_ref,
    query_ref,
    kv_ref,
    att_ref,
    near_ref,
    core_ref,
    qkv,
    att,
):
    step = pl.program_id(0)

    @pl.when(step == 0)
    def _():
        qkv[...] = dot(first_ref[...], weight_ref[:, QW:])

    @pl.when(step < MEMBERS)
    def _():
        rows = seq_rows(step)
        cosine, sine = cos_ref[...], sin_ref[...]
        for g in range(GROUPS // 2):
            v = qkv[rows, g * LANES : (g + 1) * LANES]
            query_ref[:, g * LANES : (g + 1) * LANES] = (
                v * cosine + quarter_turn(v) * sine
            ).astype(BF)
        v = qkv[rows, QW:]
        kv = jnp.where(lanes_of(v) < HEAD_DIM, v * cosine + quarter_turn(v) * sine, v)
        kv_ref[...] = kv.astype(BF)
        key2, value2 = doubled(kv)
        probs = softmax_rows(head_rows(query_ref), key2.astype(BF), mask_ref[0])
        heads = dot(probs.astype(BF), value2.astype(BF))
        for g in range(GROUPS // 2):
            pair = pair_columns(heads, g).astype(BF)
            att_ref[:, g * LANES : (g + 1) * LANES] = pair
            att[rows, g * LANES : (g + 1) * LANES] = pair

    @pl.when(step >= MEMBERS)
    def _():
        block = pl.ds(pl.multiple_of((step - MEMBERS) * QW, QW), QW)
        part = dot(att[...], weight_ref[block, :QW])
        near_ref[...] = part[: SLOTS // 2]
        core_ref[...] = part[SLOTS // 2 :].astype(BF)


def attention_back_kernel(
    middle_ref,
    weight_ref,
    first_ref,
    att_ref,
    query_ref,
    kv_ref,
    cos_ref,
    sin_ref,
    mask_ref,
    grad_ref,
    send_ref,
    upstream,
    grads,
):
    step = pl.program_id(0)

    @pl.when(step == 0)
    def _():
        total = right_product(middle_ref[:, :PANEL], weight_ref[:QW, :QW])
        for c in range(1, 4):
            total += right_product(
                middle_ref[:, c * PANEL : (c + 1) * PANEL],
                weight_ref[c * QW : (c + 1) * QW, :QW],
            )
        upstream[...] = total.astype(BF)

    @pl.when(step < MEMBERS)
    def _():
        rows = seq_rows(step)
        cosine, sine = cos_ref[...], sin_ref[...]
        key2, value2 = doubled(kv_ref[...].astype(F32))
        key2, value2 = key2.astype(BF), value2.astype(BF)
        heads, lifted = head_rows(query_ref), head_rows(upstream.at[rows])
        probs = softmax_rows(heads, key2, mask_ref[0])
        grad_value = left_product(probs.astype(BF), lifted)
        grad_value = grad_value + pltpu.roll(grad_value, HEAD_DIM, 1)
        grad_probs = right_product(lifted, value2)
        inner = jnp.sum(grad_probs * probs, axis=-1, keepdims=True)
        grad_scores = (probs * (grad_probs - inner)).astype(BF)
        grad_query = dot(grad_scores, key2)
        for g in range(GROUPS // 2):
            v = pair_columns(grad_query, g) * score_scale
            v = (v * cosine - quarter_turn(v) * sine).astype(BF)
            grad_ref[:, g * LANES : (g + 1) * LANES] = v
            grads[rows, g * LANES : (g + 1) * LANES] = v
        grad_key = left_product(grad_scores, heads)
        v = (grad_key + pltpu.roll(grad_key, HEAD_DIM, 1)) * score_scale
        grad_key = v * cosine - quarter_turn(v) * sine
        v = jnp.where(lanes_of(v) < HEAD_DIM, grad_key, grad_value).astype(BF)
        grad_ref[:, QW:] = v
        grads[rows, QW:] = v

    @pl.when(step >= MEMBERS)
    def _():
        block = pl.ds(pl.multiple_of((step - MEMBERS) * PANEL, PANEL), PANEL)
        send_ref[:, :QW] = left_product(att_ref[...], middle_ref[:, block]).astype(BF)
        send_ref[:, QW:] = left_product(first_ref[:, block], grads[...]).astype(BF)


def all_of(shape):
    return pl.BlockSpec(shape, lambda s: (0,) * len(shape), pipeline_mode=pl.Buffered(1))


def by_seq(width):
    return pl.BlockSpec((ROWS, width), lambda s: (jnp.minimum(s, MEMBERS - 1), 0))


MASK_BLOCK = pl.BlockSpec((1, ROWS, ROWS), lambda s: (jnp.minimum(s, MEMBERS - 1), 0, 0))


def attention(first_low, weights, cosine, sine, mask):
    half = pl.BlockSpec((SLOTS // 2, PANEL), lambda s: (0, jnp.maximum(s - MEMBERS, 0)))
    return pl.pallas_call(
        attention_kernel,
        grid=(2 * MEMBERS,),
        in_specs=[
            all_of((SLOTS, D)),
            all_of((D, QW + QKVW)),
            by_seq(LANES),
            by_seq(LANES),
            MASK_BLOCK,
        ],
        out_specs=[by_seq(QW), by_seq(LANES), by_seq(QW), half, half],
        out_shape=[
            jax.ShapeDtypeStruct((SLOTS, QW), BF),
            jax.ShapeDtypeStruct((SLOTS, LANES), BF),
            jax.ShapeDtypeStruct((SLOTS, QW), BF),
            jax.ShapeDtypeStruct((SLOTS // 2, D), F32),
            jax.ShapeDtypeStruct((SLOTS // 2, D), BF),
        ],
        scratch_shapes=[pltpu.VMEM((SLOTS, QKVW), F32), pltpu.VMEM((SLOTS, QW), BF)],
        compiler_params=pltpu.CompilerParams(vmem_limit_bytes=40 * 2**20),
        cost_estimate=pl.CostEstimate(
            flops=3 * 10**9, bytes_accessed=12 * 10**6, transcendentals=10**6
        ),
        name="attention",
    )(first_low, weights, cosine, sine, mask)


def attention_back(middle_all, weights, first_low, attended, query, kv, cosine, sine, mask):
    return pl.pallas_call(
        attention_back_kernel,
        grid=(2 * MEMBERS,),
        in_specs=[
            all_of((SLOTS, D)),
            all_of((D, QW + QKVW)),
            all_of((SLOTS, D)),
            all_of((SLOTS, QW)),
            by_seq(QW),
            by_seq(LANES),
            by_seq(LANES),
            by_seq(LANES),
            MASK_BLOCK,
        ],
        out_specs=[
            by_seq(QKVW),
            pl.BlockSpec((PANEL, QW + QKVW), lambda s: (jnp.maximum(s - MEMBERS, 0), 0)),
        ],
        out_shape=[
            jax.ShapeDtypeStruct((SLOTS, QKVW), BF),
            jax.ShapeDtypeStruct((D, QW + QKVW), BF),
        ],
        scratch_shapes=[pltpu.VMEM((SLOTS, QW), BF), pltpu.VMEM((SLOTS, QKVW), BF)],
        compiler_params=pltpu.CompilerParams(vmem_limit_bytes=40 * 2**20),
        cost_estimate=pl.CostEstimate(
            flops=5 * 10**9, bytes_accessed=16 * 10**6, transcendentals=10**6
        ),
        name="attention_back",
    )(middle_all, weights, first_low, attended, query, kv, cosine, sine, mask)


def first_kernel(grad_ref, weight_ref, rows_ref, rms_ref, near_ref, core_ref, gain_ref):
    grad = right_product(grad_ref[...], weight_ref[:, QW:])
    normed = rows_ref[...].astype(F32) * rms_ref[...]
    gain_ref[...] = jnp.sum(grad * normed, axis=0, keepdims=True)
    near_ref[...] = grad[: SLOTS // 2]
    core_ref[...] = grad[SLOTS // 2 :].astype(BF)


def first_grad(grad_qkv, weights, rows_in, rms):
    half = pl.BlockSpec((SLOTS // 2, PANEL), lambda i: (0, i))
    return pl.pallas_call(
        first_kernel,
        grid=(4,),
        in_specs=[
            all_of((SLOTS, QKVW)),
            pl.BlockSpec((PANEL, QW + QKVW), lambda i: (i, 0)),
            pl.BlockSpec((SLOTS, PANEL), lambda i: (0, i)),
            all_of((SLOTS, 1)),
        ],
        out_specs=[half, half, pl.BlockSpec((1, PANEL), lambda i: (0, i))],
        out_shape=[
            jax.ShapeDtypeStruct((SLOTS // 2, D), F32),
            jax.ShapeDtypeStruct((SLOTS // 2, D), BF),
            jax.ShapeDtypeStruct((1, D), F32),
        ],
        compiler_params=pltpu.CompilerParams(vmem_limit_bytes=32 * 2**20),
        cost_estimate=pl.CostEstimate(
            flops=14 * 10**8, bytes_accessed=12 * 10**6, transcendentals=0
        ),
        name="first_grad",
    )(grad_qkv, weights, rows_in, rms)


def update_kernel(
    at_ref,
    own_ref,
    near_ref,
    core_ref,
    moments_ref,
    moment_ref,
    query_ref,
    key_ref,
    value_ref,
    output_ref,
    query_moved,
    key_moved,
    value_moved,
    output_moved,
    query_new,
    key_new,
    value_new,
    output_new,
    moved,
):
    width = QKVW + PANEL
    own = 0.5 * moment_ref[...] + 0.5 * own_ref[...]
    query_moved[...] = own[:, :QW]
    key_moved[...] = own[:, QW : QW + KW]
    value_moved[...] = own[:, QW + KW : QKVW]
    output_moved[...] = own[:, QKVW:]
    rows = near_ref.shape[0]
    moved[:rows] = 0.5 * moments_ref[:rows].astype(F32) + 0.5 * near_ref[...].astype(F32)
    moved[rows:] = 0.5 * moments_ref[rows:].astype(F32) + 0.5 * core_ref[:, :width].astype(F32)
    pairs = []
    for a, order in enumerate((0, 2, 1, 3)):
        slot = pl.ds(pl.multiple_of((at_ref[0] ^ order) * W_ROWS, W_ROWS), W_ROWS)
        columns = slice(a * QW, (a + 1) * QW)
        query_new[:, columns] = query_ref[:, columns] - learn_rate * moved[slot, :QW]
        output_new[:, columns] = output_ref[:, columns] - learn_rate * moved[slot, QKVW:]
        pairs.append(moved[slot, QW:QKVW])
    for a in (0, 2):
        even, odd = pairs[a], pairs[a + 1]
        left = lanes_of(even) < HEAD_DIM
        key = jnp.where(left, even, pltpu.roll(odd, HEAD_DIM, 1))
        value = jnp.where(left, pltpu.roll(even, HEAD_DIM, 1), odd)
        columns = slice(a * KW, (a + 2) * KW)
        key_new[:, columns] = key_ref[:, columns] - learn_rate * key
        value_new[:, columns] = value_ref[:, columns] - learn_rate * value


def attention_update(at, own, near, core, moments, moment, weights):
    shapes = [(W_ROWS, w) for w in (QW, KW, KW, QW)] + [w.shape for w in weights]
    vmem = pl.BlockSpec(memory_space=pltpu.VMEM)
    return pl.pallas_call(
        update_kernel,
        in_specs=[pl.BlockSpec(memory_space=pltpu.SMEM)] + [vmem] * 9,
        out_specs=[vmem] * 8,
        out_shape=[jax.ShapeDtypeStruct(shape, F32) for shape in shapes],
        scratch_shapes=[pltpu.VMEM((MEMBERS * W_ROWS, QKVW + PANEL), F32)],
        compiler_params=pltpu.CompilerParams(vmem_limit_bytes=16 * 2**20),
        cost_estimate=pl.CostEstimate(
            flops=10**6, bytes_accessed=6 * 10**6, transcendentals=0
        ),
        name="attention_update",
    )(at, own, near, core, moments, moment, *weights)


def rounded_gain(gain):
    return lax.optimization_barrier(gain.astype(BF)).astype(F32)


def inverse_rms(v):
    return lax.rsqrt(jnp.mean(v * v, axis=-1, keepdims=True) + epsilon)


def norm_back(v, gain, grad):
    r = inverse_rms(v)
    n = v * r
    scaled = grad * gain
    return r * (scaled - n * jnp.mean(scaled * n, axis=-1, keepdims=True)), n


def panels(gate, up):
    blocks = []
    for at in range(0, UNITS, 256):
        blocks += [gate[:, at : at + 256], up[:, at : at + 256]]
    return jnp.concatenate(blocks, axis=1)


def unpanels(v):
    gate = [v[:, :256], v[:, 512:768], v[:, 1024 : 1024 + LAST]]
    up = [v[:, 256:512], v[:, 768:1024], v[:, 1024 + LAST :]]
    return jnp.concatenate(gate, axis=1), jnp.concatenate(up, axis=1)


def on_device(
    tokens,
    cotangent,
    segment_ids,
    positions,
    padding,
    attn_gain,
    query_weight,
    key_weight,
    value_weight,
    output_weight,
    mlp_gain,
    gate_weight,
    up_weight,
    down_weight,
    attn_moment,
    query_moment,
    key_moment,
    value_moment,
    output_moment,
    mlp_moment,
    gate_moment,
    up_moment,
    down_moment,
):
    member = lax.axis_index("grp")
    place = lax.axis_index("dp")
    z, y, low = place // 8, (place // 2) % 4, (place % 2) == 0

    def mine(weight, width):
        return lax.dynamic_slice_in_dim(weight, member * width, width, 1).astype(BF)

    attn_shard = jnp.concatenate(
        [mine(query_weight, QW), mine(key_weight, KW), mine(value_weight, KW)], axis=1
    )
    attn_shard = jnp.concatenate(
        [turn_pair(mine(output_weight, QW), low), pair_x(attn_shard, low)], axis=1
    )
    attn_full = plane_gather(attn_shard)

    gate_mine, up_mine = mine(gate_weight, FW), mine(up_weight, FW)
    first = panels(gate_mine[:, :UNITS], up_mine[:, :UNITS])
    second = panels(gate_mine[:, UNITS:], up_mine[:, UNITS:])
    kept, given = jnp.where(low, first, second), jnp.where(low, second, first)
    gu_shard = in_order(kept, swap_x(given), low)
    tail = gu_shard[:, 2 * PANEL :]
    pieces = [
        gu_shard[:, :PANEL],
        gu_shard[:, PANEL : 2 * PANEL],
        jnp.concatenate([tail[:W_ROWS, :256], tail[W_ROWS:, :256]], axis=1),
        jnp.concatenate([tail[32 * h : 32 * h + 32, 256:] for h in range(4)], axis=1),
        everywhere(mine(down_weight, PANEL), OWNED),
    ]
    mlp_full = plane_gather(jnp.concatenate(pieces, axis=0)).reshape(16, SHARD, PANEL)

    places = jnp.stack([segment_ids, positions, padding])[None]
    rows_in = group_gather(tokens)
    own_moment = jnp.concatenate(
        [query_moment, key_moment, value_moment, output_moment], axis=1
    )
    moments = own_moment.astype(BF)
    places, moments, upstream = lax.optimization_barrier(
        (
            jnp.concatenate([places, swap_far(places)], axis=0),
            jnp.concatenate([moments, swap_far(moments)], axis=0),
            cotangent,
        )
    )
    cot_four, cot_core = row_gather(upstream)
    places = jnp.concatenate([places, swap_core(places)], axis=0)
    moments = jnp.concatenate([moments, swap_core(moments)], axis=0)
    segments, spots, pads = places[:, 0], places[:, 1], places[:, 2]

    first_gain = rounded_gain(attn_gain)
    second_gain = rounded_gain(mlp_gain)
    inputs = rows_in.astype(F32)
    rms = inverse_rms(inputs)
    first_low = (inputs * rms * first_gain).astype(BF)

    half = HEAD_DIM // 2
    freq = 10000.0 ** (-(jnp.arange(half, dtype=F32) * 2.0 / HEAD_DIM))
    angles = spots.reshape(SLOTS, 1).astype(F32) * jnp.tile(freq, LANES // half)[None]
    cosine, sine = jnp.cos(angles), jnp.sin(angles)
    column = jnp.arange(ROWS, dtype=jnp.int32)
    allowed = jnp.logical_and(
        jnp.logical_and(
            segments[:, :, None] == segments[:, None, :],
            (column[None, :] <= column[:, None])[None],
        ),
        jnp.logical_or(pads[:, None, :] == 1, (column[None, :] == column[:, None])[None]),
    ).astype(F32)

    attn_full, first_low, cosine, sine, allowed, cot_four, moments = lax.optimization_barrier(
        (attn_full, first_low, cosine, sine, allowed, cot_four, moments)
    )
    query_rot, kv, attended, near, core = attention(first_low, attn_full, cosine, sine, allowed)
    middle = tokens.astype(F32) + group_scatter_far(near + swap_core(core).astype(F32))
    second_low = (middle * inverse_rms(middle) * second_gain).astype(BF)
    four, core_four = row_gather(second_low)
    core_four, cot_core = lax.optimization_barrier((core_four, cot_core))
    grad_gu, active, send = mlp_grads(four, core_four, cot_four, cot_core, mlp_full)
    mlp_sum = plane_scatter(send.reshape(16 * SHARD, PANEL))

    second_core = swap_core(second_grad(grad_gu, mlp_full, 1)[0])
    second_rest, second_own = second_grad(grad_gu, mlp_full, 0)
    grad_second = row_scatter(second_own, second_rest, second_core)
    back, n_second = norm_back(middle, second_gain, grad_second)
    mlp_gain_part = jnp.sum(grad_second * n_second, axis=0)
    grad_middle = cotangent.astype(F32) + back
    middle_all = group_gather(grad_middle.astype(BF))
    down_core, down_rest, down_own = down_product(active, mlp_full)
    middle_all, down_core = lax.optimization_barrier((middle_all, swap_core(down_core)))
    grad_qkv, attn_send = attention_back(
        middle_all, attn_full, first_low, attended, query_rot, kv, cosine, sine, allowed
    )
    attn_sum = plane_scatter(attn_send)

    grad_qkv, mlp_sum, down_core = lax.optimization_barrier((grad_qkv, mlp_sum, down_core))
    block_output = (middle + row_scatter(down_own, down_rest, down_core)).astype(BF)
    near, core, attn_gain_part = first_grad(grad_qkv, attn_full, rows_in, rms)
    gains = jnp.concatenate([attn_gain_part, mlp_gain_part[None]], axis=0).reshape(32, LANES)
    for pairs in (RING_Z, RING_Y):
        gains = gains + sum(lax.ppermute(gains, "dp", p) for p in pairs)
    near = near + swap_core(core).astype(F32)
    back, _ = norm_back(tokens.astype(F32), first_gain, group_scatter_far(near))
    input_grad = grad_middle + back

    mine_at = (member // 2) + 2 * (member % 2)

    def by_member(slots):
        return [
            lax.dynamic_index_in_dim(slots, mine_at ^ at, 0, keepdims=False) for at in (0, 2, 1, 3)
        ]

    def updated(weight, columns, start, size):
        moved = jnp.concatenate([block[:, start : start + size] for block in columns], axis=1)
        return weight - learn_rate * moved.astype(F32)

    wide, narrow = mlp_sum[256:320], mlp_sum[320:352]
    gu_part = jnp.concatenate(
        [
            mlp_sum[:128],
            mlp_sum[128:256],
            jnp.concatenate([wide[:, :256], wide[:, 256:]], axis=0),
            jnp.concatenate([narrow[:, h * LANES : (h + 1) * LANES] for h in range(4)], axis=0),
        ],
        axis=1,
    )
    kept, given = halves(gu_part, low)
    other = swap_x(given)
    first = unpanels(jnp.where(low, kept, other))
    second = unpanels(jnp.where(low, other, kept))
    gate_rows = jnp.concatenate([first[0], second[0]], axis=1).astype(F32)
    up_rows = jnp.concatenate([first[1], second[1]], axis=1).astype(F32)
    down_rows = everywhere(mlp_sum[352:], RETURN).astype(F32)
    gate_momentum = 0.5 * gate_moment + 0.5 * gate_rows
    up_momentum = 0.5 * up_moment + 0.5 * up_rows
    down_momentum = 0.5 * down_moment + 0.5 * down_rows
    gu_moved = jnp.concatenate([gate_momentum, up_momentum], axis=1).astype(BF)
    gu_moved, block_output = lax.optimization_barrier((gu_moved, block_output))
    gu_moved = by_member(group_gather(gu_moved).reshape(MEMBERS, W_ROWS, GUW))
    down_moved = by_member(
        group_gather(down_momentum.astype(BF)).reshape(MEMBERS, DOWN_ROWS, PANEL)
    )

    mlp_done = (
        gate_momentum,
        up_momentum,
        down_momentum,
        updated(gate_weight, gu_moved, 0, FW),
        updated(up_weight, gu_moved, FW, FW),
        updated(down_weight, down_moved, 0, PANEL),
    )
    attn_sum, gains, input_grad, block_output, mlp_done = lax.optimization_barrier(
        (attn_sum, gains, input_grad, block_output, mlp_done)
    )
    gate_momentum, up_momentum, down_momentum, gate_updated, up_updated, down_updated = mlp_done

    turned = everywhere(attn_sum[:, :QW], TURN)
    both = jnp.concatenate([attn_sum[:, QW:], turned], axis=1)
    gains = two_parts(gains)
    kept, given = halves(both, low)
    width = QKVW + PANEL
    near = swap_x(jnp.concatenate([given, gains], axis=1))
    far = swap_far(jnp.concatenate([kept, gains], axis=1))
    both_far = far_x(jnp.concatenate([given, gains], axis=1))
    own_total = kept.astype(F32) + near[:, :width].astype(F32)
    far_total = far[:, :width].astype(F32) + both_far[:, :width].astype(F32)
    gains = sum(one_part(part) for part in (gains, near[:, width:], far[:, width:], both_far[:, width:]))
    totals = jnp.concatenate([own_total, far_total], axis=0).astype(BF)
    rider = jnp.concatenate([two_parts(gains), jnp.zeros((W_ROWS, LANES), BF)], axis=0)
    other = swap_core(jnp.concatenate([totals, rider], axis=1))
    gains = gains + one_part(other[:W_ROWS, width:])
    attn_done = attention_update(
        mine_at.astype(jnp.int32).reshape(1),
        own_total,
        totals,
        other,
        moments,
        own_moment,
        (query_weight, key_weight, value_weight, output_weight),
    )

    gains = 0.5 * jnp.stack([attn_moment, mlp_moment]) + 0.5 * gains.reshape(2, D)
    return (
        block_output,
        input_grad,
        gains[0],
        *attn_done[:4],
        gains[1],
        gate_momentum,
        up_momentum,
        down_momentum,
        attn_gain - learn_rate * gains[0],
        *attn_done[4:],
        mlp_gain - learn_rate * gains[1],
        gate_updated,
        up_updated,
        down_updated,
    )


def solution(mesh):
    rows = P(("grp", "dp"), None)
    flat = P(("grp", "dp"))
    weight = P("dp", None)
    moment = P("dp", "grp")
    everyone = P()
    weights = (everyone,) + (weight,) * 4 + (everyone,) + (weight,) * 3
    moments = (everyone,) + (moment,) * 4 + (everyone,) + (moment,) * 3
    return jax.shard_map(
        on_device,
        mesh=mesh,
        in_specs=(rows, rows, flat, flat, flat) + weights + moments,
        out_specs=(rows, rows) + moments + weights,
        check_vma=False,
    )
```

```python
import jax
import jax.numpy as jnp
from jax import lax
from jax.experimental import pallas as pl
from jax.experimental.pallas import tpu as pltpu
from jax.sharding import PartitionSpec as P

D = 2048
HEAD_DIM = 64
GROUPS = 8
ROWS = 128
MEMBERS = 4
SLOTS = ROWS * MEMBERS
QW = 512
KW = 64
QKVW = QW + 2 * KW
FW = 1408
GUW = 2 * FW
PANEL = 512
DOWN_ROWS = 176
W_ROWS = 64

epsilon = 1e-05
learn_rate = 0.005
score_scale = 0.125

BF = jnp.bfloat16
F32 = jnp.float32

PLANES = [[z * 8 + y * 2 + x for z in range(4) for y in range(4)] for x in range(2)]
SWAP_X = [(i, i ^ 1) for i in range(32)]
SWAP_CORE = [(m, m ^ 1) for m in range(4)]
SWAP_FAR = [(m, m ^ 2) for m in range(4)]
SWAP_FAR_X = [(m * 32 + i, (m ^ 2) * 32 + (i ^ 1)) for m in range(4) for i in range(32)]
MZQ = [(m, z, q) for m in range(4) for z in range(4) for q in range(8)]


def spot(m, z, q):
    return m * 32 + z * 8 + q


TURN = [(spot(m, z, q), spot(z, m, q)) for m, z, q in MZQ]
TURN_X = [(spot(m, z, q), spot(z, m, q ^ 1)) for m, z, q in MZQ]
TURN_IN = [[(spot(m, z, q), spot((z + k) % 4, m, q)) for m, z, q in MZQ] for k in range(4)]
OWNED = [(spot(m, z, q), spot(z, m, (q & 3) * 2 + (q >> 2))) for m, z, q in MZQ]
RETURN = [(b, a) for a, b in OWNED]


def ring(place, k):
    return [(i, i + ((i // place + k) % 4 - i // place % 4) * place) for i in range(32)]


RING_Z = [ring(8, k) for k in (1, 2, 3)]
RING_Y = [ring(2, k) for k in (1, 2, 3)]


def swap_x(v):
    return lax.ppermute(v, "dp", SWAP_X)


def swap_core(v):
    return lax.ppermute(v, "grp", SWAP_CORE)


def swap_far(v):
    return lax.ppermute(v, "grp", SWAP_FAR)


def everywhere(v, pairs):
    return lax.ppermute(v, ("grp", "dp"), pairs)


def plane_gather(v):
    return lax.all_gather(v, "dp", axis=0, tiled=True, axis_index_groups=PLANES)


def plane_scatter(v):
    return lax.psum_scatter(
        v, "dp", scatter_dimension=0, tiled=True, axis_index_groups=PLANES
    )


def ring_scatter(v, pairs, at, extra=None):
    rows = v.shape[0] // 4

    def chunk(k):
        part = lax.dynamic_slice_in_dim(v, lax.rem(at + k, 4) * rows, rows, 0)
        return part if extra is None else jnp.concatenate([part, extra], axis=1)

    total = chunk(0).astype(F32)
    for k, p in enumerate(pairs):
        total = total + lax.ppermute(chunk(k + 1), "dp", p).astype(F32)
    return total


def group_gather(v):
    pair = jnp.concatenate([v, swap_far(v)], axis=0)
    return jnp.concatenate([pair, swap_core(pair)], axis=0)


def far_parts(near):
    return near[:ROWS], swap_far(near[ROWS:].astype(BF))


def far_x(v):
    return everywhere(v, SWAP_FAR_X)


def row_gather(v):
    four = jnp.concatenate([v, swap_x(v), swap_far(v), far_x(v)], axis=0)
    return four, swap_core(four)


def row_parts(own, rest, core):
    own = own + core[:ROWS].astype(F32)
    rest = (rest.astype(F32) + core[ROWS:].astype(F32)).astype(BF)
    low_part, far_part, far_x_part = (rest[k * ROWS : (k + 1) * ROWS] for k in range(3))
    return own, swap_x(low_part), swap_far(far_part), far_x(far_x_part)


def added(parts):
    own, *others = parts
    return sum((part.astype(F32) for part in others), own)


def in_order(own, other, low):
    return jnp.concatenate([jnp.where(low, own, other), jnp.where(low, other, own)], axis=0)


def pair_x(v, low):
    return in_order(v, swap_x(v), low)


def turn_pair(v, low):
    return in_order(everywhere(v, TURN), everywhere(v, TURN_X), low)


def halves(v, low):
    rows = v.shape[0] // 2
    return jnp.where(low, v[:rows], v[rows:]), jnp.where(low, v[rows:], v[:rows])


def two_parts(v):
    high = lax.reduce_precision(v, 8, 7)
    return jnp.concatenate([high.astype(BF), (v - high).astype(BF)], axis=0)


def one_part(v):
    rows = v.shape[0] // 2
    return v[:rows].astype(F32) + v[rows:].astype(F32)


def dot(left, right):
    return jnp.dot(left, right, preferred_element_type=F32)


def left_product(left, right):
    return lax.dot_general(left, right, (((0,), (0,)), ((), ())), preferred_element_type=F32)


def right_product(left, right):
    return lax.dot_general(left, right, (((1,), (1,)), ((), ())), preferred_element_type=F32)


ALL = 1024
UNITS = 704
LAST = 192
SHARD = 528


TAIL = [(256, 64, 256 * h, 64 * h, 0, 256) for h in range(2)]
TAIL += [(320, 32, 128 * h, 32 * h, 256, 128) for h in range(4)]


def tail_pieces(shard):
    for row, rows, column, at, start, width in TAIL:
        yield (
            shard.at[:, pl.ds(row, rows), pl.ds(column, width)],
            (slice(None), pl.ds(at, rows), pl.ds(start, width)),
        )


def tail_loads(full, tail, sems):
    return [
        pltpu.make_async_copy(src, tail.at[at], sems.at[i])
        for i, (src, at) in enumerate(tail_pieces(full))
    ]


def down_blocks(shard, down):
    return [
        (shard.at[4 * c + j, pl.ds(352, 176), :], down.at[c, pl.ds(176 * j, 176), :])
        for c in range(4)
        for j in range(4)
    ]


def mlp_kernel(
    four,
    core,
    cot_four,
    cot_core,
    panel_ref,
    full,
    ggu_ref,
    act_ref,
    send,
    down,
    tail,
    gpan,
    gtail,
    gdown,
    four_ref,
    core_ref,
    cot_four_ref,
    cot_core_ref,
    in_sem,
    row_sem,
    tail_sem,
    pan_sem,
    out_sem,
):
    step = pl.program_id(0)
    loads = [
        pltpu.make_async_copy(src, dst, in_sem.at[i])
        for i, (src, dst) in enumerate(
            [(cot_four, cot_four_ref), (cot_core, cot_core_ref)] + down_blocks(full, down)
        )
    ]
    rows_in = [
        pltpu.make_async_copy(src, dst, row_sem.at[i])
        for i, (src, dst) in enumerate([(four, four_ref), (core, core_ref)])
    ]
    tails = tail_loads(full, tail, tail_sem)

    @pl.when(step == 0)
    def _():
        for copy in rows_in + loads + tails:
            copy.start()
        for copy in rows_in + loads:
            copy.wait()

    def panel_out(at):
        return pltpu.make_async_copy(
            gpan.at[at], send.at[:, pl.ds(128 * at, 128), :], pan_sem.at[at]
        )

    def block(weights, start, width, store):
        halves_of = [dot(ref[...], weights) for ref in (four_ref, core_ref)]

        for half, (h, c_ref) in enumerate(zip(halves_of, (cot_four_ref, cot_core_ref))):
            rows = pl.ds(half * (ALL // 2), ALL // 2)
            gate, up = h[:, :width], h[:, width:]
            prod = right_product(c_ref[:, :PANEL], down[0, pl.ds(start, width), :])
            for c in range(1, 4):
                prod += right_product(
                    c_ref[:, c * PANEL : (c + 1) * PANEL], down[c, pl.ds(start, width), :]
                )
            sig = 1.0 / (1.0 + jnp.exp(-gate))
            silu = gate * sig
            act_ref[rows, :width] = (silu * up).astype(BF)
            ggu_ref[rows, :width] = (prod * up * sig * (1.0 + gate * (1.0 - sig))).astype(BF)
            ggu_ref[rows, width : 2 * width] = (prod * silu).astype(BF)
        for c in range(4):
            columns = slice(c * PANEL, (c + 1) * PANEL)
            grads = left_product(act_ref[: ALL // 2, :width], cot_four_ref[:, columns])
            grads += left_product(act_ref[ALL // 2 :, :width], cot_core_ref[:, columns])
            gdown[c, pl.ds(start, width), :] = grads.astype(BF)
        grads = left_product(four_ref[...], ggu_ref[: ALL // 2, : 2 * width])
        grads += left_product(core_ref[...], ggu_ref[ALL // 2 :, : 2 * width])
        store(grads.astype(BF))

    @pl.when(step < 2)
    def _():
        def store(grads):
            gpan[step] = grads.reshape(16, 128, PANEL)

        block(panel_ref[...].reshape(D, PANEL), pl.multiple_of(256 * step, 256), 256, store)
        panel_out(step).start()

    @pl.when(step == 2)
    def _():
        def store(grads):
            gtail[...] = grads.reshape(16, 128, 2 * LAST)

        for copy in tails:
            copy.wait()
        block(tail[...].reshape(D, 2 * LAST), 512, LAST, store)
        outs = [
            pltpu.make_async_copy(gtail.at[at], dst, tail_sem.at[i])
            for i, (dst, at) in enumerate(tail_pieces(send))
        ]
        outs += [
            pltpu.make_async_copy(src, dst, out_sem.at[i])
            for i, (dst, src) in enumerate(down_blocks(send, gdown))
        ]
        for copy in outs:
            copy.start()
        for copy in outs + [panel_out(0), panel_out(1)]:
            copy.wait()


def mlp_grads(four, core, cot_four, cot_core, full):
    return pl.pallas_call(
        mlp_kernel,
        grid=(3,),
        in_specs=[pl.BlockSpec(memory_space=pl.ANY)] * 4
        + [
            pl.BlockSpec((16, 128, PANEL), lambda i: (0, jnp.minimum(i, 1), 0)),
            pl.BlockSpec(memory_space=pl.ANY),
        ],
        out_specs=[
            pl.BlockSpec((ALL, 512), lambda i: (0, i)),
            pl.BlockSpec((ALL, 256), lambda i: (0, i)),
            pl.BlockSpec(memory_space=pl.ANY),
        ],
        out_shape=[
            jax.ShapeDtypeStruct((ALL, 1536), BF),
            jax.ShapeDtypeStruct((ALL, 768), BF),
            jax.ShapeDtypeStruct((16, SHARD, PANEL), BF),
        ],
        scratch_shapes=[
            pltpu.VMEM((4, UNITS, PANEL), BF),
            pltpu.VMEM((16, 128, 2 * LAST), BF),
            pltpu.VMEM((2, 16, 128, PANEL), BF),
            pltpu.VMEM((16, 128, 2 * LAST), BF),
            pltpu.VMEM((4, UNITS, PANEL), BF),
            pltpu.VMEM((ALL // 2, D), BF),
            pltpu.VMEM((ALL // 2, D), BF),
            pltpu.VMEM((ALL // 2, D), BF),
            pltpu.VMEM((ALL // 2, D), BF),
            pltpu.SemaphoreType.DMA((18,)),
            pltpu.SemaphoreType.DMA((2,)),
            pltpu.SemaphoreType.DMA((6,)),
            pltpu.SemaphoreType.DMA((2,)),
            pltpu.SemaphoreType.DMA((16,)),
        ],
        compiler_params=pltpu.CompilerParams(vmem_limit_bytes=56 * 2**20),
        cost_estimate=pl.CostEstimate(
            flops=18 * 10**9, bytes_accessed=45 * 10**6, transcendentals=10**6
        ),
        name="mlp_grads",
    )(four, core, cot_four, cot_core, full, full)


def split_rows(total, rest_ref, own_ref=None):
    if own_ref is None:
        rest_ref[...] = total.astype(BF)
    else:
        own_ref[...] = total[:ROWS]
        rest_ref[...] = total[ROWS : ALL // 2].astype(BF)


def second_kernel(g_ref, panel_ref, wide_ref, narrow_ref, *outs):
    *outs, tail = outs
    for row, rows, column, at, start, width in TAIL:
        piece = wide_ref if row == 256 else narrow_ref
        tail[:, at : at + rows, start : start + width] = piece[:, :, column : column + width]
    total = right_product(g_ref[:, :PANEL], panel_ref[:, :128].reshape(PANEL, PANEL))
    total += right_product(
        g_ref[:, PANEL : 2 * PANEL], panel_ref[:, 128:].reshape(PANEL, PANEL)
    )
    total += right_product(
        g_ref[:, 2 * PANEL : 2 * PANEL + 2 * LAST], tail[...].reshape(PANEL, 2 * LAST)
    )
    split_rows(total, *outs)


def second_grad(ggu, full, half):
    rows = [ALL // 2] if half else [ALL // 2 - ROWS, ROWS]
    return pl.pallas_call(
        second_kernel,
        grid=(4,),
        in_specs=[
            pl.BlockSpec((ALL // 2, 1536), lambda i: (half, 0)),
            pl.BlockSpec((4, 256, PANEL), lambda i: (i, 0, 0)),
            pl.BlockSpec((4, 64, PANEL), lambda i: (i, 4, 0)),
            pl.BlockSpec((4, 32, PANEL), lambda i: (i, 10, 0)),
        ],
        out_specs=[pl.BlockSpec((r, PANEL), lambda i: (0, i)) for r in rows],
        out_shape=[jax.ShapeDtypeStruct((r, D), kind) for r, kind in zip(rows, (BF, F32))],
        scratch_shapes=[pltpu.VMEM((4, 128, 2 * LAST), BF)],
        compiler_params=pltpu.CompilerParams(vmem_limit_bytes=58 * 2**20),
        cost_estimate=pl.CostEstimate(
            flops=3 * 10**9, bytes_accessed=10 * 10**6, transcendentals=0
        ),
        name="second_grad",
    )(ggu, full, full, full)


def down_kernel(act_ref, down_ref, core_ref, rest_ref, own_ref):
    part = dot(act_ref[:, :UNITS], down_ref[...].reshape(UNITS, PANEL))
    split_rows(part, rest_ref, own_ref)
    core_ref[...] = part[ALL // 2 :].astype(BF)


def down_product(active, full):
    rows = [ALL // 2, ALL // 2 - ROWS, ROWS]
    return pl.pallas_call(
        down_kernel,
        grid=(4,),
        in_specs=[
            pl.BlockSpec((ALL, 768), lambda c: (0, 0)),
            pl.BlockSpec((4, 176, PANEL), lambda c: (c, 2, 0)),
        ],
        out_specs=[pl.BlockSpec((r, PANEL), lambda c: (0, c)) for r in rows],
        out_shape=[jax.ShapeDtypeStruct((r, D), kind) for r, kind in zip(rows, (BF, BF, F32))],
        compiler_params=pltpu.CompilerParams(vmem_limit_bytes=58 * 2**20),
        cost_estimate=pl.CostEstimate(
            flops=3 * 10**9, bytes_accessed=12 * 10**6, transcendentals=0
        ),
        name="down_product",
    )(active, full)


LANES = 128


def lanes_of(v):
    return lax.broadcasted_iota(jnp.int32, v.shape, v.ndim - 1)


def quarter_turn(v):
    first = lanes_of(v) % HEAD_DIM < HEAD_DIM // 2
    return jnp.where(first, -pltpu.roll(v, 96, 1), pltpu.roll(v, 32, 1))


def doubled(v):
    left = lanes_of(v) < HEAD_DIM
    other = pltpu.roll(v, HEAD_DIM, 1)
    return jnp.where(left, v, other), jnp.where(left, other, v)


def head_rows(ref):
    blocks = []
    for g in range(GROUPS // 2):
        v = ref[:, g * LANES : (g + 1) * LANES].astype(F32)
        left = lanes_of(v) < HEAD_DIM
        blocks += [jnp.where(left, v, 0.0), jnp.where(left, 0.0, v)]
    return jnp.concatenate(blocks, axis=0).astype(BF)


def pair_columns(v, g):
    even = v[2 * g * ROWS : (2 * g + 1) * ROWS]
    odd = v[(2 * g + 1) * ROWS : (2 * g + 2) * ROWS]
    return jnp.where(lanes_of(even) < HEAD_DIM, even, odd)


def softmax_rows(heads, key2, mask):
    scores = right_product(heads, key2).reshape(GROUPS, ROWS, ROWS) * score_scale
    masked = jnp.where(mask[None] > 0.0, scores, -1e30)
    top = jnp.max(masked, axis=-1, keepdims=True)
    total = top + jnp.log(jnp.sum(jnp.exp(masked - top), axis=-1, keepdims=True))
    return jnp.exp(masked - total).reshape(GROUPS * ROWS, ROWS)


def seq_rows(step):
    return pl.ds(pl.multiple_of(jnp.minimum(step, MEMBERS - 1) * ROWS, ROWS), ROWS)


def attention_kernel(
    first_ref,
    weight_ref,
    cos_ref,
    sin_ref,
    mask_ref,
    query_ref,
    kv_ref,
    att_ref,
    near_ref,
    core_ref,
    qkv,
    att,
):
    step = pl.program_id(0)

    @pl.when(step == 0)
    def _():
        qkv[...] = dot(first_ref[...], weight_ref[:, QW:])

    @pl.when(step < MEMBERS)
    def _():
        rows = seq_rows(step)
        cosine, sine = cos_ref[...], sin_ref[...]
        for g in range(GROUPS // 2):
            v = qkv[rows, g * LANES : (g + 1) * LANES]
            query_ref[:, g * LANES : (g + 1) * LANES] = (
                v * cosine + quarter_turn(v) * sine
            ).astype(BF)
        v = qkv[rows, QW:]
        kv = jnp.where(lanes_of(v) < HEAD_DIM, v * cosine + quarter_turn(v) * sine, v)
        kv_ref[...] = kv.astype(BF)
        key2, value2 = doubled(kv)
        probs = softmax_rows(head_rows(query_ref), key2.astype(BF), mask_ref[0])
        heads = dot(probs.astype(BF), value2.astype(BF))
        for g in range(GROUPS // 2):
            pair = pair_columns(heads, g).astype(BF)
            att_ref[:, g * LANES : (g + 1) * LANES] = pair
            att[rows, g * LANES : (g + 1) * LANES] = pair

    @pl.when(step >= MEMBERS)
    def _():
        block = pl.ds(pl.multiple_of((step - MEMBERS) * QW, QW), QW)
        part = dot(att[...], weight_ref[block, :QW])
        near_ref[...] = part[: SLOTS // 2]
        core_ref[...] = part[SLOTS // 2 :].astype(BF)


def attention_back_kernel(
    middle_ref,
    weight_ref,
    first_ref,
    att_ref,
    query_ref,
    kv_ref,
    cos_ref,
    sin_ref,
    mask_ref,
    grad_ref,
    send_ref,
    upstream,
    grads,
):
    step = pl.program_id(0)

    @pl.when(step == 0)
    def _():
        total = right_product(middle_ref[:, :PANEL], weight_ref[:QW, :QW])
        for c in range(1, 4):
            total += right_product(
                middle_ref[:, c * PANEL : (c + 1) * PANEL],
                weight_ref[c * QW : (c + 1) * QW, :QW],
            )
        upstream[...] = total.astype(BF)

    @pl.when(step < MEMBERS)
    def _():
        rows = seq_rows(step)
        cosine, sine = cos_ref[...], sin_ref[...]
        key2, value2 = doubled(kv_ref[...].astype(F32))
        key2, value2 = key2.astype(BF), value2.astype(BF)
        heads, lifted = head_rows(query_ref), head_rows(upstream.at[rows])
        probs = softmax_rows(heads, key2, mask_ref[0])
        grad_value = left_product(probs.astype(BF), lifted)
        grad_value = grad_value + pltpu.roll(grad_value, HEAD_DIM, 1)
        grad_probs = right_product(lifted, value2)
        inner = jnp.sum(grad_probs * probs, axis=-1, keepdims=True)
        grad_scores = (probs * (grad_probs - inner)).astype(BF)
        grad_query = dot(grad_scores, key2)
        for g in range(GROUPS // 2):
            v = pair_columns(grad_query, g) * score_scale
            v = (v * cosine - quarter_turn(v) * sine).astype(BF)
            grad_ref[:, g * LANES : (g + 1) * LANES] = v
            grads[rows, g * LANES : (g + 1) * LANES] = v
        grad_key = left_product(grad_scores, heads)
        v = (grad_key + pltpu.roll(grad_key, HEAD_DIM, 1)) * score_scale
        grad_key = v * cosine - quarter_turn(v) * sine
        v = jnp.where(lanes_of(v) < HEAD_DIM, grad_key, grad_value).astype(BF)
        grad_ref[:, QW:] = v
        grads[rows, QW:] = v

    @pl.when(step >= MEMBERS)
    def _():
        block = pl.ds(pl.multiple_of((step - MEMBERS) * PANEL, PANEL), PANEL)
        send_ref[:, :QW] = left_product(att_ref[...], middle_ref[:, block]).astype(BF)
        send_ref[:, QW:] = left_product(first_ref[:, block], grads[...]).astype(BF)


def all_of(shape):
    return pl.BlockSpec(shape, lambda s: (0,) * len(shape), pipeline_mode=pl.Buffered(1))


def by_seq(width):
    return pl.BlockSpec((ROWS, width), lambda s: (jnp.minimum(s, MEMBERS - 1), 0))


MASK_BLOCK = pl.BlockSpec((1, ROWS, ROWS), lambda s: (jnp.minimum(s, MEMBERS - 1), 0, 0))


def attention(first_low, weights, cosine, sine, mask):
    half = pl.BlockSpec((SLOTS // 2, PANEL), lambda s: (0, jnp.maximum(s - MEMBERS, 0)))
    return pl.pallas_call(
        attention_kernel,
        grid=(2 * MEMBERS,),
        in_specs=[
            all_of((SLOTS, D)),
            all_of((D, QW + QKVW)),
            by_seq(LANES),
            by_seq(LANES),
            MASK_BLOCK,
        ],
        out_specs=[by_seq(QW), by_seq(LANES), by_seq(QW), half, half],
        out_shape=[
            jax.ShapeDtypeStruct((SLOTS, QW), BF),
            jax.ShapeDtypeStruct((SLOTS, LANES), BF),
            jax.ShapeDtypeStruct((SLOTS, QW), BF),
            jax.ShapeDtypeStruct((SLOTS // 2, D), F32),
            jax.ShapeDtypeStruct((SLOTS // 2, D), BF),
        ],
        scratch_shapes=[pltpu.VMEM((SLOTS, QKVW), F32), pltpu.VMEM((SLOTS, QW), BF)],
        compiler_params=pltpu.CompilerParams(vmem_limit_bytes=40 * 2**20),
        cost_estimate=pl.CostEstimate(
            flops=3 * 10**9, bytes_accessed=12 * 10**6, transcendentals=10**6
        ),
        name="attention",
    )(first_low, weights, cosine, sine, mask)


def attention_back(middle_all, weights, first_low, attended, query, kv, cosine, sine, mask):
    return pl.pallas_call(
        attention_back_kernel,
        grid=(2 * MEMBERS,),
        in_specs=[
            all_of((SLOTS, D)),
            all_of((D, QW + QKVW)),
            all_of((SLOTS, D)),
            all_of((SLOTS, QW)),
            by_seq(QW),
            by_seq(LANES),
            by_seq(LANES),
            by_seq(LANES),
            MASK_BLOCK,
        ],
        out_specs=[
            by_seq(QKVW),
            pl.BlockSpec((PANEL, QW + QKVW), lambda s: (jnp.maximum(s - MEMBERS, 0), 0)),
        ],
        out_shape=[
            jax.ShapeDtypeStruct((SLOTS, QKVW), BF),
            jax.ShapeDtypeStruct((D, QW + QKVW), BF),
        ],
        scratch_shapes=[pltpu.VMEM((SLOTS, QW), BF), pltpu.VMEM((SLOTS, QKVW), BF)],
        compiler_params=pltpu.CompilerParams(vmem_limit_bytes=58 * 2**20),
        cost_estimate=pl.CostEstimate(
            flops=5 * 10**9, bytes_accessed=16 * 10**6, transcendentals=10**6
        ),
        name="attention_back",
    )(middle_all, weights, first_low, attended, query, kv, cosine, sine, mask)


def first_kernel(grad_ref, weight_ref, rows_ref, rms_ref, near_ref, core_ref, gain_ref):
    grad = right_product(grad_ref[...], weight_ref[:, QW:])
    normed = rows_ref[...].astype(F32) * rms_ref[...]
    gain_ref[...] = jnp.sum(grad * normed, axis=0, keepdims=True)
    near_ref[...] = grad[: SLOTS // 2]
    core_ref[...] = grad[SLOTS // 2 :].astype(BF)


def first_grad(grad_qkv, weights, rows_in, rms):
    half = pl.BlockSpec((SLOTS // 2, PANEL), lambda i: (0, i))
    return pl.pallas_call(
        first_kernel,
        grid=(4,),
        in_specs=[
            all_of((SLOTS, QKVW)),
            pl.BlockSpec((PANEL, QW + QKVW), lambda i: (i, 0)),
            pl.BlockSpec((SLOTS, PANEL), lambda i: (0, i)),
            all_of((SLOTS, 1)),
        ],
        out_specs=[half, half, pl.BlockSpec((1, PANEL), lambda i: (0, i))],
        out_shape=[
            jax.ShapeDtypeStruct((SLOTS // 2, D), F32),
            jax.ShapeDtypeStruct((SLOTS // 2, D), BF),
            jax.ShapeDtypeStruct((1, D), F32),
        ],
        compiler_params=pltpu.CompilerParams(vmem_limit_bytes=32 * 2**20),
        cost_estimate=pl.CostEstimate(
            flops=14 * 10**8, bytes_accessed=12 * 10**6, transcendentals=0
        ),
        name="first_grad",
    )(grad_qkv, weights, rows_in, rms)


def update_kernel(
    at_ref,
    own_ref,
    near_ref,
    core_ref,
    moments_ref,
    moment_ref,
    query_ref,
    key_ref,
    value_ref,
    output_ref,
    query_moved,
    key_moved,
    value_moved,
    output_moved,
    query_new,
    key_new,
    value_new,
    output_new,
    moved,
):
    width = QKVW + PANEL
    own = 0.5 * moment_ref[...] + 0.5 * own_ref[...]
    query_moved[...] = own[:, :QW]
    key_moved[...] = own[:, QW : QW + KW]
    value_moved[...] = own[:, QW + KW : QKVW]
    output_moved[...] = own[:, QKVW:]
    rows = near_ref.shape[0]
    moved[:rows] = 0.5 * moments_ref[:rows].astype(F32) + 0.5 * near_ref[...].astype(F32)
    moved[rows:] = 0.5 * moments_ref[rows:].astype(F32) + 0.5 * core_ref[:, :width].astype(F32)
    pairs = []
    for a, order in enumerate((0, 2, 1, 3)):
        slot = pl.ds(pl.multiple_of((at_ref[0] ^ order) * W_ROWS, W_ROWS), W_ROWS)
        columns = slice(a * QW, (a + 1) * QW)
        query_new[:, columns] = query_ref[:, columns] - learn_rate * moved[slot, :QW]
        output_new[:, columns] = output_ref[:, columns] - learn_rate * moved[slot, QKVW:]
        pairs.append(moved[slot, QW:QKVW])
    for a in (0, 2):
        even, odd = pairs[a], pairs[a + 1]
        left = lanes_of(even) < HEAD_DIM
        key = jnp.where(left, even, pltpu.roll(odd, HEAD_DIM, 1))
        value = jnp.where(left, pltpu.roll(even, HEAD_DIM, 1), odd)
        columns = slice(a * KW, (a + 2) * KW)
        key_new[:, columns] = key_ref[:, columns] - learn_rate * key
        value_new[:, columns] = value_ref[:, columns] - learn_rate * value


def attention_update(at, own, near, core, moments, moment, weights):
    shapes = [(W_ROWS, w) for w in (QW, KW, KW, QW)] + [w.shape for w in weights]
    vmem = pl.BlockSpec(memory_space=pltpu.VMEM)
    return pl.pallas_call(
        update_kernel,
        in_specs=[pl.BlockSpec(memory_space=pltpu.SMEM)] + [vmem] * 9,
        out_specs=[vmem] * 8,
        out_shape=[jax.ShapeDtypeStruct(shape, F32) for shape in shapes],
        scratch_shapes=[pltpu.VMEM((MEMBERS * W_ROWS, QKVW + PANEL), F32)],
        compiler_params=pltpu.CompilerParams(vmem_limit_bytes=16 * 2**20),
        cost_estimate=pl.CostEstimate(
            flops=10**6, bytes_accessed=6 * 10**6, transcendentals=0
        ),
        name="attention_update",
    )(at, own, near, core, moments, moment, *weights)


def rounded_gain(gain):
    return lax.optimization_barrier(gain.astype(BF)).astype(F32)


def inverse_rms(v):
    return lax.rsqrt(jnp.mean(v * v, axis=-1, keepdims=True) + epsilon)


def norm_back(v, gain, grad):
    r = inverse_rms(v)
    n = v * r
    scaled = grad * gain
    return r * (scaled - n * jnp.mean(scaled * n, axis=-1, keepdims=True)), n


def panels(gate, up):
    blocks = []
    for at in range(0, UNITS, 256):
        blocks += [gate[:, at : at + 256], up[:, at : at + 256]]
    return jnp.concatenate(blocks, axis=1)


def unpanels(v):
    gate = [v[:, :256], v[:, 512:768], v[:, 1024 : 1024 + LAST]]
    up = [v[:, 256:512], v[:, 768:1024], v[:, 1024 + LAST :]]
    return jnp.concatenate(gate, axis=1), jnp.concatenate(up, axis=1)


def on_device(
    tokens,
    cotangent,
    segment_ids,
    positions,
    padding,
    attn_gain,
    query_weight,
    key_weight,
    value_weight,
    output_weight,
    mlp_gain,
    gate_weight,
    up_weight,
    down_weight,
    attn_moment,
    query_moment,
    key_moment,
    value_moment,
    output_moment,
    mlp_moment,
    gate_moment,
    up_moment,
    down_moment,
):
    member = lax.axis_index("grp")
    place = lax.axis_index("dp")
    z, y, low = place // 8, (place // 2) % 4, (place % 2) == 0

    def mine(weight, width):
        return lax.dynamic_slice_in_dim(weight, member * width, width, 1).astype(BF)

    attn_shard = jnp.concatenate(
        [mine(query_weight, QW), mine(key_weight, KW), mine(value_weight, KW)], axis=1
    )
    attn_shard = jnp.concatenate(
        [turn_pair(mine(output_weight, QW), low), pair_x(attn_shard, low)], axis=1
    )
    attn_full = plane_gather(attn_shard)

    gate_mine, up_mine = mine(gate_weight, FW), mine(up_weight, FW)
    first = panels(gate_mine[:, :UNITS], up_mine[:, :UNITS])
    second = panels(gate_mine[:, UNITS:], up_mine[:, UNITS:])
    kept, given = jnp.where(low, first, second), jnp.where(low, second, first)
    gu_shard = in_order(kept, swap_x(given), low)
    tail = gu_shard[:, 2 * PANEL :]
    pieces = [
        gu_shard[:, :PANEL],
        gu_shard[:, PANEL : 2 * PANEL],
        jnp.concatenate([tail[:W_ROWS, :256], tail[W_ROWS:, :256]], axis=1),
        jnp.concatenate([tail[32 * h : 32 * h + 32, 256:] for h in range(4)], axis=1),
        everywhere(mine(down_weight, PANEL), OWNED),
    ]
    mlp_full = plane_gather(jnp.concatenate(pieces, axis=0)).reshape(16, SHARD, PANEL)

    places = jnp.stack([segment_ids, positions, padding])[None]
    rows_in = group_gather(tokens)
    own_moment = jnp.concatenate(
        [query_moment, key_moment, value_moment, output_moment], axis=1
    )
    moments = own_moment.astype(BF)
    places, moments, upstream = lax.optimization_barrier(
        (
            jnp.concatenate([places, swap_far(places)], axis=0),
            jnp.concatenate([moments, swap_far(moments)], axis=0),
            cotangent,
        )
    )
    cot_four, cot_core = row_gather(upstream)
    places = jnp.concatenate([places, swap_core(places)], axis=0)
    moments = jnp.concatenate([moments, swap_core(moments)], axis=0)
    segments, spots, pads = places[:, 0], places[:, 1], places[:, 2]

    first_gain = rounded_gain(attn_gain)
    second_gain = rounded_gain(mlp_gain)
    inputs = rows_in.astype(F32)
    rms = inverse_rms(inputs)
    first_low = (inputs * rms * first_gain).astype(BF)

    half = HEAD_DIM // 2
    freq = 10000.0 ** (-(jnp.arange(half, dtype=F32) * 2.0 / HEAD_DIM))
    angles = spots.reshape(SLOTS, 1).astype(F32) * jnp.tile(freq, LANES // half)[None]
    cosine, sine = jnp.cos(angles), jnp.sin(angles)
    column = jnp.arange(ROWS, dtype=jnp.int32)
    allowed = jnp.logical_and(
        jnp.logical_and(
            segments[:, :, None] == segments[:, None, :],
            (column[None, :] <= column[:, None])[None],
        ),
        jnp.logical_or(pads[:, None, :] == 1, (column[None, :] == column[:, None])[None]),
    ).astype(F32)

    attn_full, first_low, cosine, sine, allowed, cot_four, moments = lax.optimization_barrier(
        (attn_full, first_low, cosine, sine, allowed, cot_four, moments)
    )
    query_rot, kv, attended, near, core = attention(first_low, attn_full, cosine, sine, allowed)
    middle = tokens.astype(F32) + added(far_parts(near + swap_core(core).astype(F32)))
    second_low = (middle * inverse_rms(middle) * second_gain).astype(BF)
    four, core_four = row_gather(second_low)
    core_four, cot_core = lax.optimization_barrier((core_four, cot_core))
    grad_gu, active, send = mlp_grads(four, core_four, cot_four, cot_core, mlp_full)
    mlp_sum = plane_scatter(send.reshape(16 * SHARD, PANEL))

    second_core = swap_core(second_grad(grad_gu, mlp_full, 1)[0])
    second_rest, second_own = second_grad(grad_gu, mlp_full, 0)
    grad_second = added(row_parts(second_own, second_rest, second_core))
    back, n_second = norm_back(middle, second_gain, grad_second)
    mlp_gain_part = jnp.sum(grad_second * n_second, axis=0)
    grad_middle = cotangent.astype(F32) + back
    middle_all = group_gather(grad_middle.astype(BF))
    down_core, down_rest, down_own = down_product(active, mlp_full)
    middle_all, down_core = lax.optimization_barrier((middle_all, swap_core(down_core)))
    grad_qkv, attn_send = attention_back(
        middle_all, attn_full, first_low, attended, query_rot, kv, cosine, sine, allowed
    )
    attn_sum = plane_scatter(attn_send)

    grad_qkv, mlp_sum, down_core = lax.optimization_barrier((grad_qkv, mlp_sum, down_core))
    block_parts = row_parts(down_own, down_rest, down_core)
    near, core, attn_gain_part = first_grad(grad_qkv, attn_full, rows_in, rms)
    gains = jnp.concatenate([attn_gain_part, mlp_gain_part[None]], axis=0).reshape(32, LANES)
    gains = gains + sum(lax.ppermute(gains, "dp", p) for p in RING_Z)
    near, gains = lax.optimization_barrier((near + swap_core(core).astype(F32), gains))
    gains = gains + sum(lax.ppermute(gains, "dp", p) for p in RING_Y)
    first_parts = far_parts(near)

    mine_at = (member // 2) + 2 * (member % 2)

    def by_member(slots):
        return [
            lax.dynamic_index_in_dim(slots, mine_at ^ at, 0, keepdims=False) for at in (0, 2, 1, 3)
        ]

    def updated(weight, columns, start, size):
        moved = jnp.concatenate([block[:, start : start + size] for block in columns], axis=1)
        return weight - learn_rate * moved.astype(F32)

    wide, narrow = mlp_sum[256:320], mlp_sum[320:352]
    gu_part = jnp.concatenate(
        [
            mlp_sum[:128],
            mlp_sum[128:256],
            jnp.concatenate([wide[:, :256], wide[:, 256:]], axis=0),
            jnp.concatenate([narrow[:, h * LANES : (h + 1) * LANES] for h in range(4)], axis=0),
        ],
        axis=1,
    )
    kept, given = halves(gu_part, low)
    other = swap_x(given)
    first = unpanels(jnp.where(low, kept, other))
    second = unpanels(jnp.where(low, other, kept))
    gate_rows = jnp.concatenate([first[0], second[0]], axis=1).astype(F32)
    up_rows = jnp.concatenate([first[1], second[1]], axis=1).astype(F32)
    down_rows = everywhere(mlp_sum[352:], RETURN).astype(F32)
    gate_momentum = 0.5 * gate_moment + 0.5 * gate_rows
    up_momentum = 0.5 * up_moment + 0.5 * up_rows
    down_momentum = 0.5 * down_moment + 0.5 * down_rows
    gu_moved = jnp.concatenate([gate_momentum, up_momentum], axis=1).astype(BF)
    gu_moved, block_parts = lax.optimization_barrier((gu_moved, block_parts))
    gu_moved, down_moved = group_gather(gu_moved), group_gather(down_momentum.astype(BF))

    attn_sum, gains, first_parts, block_parts, gu_moved, down_moved = lax.optimization_barrier(
        (attn_sum, gains, first_parts, block_parts, gu_moved, down_moved)
    )
    block_output = (middle + added(block_parts)).astype(BF)
    back, _ = norm_back(tokens.astype(F32), first_gain, added(first_parts))
    input_grad = grad_middle + back
    gu_moved = by_member(gu_moved.reshape(MEMBERS, W_ROWS, GUW))
    down_moved = by_member(down_moved.reshape(MEMBERS, DOWN_ROWS, PANEL))
    gate_updated = updated(gate_weight, gu_moved, 0, FW)
    up_updated = updated(up_weight, gu_moved, FW, FW)
    down_updated = updated(down_weight, down_moved, 0, PANEL)

    def row_sums(part, rider):
        width = part.shape[1]
        kept, given = halves(part, low)
        if rider is not None:
            kept, given = (jnp.concatenate([v, rider], axis=1) for v in (kept, given))
        near, far, both = swap_x(given), swap_far(kept), far_x(given)
        own_sum = kept[:, :width].astype(F32) + near[:, :width].astype(F32)
        far_sum = far[:, :width].astype(F32) + both[:, :width].astype(F32)
        return own_sum, far_sum, [v[:, width:] for v in (kept, near, far, both)]

    width = QKVW + PANEL
    turned = everywhere(attn_sum[:, :QW], TURN)
    own_qkv, far_qkv, riders = row_sums(attn_sum[:, QW:], two_parts(gains))
    own_out, far_out, _ = row_sums(turned, None)
    gains = sum(one_part(part) for part in riders)
    own_total = jnp.concatenate([own_qkv, own_out], axis=1)
    far_total = jnp.concatenate([far_qkv, far_out], axis=1)
    totals = jnp.concatenate([own_total, far_total], axis=0).astype(BF)
    rider = jnp.concatenate([two_parts(gains), jnp.zeros((W_ROWS, LANES), BF)], axis=0)
    other = swap_core(jnp.concatenate([totals, rider], axis=1))
    gains = gains + one_part(other[:W_ROWS, width:])
    attn_done = attention_update(
        mine_at.astype(jnp.int32).reshape(1),
        own_total,
        totals,
        other,
        moments,
        own_moment,
        (query_weight, key_weight, value_weight, output_weight),
    )

    gains = 0.5 * jnp.stack([attn_moment, mlp_moment]) + 0.5 * gains.reshape(2, D)
    return (
        block_output,
        input_grad,
        gains[0],
        *attn_done[:4],
        gains[1],
        gate_momentum,
        up_momentum,
        down_momentum,
        attn_gain - learn_rate * gains[0],
        *attn_done[4:],
        mlp_gain - learn_rate * gains[1],
        gate_updated,
        up_updated,
        down_updated,
    )


def solution(mesh):
    rows = P(("grp", "dp"), None)
    flat = P(("grp", "dp"))
    weight = P("dp", None)
    moment = P("dp", "grp")
    everyone = P()
    weights = (everyone,) + (weight,) * 4 + (everyone,) + (weight,) * 3
    moments = (everyone,) + (moment,) * 4 + (everyone,) + (moment,) * 3
    return jax.shard_map(
        on_device,
        mesh=mesh,
        in_specs=(rows, rows, flat, flat, flat) + weights + moments,
        out_specs=(rows, rows) + moments + weights,
        check_vma=False,
    )
```

```python
import jax
import jax.numpy as jnp
from jax import lax
from jax.experimental import pallas as pl
from jax.experimental.pallas import tpu as pltpu
from jax.sharding import PartitionSpec as P

D = 2048
HEAD_DIM = 64
GROUPS = 8
ROWS = 128
MEMBERS = 4
SLOTS = ROWS * MEMBERS
QW = 512
KW = 64
QKVW = QW + 2 * KW
FW = 1408
GUW = 2 * FW
PANEL = 512
DOWN_ROWS = 176
W_ROWS = 64

epsilon = 1e-05
learn_rate = 0.005
score_scale = 0.125

BF = jnp.bfloat16
F32 = jnp.float32

PLANES = [[z * 8 + y * 2 + x for z in range(4) for y in range(4)] for x in range(2)]
SWAP_X = [(i, i ^ 1) for i in range(32)]
SWAP_CORE = [(m, m ^ 1) for m in range(4)]
SWAP_FAR = [(m, m ^ 2) for m in range(4)]
SWAP_FAR_X = [(m * 32 + i, (m ^ 2) * 32 + (i ^ 1)) for m in range(4) for i in range(32)]
MZQ = [(m, z, q) for m in range(4) for z in range(4) for q in range(8)]


def spot(m, z, q):
    return m * 32 + z * 8 + q


TURN = [(spot(m, z, q), spot(z, m, q)) for m, z, q in MZQ]
TURN_X = [(spot(m, z, q), spot(z, m, q ^ 1)) for m, z, q in MZQ]
TURN_IN = [[(spot(m, z, q), spot((z + k) % 4, m, q)) for m, z, q in MZQ] for k in range(4)]
OWNED = [(spot(m, z, q), spot(z, m, (q & 3) * 2 + (q >> 2))) for m, z, q in MZQ]
RETURN = [(b, a) for a, b in OWNED]


def ring(place, k):
    return [(i, i + ((i // place + k) % 4 - i // place % 4) * place) for i in range(32)]


RING_Z = [ring(8, k) for k in (1, 2, 3)]
RING_Y = [ring(2, k) for k in (1, 2, 3)]


def swap_x(v):
    return lax.ppermute(v, "dp", SWAP_X)


def swap_core(v):
    return lax.ppermute(v, "grp", SWAP_CORE)


def swap_far(v):
    return lax.ppermute(v, "grp", SWAP_FAR)


def everywhere(v, pairs):
    return lax.ppermute(v, ("grp", "dp"), pairs)


def plane_gather(v):
    return lax.all_gather(v, "dp", axis=0, tiled=True, axis_index_groups=PLANES)


def plane_scatter(v):
    return lax.psum_scatter(
        v, "dp", scatter_dimension=0, tiled=True, axis_index_groups=PLANES
    )


def ring_scatter(v, pairs, at, extra=None):
    rows = v.shape[0] // 4

    def chunk(k):
        part = lax.dynamic_slice_in_dim(v, lax.rem(at + k, 4) * rows, rows, 0)
        return part if extra is None else jnp.concatenate([part, extra], axis=1)

    total = chunk(0).astype(F32)
    for k, p in enumerate(pairs):
        total = total + lax.ppermute(chunk(k + 1), "dp", p).astype(F32)
    return total


def group_gather(v):
    pair = jnp.concatenate([v, swap_far(v)], axis=0)
    return jnp.concatenate([pair, swap_core(pair)], axis=0)


def group_scatter_far(near):
    return near[:ROWS] + swap_far(near[ROWS:].astype(BF)).astype(F32)


def far_x(v):
    return everywhere(v, SWAP_FAR_X)


def row_gather(v):
    four = jnp.concatenate([v, swap_x(v), swap_far(v), far_x(v)], axis=0)
    return four, swap_core(four)


def row_scatter(own, rest, core):
    own = own + core[:ROWS].astype(F32)
    rest = (rest.astype(F32) + core[ROWS:].astype(F32)).astype(BF)
    low_part, far_part, far_x_part = (rest[k * ROWS : (k + 1) * ROWS] for k in range(3))
    return (
        own
        + swap_x(low_part).astype(F32)
        + swap_far(far_part).astype(F32)
        + far_x(far_x_part).astype(F32)
    )


def in_order(own, other, low):
    return jnp.concatenate([jnp.where(low, own, other), jnp.where(low, other, own)], axis=0)


def pair_x(v, low):
    return in_order(v, swap_x(v), low)


def turn_pair(v, low):
    return in_order(everywhere(v, TURN), everywhere(v, TURN_X), low)


def halves(v, low):
    rows = v.shape[0] // 2
    return jnp.where(low, v[:rows], v[rows:]), jnp.where(low, v[rows:], v[:rows])


def two_parts(v):
    high = lax.reduce_precision(v, 8, 7)
    return jnp.concatenate([high.astype(BF), (v - high).astype(BF)], axis=0)


def one_part(v):
    rows = v.shape[0] // 2
    return v[:rows].astype(F32) + v[rows:].astype(F32)


def dot(left, right):
    return jnp.dot(left, right, preferred_element_type=F32)


def left_product(left, right):
    return lax.dot_general(left, right, (((0,), (0,)), ((), ())), preferred_element_type=F32)


def right_product(left, right):
    return lax.dot_general(left, right, (((1,), (1,)), ((), ())), preferred_element_type=F32)


ALL = 1024
UNITS = 704
LAST = 192
SHARD = 528


TAIL = [(256, 64, 256 * h, 64 * h, 0, 256) for h in range(2)]
TAIL += [(320, 32, 128 * h, 32 * h, 256, 128) for h in range(4)]


def tail_pieces(shard):
    for row, rows, column, at, start, width in TAIL:
        yield (
            shard.at[:, pl.ds(row, rows), pl.ds(column, width)],
            (slice(None), pl.ds(at, rows), pl.ds(start, width)),
        )


def tail_loads(full, tail, sems):
    return [
        pltpu.make_async_copy(src, tail.at[at], sems.at[i])
        for i, (src, at) in enumerate(tail_pieces(full))
    ]


def down_blocks(shard, down):
    return [
        (shard.at[4 * c + j, pl.ds(352, 176), :], down.at[c, pl.ds(176 * j, 176), :])
        for c in range(4)
        for j in range(4)
    ]


def mlp_kernel(
    four,
    core,
    cot_four,
    cot_core,
    panel_ref,
    full,
    ggu_ref,
    act_ref,
    send,
    down,
    tail,
    gpan,
    gtail,
    gdown,
    four_ref,
    core_ref,
    cot_four_ref,
    cot_core_ref,
    in_sem,
    row_sem,
    tail_sem,
    pan_sem,
    out_sem,
):
    step = pl.program_id(0)
    loads = [
        pltpu.make_async_copy(src, dst, in_sem.at[i])
        for i, (src, dst) in enumerate(
            [(cot_four, cot_four_ref), (cot_core, cot_core_ref)] + down_blocks(full, down)
        )
    ]
    rows_in = [
        pltpu.make_async_copy(src, dst, row_sem.at[i])
        for i, (src, dst) in enumerate([(four, four_ref), (core, core_ref)])
    ]
    tails = tail_loads(full, tail, tail_sem)

    @pl.when(step == 0)
    def _():
        for copy in rows_in + loads + tails:
            copy.start()
        for copy in rows_in + loads:
            copy.wait()

    def panel_out(at):
        return pltpu.make_async_copy(
            gpan.at[at], send.at[:, pl.ds(128 * at, 128), :], pan_sem.at[at]
        )

    def block(weights, start, width, store):
        halves_of = [dot(ref[...], weights) for ref in (four_ref, core_ref)]

        for half, (h, c_ref) in enumerate(zip(halves_of, (cot_four_ref, cot_core_ref))):
            rows = pl.ds(half * (ALL // 2), ALL // 2)
            gate, up = h[:, :width], h[:, width:]
            prod = right_product(c_ref[:, :PANEL], down[0, pl.ds(start, width), :])
            for c in range(1, 4):
                prod += right_product(
                    c_ref[:, c * PANEL : (c + 1) * PANEL], down[c, pl.ds(start, width), :]
                )
            sig = 1.0 / (1.0 + jnp.exp(-gate))
            silu = gate * sig
            act_ref[rows, :width] = (silu * up).astype(BF)
            ggu_ref[rows, :width] = (prod * up * sig * (1.0 + gate * (1.0 - sig))).astype(BF)
            ggu_ref[rows, width : 2 * width] = (prod * silu).astype(BF)
        for c in range(4):
            columns = slice(c * PANEL, (c + 1) * PANEL)
            grads = left_product(act_ref[: ALL // 2, :width], cot_four_ref[:, columns])
            grads += left_product(act_ref[ALL // 2 :, :width], cot_core_ref[:, columns])
            gdown[c, pl.ds(start, width), :] = grads.astype(BF)
        grads = left_product(four_ref[...], ggu_ref[: ALL // 2, : 2 * width])
        grads += left_product(core_ref[...], ggu_ref[ALL // 2 :, : 2 * width])
        store(grads.astype(BF))

    @pl.when(step < 2)
    def _():
        def store(grads):
            gpan[step] = grads.reshape(16, 128, PANEL)

        block(panel_ref[...].reshape(D, PANEL), pl.multiple_of(256 * step, 256), 256, store)
        panel_out(step).start()

    @pl.when(step == 2)
    def _():
        def store(grads):
            gtail[...] = grads.reshape(16, 128, 2 * LAST)

        for copy in tails:
            copy.wait()
        block(tail[...].reshape(D, 2 * LAST), 512, LAST, store)
        outs = [
            pltpu.make_async_copy(gtail.at[at], dst, tail_sem.at[i])
            for i, (dst, at) in enumerate(tail_pieces(send))
        ]
        outs += [
            pltpu.make_async_copy(src, dst, out_sem.at[i])
            for i, (dst, src) in enumerate(down_blocks(send, gdown))
        ]
        for copy in outs:
            copy.start()
        for copy in outs + [panel_out(0), panel_out(1)]:
            copy.wait()


def mlp_grads(four, core, cot_four, cot_core, full):
    return pl.pallas_call(
        mlp_kernel,
        grid=(3,),
        in_specs=[pl.BlockSpec(memory_space=pl.ANY)] * 4
        + [
            pl.BlockSpec((16, 128, PANEL), lambda i: (0, jnp.minimum(i, 1), 0)),
            pl.BlockSpec(memory_space=pl.ANY),
        ],
        out_specs=[
            pl.BlockSpec((ALL, 512), lambda i: (0, i)),
            pl.BlockSpec((ALL, 256), lambda i: (0, i)),
            pl.BlockSpec(memory_space=pl.ANY),
        ],
        out_shape=[
            jax.ShapeDtypeStruct((ALL, 1536), BF),
            jax.ShapeDtypeStruct((ALL, 768), BF),
            jax.ShapeDtypeStruct((16, SHARD, PANEL), BF),
        ],
        scratch_shapes=[
            pltpu.VMEM((4, UNITS, PANEL), BF),
            pltpu.VMEM((16, 128, 2 * LAST), BF),
            pltpu.VMEM((2, 16, 128, PANEL), BF),
            pltpu.VMEM((16, 128, 2 * LAST), BF),
            pltpu.VMEM((4, UNITS, PANEL), BF),
            pltpu.VMEM((ALL // 2, D), BF),
            pltpu.VMEM((ALL // 2, D), BF),
            pltpu.VMEM((ALL // 2, D), BF),
            pltpu.VMEM((ALL // 2, D), BF),
            pltpu.SemaphoreType.DMA((18,)),
            pltpu.SemaphoreType.DMA((2,)),
            pltpu.SemaphoreType.DMA((6,)),
            pltpu.SemaphoreType.DMA((2,)),
            pltpu.SemaphoreType.DMA((16,)),
        ],
        compiler_params=pltpu.CompilerParams(vmem_limit_bytes=56 * 2**20),
        cost_estimate=pl.CostEstimate(
            flops=18 * 10**9, bytes_accessed=45 * 10**6, transcendentals=10**6
        ),
        name="mlp_grads",
    )(four, core, cot_four, cot_core, full, full)


def split_rows(total, rest_ref, own_ref=None):
    if own_ref is None:
        rest_ref[...] = total.astype(BF)
    else:
        own_ref[...] = total[:ROWS]
        rest_ref[...] = total[ROWS : ALL // 2].astype(BF)


def second_kernel(g_ref, panel_ref, wide_ref, narrow_ref, *outs):
    *outs, tail = outs
    for row, rows, column, at, start, width in TAIL:
        piece = wide_ref if row == 256 else narrow_ref
        tail[:, at : at + rows, start : start + width] = piece[:, :, column : column + width]
    total = right_product(g_ref[:, :PANEL], panel_ref[:, :128].reshape(PANEL, PANEL))
    total += right_product(
        g_ref[:, PANEL : 2 * PANEL], panel_ref[:, 128:].reshape(PANEL, PANEL)
    )
    total += right_product(
        g_ref[:, 2 * PANEL : 2 * PANEL + 2 * LAST], tail[...].reshape(PANEL, 2 * LAST)
    )
    split_rows(total, *outs)


def second_grad(ggu, full, half):
    rows = [ALL // 2] if half else [ALL // 2 - ROWS, ROWS]
    return pl.pallas_call(
        second_kernel,
        grid=(4,),
        in_specs=[
            pl.BlockSpec((ALL // 2, 1536), lambda i: (half, 0)),
            pl.BlockSpec((4, 256, PANEL), lambda i: (i, 0, 0)),
            pl.BlockSpec((4, 64, PANEL), lambda i: (i, 4, 0)),
            pl.BlockSpec((4, 32, PANEL), lambda i: (i, 10, 0)),
        ],
        out_specs=[pl.BlockSpec((r, PANEL), lambda i: (0, i)) for r in rows],
        out_shape=[jax.ShapeDtypeStruct((r, D), kind) for r, kind in zip(rows, (BF, F32))],
        scratch_shapes=[pltpu.VMEM((4, 128, 2 * LAST), BF)],
        compiler_params=pltpu.CompilerParams(vmem_limit_bytes=58 * 2**20),
        cost_estimate=pl.CostEstimate(
            flops=3 * 10**9, bytes_accessed=10 * 10**6, transcendentals=0
        ),
        name="second_grad",
    )(ggu, full, full, full)


def down_kernel(act_ref, down_ref, core_ref, rest_ref, own_ref):
    part = dot(act_ref[:, :UNITS], down_ref[...].reshape(UNITS, PANEL))
    split_rows(part, rest_ref, own_ref)
    core_ref[...] = part[ALL // 2 :].astype(BF)


def down_product(active, full):
    rows = [ALL // 2, ALL // 2 - ROWS, ROWS]
    return pl.pallas_call(
        down_kernel,
        grid=(4,),
        in_specs=[
            pl.BlockSpec((ALL, 768), lambda c: (0, 0)),
            pl.BlockSpec((4, 176, PANEL), lambda c: (c, 2, 0)),
        ],
        out_specs=[pl.BlockSpec((r, PANEL), lambda c: (0, c)) for r in rows],
        out_shape=[jax.ShapeDtypeStruct((r, D), kind) for r, kind in zip(rows, (BF, BF, F32))],
        compiler_params=pltpu.CompilerParams(vmem_limit_bytes=58 * 2**20),
        cost_estimate=pl.CostEstimate(
            flops=3 * 10**9, bytes_accessed=12 * 10**6, transcendentals=0
        ),
        name="down_product",
    )(active, full)


LANES = 128


def lanes_of(v):
    return lax.broadcasted_iota(jnp.int32, v.shape, v.ndim - 1)


def quarter_turn(v):
    first = lanes_of(v) % HEAD_DIM < HEAD_DIM // 2
    return jnp.where(first, -pltpu.roll(v, 96, 1), pltpu.roll(v, 32, 1))


def doubled(v):
    left = lanes_of(v) < HEAD_DIM
    other = pltpu.roll(v, HEAD_DIM, 1)
    return jnp.where(left, v, other), jnp.where(left, other, v)


def head_rows(ref):
    blocks = []
    for g in range(GROUPS // 2):
        v = ref[:, g * LANES : (g + 1) * LANES].astype(F32)
        left = lanes_of(v) < HEAD_DIM
        blocks += [jnp.where(left, v, 0.0), jnp.where(left, 0.0, v)]
    return jnp.concatenate(blocks, axis=0).astype(BF)


def pair_columns(v, g):
    even = v[2 * g * ROWS : (2 * g + 1) * ROWS]
    odd = v[(2 * g + 1) * ROWS : (2 * g + 2) * ROWS]
    return jnp.where(lanes_of(even) < HEAD_DIM, even, odd)


def softmax_rows(heads, key2, mask):
    scores = right_product(heads, key2).reshape(GROUPS, ROWS, ROWS) * score_scale
    masked = jnp.where(mask[None] > 0.0, scores, -1e30)
    top = jnp.max(masked, axis=-1, keepdims=True)
    total = top + jnp.log(jnp.sum(jnp.exp(masked - top), axis=-1, keepdims=True))
    return jnp.exp(masked - total).reshape(GROUPS * ROWS, ROWS)


def seq_rows(step):
    return pl.ds(pl.multiple_of(jnp.minimum(step, MEMBERS - 1) * ROWS, ROWS), ROWS)


def attention_kernel(
    first_ref,
    weight_ref,
    cos_ref,
    sin_ref,
    mask_ref,
    query_ref,
    kv_ref,
    att_ref,
    near_ref,
    core_ref,
    qkv,
    att,
):
    step = pl.program_id(0)

    @pl.when(step == 0)
    def _():
        qkv[...] = dot(first_ref[...], weight_ref[:, QW:])

    @pl.when(step < MEMBERS)
    def _():
        rows = seq_rows(step)
        cosine, sine = cos_ref[...], sin_ref[...]
        for g in range(GROUPS // 2):
            v = qkv[rows, g * LANES : (g + 1) * LANES]
            query_ref[:, g * LANES : (g + 1) * LANES] = (
                v * cosine + quarter_turn(v) * sine
            ).astype(BF)
        v = qkv[rows, QW:]
        kv = jnp.where(lanes_of(v) < HEAD_DIM, v * cosine + quarter_turn(v) * sine, v)
        kv_ref[...] = kv.astype(BF)
        key2, value2 = doubled(kv)
        probs = softmax_rows(head_rows(query_ref), key2.astype(BF), mask_ref[0])
        heads = dot(probs.astype(BF), value2.astype(BF))
        for g in range(GROUPS // 2):
            pair = pair_columns(heads, g).astype(BF)
            att_ref[:, g * LANES : (g + 1) * LANES] = pair
            att[rows, g * LANES : (g + 1) * LANES] = pair

    @pl.when(step >= MEMBERS)
    def _():
        block = pl.ds(pl.multiple_of((step - MEMBERS) * QW, QW), QW)
        part = dot(att[...], weight_ref[block, :QW])
        near_ref[...] = part[: SLOTS // 2]
        core_ref[...] = part[SLOTS // 2 :].astype(BF)


def attention_back_kernel(
    middle_ref,
    weight_ref,
    first_ref,
    att_ref,
    query_ref,
    kv_ref,
    cos_ref,
    sin_ref,
    mask_ref,
    grad_ref,
    send_ref,
    upstream,
    grads,
):
    step = pl.program_id(0)

    @pl.when(step == 0)
    def _():
        total = right_product(middle_ref[:, :PANEL], weight_ref[:QW, :QW])
        for c in range(1, 4):
            total += right_product(
                middle_ref[:, c * PANEL : (c + 1) * PANEL],
                weight_ref[c * QW : (c + 1) * QW, :QW],
            )
        upstream[...] = total.astype(BF)

    @pl.when(step < MEMBERS)
    def _():
        rows = seq_rows(step)
        cosine, sine = cos_ref[...], sin_ref[...]
        key2, value2 = doubled(kv_ref[...].astype(F32))
        key2, value2 = key2.astype(BF), value2.astype(BF)
        heads, lifted = head_rows(query_ref), head_rows(upstream.at[rows])
        probs = softmax_rows(heads, key2, mask_ref[0])
        grad_value = left_product(probs.astype(BF), lifted)
        grad_value = grad_value + pltpu.roll(grad_value, HEAD_DIM, 1)
        grad_probs = right_product(lifted, value2)
        inner = jnp.sum(grad_probs * probs, axis=-1, keepdims=True)
        grad_scores = (probs * (grad_probs - inner)).astype(BF)
        grad_query = dot(grad_scores, key2)
        for g in range(GROUPS // 2):
            v = pair_columns(grad_query, g) * score_scale
            v = (v * cosine - quarter_turn(v) * sine).astype(BF)
            grad_ref[:, g * LANES : (g + 1) * LANES] = v
            grads[rows, g * LANES : (g + 1) * LANES] = v
        grad_key = left_product(grad_scores, heads)
        v = (grad_key + pltpu.roll(grad_key, HEAD_DIM, 1)) * score_scale
        grad_key = v * cosine - quarter_turn(v) * sine
        v = jnp.where(lanes_of(v) < HEAD_DIM, grad_key, grad_value).astype(BF)
        grad_ref[:, QW:] = v
        grads[rows, QW:] = v

    @pl.when(step >= MEMBERS)
    def _():
        block = pl.ds(pl.multiple_of((step - MEMBERS) * PANEL, PANEL), PANEL)
        send_ref[:, :QW] = left_product(att_ref[...], middle_ref[:, block]).astype(BF)
        send_ref[:, QW:] = left_product(first_ref[:, block], grads[...]).astype(BF)


def all_of(shape):
    return pl.BlockSpec(shape, lambda s: (0,) * len(shape), pipeline_mode=pl.Buffered(1))


def by_seq(width):
    return pl.BlockSpec((ROWS, width), lambda s: (jnp.minimum(s, MEMBERS - 1), 0))


MASK_BLOCK = pl.BlockSpec((1, ROWS, ROWS), lambda s: (jnp.minimum(s, MEMBERS - 1), 0, 0))


def attention(first_low, weights, cosine, sine, mask):
    half = pl.BlockSpec((SLOTS // 2, PANEL), lambda s: (0, jnp.maximum(s - MEMBERS, 0)))
    return pl.pallas_call(
        attention_kernel,
        grid=(2 * MEMBERS,),
        in_specs=[
            all_of((SLOTS, D)),
            all_of((D, QW + QKVW)),
            by_seq(LANES),
            by_seq(LANES),
            MASK_BLOCK,
        ],
        out_specs=[by_seq(QW), by_seq(LANES), by_seq(QW), half, half],
        out_shape=[
            jax.ShapeDtypeStruct((SLOTS, QW), BF),
            jax.ShapeDtypeStruct((SLOTS, LANES), BF),
            jax.ShapeDtypeStruct((SLOTS, QW), BF),
            jax.ShapeDtypeStruct((SLOTS // 2, D), F32),
            jax.ShapeDtypeStruct((SLOTS // 2, D), BF),
        ],
        scratch_shapes=[pltpu.VMEM((SLOTS, QKVW), F32), pltpu.VMEM((SLOTS, QW), BF)],
        compiler_params=pltpu.CompilerParams(vmem_limit_bytes=40 * 2**20),
        cost_estimate=pl.CostEstimate(
            flops=3 * 10**9, bytes_accessed=12 * 10**6, transcendentals=10**6
        ),
        name="attention",
    )(first_low, weights, cosine, sine, mask)


def attention_back(middle_all, weights, first_low, attended, query, kv, cosine, sine, mask):
    return pl.pallas_call(
        attention_back_kernel,
        grid=(2 * MEMBERS,),
        in_specs=[
            all_of((SLOTS, D)),
            all_of((D, QW + QKVW)),
            all_of((SLOTS, D)),
            all_of((SLOTS, QW)),
            by_seq(QW),
            by_seq(LANES),
            by_seq(LANES),
            by_seq(LANES),
            MASK_BLOCK,
        ],
        out_specs=[
            by_seq(QKVW),
            pl.BlockSpec((PANEL, QW + QKVW), lambda s: (jnp.maximum(s - MEMBERS, 0), 0)),
        ],
        out_shape=[
            jax.ShapeDtypeStruct((SLOTS, QKVW), BF),
            jax.ShapeDtypeStruct((D, QW + QKVW), BF),
        ],
        scratch_shapes=[pltpu.VMEM((SLOTS, QW), BF), pltpu.VMEM((SLOTS, QKVW), BF)],
        compiler_params=pltpu.CompilerParams(vmem_limit_bytes=40 * 2**20),
        cost_estimate=pl.CostEstimate(
            flops=5 * 10**9, bytes_accessed=16 * 10**6, transcendentals=10**6
        ),
        name="attention_back",
    )(middle_all, weights, first_low, attended, query, kv, cosine, sine, mask)


def first_kernel(grad_ref, weight_ref, rows_ref, rms_ref, near_ref, core_ref, gain_ref):
    grad = right_product(grad_ref[...], weight_ref[:, QW:])
    normed = rows_ref[...].astype(F32) * rms_ref[...]
    gain_ref[...] = jnp.sum(grad * normed, axis=0, keepdims=True)
    near_ref[...] = grad[: SLOTS // 2]
    core_ref[...] = grad[SLOTS // 2 :].astype(BF)


def first_grad(grad_qkv, weights, rows_in, rms):
    half = pl.BlockSpec((SLOTS // 2, PANEL), lambda i: (0, i))
    return pl.pallas_call(
        first_kernel,
        grid=(4,),
        in_specs=[
            all_of((SLOTS, QKVW)),
            pl.BlockSpec((PANEL, QW + QKVW), lambda i: (i, 0)),
            pl.BlockSpec((SLOTS, PANEL), lambda i: (0, i)),
            all_of((SLOTS, 1)),
        ],
        out_specs=[half, half, pl.BlockSpec((1, PANEL), lambda i: (0, i))],
        out_shape=[
            jax.ShapeDtypeStruct((SLOTS // 2, D), F32),
            jax.ShapeDtypeStruct((SLOTS // 2, D), BF),
            jax.ShapeDtypeStruct((1, D), F32),
        ],
        compiler_params=pltpu.CompilerParams(vmem_limit_bytes=32 * 2**20),
        cost_estimate=pl.CostEstimate(
            flops=10**6, bytes_accessed=10**5, transcendentals=0
        ),
        name="first_grad",
    )(grad_qkv, weights, rows_in, rms)


def update_kernel(
    at_ref,
    own_ref,
    near_ref,
    core_ref,
    moments_ref,
    moment_ref,
    query_ref,
    key_ref,
    value_ref,
    output_ref,
    query_moved,
    key_moved,
    value_moved,
    output_moved,
    query_new,
    key_new,
    value_new,
    output_new,
    moved,
):
    width = QKVW + PANEL
    own = 0.5 * moment_ref[...] + 0.5 * own_ref[...]
    query_moved[...] = own[:, :QW]
    key_moved[...] = own[:, QW : QW + KW]
    value_moved[...] = own[:, QW + KW : QKVW]
    output_moved[...] = own[:, QKVW:]
    rows = near_ref.shape[0]
    moved[:rows] = 0.5 * moments_ref[:rows].astype(F32) + 0.5 * near_ref[...].astype(F32)
    moved[rows:] = 0.5 * moments_ref[rows:].astype(F32) + 0.5 * core_ref[:, :width].astype(F32)
    pairs = []
    for a, order in enumerate((0, 2, 1, 3)):
        slot = pl.ds(pl.multiple_of((at_ref[0] ^ order) * W_ROWS, W_ROWS), W_ROWS)
        columns = slice(a * QW, (a + 1) * QW)
        query_new[:, columns] = query_ref[:, columns] - learn_rate * moved[slot, :QW]
        output_new[:, columns] = output_ref[:, columns] - learn_rate * moved[slot, QKVW:]
        pairs.append(moved[slot, QW:QKVW])
    for a in (0, 2):
        even, odd = pairs[a], pairs[a + 1]
        left = lanes_of(even) < HEAD_DIM
        key = jnp.where(left, even, pltpu.roll(odd, HEAD_DIM, 1))
        value = jnp.where(left, pltpu.roll(even, HEAD_DIM, 1), odd)
        columns = slice(a * KW, (a + 2) * KW)
        key_new[:, columns] = key_ref[:, columns] - learn_rate * key
        value_new[:, columns] = value_ref[:, columns] - learn_rate * value


def attention_update(at, own, near, core, moments, moment, weights):
    shapes = [(W_ROWS, w) for w in (QW, KW, KW, QW)] + [w.shape for w in weights]
    vmem = pl.BlockSpec(memory_space=pltpu.VMEM)
    return pl.pallas_call(
        update_kernel,
        in_specs=[pl.BlockSpec(memory_space=pltpu.SMEM)] + [vmem] * 9,
        out_specs=[vmem] * 8,
        out_shape=[jax.ShapeDtypeStruct(shape, F32) for shape in shapes],
        scratch_shapes=[pltpu.VMEM((MEMBERS * W_ROWS, QKVW + PANEL), F32)],
        compiler_params=pltpu.CompilerParams(vmem_limit_bytes=16 * 2**20),
        cost_estimate=pl.CostEstimate(
            flops=10**6, bytes_accessed=6 * 10**6, transcendentals=0
        ),
        name="attention_update",
    )(at, own, near, core, moments, moment, *weights)


def rounded_gain(gain):
    return lax.optimization_barrier(gain.astype(BF)).astype(F32)


def inverse_rms(v):
    return lax.rsqrt(jnp.mean(v * v, axis=-1, keepdims=True) + epsilon)


def norm_back(v, gain, grad):
    r = inverse_rms(v)
    n = v * r
    scaled = grad * gain
    return r * (scaled - n * jnp.mean(scaled * n, axis=-1, keepdims=True)), n


def panels(gate, up):
    blocks = []
    for at in range(0, UNITS, 256):
        blocks += [gate[:, at : at + 256], up[:, at : at + 256]]
    return jnp.concatenate(blocks, axis=1)


def unpanels(v):
    gate = [v[:, :256], v[:, 512:768], v[:, 1024 : 1024 + LAST]]
    up = [v[:, 256:512], v[:, 768:1024], v[:, 1024 + LAST :]]
    return jnp.concatenate(gate, axis=1), jnp.concatenate(up, axis=1)


def on_device(
    tokens,
    cotangent,
    segment_ids,
    positions,
    padding,
    attn_gain,
    query_weight,
    key_weight,
    value_weight,
    output_weight,
    mlp_gain,
    gate_weight,
    up_weight,
    down_weight,
    attn_moment,
    query_moment,
    key_moment,
    value_moment,
    output_moment,
    mlp_moment,
    gate_moment,
    up_moment,
    down_moment,
):
    member = lax.axis_index("grp")
    place = lax.axis_index("dp")
    z, y, low = place // 8, (place // 2) % 4, (place % 2) == 0

    def mine(weight, width):
        return lax.dynamic_slice_in_dim(weight, member * width, width, 1).astype(BF)

    attn_shard = jnp.concatenate(
        [mine(query_weight, QW), mine(key_weight, KW), mine(value_weight, KW)], axis=1
    )
    attn_shard = jnp.concatenate(
        [turn_pair(mine(output_weight, QW), low), pair_x(attn_shard, low)], axis=1
    )
    attn_full = plane_gather(attn_shard)

    gate_mine, up_mine = mine(gate_weight, FW), mine(up_weight, FW)
    first = panels(gate_mine[:, :UNITS], up_mine[:, :UNITS])
    second = panels(gate_mine[:, UNITS:], up_mine[:, UNITS:])
    kept, given = jnp.where(low, first, second), jnp.where(low, second, first)
    gu_shard = in_order(kept, swap_x(given), low)
    tail = gu_shard[:, 2 * PANEL :]
    pieces = [
        gu_shard[:, :PANEL],
        gu_shard[:, PANEL : 2 * PANEL],
        jnp.concatenate([tail[:W_ROWS, :256], tail[W_ROWS:, :256]], axis=1),
        jnp.concatenate([tail[32 * h : 32 * h + 32, 256:] for h in range(4)], axis=1),
        everywhere(mine(down_weight, PANEL), OWNED),
    ]
    mlp_full = plane_gather(jnp.concatenate(pieces, axis=0)).reshape(16, SHARD, PANEL)

    places = jnp.stack([segment_ids, positions, padding])[None]
    rows_in = group_gather(tokens)
    own_moment = jnp.concatenate(
        [query_moment, key_moment, value_moment, output_moment], axis=1
    )
    moments = own_moment.astype(BF)
    places, moments, upstream = lax.optimization_barrier(
        (
            jnp.concatenate([places, swap_far(places)], axis=0),
            jnp.concatenate([moments, swap_far(moments)], axis=0),
            cotangent,
        )
    )
    cot_four, cot_core = row_gather(upstream)
    places = jnp.concatenate([places, swap_core(places)], axis=0)
    moments = jnp.concatenate([moments, swap_core(moments)], axis=0)
    segments, spots, pads = places[:, 0], places[:, 1], places[:, 2]

    first_gain = rounded_gain(attn_gain)
    second_gain = rounded_gain(mlp_gain)
    inputs = rows_in.astype(F32)
    rms = inverse_rms(inputs)
    first_low = (inputs * rms * first_gain).astype(BF)

    half = HEAD_DIM // 2
    freq = 10000.0 ** (-(jnp.arange(half, dtype=F32) * 2.0 / HEAD_DIM))
    angles = spots.reshape(SLOTS, 1).astype(F32) * jnp.tile(freq, LANES // half)[None]
    cosine, sine = jnp.cos(angles), jnp.sin(angles)
    column = jnp.arange(ROWS, dtype=jnp.int32)
    allowed = jnp.logical_and(
        jnp.logical_and(
            segments[:, :, None] == segments[:, None, :],
            (column[None, :] <= column[:, None])[None],
        ),
        jnp.logical_or(pads[:, None, :] == 1, (column[None, :] == column[:, None])[None]),
    ).astype(F32)

    attn_full, first_low, cosine, sine, allowed, cot_four, moments = lax.optimization_barrier(
        (attn_full, first_low, cosine, sine, allowed, cot_four, moments)
    )
    query_rot, kv, attended, near, core = attention(first_low, attn_full, cosine, sine, allowed)
    middle = tokens.astype(F32) + group_scatter_far(near + swap_core(core).astype(F32))
    second_low = (middle * inverse_rms(middle) * second_gain).astype(BF)
    four, core_four = row_gather(second_low)
    core_four, cot_core = lax.optimization_barrier((core_four, cot_core))
    grad_gu, active, send = mlp_grads(four, core_four, cot_four, cot_core, mlp_full)
    mlp_sum = plane_scatter(send.reshape(16 * SHARD, PANEL))

    second_core = swap_core(second_grad(grad_gu, mlp_full, 1)[0])
    second_rest, second_own = second_grad(grad_gu, mlp_full, 0)
    grad_second = row_scatter(second_own, second_rest, second_core)
    back, n_second = norm_back(middle, second_gain, grad_second)
    mlp_gain_part = jnp.sum(grad_second * n_second, axis=0)
    grad_middle = cotangent.astype(F32) + back
    middle_all = group_gather(grad_middle.astype(BF))
    down_core, down_rest, down_own = down_product(active, mlp_full)
    middle_all, down_core = lax.optimization_barrier((middle_all, swap_core(down_core)))
    grad_qkv, attn_send = attention_back(
        middle_all, attn_full, first_low, attended, query_rot, kv, cosine, sine, allowed
    )
    attn_sum = plane_scatter(attn_send)

    grad_qkv, mlp_sum, down_core = lax.optimization_barrier((grad_qkv, mlp_sum, down_core))
    block_output = (middle + row_scatter(down_own, down_rest, down_core)).astype(BF)
    near, core, attn_gain_part = first_grad(grad_qkv, attn_full, rows_in, rms)
    gains = jnp.concatenate([attn_gain_part, mlp_gain_part[None]], axis=0).reshape(32, LANES)
    gains = gains + sum(lax.ppermute(gains, "dp", p) for p in RING_Z)
    near = near + swap_core(core).astype(F32)
    first_far = swap_far(near[ROWS:].astype(BF))

    mine_at = (member // 2) + 2 * (member % 2)

    def by_member(slots):
        return [
            lax.dynamic_index_in_dim(slots, mine_at ^ at, 0, keepdims=False) for at in (0, 2, 1, 3)
        ]

    def updated(weight, columns, start, size):
        moved = jnp.concatenate([block[:, start : start + size] for block in columns], axis=1)
        return weight - learn_rate * moved.astype(F32)

    wide, narrow = mlp_sum[256:320], mlp_sum[320:352]
    gu_part = jnp.concatenate(
        [
            mlp_sum[:128],
            mlp_sum[128:256],
            jnp.concatenate([wide[:, :256], wide[:, 256:]], axis=0),
            jnp.concatenate([narrow[:, h * LANES : (h + 1) * LANES] for h in range(4)], axis=0),
        ],
        axis=1,
    )
    kept, given = halves(gu_part, low)
    other = swap_x(given)
    first = unpanels(jnp.where(low, kept, other))
    second = unpanels(jnp.where(low, other, kept))
    gate_rows = jnp.concatenate([first[0], second[0]], axis=1).astype(F32)
    up_rows = jnp.concatenate([first[1], second[1]], axis=1).astype(F32)
    down_rows = everywhere(mlp_sum[352:], RETURN).astype(F32)
    gate_momentum = 0.5 * gate_moment + 0.5 * gate_rows
    up_momentum = 0.5 * up_moment + 0.5 * up_rows
    down_momentum = 0.5 * down_moment + 0.5 * down_rows
    gu_moved = jnp.concatenate([gate_momentum, up_momentum], axis=1).astype(BF)
    gu_moved, block_output, gains = lax.optimization_barrier((gu_moved, block_output, gains))
    gains = gains + sum(lax.ppermute(gains, "dp", p) for p in RING_Y)
    gu_far = swap_far(gu_moved)
    gu_far, first_far = lax.optimization_barrier((gu_far, first_far))
    gu_moved = jnp.concatenate([gu_moved, gu_far], axis=0)
    gu_core = swap_core(gu_moved)
    down_moved = group_gather(down_momentum.astype(BF))
    attn_sum, gains, first_far, block_output, gu_core, down_moved = lax.optimization_barrier(
        (attn_sum, gains, first_far, block_output, gu_core, down_moved)
    )
    back, _ = norm_back(tokens.astype(F32), first_gain, near[:ROWS] + first_far.astype(F32))
    input_grad = grad_middle + back
    gu_moved = jnp.concatenate([gu_moved, gu_core], axis=0)
    gu_moved = by_member(gu_moved.reshape(MEMBERS, W_ROWS, GUW))
    down_moved = by_member(down_moved.reshape(MEMBERS, DOWN_ROWS, PANEL))
    gate_updated = updated(gate_weight, gu_moved, 0, FW)
    up_updated = updated(up_weight, gu_moved, FW, FW)
    down_updated = updated(down_weight, down_moved, 0, PANEL)

    turned = everywhere(attn_sum[:, :QW], TURN)
    both = jnp.concatenate([attn_sum[:, QW:], turned], axis=1)
    gains = two_parts(gains)
    kept, given = halves(both, low)
    width = QKVW + PANEL
    near = swap_x(jnp.concatenate([given, gains], axis=1))
    far = swap_far(jnp.concatenate([kept, gains], axis=1))
    both_far = far_x(jnp.concatenate([given, gains], axis=1))
    own_total = kept.astype(F32) + near[:, :width].astype(F32)
    far_total = far[:, :width].astype(F32) + both_far[:, :width].astype(F32)
    gains = sum(one_part(part) for part in (gains, near[:, width:], far[:, width:], both_far[:, width:]))
    totals = jnp.concatenate([own_total, far_total], axis=0).astype(BF)
    rider = jnp.concatenate([two_parts(gains), jnp.zeros((W_ROWS, LANES), BF)], axis=0)
    other = swap_core(jnp.concatenate([totals, rider], axis=1))
    gains = gains + one_part(other[:W_ROWS, width:])
    attn_done = attention_update(
        mine_at.astype(jnp.int32).reshape(1),
        own_total,
        totals,
        other,
        moments,
        own_moment,
        (query_weight, key_weight, value_weight, output_weight),
    )

    gains = 0.5 * jnp.stack([attn_moment, mlp_moment]) + 0.5 * gains.reshape(2, D)
    return (
        block_output,
        input_grad,
        gains[0],
        *attn_done[:4],
        gains[1],
        gate_momentum,
        up_momentum,
        down_momentum,
        attn_gain - learn_rate * gains[0],
        *attn_done[4:],
        mlp_gain - learn_rate * gains[1],
        gate_updated,
        up_updated,
        down_updated,
    )


def solution(mesh):
    rows = P(("grp", "dp"), None)
    flat = P(("grp", "dp"))
    weight = P("dp", None)
    moment = P("dp", "grp")
    everyone = P()
    weights = (everyone,) + (weight,) * 4 + (everyone,) + (weight,) * 3
    moments = (everyone,) + (moment,) * 4 + (everyone,) + (moment,) * 3
    return jax.shard_map(
        on_device,
        mesh=mesh,
        in_specs=(rows, rows, flat, flat, flat) + weights + moments,
        out_specs=(rows, rows) + moments + weights,
        check_vma=False,
    )
```

```python
import jax
import jax.numpy as jnp
from jax import lax
from jax.experimental import pallas as pl
from jax.experimental.pallas import tpu as pltpu
from jax.sharding import PartitionSpec as P

D = 2048
HEAD_DIM = 64
GROUPS = 8
ROWS = 128
MEMBERS = 4
SLOTS = ROWS * MEMBERS
QW = 512
KW = 64
QKVW = QW + 2 * KW
FW = 1408
GUW = 2 * FW
PANEL = 512
DOWN_ROWS = 176
W_ROWS = 64

epsilon = 1e-05
learn_rate = 0.005
score_scale = 0.125

BF = jnp.bfloat16
F32 = jnp.float32

PLANES = [[z * 8 + y * 2 + x for z in range(4) for y in range(4)] for x in range(2)]
SWAP_X = [(i, i ^ 1) for i in range(32)]
SWAP_CORE = [(m, m ^ 1) for m in range(4)]
SWAP_FAR = [(m, m ^ 2) for m in range(4)]
SWAP_FAR_X = [(m * 32 + i, (m ^ 2) * 32 + (i ^ 1)) for m in range(4) for i in range(32)]
MZQ = [(m, z, q) for m in range(4) for z in range(4) for q in range(8)]


def spot(m, z, q):
    return m * 32 + z * 8 + q


TURN = [(spot(m, z, q), spot(z, m, q)) for m, z, q in MZQ]
TURN_X = [(spot(m, z, q), spot(z, m, q ^ 1)) for m, z, q in MZQ]
TURN_IN = [[(spot(m, z, q), spot((z + k) % 4, m, q)) for m, z, q in MZQ] for k in range(4)]
OWNED = [(spot(m, z, q), spot(z, m, (q & 3) * 2 + (q >> 2))) for m, z, q in MZQ]
RETURN = [(b, a) for a, b in OWNED]


def ring(place, k):
    return [(i, i + ((i // place + k) % 4 - i // place % 4) * place) for i in range(32)]


RING_Z = [ring(8, k) for k in (1, 2, 3)]
RING_Y = [ring(2, k) for k in (1, 2, 3)]


def swap_x(v):
    return lax.ppermute(v, "dp", SWAP_X)


def swap_core(v):
    return lax.ppermute(v, "grp", SWAP_CORE)


def swap_far(v):
    return lax.ppermute(v, "grp", SWAP_FAR)


def everywhere(v, pairs):
    return lax.ppermute(v, ("grp", "dp"), pairs)


def plane_gather(v):
    return lax.all_gather(v, "dp", axis=0, tiled=True, axis_index_groups=PLANES)


def plane_scatter(v):
    return lax.psum_scatter(
        v, "dp", scatter_dimension=0, tiled=True, axis_index_groups=PLANES
    )


def ring_scatter(v, pairs, at, extra=None):
    rows = v.shape[0] // 4

    def chunk(k):
        part = lax.dynamic_slice_in_dim(v, lax.rem(at + k, 4) * rows, rows, 0)
        return part if extra is None else jnp.concatenate([part, extra], axis=1)

    total = chunk(0).astype(F32)
    for k, p in enumerate(pairs):
        total = total + lax.ppermute(chunk(k + 1), "dp", p).astype(F32)
    return total


def group_gather(v):
    pair = jnp.concatenate([v, swap_far(v)], axis=0)
    return jnp.concatenate([pair, swap_core(pair)], axis=0)


def group_scatter_far(near):
    return near[:ROWS] + swap_far(near[ROWS:].astype(BF)).astype(F32)


def far_x(v):
    return everywhere(v, SWAP_FAR_X)


def row_gather(v):
    four = jnp.concatenate([v, swap_x(v), swap_far(v), far_x(v)], axis=0)
    return four, swap_core(four)


def row_scatter(own, rest, core):
    own = own + core[:ROWS].astype(F32)
    rest = (rest.astype(F32) + core[ROWS:].astype(F32)).astype(BF)
    low_part, far_part, far_x_part = (rest[k * ROWS : (k + 1) * ROWS] for k in range(3))
    return (
        own
        + swap_x(low_part).astype(F32)
        + swap_far(far_part).astype(F32)
        + far_x(far_x_part).astype(F32)
    )


def in_order(own, other, low):
    return jnp.concatenate([jnp.where(low, own, other), jnp.where(low, other, own)], axis=0)


def pair_x(v, low):
    return in_order(v, swap_x(v), low)


def turn_pair(v, low):
    return in_order(everywhere(v, TURN), everywhere(v, TURN_X), low)


def halves(v, low):
    rows = v.shape[0] // 2
    return jnp.where(low, v[:rows], v[rows:]), jnp.where(low, v[rows:], v[:rows])


def two_parts(v):
    high = lax.reduce_precision(v, 8, 7)
    return jnp.concatenate([high.astype(BF), (v - high).astype(BF)], axis=0)


def one_part(v):
    rows = v.shape[0] // 2
    return v[:rows].astype(F32) + v[rows:].astype(F32)


def dot(left, right):
    return jnp.dot(left, right, preferred_element_type=F32)


def left_product(left, right):
    return lax.dot_general(left, right, (((0,), (0,)), ((), ())), preferred_element_type=F32)


def right_product(left, right):
    return lax.dot_general(left, right, (((1,), (1,)), ((), ())), preferred_element_type=F32)


ALL = 1024
UNITS = 704
LAST = 192
SHARD = 528


TAIL = [(256, 64, 256 * h, 64 * h, 0, 256) for h in range(2)]
TAIL += [(320, 32, 128 * h, 32 * h, 256, 128) for h in range(4)]


def tail_pieces(shard):
    for row, rows, column, at, start, width in TAIL:
        yield (
            shard.at[:, pl.ds(row, rows), pl.ds(column, width)],
            (slice(None), pl.ds(at, rows), pl.ds(start, width)),
        )


def tail_loads(full, tail, sems):
    return [
        pltpu.make_async_copy(src, tail.at[at], sems.at[i])
        for i, (src, at) in enumerate(tail_pieces(full))
    ]


def down_blocks(shard, down):
    return [
        (shard.at[4 * c + j, pl.ds(352, 176), :], down.at[c, pl.ds(176 * j, 176), :])
        for c in range(4)
        for j in range(4)
    ]


def mlp_kernel(
    four,
    core,
    cot_four,
    cot_core,
    panel_ref,
    full,
    ggu_ref,
    act_ref,
    send,
    down,
    tail,
    gpan,
    gtail,
    gdown,
    four_ref,
    core_ref,
    cot_four_ref,
    cot_core_ref,
    in_sem,
    row_sem,
    tail_sem,
    pan_sem,
    out_sem,
):
    step = pl.program_id(0)
    loads = [
        pltpu.make_async_copy(src, dst, in_sem.at[i])
        for i, (src, dst) in enumerate(
            [(cot_four, cot_four_ref), (cot_core, cot_core_ref)] + down_blocks(full, down)
        )
    ]
    rows_in = [
        pltpu.make_async_copy(src, dst, row_sem.at[i])
        for i, (src, dst) in enumerate([(four, four_ref), (core, core_ref)])
    ]
    tails = tail_loads(full, tail, tail_sem)

    @pl.when(step == 0)
    def _():
        for copy in rows_in + loads + tails:
            copy.start()
        for copy in rows_in + loads:
            copy.wait()

    def panel_out(at):
        return pltpu.make_async_copy(
            gpan.at[at], send.at[:, pl.ds(128 * at, 128), :], pan_sem.at[at]
        )

    def block(weights, start, width, store):
        halves_of = [dot(ref[...], weights) for ref in (four_ref, core_ref)]

        for half, (h, c_ref) in enumerate(zip(halves_of, (cot_four_ref, cot_core_ref))):
            rows = pl.ds(half * (ALL // 2), ALL // 2)
            gate, up = h[:, :width], h[:, width:]
            prod = right_product(c_ref[:, :PANEL], down[0, pl.ds(start, width), :])
            for c in range(1, 4):
                prod += right_product(
                    c_ref[:, c * PANEL : (c + 1) * PANEL], down[c, pl.ds(start, width), :]
                )
            sig = 1.0 / (1.0 + jnp.exp(-gate))
            silu = gate * sig
            act_ref[rows, :width] = (silu * up).astype(BF)
            ggu_ref[rows, :width] = (prod * up * sig * (1.0 + gate * (1.0 - sig))).astype(BF)
            ggu_ref[rows, width : 2 * width] = (prod * silu).astype(BF)
        for c in range(4):
            columns = slice(c * PANEL, (c + 1) * PANEL)
            grads = left_product(act_ref[: ALL // 2, :width], cot_four_ref[:, columns])
            grads += left_product(act_ref[ALL // 2 :, :width], cot_core_ref[:, columns])
            gdown[c, pl.ds(start, width), :] = grads.astype(BF)
        grads = left_product(four_ref[...], ggu_ref[: ALL // 2, : 2 * width])
        grads += left_product(core_ref[...], ggu_ref[ALL // 2 :, : 2 * width])
        store(grads.astype(BF))

    @pl.when(step < 2)
    def _():
        def store(grads):
            gpan[step] = grads.reshape(16, 128, PANEL)

        block(panel_ref[...].reshape(D, PANEL), pl.multiple_of(256 * step, 256), 256, store)
        panel_out(step).start()

    @pl.when(step == 2)
    def _():
        def store(grads):
            gtail[...] = grads.reshape(16, 128, 2 * LAST)

        for copy in tails:
            copy.wait()
        block(tail[...].reshape(D, 2 * LAST), 512, LAST, store)
        outs = [
            pltpu.make_async_copy(gtail.at[at], dst, tail_sem.at[i])
            for i, (dst, at) in enumerate(tail_pieces(send))
        ]
        outs += [
            pltpu.make_async_copy(src, dst, out_sem.at[i])
            for i, (dst, src) in enumerate(down_blocks(send, gdown))
        ]
        for copy in outs:
            copy.start()
        for copy in outs + [panel_out(0), panel_out(1)]:
            copy.wait()


def mlp_grads(four, core, cot_four, cot_core, full):
    return pl.pallas_call(
        mlp_kernel,
        grid=(3,),
        in_specs=[pl.BlockSpec(memory_space=pl.ANY)] * 4
        + [
            pl.BlockSpec((16, 128, PANEL), lambda i: (0, jnp.minimum(i, 1), 0)),
            pl.BlockSpec(memory_space=pl.ANY),
        ],
        out_specs=[
            pl.BlockSpec((ALL, 512), lambda i: (0, i)),
            pl.BlockSpec((ALL, 256), lambda i: (0, i)),
            pl.BlockSpec(memory_space=pl.ANY),
        ],
        out_shape=[
            jax.ShapeDtypeStruct((ALL, 1536), BF),
            jax.ShapeDtypeStruct((ALL, 768), BF),
            jax.ShapeDtypeStruct((16, SHARD, PANEL), BF),
        ],
        scratch_shapes=[
            pltpu.VMEM((4, UNITS, PANEL), BF),
            pltpu.VMEM((16, 128, 2 * LAST), BF),
            pltpu.VMEM((2, 16, 128, PANEL), BF),
            pltpu.VMEM((16, 128, 2 * LAST), BF),
            pltpu.VMEM((4, UNITS, PANEL), BF),
            pltpu.VMEM((ALL // 2, D), BF),
            pltpu.VMEM((ALL // 2, D), BF),
            pltpu.VMEM((ALL // 2, D), BF),
            pltpu.VMEM((ALL // 2, D), BF),
            pltpu.SemaphoreType.DMA((18,)),
            pltpu.SemaphoreType.DMA((2,)),
            pltpu.SemaphoreType.DMA((6,)),
            pltpu.SemaphoreType.DMA((2,)),
            pltpu.SemaphoreType.DMA((16,)),
        ],
        compiler_params=pltpu.CompilerParams(vmem_limit_bytes=56 * 2**20),
        cost_estimate=pl.CostEstimate(
            flops=18 * 10**9, bytes_accessed=45 * 10**6, transcendentals=10**6
        ),
        name="mlp_grads",
    )(four, core, cot_four, cot_core, full, full)


def split_rows(total, rest_ref, own_ref=None):
    if own_ref is None:
        rest_ref[...] = total.astype(BF)
    else:
        own_ref[...] = total[:ROWS]
        rest_ref[...] = total[ROWS : ALL // 2].astype(BF)


def second_kernel(g_ref, panel_ref, wide_ref, narrow_ref, *outs):
    *outs, tail = outs
    for row, rows, column, at, start, width in TAIL:
        piece = wide_ref if row == 256 else narrow_ref
        tail[:, at : at + rows, start : start + width] = piece[:, :, column : column + width]
    total = right_product(g_ref[:, :PANEL], panel_ref[:, :128].reshape(PANEL, PANEL))
    total += right_product(
        g_ref[:, PANEL : 2 * PANEL], panel_ref[:, 128:].reshape(PANEL, PANEL)
    )
    total += right_product(
        g_ref[:, 2 * PANEL : 2 * PANEL + 2 * LAST], tail[...].reshape(PANEL, 2 * LAST)
    )
    split_rows(total, *outs)


def second_grad(ggu, full, half):
    rows = [ALL // 2] if half else [ALL // 2 - ROWS, ROWS]
    return pl.pallas_call(
        second_kernel,
        grid=(4,),
        in_specs=[
            pl.BlockSpec((ALL // 2, 1536), lambda i: (half, 0)),
            pl.BlockSpec((4, 256, PANEL), lambda i: (i, 0, 0)),
            pl.BlockSpec((4, 64, PANEL), lambda i: (i, 4, 0)),
            pl.BlockSpec((4, 32, PANEL), lambda i: (i, 10, 0)),
        ],
        out_specs=[pl.BlockSpec((r, PANEL), lambda i: (0, i)) for r in rows],
        out_shape=[jax.ShapeDtypeStruct((r, D), kind) for r, kind in zip(rows, (BF, F32))],
        scratch_shapes=[pltpu.VMEM((4, 128, 2 * LAST), BF)],
        compiler_params=pltpu.CompilerParams(vmem_limit_bytes=58 * 2**20),
        cost_estimate=pl.CostEstimate(
            flops=3 * 10**9, bytes_accessed=10 * 10**6, transcendentals=0
        ),
        name="second_grad",
    )(ggu, full, full, full)


def down_kernel(act_ref, down_ref, core_ref, rest_ref, own_ref):
    part = dot(act_ref[:, :UNITS], down_ref[...].reshape(UNITS, PANEL))
    split_rows(part, rest_ref, own_ref)
    core_ref[...] = part[ALL // 2 :].astype(BF)


def down_product(active, full):
    rows = [ALL // 2, ALL // 2 - ROWS, ROWS]
    return pl.pallas_call(
        down_kernel,
        grid=(4,),
        in_specs=[
            pl.BlockSpec((ALL, 768), lambda c: (0, 0)),
            pl.BlockSpec((4, 176, PANEL), lambda c: (c, 2, 0)),
        ],
        out_specs=[pl.BlockSpec((r, PANEL), lambda c: (0, c)) for r in rows],
        out_shape=[jax.ShapeDtypeStruct((r, D), kind) for r, kind in zip(rows, (BF, BF, F32))],
        compiler_params=pltpu.CompilerParams(vmem_limit_bytes=58 * 2**20),
        cost_estimate=pl.CostEstimate(
            flops=3 * 10**9, bytes_accessed=12 * 10**6, transcendentals=0
        ),
        name="down_product",
    )(active, full)


LANES = 128


def lanes_of(v):
    return lax.broadcasted_iota(jnp.int32, v.shape, v.ndim - 1)


def quarter_turn(v):
    first = lanes_of(v) % HEAD_DIM < HEAD_DIM // 2
    return jnp.where(first, -pltpu.roll(v, 96, 1), pltpu.roll(v, 32, 1))


def doubled(v):
    left = lanes_of(v) < HEAD_DIM
    other = pltpu.roll(v, HEAD_DIM, 1)
    return jnp.where(left, v, other), jnp.where(left, other, v)


def head_rows(ref):
    blocks = []
    for g in range(GROUPS // 2):
        v = ref[:, g * LANES : (g + 1) * LANES].astype(F32)
        left = lanes_of(v) < HEAD_DIM
        blocks += [jnp.where(left, v, 0.0), jnp.where(left, 0.0, v)]
    return jnp.concatenate(blocks, axis=0).astype(BF)


def pair_columns(v, g):
    even = v[2 * g * ROWS : (2 * g + 1) * ROWS]
    odd = v[(2 * g + 1) * ROWS : (2 * g + 2) * ROWS]
    return jnp.where(lanes_of(even) < HEAD_DIM, even, odd)


def softmax_rows(heads, key2, mask):
    scores = right_product(heads, key2).reshape(GROUPS, ROWS, ROWS) * score_scale
    masked = jnp.where(mask[None] > 0.0, scores, -1e30)
    top = jnp.max(masked, axis=-1, keepdims=True)
    total = top + jnp.log(jnp.sum(jnp.exp(masked - top), axis=-1, keepdims=True))
    return jnp.exp(masked - total).reshape(GROUPS * ROWS, ROWS)


def seq_rows(step):
    return pl.ds(pl.multiple_of(jnp.minimum(step, MEMBERS - 1) * ROWS, ROWS), ROWS)


def attention_kernel(
    first_ref,
    weight_ref,
    cos_ref,
    sin_ref,
    mask_ref,
    query_ref,
    kv_ref,
    att_ref,
    near_ref,
    core_ref,
    qkv,
    att,
):
    step = pl.program_id(0)

    @pl.when(step == 0)
    def _():
        qkv[...] = dot(first_ref[...], weight_ref[:, QW:])

    @pl.when(step < MEMBERS)
    def _():
        rows = seq_rows(step)
        cosine, sine = cos_ref[...], sin_ref[...]
        for g in range(GROUPS // 2):
            v = qkv[rows, g * LANES : (g + 1) * LANES]
            query_ref[:, g * LANES : (g + 1) * LANES] = (
                v * cosine + quarter_turn(v) * sine
            ).astype(BF)
        v = qkv[rows, QW:]
        kv = jnp.where(lanes_of(v) < HEAD_DIM, v * cosine + quarter_turn(v) * sine, v)
        kv_ref[...] = kv.astype(BF)
        key2, value2 = doubled(kv)
        probs = softmax_rows(head_rows(query_ref), key2.astype(BF), mask_ref[0])
        heads = dot(probs.astype(BF), value2.astype(BF))
        for g in range(GROUPS // 2):
            pair = pair_columns(heads, g).astype(BF)
            att_ref[:, g * LANES : (g + 1) * LANES] = pair
            att[rows, g * LANES : (g + 1) * LANES] = pair

    @pl.when(step >= MEMBERS)
    def _():
        block = pl.ds(pl.multiple_of((step - MEMBERS) * QW, QW), QW)
        part = dot(att[...], weight_ref[block, :QW])
        near_ref[...] = part[: SLOTS // 2]
        core_ref[...] = part[SLOTS // 2 :].astype(BF)


def attention_back_kernel(
    middle_ref,
    weight_ref,
    first_ref,
    att_ref,
    query_ref,
    kv_ref,
    cos_ref,
    sin_ref,
    mask_ref,
    grad_ref,
    send,
    upstream,
    grads,
    buffers,
    sems,
):
    step = pl.program_id(0)

    @pl.when(step == 0)
    def _():
        total = right_product(middle_ref[:, :PANEL], weight_ref[:QW, :QW])
        for c in range(1, 4):
            total += right_product(
                middle_ref[:, c * PANEL : (c + 1) * PANEL],
                weight_ref[c * QW : (c + 1) * QW, :QW],
            )
        upstream[...] = total.astype(BF)

    @pl.when(step < MEMBERS)
    def _():
        rows = seq_rows(step)
        cosine, sine = cos_ref[...], sin_ref[...]
        key2, value2 = doubled(kv_ref[...].astype(F32))
        key2, value2 = key2.astype(BF), value2.astype(BF)
        heads, lifted = head_rows(query_ref), head_rows(upstream.at[rows])
        probs = softmax_rows(heads, key2, mask_ref[0])
        grad_value = left_product(probs.astype(BF), lifted)
        grad_value = grad_value + pltpu.roll(grad_value, HEAD_DIM, 1)
        grad_probs = right_product(lifted, value2)
        inner = jnp.sum(grad_probs * probs, axis=-1, keepdims=True)
        grad_scores = (probs * (grad_probs - inner)).astype(BF)
        grad_query = dot(grad_scores, key2)
        for g in range(GROUPS // 2):
            v = pair_columns(grad_query, g) * score_scale
            v = (v * cosine - quarter_turn(v) * sine).astype(BF)
            grad_ref[:, g * LANES : (g + 1) * LANES] = v
            grads[rows, g * LANES : (g + 1) * LANES] = v
        grad_key = left_product(grad_scores, heads)
        v = (grad_key + pltpu.roll(grad_key, HEAD_DIM, 1)) * score_scale
        grad_key = v * cosine - quarter_turn(v) * sine
        v = jnp.where(lanes_of(v) < HEAD_DIM, grad_key, grad_value).astype(BF)
        grad_ref[:, QW:] = v
        grads[rows, QW:] = v

    @pl.when(step >= MEMBERS)
    def _():
        at = step - MEMBERS

        def leaving(i):
            slot = lax.rem(i, 2)
            rows = pl.ds(pl.multiple_of(i * PANEL, PANEL), PANEL)
            return pltpu.make_async_copy(buffers.at[slot], send.at[rows, :], sems.at[slot])

        @pl.when(at >= 2)
        def _():
            leaving(at - 2).wait()

        block = pl.ds(pl.multiple_of(at * PANEL, PANEL), PANEL)
        slot = lax.rem(at, 2)
        buffers[slot, :, :QW] = left_product(att_ref[...], middle_ref[:, block]).astype(BF)
        buffers[slot, :, QW:] = left_product(first_ref[:, block], grads[...]).astype(BF)
        leaving(at).start()

        @pl.when(at == MEMBERS - 1)
        def _():
            leaving(at - 1).wait()
            leaving(at).wait()


def all_of(shape):
    return pl.BlockSpec(shape, lambda s: (0,) * len(shape), pipeline_mode=pl.Buffered(1))


def by_seq(width):
    return pl.BlockSpec((ROWS, width), lambda s: (jnp.minimum(s, MEMBERS - 1), 0))


MASK_BLOCK = pl.BlockSpec((1, ROWS, ROWS), lambda s: (jnp.minimum(s, MEMBERS - 1), 0, 0))


def attention(first_low, weights, cosine, sine, mask):
    half = pl.BlockSpec((SLOTS // 2, PANEL), lambda s: (0, jnp.maximum(s - MEMBERS, 0)))
    return pl.pallas_call(
        attention_kernel,
        grid=(2 * MEMBERS,),
        in_specs=[
            all_of((SLOTS, D)),
            all_of((D, QW + QKVW)),
            by_seq(LANES),
            by_seq(LANES),
            MASK_BLOCK,
        ],
        out_specs=[by_seq(QW), by_seq(LANES), by_seq(QW), half, half],
        out_shape=[
            jax.ShapeDtypeStruct((SLOTS, QW), BF),
            jax.ShapeDtypeStruct((SLOTS, LANES), BF),
            jax.ShapeDtypeStruct((SLOTS, QW), BF),
            jax.ShapeDtypeStruct((SLOTS // 2, D), F32),
            jax.ShapeDtypeStruct((SLOTS // 2, D), BF),
        ],
        scratch_shapes=[pltpu.VMEM((SLOTS, QKVW), F32), pltpu.VMEM((SLOTS, QW), BF)],
        compiler_params=pltpu.CompilerParams(vmem_limit_bytes=40 * 2**20),
        cost_estimate=pl.CostEstimate(
            flops=3 * 10**9, bytes_accessed=12 * 10**6, transcendentals=10**6
        ),
        name="attention",
    )(first_low, weights, cosine, sine, mask)


def attention_back(middle_all, weights, first_low, attended, query, kv, cosine, sine, mask):
    return pl.pallas_call(
        attention_back_kernel,
        grid=(2 * MEMBERS,),
        in_specs=[
            all_of((SLOTS, D)),
            all_of((D, QW + QKVW)),
            all_of((SLOTS, D)),
            all_of((SLOTS, QW)),
            by_seq(QW),
            by_seq(LANES),
            by_seq(LANES),
            by_seq(LANES),
            MASK_BLOCK,
        ],
        out_specs=[
            by_seq(QKVW),
            pl.BlockSpec(memory_space=pltpu.HBM),
        ],
        out_shape=[
            jax.ShapeDtypeStruct((SLOTS, QKVW), BF),
            jax.ShapeDtypeStruct((D, QW + QKVW), BF),
        ],
        scratch_shapes=[
            pltpu.VMEM((SLOTS, QW), BF),
            pltpu.VMEM((SLOTS, QKVW), BF),
            pltpu.VMEM((2, PANEL, QW + QKVW), BF),
            pltpu.SemaphoreType.DMA((2,)),
        ],
        compiler_params=pltpu.CompilerParams(vmem_limit_bytes=40 * 2**20),
        cost_estimate=pl.CostEstimate(
            flops=5 * 10**9, bytes_accessed=16 * 10**6, transcendentals=10**6
        ),
        name="attention_back",
    )(middle_all, weights, first_low, attended, query, kv, cosine, sine, mask)


def first_kernel(grad_ref, weight_ref, rows_ref, rms_ref, near_ref, core_ref, gain_ref):
    grad = right_product(grad_ref[...], weight_ref[:, QW:])
    normed = rows_ref[...].astype(F32) * rms_ref[...]
    gain_ref[...] = jnp.sum(grad * normed, axis=0, keepdims=True)
    near_ref[...] = grad[: SLOTS // 2]
    core_ref[...] = grad[SLOTS // 2 :].astype(BF)


def first_grad(grad_qkv, weights, rows_in, rms):
    half = pl.BlockSpec((SLOTS // 2, PANEL), lambda i: (0, i))
    return pl.pallas_call(
        first_kernel,
        grid=(4,),
        in_specs=[
            all_of((SLOTS, QKVW)),
            pl.BlockSpec((PANEL, QW + QKVW), lambda i: (i, 0)),
            pl.BlockSpec((SLOTS, PANEL), lambda i: (0, i)),
            all_of((SLOTS, 1)),
        ],
        out_specs=[half, half, pl.BlockSpec((1, PANEL), lambda i: (0, i))],
        out_shape=[
            jax.ShapeDtypeStruct((SLOTS // 2, D), F32),
            jax.ShapeDtypeStruct((SLOTS // 2, D), BF),
            jax.ShapeDtypeStruct((1, D), F32),
        ],
        compiler_params=pltpu.CompilerParams(vmem_limit_bytes=32 * 2**20),
        cost_estimate=pl.CostEstimate(
            flops=14 * 10**8, bytes_accessed=12 * 10**6, transcendentals=0
        ),
        name="first_grad",
    )(grad_qkv, weights, rows_in, rms)


def update_kernel(
    at_ref,
    own_ref,
    near_ref,
    core_ref,
    moments_ref,
    moment_ref,
    query_ref,
    key_ref,
    value_ref,
    output_ref,
    query_moved,
    key_moved,
    value_moved,
    output_moved,
    query_new,
    key_new,
    value_new,
    output_new,
    moved,
):
    width = QKVW + PANEL
    own = 0.5 * moment_ref[...] + 0.5 * own_ref[...]
    query_moved[...] = own[:, :QW]
    key_moved[...] = own[:, QW : QW + KW]
    value_moved[...] = own[:, QW + KW : QKVW]
    output_moved[...] = own[:, QKVW:]
    rows = near_ref.shape[0]
    moved[:rows] = 0.5 * moments_ref[:rows].astype(F32) + 0.5 * near_ref[...].astype(F32)
    moved[rows:] = 0.5 * moments_ref[rows:].astype(F32) + 0.5 * core_ref[:, :width].astype(F32)
    pairs = []
    for a, order in enumerate((0, 2, 1, 3)):
        slot = pl.ds(pl.multiple_of((at_ref[0] ^ order) * W_ROWS, W_ROWS), W_ROWS)
        columns = slice(a * QW, (a + 1) * QW)
        query_new[:, columns] = query_ref[:, columns] - learn_rate * moved[slot, :QW]
        output_new[:, columns] = output_ref[:, columns] - learn_rate * moved[slot, QKVW:]
        pairs.append(moved[slot, QW:QKVW])
    for a in (0, 2):
        even, odd = pairs[a], pairs[a + 1]
        left = lanes_of(even) < HEAD_DIM
        key = jnp.where(left, even, pltpu.roll(odd, HEAD_DIM, 1))
        value = jnp.where(left, pltpu.roll(even, HEAD_DIM, 1), odd)
        columns = slice(a * KW, (a + 2) * KW)
        key_new[:, columns] = key_ref[:, columns] - learn_rate * key
        value_new[:, columns] = value_ref[:, columns] - learn_rate * value


def attention_update(at, own, near, core, moments, moment, weights):
    shapes = [(W_ROWS, w) for w in (QW, KW, KW, QW)] + [w.shape for w in weights]
    vmem = pl.BlockSpec(memory_space=pltpu.VMEM)
    return pl.pallas_call(
        update_kernel,
        in_specs=[pl.BlockSpec(memory_space=pltpu.SMEM)] + [vmem] * 9,
        out_specs=[vmem] * 8,
        out_shape=[jax.ShapeDtypeStruct(shape, F32) for shape in shapes],
        scratch_shapes=[pltpu.VMEM((MEMBERS * W_ROWS, QKVW + PANEL), F32)],
        compiler_params=pltpu.CompilerParams(vmem_limit_bytes=16 * 2**20),
        cost_estimate=pl.CostEstimate(
            flops=10**6, bytes_accessed=6 * 10**6, transcendentals=0
        ),
        name="attention_update",
    )(at, own, near, core, moments, moment, *weights)


def rounded_gain(gain):
    return lax.optimization_barrier(gain.astype(BF)).astype(F32)


def inverse_rms(v):
    return lax.rsqrt(jnp.mean(v * v, axis=-1, keepdims=True) + epsilon)


def norm_back(v, gain, grad):
    r = inverse_rms(v)
    n = v * r
    scaled = grad * gain
    return r * (scaled - n * jnp.mean(scaled * n, axis=-1, keepdims=True)), n


def panels(gate, up):
    blocks = []
    for at in range(0, UNITS, 256):
        blocks += [gate[:, at : at + 256], up[:, at : at + 256]]
    return jnp.concatenate(blocks, axis=1)


def unpanels(v):
    gate = [v[:, :256], v[:, 512:768], v[:, 1024 : 1024 + LAST]]
    up = [v[:, 256:512], v[:, 768:1024], v[:, 1024 + LAST :]]
    return jnp.concatenate(gate, axis=1), jnp.concatenate(up, axis=1)


def on_device(
    tokens,
    cotangent,
    segment_ids,
    positions,
    padding,
    attn_gain,
    query_weight,
    key_weight,
    value_weight,
    output_weight,
    mlp_gain,
    gate_weight,
    up_weight,
    down_weight,
    attn_moment,
    query_moment,
    key_moment,
    value_moment,
    output_moment,
    mlp_moment,
    gate_moment,
    up_moment,
    down_moment,
):
    member = lax.axis_index("grp")
    place = lax.axis_index("dp")
    z, y, low = place // 8, (place // 2) % 4, (place % 2) == 0

    def mine(weight, width):
        return lax.dynamic_slice_in_dim(weight, member * width, width, 1).astype(BF)

    attn_shard = jnp.concatenate(
        [mine(query_weight, QW), mine(key_weight, KW), mine(value_weight, KW)], axis=1
    )
    attn_shard = jnp.concatenate(
        [turn_pair(mine(output_weight, QW), low), pair_x(attn_shard, low)], axis=1
    )
    attn_full = plane_gather(attn_shard)

    gate_mine, up_mine = mine(gate_weight, FW), mine(up_weight, FW)
    first = panels(gate_mine[:, :UNITS], up_mine[:, :UNITS])
    second = panels(gate_mine[:, UNITS:], up_mine[:, UNITS:])
    kept, given = jnp.where(low, first, second), jnp.where(low, second, first)
    gu_shard = in_order(kept, swap_x(given), low)
    tail = gu_shard[:, 2 * PANEL :]
    pieces = [
        gu_shard[:, :PANEL],
        gu_shard[:, PANEL : 2 * PANEL],
        jnp.concatenate([tail[:W_ROWS, :256], tail[W_ROWS:, :256]], axis=1),
        jnp.concatenate([tail[32 * h : 32 * h + 32, 256:] for h in range(4)], axis=1),
        everywhere(mine(down_weight, PANEL), OWNED),
    ]
    mlp_full = plane_gather(jnp.concatenate(pieces, axis=0)).reshape(16, SHARD, PANEL)

    places = jnp.stack([segment_ids, positions, padding])[None]
    rows_in = group_gather(tokens)
    own_moment = jnp.concatenate(
        [query_moment, key_moment, value_moment, output_moment], axis=1
    )
    moments = own_moment.astype(BF)
    places, moments, upstream = lax.optimization_barrier(
        (
            jnp.concatenate([places, swap_far(places)], axis=0),
            jnp.concatenate([moments, swap_far(moments)], axis=0),
            cotangent,
        )
    )
    cot_four, cot_core = row_gather(upstream)
    places = jnp.concatenate([places, swap_core(places)], axis=0)
    moments = jnp.concatenate([moments, swap_core(moments)], axis=0)
    segments, spots, pads = places[:, 0], places[:, 1], places[:, 2]

    first_gain = rounded_gain(attn_gain)
    second_gain = rounded_gain(mlp_gain)
    inputs = rows_in.astype(F32)
    rms = inverse_rms(inputs)
    first_low = (inputs * rms * first_gain).astype(BF)

    half = HEAD_DIM // 2
    freq = 10000.0 ** (-(jnp.arange(half, dtype=F32) * 2.0 / HEAD_DIM))
    angles = spots.reshape(SLOTS, 1).astype(F32) * jnp.tile(freq, LANES // half)[None]
    cosine, sine = jnp.cos(angles), jnp.sin(angles)
    column = jnp.arange(ROWS, dtype=jnp.int32)
    allowed = jnp.logical_and(
        jnp.logical_and(
            segments[:, :, None] == segments[:, None, :],
            (column[None, :] <= column[:, None])[None],
        ),
        jnp.logical_or(pads[:, None, :] == 1, (column[None, :] == column[:, None])[None]),
    ).astype(F32)

    attn_full, first_low, cosine, sine, allowed, cot_four, moments = lax.optimization_barrier(
        (attn_full, first_low, cosine, sine, allowed, cot_four, moments)
    )
    query_rot, kv, attended, near, core = attention(first_low, attn_full, cosine, sine, allowed)
    middle = tokens.astype(F32) + group_scatter_far(near + swap_core(core).astype(F32))
    second_low = (middle * inverse_rms(middle) * second_gain).astype(BF)
    four, core_four = row_gather(second_low)
    core_four, cot_core = lax.optimization_barrier((core_four, cot_core))
    grad_gu, active, send = mlp_grads(four, core_four, cot_four, cot_core, mlp_full)
    mlp_sum = plane_scatter(send.reshape(16 * SHARD, PANEL))

    second_core = swap_core(second_grad(grad_gu, mlp_full, 1)[0])
    second_rest, second_own = second_grad(grad_gu, mlp_full, 0)
    grad_second = row_scatter(second_own, second_rest, second_core)
    back, n_second = norm_back(middle, second_gain, grad_second)
    mlp_gain_part = jnp.sum(grad_second * n_second, axis=0)
    grad_middle = cotangent.astype(F32) + back
    middle_all = group_gather(grad_middle.astype(BF))
    down_core, down_rest, down_own = down_product(active, mlp_full)
    middle_all, down_core = lax.optimization_barrier((middle_all, swap_core(down_core)))
    grad_qkv, attn_send = attention_back(
        middle_all, attn_full, first_low, attended, query_rot, kv, cosine, sine, allowed
    )
    attn_sum = plane_scatter(attn_send)

    grad_qkv, mlp_sum, down_core = lax.optimization_barrier((grad_qkv, mlp_sum, down_core))
    block_output = (middle + row_scatter(down_own, down_rest, down_core)).astype(BF)
    near, core, attn_gain_part = first_grad(grad_qkv, attn_full, rows_in, rms)
    gains = jnp.concatenate([attn_gain_part, mlp_gain_part[None]], axis=0).reshape(32, LANES)
    for pairs in (RING_Z, RING_Y):
        gains = gains + sum(lax.ppermute(gains, "dp", p) for p in pairs)
    near = near + swap_core(core).astype(F32)
    back, _ = norm_back(tokens.astype(F32), first_gain, group_scatter_far(near))
    input_grad = grad_middle + back

    mine_at = (member // 2) + 2 * (member % 2)

    def by_member(slots):
        return [
            lax.dynamic_index_in_dim(slots, mine_at ^ at, 0, keepdims=False) for at in (0, 2, 1, 3)
        ]

    def updated(weight, columns, start, size):
        moved = jnp.concatenate([block[:, start : start + size] for block in columns], axis=1)
        return weight - learn_rate * moved.astype(F32)

    wide, narrow = mlp_sum[256:320], mlp_sum[320:352]
    gu_part = jnp.concatenate(
        [
            mlp_sum[:128],
            mlp_sum[128:256],
            jnp.concatenate([wide[:, :256], wide[:, 256:]], axis=0),
            jnp.concatenate([narrow[:, h * LANES : (h + 1) * LANES] for h in range(4)], axis=0),
        ],
        axis=1,
    )
    kept, given = halves(gu_part, low)
    other = swap_x(given)
    first = unpanels(jnp.where(low, kept, other))
    second = unpanels(jnp.where(low, other, kept))
    gate_rows = jnp.concatenate([first[0], second[0]], axis=1).astype(F32)
    up_rows = jnp.concatenate([first[1], second[1]], axis=1).astype(F32)
    down_rows = everywhere(mlp_sum[352:], RETURN).astype(F32)
    gate_momentum = 0.5 * gate_moment + 0.5 * gate_rows
    up_momentum = 0.5 * up_moment + 0.5 * up_rows
    down_momentum = 0.5 * down_moment + 0.5 * down_rows
    gu_moved = jnp.concatenate([gate_momentum, up_momentum], axis=1).astype(BF)
    gu_moved, block_output = lax.optimization_barrier((gu_moved, block_output))
    gu_moved = by_member(group_gather(gu_moved).reshape(MEMBERS, W_ROWS, GUW))
    down_moved = by_member(
        group_gather(down_momentum.astype(BF)).reshape(MEMBERS, DOWN_ROWS, PANEL)
    )

    mlp_done = (
        gate_momentum,
        up_momentum,
        down_momentum,
        updated(gate_weight, gu_moved, 0, FW),
        updated(up_weight, gu_moved, FW, FW),
        updated(down_weight, down_moved, 0, PANEL),
    )
    attn_sum, gains, input_grad, block_output, mlp_done = lax.optimization_barrier(
        (attn_sum, gains, input_grad, block_output, mlp_done)
    )
    gate_momentum, up_momentum, down_momentum, gate_updated, up_updated, down_updated = mlp_done

    turned = everywhere(attn_sum[:, :QW], TURN)
    both = jnp.concatenate([attn_sum[:, QW:], turned], axis=1)
    gains = two_parts(gains)
    kept, given = halves(both, low)
    width = QKVW + PANEL
    near = swap_x(jnp.concatenate([given, gains], axis=1))
    far = swap_far(jnp.concatenate([kept, gains], axis=1))
    both_far = far_x(jnp.concatenate([given, gains], axis=1))
    own_total = kept.astype(F32) + near[:, :width].astype(F32)
    far_total = far[:, :width].astype(F32) + both_far[:, :width].astype(F32)
    gains = sum(one_part(part) for part in (gains, near[:, width:], far[:, width:], both_far[:, width:]))
    totals = jnp.concatenate([own_total, far_total], axis=0).astype(BF)
    rider = jnp.concatenate([two_parts(gains), jnp.zeros((W_ROWS, LANES), BF)], axis=0)
    other = swap_core(jnp.concatenate([totals, rider], axis=1))
    gains = gains + one_part(other[:W_ROWS, width:])
    attn_done = attention_update(
        mine_at.astype(jnp.int32).reshape(1),
        own_total,
        totals,
        other,
        moments,
        own_moment,
        (query_weight, key_weight, value_weight, output_weight),
    )

    gains = 0.5 * jnp.stack([attn_moment, mlp_moment]) + 0.5 * gains.reshape(2, D)
    return (
        block_output,
        input_grad,
        gains[0],
        *attn_done[:4],
        gains[1],
        gate_momentum,
        up_momentum,
        down_momentum,
        attn_gain - learn_rate * gains[0],
        *attn_done[4:],
        mlp_gain - learn_rate * gains[1],
        gate_updated,
        up_updated,
        down_updated,
    )


def solution(mesh):
    rows = P(("grp", "dp"), None)
    flat = P(("grp", "dp"))
    weight = P("dp", None)
    moment = P("dp", "grp")
    everyone = P()
    weights = (everyone,) + (weight,) * 4 + (everyone,) + (weight,) * 3
    moments = (everyone,) + (moment,) * 4 + (everyone,) + (moment,) * 3
    return jax.shard_map(
        on_device,
        mesh=mesh,
        in_specs=(rows, rows, flat, flat, flat) + weights + moments,
        out_specs=(rows, rows) + moments + weights,
        check_vma=False,
    )
```

```python
import jax
import jax.numpy as jnp
from jax import lax
from jax.experimental import pallas as pl
from jax.experimental.pallas import tpu as pltpu
from jax.sharding import PartitionSpec as P

D = 2048
HEAD_DIM = 64
GROUPS = 8
ROWS = 128
MEMBERS = 4
SLOTS = ROWS * MEMBERS
QW = 512
KW = 64
QKVW = QW + 2 * KW
FW = 1408
GUW = 2 * FW
PANEL = 512
DOWN_ROWS = 176
W_ROWS = 64

epsilon = 1e-05
learn_rate = 0.005
score_scale = 0.125

BF = jnp.bfloat16
F32 = jnp.float32

PLANES = [[z * 8 + y * 2 + x for z in range(4) for y in range(4)] for x in range(2)]
SWAP_X = [(i, i ^ 1) for i in range(32)]
SWAP_CORE = [(m, m ^ 1) for m in range(4)]
SWAP_FAR = [(m, m ^ 2) for m in range(4)]
SWAP_FAR_X = [(m * 32 + i, (m ^ 2) * 32 + (i ^ 1)) for m in range(4) for i in range(32)]
MZQ = [(m, z, q) for m in range(4) for z in range(4) for q in range(8)]


def spot(m, z, q):
    return m * 32 + z * 8 + q


TURN = [(spot(m, z, q), spot(z, m, q)) for m, z, q in MZQ]
TURN_X = [(spot(m, z, q), spot(z, m, q ^ 1)) for m, z, q in MZQ]
TURN_IN = [[(spot(m, z, q), spot((z + k) % 4, m, q)) for m, z, q in MZQ] for k in range(4)]
OWNED = [(spot(m, z, q), spot(z, m, (q & 3) * 2 + (q >> 2))) for m, z, q in MZQ]
RETURN = [(b, a) for a, b in OWNED]


def ring(place, k):
    return [(i, i + ((i // place + k) % 4 - i // place % 4) * place) for i in range(32)]


RING_Z = [ring(8, k) for k in (1, 2, 3)]
RING_Y = [ring(2, k) for k in (1, 2, 3)]


def swap_x(v):
    return lax.ppermute(v, "dp", SWAP_X)


def swap_core(v):
    return lax.ppermute(v, "grp", SWAP_CORE)


def swap_far(v):
    return lax.ppermute(v, "grp", SWAP_FAR)


def everywhere(v, pairs):
    return lax.ppermute(v, ("grp", "dp"), pairs)


def plane_gather(v):
    return lax.all_gather(v, "dp", axis=0, tiled=True, axis_index_groups=PLANES)


def plane_scatter(v):
    return lax.psum_scatter(
        v, "dp", scatter_dimension=0, tiled=True, axis_index_groups=PLANES
    )


def ring_scatter(v, pairs, at, extra=None):
    rows = v.shape[0] // 4

    def chunk(k):
        part = lax.dynamic_slice_in_dim(v, lax.rem(at + k, 4) * rows, rows, 0)
        return part if extra is None else jnp.concatenate([part, extra], axis=1)

    total = chunk(0).astype(F32)
    for k, p in enumerate(pairs):
        total = total + lax.ppermute(chunk(k + 1), "dp", p).astype(F32)
    return total


def group_gather(v):
    pair = jnp.concatenate([v, swap_far(v)], axis=0)
    return jnp.concatenate([pair, swap_core(pair)], axis=0)


def group_scatter_far(near):
    return near[:ROWS] + swap_far(near[ROWS:].astype(BF)).astype(F32)


def far_x(v):
    return everywhere(v, SWAP_FAR_X)


def row_gather(v):
    four = jnp.concatenate([v, swap_x(v), swap_far(v), far_x(v)], axis=0)
    return four, swap_core(four)


def row_scatter(own, rest, core):
    own = own + core[:ROWS].astype(F32)
    rest = (rest.astype(F32) + core[ROWS:].astype(F32)).astype(BF)
    low_part, far_part, far_x_part = (rest[k * ROWS : (k + 1) * ROWS] for k in range(3))
    return (
        own
        + swap_x(low_part).astype(F32)
        + swap_far(far_part).astype(F32)
        + far_x(far_x_part).astype(F32)
    )


def in_order(own, other, low):
    return jnp.concatenate([jnp.where(low, own, other), jnp.where(low, other, own)], axis=0)


def pair_x(v, low):
    return in_order(v, swap_x(v), low)


def turn_pair(v, low):
    return in_order(everywhere(v, TURN), everywhere(v, TURN_X), low)


def halves(v, low):
    rows = v.shape[0] // 2
    return jnp.where(low, v[:rows], v[rows:]), jnp.where(low, v[rows:], v[:rows])


def two_parts(v):
    high = lax.reduce_precision(v, 8, 7)
    return jnp.concatenate([high.astype(BF), (v - high).astype(BF)], axis=0)


def one_part(v):
    rows = v.shape[0] // 2
    return v[:rows].astype(F32) + v[rows:].astype(F32)


def dot(left, right):
    return jnp.dot(left, right, preferred_element_type=F32)


def left_product(left, right):
    return lax.dot_general(left, right, (((0,), (0,)), ((), ())), preferred_element_type=F32)


def right_product(left, right):
    return lax.dot_general(left, right, (((1,), (1,)), ((), ())), preferred_element_type=F32)


ALL = 1024
UNITS = 704
LAST = 192
SHARD = 528


TAIL = [(256, 64, 256 * h, 64 * h, 0, 256) for h in range(2)]
TAIL += [(320, 32, 128 * h, 32 * h, 256, 128) for h in range(4)]


def tail_pieces(shard):
    for row, rows, column, at, start, width in TAIL:
        yield (
            shard.at[:, pl.ds(row, rows), pl.ds(column, width)],
            (slice(None), pl.ds(at, rows), pl.ds(start, width)),
        )


def tail_loads(full, tail, sems):
    return [
        pltpu.make_async_copy(src, tail.at[at], sems.at[i])
        for i, (src, at) in enumerate(tail_pieces(full))
    ]


def down_blocks(shard, down):
    return [
        (shard.at[4 * c + j, pl.ds(352, 176), :], down.at[c, pl.ds(176 * j, 176), :])
        for c in range(4)
        for j in range(4)
    ]


def mlp_kernel(
    four,
    core,
    cot_four,
    cot_core,
    panel_ref,
    full,
    ggu_ref,
    act_ref,
    send,
    down,
    tail,
    gpan,
    gtail,
    gdown,
    four_ref,
    core_ref,
    cot_four_ref,
    cot_core_ref,
    in_sem,
    row_sem,
    tail_sem,
    pan_sem,
    out_sem,
):
    step = pl.program_id(0)
    loads = [
        pltpu.make_async_copy(src, dst, in_sem.at[i])
        for i, (src, dst) in enumerate(
            [(cot_four, cot_four_ref), (cot_core, cot_core_ref)] + down_blocks(full, down)
        )
    ]
    rows_in = [
        pltpu.make_async_copy(src, dst, row_sem.at[i])
        for i, (src, dst) in enumerate([(four, four_ref), (core, core_ref)])
    ]
    tails = tail_loads(full, tail, tail_sem)

    @pl.when(step == 0)
    def _():
        for copy in rows_in + loads + tails:
            copy.start()
        for copy in rows_in + loads:
            copy.wait()

    def panel_out(at):
        return pltpu.make_async_copy(
            gpan.at[at], send.at[:, pl.ds(128 * at, 128), :], pan_sem.at[at]
        )

    def block(weights, start, width, store):
        halves_of = [dot(ref[...], weights) for ref in (four_ref, core_ref)]

        for half, (h, c_ref) in enumerate(zip(halves_of, (cot_four_ref, cot_core_ref))):
            rows = pl.ds(half * (ALL // 2), ALL // 2)
            gate, up = h[:, :width], h[:, width:]
            prod = right_product(c_ref[:, :PANEL], down[0, pl.ds(start, width), :])
            for c in range(1, 4):
                prod += right_product(
                    c_ref[:, c * PANEL : (c + 1) * PANEL], down[c, pl.ds(start, width), :]
                )
            sig = 1.0 / (1.0 + jnp.exp(-gate))
            silu = gate * sig
            act_ref[rows, :width] = (silu * up).astype(BF)
            ggu_ref[rows, :width] = (prod * up * sig * (1.0 + gate * (1.0 - sig))).astype(BF)
            ggu_ref[rows, width : 2 * width] = (prod * silu).astype(BF)
        for c in range(4):
            columns = slice(c * PANEL, (c + 1) * PANEL)
            grads = left_product(act_ref[: ALL // 2, :width], cot_four_ref[:, columns])
            grads += left_product(act_ref[ALL // 2 :, :width], cot_core_ref[:, columns])
            gdown[c, pl.ds(start, width), :] = grads.astype(BF)
        grads = left_product(four_ref[...], ggu_ref[: ALL // 2, : 2 * width])
        grads += left_product(core_ref[...], ggu_ref[ALL // 2 :, : 2 * width])
        store(grads.astype(BF))

    @pl.when(step < 2)
    def _():
        def store(grads):
            gpan[step] = grads.reshape(16, 128, PANEL)

        block(panel_ref[...].reshape(D, PANEL), pl.multiple_of(256 * step, 256), 256, store)
        panel_out(step).start()

    @pl.when(step == 2)
    def _():
        def store(grads):
            gtail[...] = grads.reshape(16, 128, 2 * LAST)

        for copy in tails:
            copy.wait()
        block(tail[...].reshape(D, 2 * LAST), 512, LAST, store)
        outs = [
            pltpu.make_async_copy(gtail.at[at], dst, tail_sem.at[i])
            for i, (dst, at) in enumerate(tail_pieces(send))
        ]
        outs += [
            pltpu.make_async_copy(src, dst, out_sem.at[i])
            for i, (dst, src) in enumerate(down_blocks(send, gdown))
        ]
        for copy in outs:
            copy.start()
        for copy in outs + [panel_out(0), panel_out(1)]:
            copy.wait()


def mlp_grads(four, core, cot_four, cot_core, full):
    return pl.pallas_call(
        mlp_kernel,
        grid=(3,),
        in_specs=[pl.BlockSpec(memory_space=pl.ANY)] * 4
        + [
            pl.BlockSpec((16, 128, PANEL), lambda i: (0, jnp.minimum(i, 1), 0)),
            pl.BlockSpec(memory_space=pl.ANY),
        ],
        out_specs=[
            pl.BlockSpec((ALL, 512), lambda i: (0, i)),
            pl.BlockSpec((ALL, 256), lambda i: (0, i)),
            pl.BlockSpec(memory_space=pl.ANY),
        ],
        out_shape=[
            jax.ShapeDtypeStruct((ALL, 1536), BF),
            jax.ShapeDtypeStruct((ALL, 768), BF),
            jax.ShapeDtypeStruct((16, SHARD, PANEL), BF),
        ],
        scratch_shapes=[
            pltpu.VMEM((4, UNITS, PANEL), BF),
            pltpu.VMEM((16, 128, 2 * LAST), BF),
            pltpu.VMEM((2, 16, 128, PANEL), BF),
            pltpu.VMEM((16, 128, 2 * LAST), BF),
            pltpu.VMEM((4, UNITS, PANEL), BF),
            pltpu.VMEM((ALL // 2, D), BF),
            pltpu.VMEM((ALL // 2, D), BF),
            pltpu.VMEM((ALL // 2, D), BF),
            pltpu.VMEM((ALL // 2, D), BF),
            pltpu.SemaphoreType.DMA((18,)),
            pltpu.SemaphoreType.DMA((2,)),
            pltpu.SemaphoreType.DMA((6,)),
            pltpu.SemaphoreType.DMA((2,)),
            pltpu.SemaphoreType.DMA((16,)),
        ],
        compiler_params=pltpu.CompilerParams(vmem_limit_bytes=56 * 2**20),
        cost_estimate=pl.CostEstimate(
            flops=18 * 10**9, bytes_accessed=45 * 10**6, transcendentals=10**6
        ),
        name="mlp_grads",
    )(four, core, cot_four, cot_core, full, full)


def split_rows(total, rest_ref, own_ref=None):
    if own_ref is None:
        rest_ref[...] = total.astype(BF)
    else:
        own_ref[...] = total[:ROWS]
        rest_ref[...] = total[ROWS : ALL // 2].astype(BF)


def second_kernel(g_ref, panel_ref, wide_ref, narrow_ref, *outs):
    *outs, tail = outs
    for row, rows, column, at, start, width in TAIL:
        piece = wide_ref if row == 256 else narrow_ref
        tail[:, at : at + rows, start : start + width] = piece[:, :, column : column + width]
    total = right_product(g_ref[:, :PANEL], panel_ref[:, :128].reshape(PANEL, PANEL))
    total += right_product(
        g_ref[:, PANEL : 2 * PANEL], panel_ref[:, 128:].reshape(PANEL, PANEL)
    )
    total += right_product(
        g_ref[:, 2 * PANEL : 2 * PANEL + 2 * LAST], tail[...].reshape(PANEL, 2 * LAST)
    )
    split_rows(total, *outs)


def second_grad(ggu, full, half):
    rows = [ALL // 2] if half else [ALL // 2 - ROWS, ROWS]
    return pl.pallas_call(
        second_kernel,
        grid=(4,),
        in_specs=[
            pl.BlockSpec((ALL // 2, 1536), lambda i: (half, 0)),
            pl.BlockSpec((4, 256, PANEL), lambda i: (i, 0, 0)),
            pl.BlockSpec((4, 64, PANEL), lambda i: (i, 4, 0)),
            pl.BlockSpec((4, 32, PANEL), lambda i: (i, 10, 0)),
        ],
        out_specs=[pl.BlockSpec((r, PANEL), lambda i: (0, i)) for r in rows],
        out_shape=[jax.ShapeDtypeStruct((r, D), kind) for r, kind in zip(rows, (BF, F32))],
        scratch_shapes=[pltpu.VMEM((4, 128, 2 * LAST), BF)],
        compiler_params=pltpu.CompilerParams(vmem_limit_bytes=58 * 2**20),
        cost_estimate=pl.CostEstimate(
            flops=3 * 10**9, bytes_accessed=10 * 10**6, transcendentals=0
        ),
        name="second_grad",
    )(ggu, full, full, full)


def down_kernel(act_ref, down_ref, core_ref, rest_ref, own_ref):
    part = dot(act_ref[:, :UNITS], down_ref[...].reshape(UNITS, PANEL))
    split_rows(part, rest_ref, own_ref)
    core_ref[...] = part[ALL // 2 :].astype(BF)


def down_product(active, full):
    rows = [ALL // 2, ALL // 2 - ROWS, ROWS]
    return pl.pallas_call(
        down_kernel,
        grid=(4,),
        in_specs=[
            pl.BlockSpec((ALL, 768), lambda c: (0, 0)),
            pl.BlockSpec((4, 176, PANEL), lambda c: (c, 2, 0)),
        ],
        out_specs=[pl.BlockSpec((r, PANEL), lambda c: (0, c)) for r in rows],
        out_shape=[jax.ShapeDtypeStruct((r, D), kind) for r, kind in zip(rows, (BF, BF, F32))],
        compiler_params=pltpu.CompilerParams(vmem_limit_bytes=58 * 2**20),
        cost_estimate=pl.CostEstimate(
            flops=3 * 10**9, bytes_accessed=12 * 10**6, transcendentals=0
        ),
        name="down_product",
    )(active, full)


LANES = 128


def lanes_of(v):
    return lax.broadcasted_iota(jnp.int32, v.shape, v.ndim - 1)


def quarter_turn(v):
    first = lanes_of(v) % HEAD_DIM < HEAD_DIM // 2
    return jnp.where(first, -pltpu.roll(v, 96, 1), pltpu.roll(v, 32, 1))


def doubled(v):
    left = lanes_of(v) < HEAD_DIM
    other = pltpu.roll(v, HEAD_DIM, 1)
    return jnp.where(left, v, other), jnp.where(left, other, v)


def head_rows(ref):
    blocks = []
    for g in range(GROUPS // 2):
        v = ref[:, g * LANES : (g + 1) * LANES].astype(F32)
        left = lanes_of(v) < HEAD_DIM
        blocks += [jnp.where(left, v, 0.0), jnp.where(left, 0.0, v)]
    return jnp.concatenate(blocks, axis=0).astype(BF)


def pair_columns(v, g):
    even = v[2 * g * ROWS : (2 * g + 1) * ROWS]
    odd = v[(2 * g + 1) * ROWS : (2 * g + 2) * ROWS]
    return jnp.where(lanes_of(even) < HEAD_DIM, even, odd)


def softmax_rows(heads, key2, mask):
    scores = right_product(heads, key2).reshape(GROUPS, ROWS, ROWS) * score_scale
    masked = jnp.where(mask[None] > 0.0, scores, -1e30)
    top = jnp.max(masked, axis=-1, keepdims=True)
    total = top + jnp.log(jnp.sum(jnp.exp(masked - top), axis=-1, keepdims=True))
    return jnp.exp(masked - total).reshape(GROUPS * ROWS, ROWS)


def seq_rows(step):
    return pl.ds(pl.multiple_of(jnp.minimum(step, MEMBERS - 1) * ROWS, ROWS), ROWS)


def attention_kernel(
    first_ref,
    weight_ref,
    cos_ref,
    sin_ref,
    mask_ref,
    query_ref,
    kv_ref,
    att_ref,
    near_ref,
    core_ref,
    qkv,
    att,
):
    step = pl.program_id(0)

    @pl.when(step == 0)
    def _():
        qkv[...] = dot(first_ref[...], weight_ref[:, QW:])

    @pl.when(step < MEMBERS)
    def _():
        rows = seq_rows(step)
        cosine, sine = cos_ref[...], sin_ref[...]
        for g in range(GROUPS // 2):
            v = qkv[rows, g * LANES : (g + 1) * LANES]
            query_ref[:, g * LANES : (g + 1) * LANES] = (
                v * cosine + quarter_turn(v) * sine
            ).astype(BF)
        v = qkv[rows, QW:]
        kv = jnp.where(lanes_of(v) < HEAD_DIM, v * cosine + quarter_turn(v) * sine, v)
        kv_ref[...] = kv.astype(BF)
        key2, value2 = doubled(kv)
        probs = softmax_rows(head_rows(query_ref), key2.astype(BF), mask_ref[0])
        heads = dot(probs.astype(BF), value2.astype(BF))
        for g in range(GROUPS // 2):
            pair = pair_columns(heads, g).astype(BF)
            att_ref[:, g * LANES : (g + 1) * LANES] = pair
            att[rows, g * LANES : (g + 1) * LANES] = pair

    @pl.when(step >= MEMBERS)
    def _():
        block = pl.ds(pl.multiple_of((step - MEMBERS) * QW, QW), QW)
        part = dot(att[...], weight_ref[block, :QW])
        near_ref[...] = part[: SLOTS // 2]
        core_ref[...] = part[SLOTS // 2 :].astype(BF)


def attention_back_kernel(
    middle_ref,
    weight_ref,
    first_ref,
    att_ref,
    query_ref,
    kv_ref,
    cos_ref,
    sin_ref,
    mask_ref,
    grad_ref,
    send_ref,
    upstream,
    grads,
):
    step = pl.program_id(0)

    @pl.when(step == 0)
    def _():
        total = right_product(middle_ref[:, :PANEL], weight_ref[:QW, :QW])
        for c in range(1, 4):
            total += right_product(
                middle_ref[:, c * PANEL : (c + 1) * PANEL],
                weight_ref[c * QW : (c + 1) * QW, :QW],
            )
        upstream[...] = total.astype(BF)

    @pl.when(step < MEMBERS)
    def _():
        rows = seq_rows(step)
        cosine, sine = cos_ref[...], sin_ref[...]
        key2, value2 = doubled(kv_ref[...].astype(F32))
        key2, value2 = key2.astype(BF), value2.astype(BF)
        heads, lifted = head_rows(query_ref), head_rows(upstream.at[rows])
        probs = softmax_rows(heads, key2, mask_ref[0])
        grad_value = left_product(probs.astype(BF), lifted)
        grad_value = grad_value + pltpu.roll(grad_value, HEAD_DIM, 1)
        grad_probs = right_product(lifted, value2)
        inner = jnp.sum(grad_probs * probs, axis=-1, keepdims=True)
        grad_scores = (probs * (grad_probs - inner)).astype(BF)
        grad_query = dot(grad_scores, key2)
        for g in range(GROUPS // 2):
            v = pair_columns(grad_query, g) * score_scale
            v = (v * cosine - quarter_turn(v) * sine).astype(BF)
            grad_ref[:, g * LANES : (g + 1) * LANES] = v
            grads[rows, g * LANES : (g + 1) * LANES] = v
        grad_key = left_product(grad_scores, heads)
        v = (grad_key + pltpu.roll(grad_key, HEAD_DIM, 1)) * score_scale
        grad_key = v * cosine - quarter_turn(v) * sine
        v = jnp.where(lanes_of(v) < HEAD_DIM, grad_key, grad_value).astype(BF)
        grad_ref[:, QW:] = v
        grads[rows, QW:] = v

    @pl.when(step >= MEMBERS)
    def _():
        block = pl.ds(pl.multiple_of((step - MEMBERS) * PANEL, PANEL), PANEL)
        send_ref[:, :QW] = left_product(att_ref[...], middle_ref[:, block]).astype(BF)
        send_ref[:, QW:] = left_product(first_ref[:, block], grads[...]).astype(BF)


def all_of(shape):
    return pl.BlockSpec(shape, lambda s: (0,) * len(shape), pipeline_mode=pl.Buffered(1))


def by_seq(width):
    return pl.BlockSpec((ROWS, width), lambda s: (jnp.minimum(s, MEMBERS - 1), 0))


MASK_BLOCK = pl.BlockSpec((1, ROWS, ROWS), lambda s: (jnp.minimum(s, MEMBERS - 1), 0, 0))


def attention(first_low, weights, cosine, sine, mask):
    half = pl.BlockSpec((SLOTS // 2, PANEL), lambda s: (0, jnp.maximum(s - MEMBERS, 0)))
    return pl.pallas_call(
        attention_kernel,
        grid=(2 * MEMBERS,),
        in_specs=[
            all_of((SLOTS, D)),
            all_of((D, QW + QKVW)),
            by_seq(LANES),
            by_seq(LANES),
            MASK_BLOCK,
        ],
        out_specs=[by_seq(QW), by_seq(LANES), by_seq(QW), half, half],
        out_shape=[
            jax.ShapeDtypeStruct((SLOTS, QW), BF),
            jax.ShapeDtypeStruct((SLOTS, LANES), BF),
            jax.ShapeDtypeStruct((SLOTS, QW), BF),
            jax.ShapeDtypeStruct((SLOTS // 2, D), F32),
            jax.ShapeDtypeStruct((SLOTS // 2, D), BF),
        ],
        scratch_shapes=[pltpu.VMEM((SLOTS, QKVW), F32), pltpu.VMEM((SLOTS, QW), BF)],
        compiler_params=pltpu.CompilerParams(vmem_limit_bytes=40 * 2**20),
        cost_estimate=pl.CostEstimate(
            flops=3 * 10**9, bytes_accessed=12 * 10**6, transcendentals=10**6
        ),
        name="attention",
    )(first_low, weights, cosine, sine, mask)


def attention_back(middle_all, weights, first_low, attended, query, kv, cosine, sine, mask):
    return pl.pallas_call(
        attention_back_kernel,
        grid=(2 * MEMBERS,),
        in_specs=[
            all_of((SLOTS, D)),
            all_of((D, QW + QKVW)),
            all_of((SLOTS, D)),
            all_of((SLOTS, QW)),
            by_seq(QW),
            by_seq(LANES),
            by_seq(LANES),
            by_seq(LANES),
            MASK_BLOCK,
        ],
        out_specs=[
            by_seq(QKVW),
            pl.BlockSpec((PANEL, QW + QKVW), lambda s: (jnp.maximum(s - MEMBERS, 0), 0)),
        ],
        out_shape=[
            jax.ShapeDtypeStruct((SLOTS, QKVW), BF),
            jax.ShapeDtypeStruct((D, QW + QKVW), BF),
        ],
        scratch_shapes=[pltpu.VMEM((SLOTS, QW), BF), pltpu.VMEM((SLOTS, QKVW), BF)],
        compiler_params=pltpu.CompilerParams(vmem_limit_bytes=40 * 2**20),
        cost_estimate=pl.CostEstimate(
            flops=5 * 10**9, bytes_accessed=16 * 10**6, transcendentals=10**6
        ),
        name="attention_back",
    )(middle_all, weights, first_low, attended, query, kv, cosine, sine, mask)


def first_kernel(grad_ref, weight_ref, rows_ref, rms_ref, near_ref, core_ref, gain_ref):
    grad = right_product(grad_ref[...], weight_ref[:, QW:])
    normed = rows_ref[...].astype(F32) * rms_ref[...]
    gain_ref[...] = jnp.sum(grad * normed, axis=0, keepdims=True)
    near_ref[...] = grad[: SLOTS // 2]
    core_ref[...] = grad[SLOTS // 2 :].astype(BF)


def first_grad(grad_qkv, weights, rows_in, rms):
    half = pl.BlockSpec((SLOTS // 2, PANEL), lambda i: (0, i))
    return pl.pallas_call(
        first_kernel,
        grid=(4,),
        in_specs=[
            all_of((SLOTS, QKVW)),
            pl.BlockSpec((PANEL, QW + QKVW), lambda i: (i, 0)),
            pl.BlockSpec((SLOTS, PANEL), lambda i: (0, i)),
            all_of((SLOTS, 1)),
        ],
        out_specs=[half, half, pl.BlockSpec((1, PANEL), lambda i: (0, i))],
        out_shape=[
            jax.ShapeDtypeStruct((SLOTS // 2, D), F32),
            jax.ShapeDtypeStruct((SLOTS // 2, D), BF),
            jax.ShapeDtypeStruct((1, D), F32),
        ],
        compiler_params=pltpu.CompilerParams(vmem_limit_bytes=32 * 2**20),
        cost_estimate=pl.CostEstimate(
            flops=14 * 10**8, bytes_accessed=12 * 10**6, transcendentals=0
        ),
        name="first_grad",
    )(grad_qkv, weights, rows_in, rms)


def update_kernel(
    at_ref,
    own_ref,
    near_ref,
    core_ref,
    moments_ref,
    moment_ref,
    query_ref,
    key_ref,
    value_ref,
    output_ref,
    query_moved,
    key_moved,
    value_moved,
    output_moved,
    query_new,
    key_new,
    value_new,
    output_new,
    moved,
):
    width = QKVW + PANEL
    own = 0.5 * moment_ref[...] + 0.5 * own_ref[...]
    query_moved[...] = own[:, :QW]
    key_moved[...] = own[:, QW : QW + KW]
    value_moved[...] = own[:, QW + KW : QKVW]
    output_moved[...] = own[:, QKVW:]
    rows = near_ref.shape[0]
    moved[:rows] = 0.5 * moments_ref[:rows].astype(F32) + 0.5 * near_ref[...].astype(F32)
    moved[rows:] = 0.5 * moments_ref[rows:].astype(F32) + 0.5 * core_ref[:, :width].astype(F32)
    pairs = []
    for a, order in enumerate((0, 2, 1, 3)):
        slot = pl.ds(pl.multiple_of((at_ref[0] ^ order) * W_ROWS, W_ROWS), W_ROWS)
        columns = slice(a * QW, (a + 1) * QW)
        query_new[:, columns] = query_ref[:, columns] - learn_rate * moved[slot, :QW]
        output_new[:, columns] = output_ref[:, columns] - learn_rate * moved[slot, QKVW:]
        pairs.append(moved[slot, QW:QKVW])
    for a in (0, 2):
        even, odd = pairs[a], pairs[a + 1]
        left = lanes_of(even) < HEAD_DIM
        key = jnp.where(left, even, pltpu.roll(odd, HEAD_DIM, 1))
        value = jnp.where(left, pltpu.roll(even, HEAD_DIM, 1), odd)
        columns = slice(a * KW, (a + 2) * KW)
        key_new[:, columns] = key_ref[:, columns] - learn_rate * key
        value_new[:, columns] = value_ref[:, columns] - learn_rate * value


def attention_update(at, own, near, core, moments, moment, weights):
    shapes = [(W_ROWS, w) for w in (QW, KW, KW, QW)] + [w.shape for w in weights]
    vmem = pl.BlockSpec(memory_space=pltpu.VMEM)
    return pl.pallas_call(
        update_kernel,
        in_specs=[pl.BlockSpec(memory_space=pltpu.SMEM)] + [vmem] * 9,
        out_specs=[vmem] * 8,
        out_shape=[jax.ShapeDtypeStruct(shape, F32) for shape in shapes],
        scratch_shapes=[pltpu.VMEM((MEMBERS * W_ROWS, QKVW + PANEL), F32)],
        compiler_params=pltpu.CompilerParams(vmem_limit_bytes=16 * 2**20),
        cost_estimate=pl.CostEstimate(
            flops=10**6, bytes_accessed=6 * 10**6, transcendentals=0
        ),
        name="attention_update",
    )(at, own, near, core, moments, moment, *weights)


def rounded_gain(gain):
    return lax.optimization_barrier(gain.astype(BF)).astype(F32)


def inverse_rms(v):
    return lax.rsqrt(jnp.mean(v * v, axis=-1, keepdims=True) + epsilon)


def norm_back(v, gain, grad):
    r = inverse_rms(v)
    n = v * r
    scaled = grad * gain
    return r * (scaled - n * jnp.mean(scaled * n, axis=-1, keepdims=True)), n


def panels(gate, up):
    blocks = []
    for at in range(0, UNITS, 256):
        blocks += [gate[:, at : at + 256], up[:, at : at + 256]]
    return jnp.concatenate(blocks, axis=1)


def unpanels(v):
    gate = [v[:, :256], v[:, 512:768], v[:, 1024 : 1024 + LAST]]
    up = [v[:, 256:512], v[:, 768:1024], v[:, 1024 + LAST :]]
    return jnp.concatenate(gate, axis=1), jnp.concatenate(up, axis=1)


def on_device(
    tokens,
    cotangent,
    segment_ids,
    positions,
    padding,
    attn_gain,
    query_weight,
    key_weight,
    value_weight,
    output_weight,
    mlp_gain,
    gate_weight,
    up_weight,
    down_weight,
    attn_moment,
    query_moment,
    key_moment,
    value_moment,
    output_moment,
    mlp_moment,
    gate_moment,
    up_moment,
    down_moment,
):
    member = lax.axis_index("grp")
    place = lax.axis_index("dp")
    z, y, low = place // 8, (place // 2) % 4, (place % 2) == 0

    def mine(weight, width):
        return lax.dynamic_slice_in_dim(weight, member * width, width, 1).astype(BF)

    attn_shard = jnp.concatenate(
        [mine(query_weight, QW), mine(key_weight, KW), mine(value_weight, KW)], axis=1
    )
    attn_shard = jnp.concatenate(
        [turn_pair(mine(output_weight, QW), low), pair_x(attn_shard, low)], axis=1
    )
    attn_full = plane_gather(attn_shard)

    gate_mine, up_mine = mine(gate_weight, FW), mine(up_weight, FW)
    first = panels(gate_mine[:, :UNITS], up_mine[:, :UNITS])
    second = panels(gate_mine[:, UNITS:], up_mine[:, UNITS:])
    kept, given = jnp.where(low, first, second), jnp.where(low, second, first)
    gu_shard = in_order(kept, swap_x(given), low)
    tail = gu_shard[:, 2 * PANEL :]
    pieces = [
        gu_shard[:, :PANEL],
        gu_shard[:, PANEL : 2 * PANEL],
        jnp.concatenate([tail[:W_ROWS, :256], tail[W_ROWS:, :256]], axis=1),
        jnp.concatenate([tail[32 * h : 32 * h + 32, 256:] for h in range(4)], axis=1),
        everywhere(mine(down_weight, PANEL), OWNED),
    ]
    mlp_full = plane_gather(jnp.concatenate(pieces, axis=0)).reshape(16, SHARD, PANEL)

    places = jnp.stack([segment_ids, positions, padding])[None]
    rows_in = group_gather(tokens)
    own_moment = jnp.concatenate(
        [query_moment, key_moment, value_moment, output_moment], axis=1
    )
    moments = own_moment.astype(BF)
    places, moments, upstream = lax.optimization_barrier(
        (
            jnp.concatenate([places, swap_far(places)], axis=0),
            jnp.concatenate([moments, swap_far(moments)], axis=0),
            cotangent,
        )
    )
    cot_four, cot_core = row_gather(upstream)
    places = jnp.concatenate([places, swap_core(places)], axis=0)
    moments = jnp.concatenate([moments, swap_core(moments)], axis=0)
    segments, spots, pads = places[:, 0], places[:, 1], places[:, 2]

    first_gain = rounded_gain(attn_gain)
    second_gain = rounded_gain(mlp_gain)
    inputs = rows_in.astype(F32)
    rms = inverse_rms(inputs)
    first_low = (inputs * rms * first_gain).astype(BF)

    half = HEAD_DIM // 2
    freq = 10000.0 ** (-(jnp.arange(half, dtype=F32) * 2.0 / HEAD_DIM))
    angles = spots.reshape(SLOTS, 1).astype(F32) * jnp.tile(freq, LANES // half)[None]
    cosine, sine = jnp.cos(angles), jnp.sin(angles)
    column = jnp.arange(ROWS, dtype=jnp.int32)
    allowed = jnp.logical_and(
        jnp.logical_and(
            segments[:, :, None] == segments[:, None, :],
            (column[None, :] <= column[:, None])[None],
        ),
        jnp.logical_or(pads[:, None, :] == 1, (column[None, :] == column[:, None])[None]),
    ).astype(F32)

    attn_full, first_low, cosine, sine, allowed, cot_four, moments = lax.optimization_barrier(
        (attn_full, first_low, cosine, sine, allowed, cot_four, moments)
    )
    query_rot, kv, attended, near, core = attention(first_low, attn_full, cosine, sine, allowed)
    middle = tokens.astype(F32) + group_scatter_far(near + swap_core(core).astype(F32))
    second_low = (middle * inverse_rms(middle) * second_gain).astype(BF)
    four, core_four = row_gather(second_low)
    core_four, cot_core = lax.optimization_barrier((core_four, cot_core))
    grad_gu, active, send = mlp_grads(four, core_four, cot_four, cot_core, mlp_full)
    mlp_sum = plane_scatter(send.reshape(16 * SHARD, PANEL))

    second_core = swap_core(second_grad(grad_gu, mlp_full, 1)[0])
    second_rest, second_own = second_grad(grad_gu, mlp_full, 0)
    grad_second = row_scatter(second_own, second_rest, second_core)
    back, n_second = norm_back(middle, second_gain, grad_second)
    mlp_gain_part = jnp.sum(grad_second * n_second, axis=0)
    grad_middle = cotangent.astype(F32) + back
    middle_all = group_gather(grad_middle.astype(BF))
    down_core, down_rest, down_own = down_product(active, mlp_full)
    middle_all, down_core = lax.optimization_barrier((middle_all, swap_core(down_core)))
    grad_qkv, attn_send = attention_back(
        middle_all, attn_full, first_low, attended, query_rot, kv, cosine, sine, allowed
    )
    attn_sum = plane_scatter(attn_send)

    grad_qkv, mlp_sum, down_core = lax.optimization_barrier((grad_qkv, mlp_sum, down_core))
    block_output = (middle + row_scatter(down_own, down_rest, down_core)).astype(BF)
    near, core, attn_gain_part = first_grad(grad_qkv, attn_full, rows_in, rms)
    gains = jnp.concatenate([attn_gain_part, mlp_gain_part[None]], axis=0).reshape(32, LANES)
    for pairs in (RING_Z, RING_Y):
        gains = gains + sum(lax.ppermute(gains, "dp", p) for p in pairs)
    near = near + swap_core(core).astype(F32)
    back, _ = norm_back(tokens.astype(F32), first_gain, group_scatter_far(near))
    input_grad = grad_middle + back

    mine_at = (member // 2) + 2 * (member % 2)

    def by_member(slots):
        return [
            lax.dynamic_index_in_dim(slots, mine_at ^ at, 0, keepdims=False) for at in (0, 2, 1, 3)
        ]

    def updated(weight, columns, start, size):
        moved = jnp.concatenate([block[:, start : start + size] for block in columns], axis=1)
        return weight - learn_rate * moved.astype(F32)

    wide, narrow = mlp_sum[256:320], mlp_sum[320:352]
    gu_part = jnp.concatenate(
        [
            mlp_sum[:128],
            mlp_sum[128:256],
            jnp.concatenate([wide[:, :256], wide[:, 256:]], axis=0),
            jnp.concatenate([narrow[:, h * LANES : (h + 1) * LANES] for h in range(4)], axis=0),
        ],
        axis=1,
    )
    kept, given = halves(gu_part, low)
    other = swap_x(given)
    first = unpanels(jnp.where(low, kept, other))
    second = unpanels(jnp.where(low, other, kept))
    gate_rows = jnp.concatenate([first[0], second[0]], axis=1).astype(F32)
    up_rows = jnp.concatenate([first[1], second[1]], axis=1).astype(F32)
    down_rows = everywhere(mlp_sum[352:], RETURN).astype(F32)
    gate_momentum = 0.5 * gate_moment + 0.5 * gate_rows
    up_momentum = 0.5 * up_moment + 0.5 * up_rows
    down_momentum = 0.5 * down_moment + 0.5 * down_rows
    gu_moved = jnp.concatenate([gate_momentum, up_momentum], axis=1).astype(BF)
    gu_moved, block_output = lax.optimization_barrier((gu_moved, block_output))
    gu_moved, down_moved = group_gather(gu_moved), group_gather(down_momentum.astype(BF))

    attn_sum, gains, input_grad, block_output, gu_moved, down_moved = lax.optimization_barrier(
        (attn_sum, gains, input_grad, block_output, gu_moved, down_moved)
    )
    gu_moved = by_member(gu_moved.reshape(MEMBERS, W_ROWS, GUW))
    down_moved = by_member(down_moved.reshape(MEMBERS, DOWN_ROWS, PANEL))
    gate_updated = updated(gate_weight, gu_moved, 0, FW)
    up_updated = updated(up_weight, gu_moved, FW, FW)
    down_updated = updated(down_weight, down_moved, 0, PANEL)

    turned = everywhere(attn_sum[:, :QW], TURN)
    both = jnp.concatenate([attn_sum[:, QW:], turned], axis=1)
    gains = two_parts(gains)
    kept, given = halves(both, low)
    width = QKVW + PANEL
    near = swap_x(jnp.concatenate([given, gains], axis=1))
    far = swap_far(jnp.concatenate([kept, gains], axis=1))
    both_far = far_x(jnp.concatenate([given, gains], axis=1))
    own_total = kept.astype(F32) + near[:, :width].astype(F32)
    far_total = far[:, :width].astype(F32) + both_far[:, :width].astype(F32)
    gains = sum(one_part(part) for part in (gains, near[:, width:], far[:, width:], both_far[:, width:]))
    totals = jnp.concatenate([own_total, far_total], axis=0).astype(BF)
    rider = jnp.concatenate([two_parts(gains), jnp.zeros((W_ROWS, LANES), BF)], axis=0)
    other = swap_core(jnp.concatenate([totals, rider], axis=1))
    gains = gains + one_part(other[:W_ROWS, width:])
    attn_done = attention_update(
        mine_at.astype(jnp.int32).reshape(1),
        own_total,
        totals,
        other,
        moments,
        own_moment,
        (query_weight, key_weight, value_weight, output_weight),
    )

    gains = 0.5 * jnp.stack([attn_moment, mlp_moment]) + 0.5 * gains.reshape(2, D)
    return (
        block_output,
        input_grad,
        gains[0],
        *attn_done[:4],
        gains[1],
        gate_momentum,
        up_momentum,
        down_momentum,
        attn_gain - learn_rate * gains[0],
        *attn_done[4:],
        mlp_gain - learn_rate * gains[1],
        gate_updated,
        up_updated,
        down_updated,
    )


def solution(mesh):
    rows = P(("grp", "dp"), None)
    flat = P(("grp", "dp"))
    weight = P("dp", None)
    moment = P("dp", "grp")
    everyone = P()
    weights = (everyone,) + (weight,) * 4 + (everyone,) + (weight,) * 3
    moments = (everyone,) + (moment,) * 4 + (everyone,) + (moment,) * 3
    return jax.shard_map(
        on_device,
        mesh=mesh,
        in_specs=(rows, rows, flat, flat, flat) + weights + moments,
        out_specs=(rows, rows) + moments + weights,
        check_vma=False,
    )
```
